32 devices in a mesh: seq: 8 (over z, x), wt: 4 (over y, core).
Axes of the slice: x: 2, y: 2, z: 4, core: 2. Of those that a mesh axis runs over, the one named last changes fastest.
Arguments:
- hidden: bfloat16 [4, 1536, 1536], P('wt', 'seq'), may hold values from -6 to 6
- cotangent: bfloat16 [4, 1536, 1536], P('wt', 'seq'), may hold values from -6 to 6
- segments: int32 [4, 1536], P('wt'), may hold values from 767 to 1535, as said below
- valid: int32 [4, 1536], P('wt', 'seq'), may hold values from 0 to 1
- in_w: float32 [1536, 6448], P(('seq', 'wt')), may hold values from -0.15625 to 0.15625
- in_m: float32 [1536, 6448], P(('seq', 'wt')), may hold values from -128 to 128
- in_v: float32 [1536, 6448], P(('seq', 'wt')), may hold values from 552.96 to 2211.84
- out_w: float32 [3072, 1536], P(('seq', 'wt')), may hold values from -0.109375 to 0.109375
- out_m: float32 [3072, 1536], P(('seq', 'wt')), may hold values from -384 to 384
- out_v: float32 [3072, 1536], P(('seq', 'wt')), may hold values from 3932.16 to 15728.64
- small_w: float32 [21392], replicated, may hold values from -8 to 1.5, as said below
- small_m: float32 [21392], replicated, may hold values from -313.5347 to 313.5347
- small_v: float32 [21392], replicated, may hold values from 245.76 to 24576
Outputs:
- output: bfloat16 [4, 1536, 1536], P('wt', 'seq')
- grad_hidden: float32 [4, 1536, 1536], P('wt', 'seq')
- in_m_new: float32 [1536, 6448], P(('seq', 'wt'))
- in_v_new: float32 [1536, 6448], P(('seq', 'wt'))
- in_w_new: float32 [1536, 6448], P(('seq', 'wt'))
- out_m_new: float32 [3072, 1536], P(('seq', 'wt'))
- out_v_new: float32 [3072, 1536], P(('seq', 'wt'))
- out_w_new: float32 [3072, 1536], P(('seq', 'wt'))
- small_m_new: float32 [21392], replicated
- small_v_new: float32 [21392], replicated
- small_w_new: float32 [21392], replicated
- rms: float32 [2], replicated
The draws below stay inside these ranges and needn't reach their ends.
Inputs may be any that keep to these rules, and one draw needn't show every extreme that they name: `segments`: each token's number is the position, within its stream, of the last token of its document, so numbers never fall along a stream; a new document begins at every multiple of 4096; a document holds at most 2000 tokens; the first document of every stream holds between min(2000, 1536) // 2 and min(2000, 1336) tokens. `small_w`: in order: gains within 0.5 to 1.5, convolution weights and biases within -0.5 to 0.5, dt_bias within -8 to -3, a_log within 0 to 1.5, skip within 0.2 to 1.
All inputs are finite; a program needn't handle non-finite values.
Results may differ from the reference program's by a relative error of at most 0.0081.
The reference program's roundings to bfloat16 on the way count: a program that leaves them out, or rounds other values in their place, can miss the bound.
Values may be sent and summed in bfloat16 or wider, within the bound.
A program may use at most 256 MiB of HBM per device.

```python
import math
import jax
import jax.numpy as jnp
from jax import lax

D = 1536
D_INNER = 3072
HEADS = 48
HEADDIM = 64
STATE = 128
CONV = 4
SPAN = 256
STEP = 4
SEQ_LEN = 4096
DOC_MIN = 200
DOC_MAX = 2000
PROJ = 6448
CONVCH = 3328
SMALL = 21392
GROUPS = 4
STREAM = 1536
TOKENS_ALL = 6144


def stream_segments(key):
    doc_count = STREAM // DOC_MIN + 2
    first_low = min(DOC_MAX, STREAM) // 2
    first_high = max(first_low, min(DOC_MAX, STREAM - DOC_MIN))
    first_key, rest_key = jax.random.split(key)
    first_doc = jax.random.randint(first_key, (1,), first_low, first_high + 1).astype(jnp.int32)
    lengths = jax.random.randint(rest_key, (doc_count,), DOC_MIN, DOC_MAX + 1)
    lengths = jnp.concatenate([first_doc, lengths[1:].astype(jnp.int32)])
    doc_ends = jnp.cumsum(lengths)
    places = jnp.arange(STREAM, dtype=jnp.int32)
    doc_start = jnp.any(places[:, None] == doc_ends[None, :], axis=1)
    new_start = doc_start | (places % SEQ_LEN == 0)
    next_start = jnp.concatenate([new_start[1:], jnp.ones((1,), dtype=bool)])
    marker = jnp.where(next_start, places, STREAM)
    return lax.cummin(marker, axis=0, reverse=True).astype(jnp.int32)


def draw_segments(key, part):
    key = jax.random.fold_in(key, 11)
    return jax.vmap(stream_segments)(jax.random.split(key, GROUPS))


def draw_valid(key, part):
    key = jax.random.fold_in(key, 12)
    places = jnp.arange(GROUPS, dtype=jnp.int32)[:, None] * STREAM + jnp.arange(STREAM, dtype=jnp.int32)[None, :]
    bounds = 250 + 700 * places // (GROUPS * STREAM)
    picks = jax.random.randint(key, (GROUPS, STREAM), 0, 1000)
    return (picks < bounds).astype(jnp.int32)


def draw_hidden(key, part):
    key = jax.random.fold_in(key, 16)
    values = jnp.clip(jax.random.normal(key, (GROUPS, STREAM, D), jnp.float32), -6.0, 6.0)
    return values.astype(jnp.bfloat16)


def small_scales():
    marks = jnp.arange(SMALL, dtype=jnp.int32)
    conv_end = D + D_INNER + CONV * CONVCH
    limits = [D, D + D_INNER, conv_end, conv_end + CONVCH, conv_end + CONVCH + HEADS, conv_end + CONVCH + 2 * HEADS]
    factors = [0.3, 0.3, 0.2, 0.2, 0.3, 0.3, 1.0]
    scales = jnp.full((SMALL,), factors[-1], jnp.float32)
    for limit_at, factor in reversed(list(zip(limits, factors[:-1]))):
        scales = jnp.where(marks < limit_at, factor, scales)
    return scales * TOKENS_ALL ** 0.5


def draw_small_w(key, part):
    key = jax.random.fold_in(key, 13)
    sub_keys = jax.random.split(key, 7)
    pre_gain = jax.random.uniform(sub_keys[0], (D,), jnp.float32, 0.5, 1.5)
    norm_gain = jax.random.uniform(sub_keys[1], (D_INNER,), jnp.float32, 0.5, 1.5)
    conv_weight = jax.random.uniform(sub_keys[2], (CONV * CONVCH,), jnp.float32, -0.5, 0.5)
    conv_bias = jax.random.uniform(sub_keys[3], (CONVCH,), jnp.float32, -0.5, 0.5)
    dt_shift = jax.random.uniform(sub_keys[4], (HEADS,), jnp.float32, -8.0, -3.0)
    a_logs = jax.random.uniform(sub_keys[5], (HEADS,), jnp.float32, 0.0, 1.5)
    skips = jax.random.uniform(sub_keys[6], (HEADS,), jnp.float32, 0.2, 1.0)
    return jnp.concatenate([pre_gain, norm_gain, conv_weight, conv_bias, dt_shift, a_logs, skips])


def draw_small_m(key, part):
    key = jax.random.fold_in(key, 14)
    return jnp.clip(jax.random.normal(key, (SMALL,), jnp.float32), -4.0, 4.0) * small_scales()


def draw_small_v(key, part):
    key = jax.random.fold_in(key, 15)
    spread = jax.random.uniform(key, (SMALL,), jnp.float32)
    return small_scales() ** 2 * jnp.exp(spread * jnp.log(4.0))


def levels(stream_key, shape, cuts, least, high):
    def one(axis_at, blocks):
        draws = jax.random.uniform(jax.random.fold_in(jax.random.fold_in(stream_key, 6), axis_at), (blocks,), jnp.float32, least / len(cuts), high / len(cuts))
        return jnp.repeat(jnp.exp(draws), shape[axis_at] // blocks).reshape((-1,) + (1,) * (len(shape) - axis_at - 1))

    level = one(*cuts[0])
    for cut in cuts[1:]:
        level = level * one(*cut)
    return level


def normal_values(rng, extent, deviation, limit, cuts=(), kind=jnp.bfloat16):
    result = jax.random.normal(rng, extent, jnp.float32) * deviation
    if len(cuts) > 0:
        result = levels(rng, extent, cuts, -0.22, 0.18) * result
    return jnp.clip(result, min=-limit, max=limit).astype(kind)


def setup_inputs(seed: int = 0) -> dict:
    splits = jax.random.split(jax.random.key(seed), 14)
    return {
        "hidden": draw_hidden(jax.random.fold_in(splits[13], 71), 0),
        "cotangent": normal_values(splits[1], (GROUPS, STREAM, D), 1.0, 6.0, ((0, 4), (1, 8))),
        "segments": draw_segments(jax.random.fold_in(splits[13], 71), 0),
        "valid": draw_valid(jax.random.fold_in(splits[13], 71), 0),
        "in_w": normal_values(splits[4], (D, PROJ), D ** -0.5, 0.15625, ((0, 32),), jnp.float32),
        "in_m": normal_values(splits[5], (D, PROJ), (0.3 * TOKENS_ALL ** 0.5), 128.0, ((0, 32),), jnp.float32),
        "in_v": jnp.clip(jnp.exp(math.log(2211.84) - 1.3862944 * jax.random.uniform(splits[6], (D, PROJ), jnp.float32) ** levels(splits[6], (D, PROJ), ((0, 32),), -0.2, 0.2)), 552.96, 2211.84),
        "out_w": normal_values(splits[7], (D_INNER, D), D_INNER ** -0.5, 0.109375, ((0, 32),), jnp.float32),
        "out_m": normal_values(splits[8], (D_INNER, D), (0.8 * TOKENS_ALL ** 0.5), 384.0, ((0, 32),), jnp.float32),
        "out_v": jnp.clip(jnp.exp(math.log(15728.64) - 1.3862944 * jax.random.uniform(splits[9], (D_INNER, D), jnp.float32) ** levels(splits[9], (D_INNER, D), ((0, 32),), -0.2, 0.2)), 3932.16, 15728.64),
        "small_w": draw_small_w(jax.random.fold_in(splits[13], 71), 0),
        "small_m": draw_small_m(jax.random.fold_in(splits[13], 71), 0),
        "small_v": draw_small_v(jax.random.fold_in(splits[13], 71), 0),
    }


@jax.custom_vjp
def low(v):
    return lax.optimization_barrier(v.astype(jnp.bfloat16)).astype(jnp.float32)

@jax.custom_vjp
def low_back(v):
    return v

def low_keep(v):
    return (low(v), None)

def low_pass(kept, grad):
    return (grad,)

def back_keep(v):
    return (v, None)

def back_low(kept, grad):
    return (low(grad),)
low.defvjp(low_keep, low_pass)
low_back.defvjp(back_keep, back_low)
exact_prec = lax.Precision.HIGHEST
norm_eps = 1e-05
adam_eps = 1e-08

def unpack_small(small):
    first = D
    second = first + D_INNER
    third = second + CONV * CONVCH
    fourth = third + CONVCH
    fifth = fourth + HEADS
    sixth = fifth + HEADS
    return (small[:first], small[first:second], small[second:third].reshape(CONV, CONVCH), small[third:fourth], small[fourth:fifth], small[fifth:sixth], small[sixth:])

def ssd_head(x_rows, b_rows, c_rows, dt_rows, a_rate, skip_one, seg):
    length = x_rows.shape[0]
    blocks = length // SPAN
    x_blocks = x_rows.reshape(blocks, SPAN, -1)
    b_blocks = b_rows.reshape(blocks, SPAN, -1)
    c_blocks = c_rows.reshape(blocks, SPAN, -1)
    dt_blocks = dt_rows.reshape(blocks, SPAN)
    cumulative = jnp.cumsum(dt_blocks * a_rate, axis=1)
    seg_blocks = seg.reshape(blocks, SPAN)
    seg_prev = jnp.concatenate([jnp.full((1,), -1, jnp.int32), seg_blocks[:-1, -1]])
    causal = jnp.arange(SPAN)[:, None] >= jnp.arange(SPAN)[None, :]
    same_doc = (seg_blocks[:, :, None] == seg_blocks[:, None, :]) & causal[None]
    log_gap = cumulative[:, :, None] - cumulative[:, None, :]
    decay_mat = jnp.where(same_doc, jnp.exp(jnp.where(same_doc, log_gap, 0.0)), 0.0)
    scores = jnp.einsum('ctn,csn->cts', c_blocks, b_blocks, precision=exact_prec)
    weighted = scores * decay_mat * dt_blocks[:, None, :]
    y_intra = jnp.einsum('cts,csp->ctp', weighted, x_blocks, precision=exact_prec)
    tail_sum = cumulative[:, -1:]
    keep_end = seg_blocks == seg_blocks[:, -1:]
    end_weight = jnp.where(keep_end, jnp.exp(jnp.where(keep_end, tail_sum - cumulative, 0.0)), 0.0) * dt_blocks
    local_state = jnp.einsum('csn,csp->cnp', b_blocks, end_weight[:, :, None] * x_blocks, precision=exact_prec)
    carry_ok = seg_blocks[:, -1] == seg_prev
    block_decay = jnp.where(carry_ok, jnp.exp(tail_sum[:, 0]), 0.0)

    def advance(carried, pieces):
        factor, fresh_state = pieces
        return (factor * carried + fresh_state, carried)
    start_state = jnp.zeros((b_rows.shape[1], x_rows.shape[1]), jnp.float32)
    unused, state_in = lax.scan(advance, start_state, (block_decay, local_state))
    inflow = seg_blocks == seg_prev[:, None]
    inflow_gain = jnp.where(inflow, jnp.exp(cumulative), 0.0)
    y_inter = jnp.einsum('ctn,cnp->ctp', c_blocks, state_in, precision=exact_prec) * inflow_gain[:, :, None]
    return (y_intra + y_inter + skip_one * x_blocks).reshape(length, -1)

def group_forward(resid, seg, w_in, w_out, small):
    pre_gain, norm_gain, conv_weight, conv_bias, dt_bias, a_log, skip_gain = unpack_small(small)
    length = resid.shape[0]
    scale_pre = lax.rsqrt(lax.optimization_barrier(jnp.mean(resid * resid, axis=1, keepdims=True)) + norm_eps)
    x_normed = low(resid * scale_pre * pre_gain)
    projected = low_back(jnp.dot(x_normed, w_in, precision=exact_prec, preferred_element_type=jnp.float32))
    gate_pre = projected[:, :D_INNER]
    conv_in = low(projected[:, D_INNER:D_INNER + CONVCH])
    dt_raw = low(projected[:, D_INNER + CONVCH:])
    rim_rows = CONV - 1
    padded = jnp.concatenate([jnp.zeros((rim_rows, CONVCH), jnp.float32), conv_in], axis=0)
    seg_pad = jnp.concatenate([jnp.full((rim_rows,), -1, jnp.int32), seg])
    total = conv_bias[None, :]
    for tap_index in range(CONV):
        same_tap = (seg_pad[tap_index:tap_index + length] == seg).astype(jnp.float32)[:, None]
        total = total + conv_weight[tap_index] * padded[tap_index:tap_index + length] * same_tap
    activated = jax.nn.silu(total)
    x_scan = low(low_back(activated[:, :D_INNER]))
    b_mat = low(activated[:, D_INNER:D_INNER + STATE])
    c_mat = low(activated[:, D_INNER + STATE:])
    dt_all = jax.nn.softplus(dt_raw + dt_bias)
    rates = -jnp.exp(a_log)
    heads_x = jnp.transpose(x_scan.reshape(length, HEADS, HEADDIM), (1, 0, 2))

    def one_head(pieces):
        x_rows, dt_rows, a_rate, skip_one = pieces
        return ssd_head(x_rows, b_mat, c_mat, dt_rows, a_rate, skip_one, seg)
    y_heads = lax.map(jax.checkpoint(one_head), (heads_x, dt_all.T, rates, skip_gain))
    y_all = low(low_back(jnp.transpose(y_heads, (1, 0, 2)).reshape(length, D_INNER)))
    gated = y_all * jax.nn.silu(gate_pre)
    scale_gate = lax.rsqrt(lax.optimization_barrier(jnp.mean(gated * gated, axis=1, keepdims=True)) + norm_eps)
    normed = low(gated * scale_gate * norm_gain)
    mixer = jnp.dot(normed, w_out, precision=exact_prec, preferred_element_type=jnp.float32)
    return (resid + mixer, mixer)

def adamw(weight, moment, second, grad, rate, decay):
    moment_new = 0.5 * moment + 0.5 * grad
    second_new = 0.5 * second + 0.5 * grad * grad
    first_hat = moment_new / (1.0 - 0.5 ** STEP)
    second_hat = second_new / (1.0 - 0.5 ** STEP)
    weight_new = weight - rate * (first_hat / (jnp.sqrt(second_hat) + adam_eps) + decay * weight)
    return (moment_new, second_new, weight_new)

def reference(hidden, cotangent, segments, valid, in_w, in_m, in_v, out_w, out_m, out_v, small_w, small_m, small_v):
    resid = hidden.astype(jnp.float32)

    def forward(resid_all, in_master, out_master, small_all):
        w_in = low(in_master)
        w_out = low(out_master)

        def one_group(pieces):
            resid_rows, seg_rows = pieces
            return group_forward(resid_rows, seg_rows, w_in, w_out, small_all)
        return lax.map(jax.checkpoint(one_group), (resid_all, segments))
    (summed, mixer), pull = jax.vjp(forward, resid, in_w, out_w, small_w)
    valid_rows = valid.astype(jnp.float32)
    back = cotangent.astype(jnp.float32) * valid_rows[..., None]
    grad_hidden, grad_in, grad_out, grad_small = pull((back, jnp.zeros_like(mixer)))
    in_m_new, in_v_new, in_w_new = adamw(in_w, in_m, in_v, grad_in, 0.02, 0.1)
    out_m_new, out_v_new, out_w_new = adamw(out_w, out_m, out_v, grad_out, 0.02, 0.1)
    small_m_new, small_v_new, small_w_new = adamw(small_w, small_m, small_v, grad_small, 0.2, 0.0)
    valid_count = jnp.sum(valid_rows)
    res_sq = jnp.sum(valid_rows * lax.optimization_barrier(jnp.sum(resid * resid, axis=2)))
    mix_sq = jnp.sum(valid_rows * lax.optimization_barrier(jnp.sum(mixer * mixer, axis=2)))
    rms = jnp.stack([jnp.sqrt(res_sq / (valid_count * D)), jnp.sqrt(mix_sq / (valid_count * D))])
    return (summed.astype(jnp.bfloat16), grad_hidden, in_m_new, in_v_new, in_w_new, out_m_new, out_v_new, out_w_new, small_m_new, small_v_new, small_w_new, rms)
```

```python
import functools

import jax
import jax.numpy as jnp
from jax import lax
from jax.experimental import pallas as pl
from jax.experimental.pallas import tpu as pltpu
from jax.sharding import Mesh
from jax.sharding import PartitionSpec as P

D = 1536
D_INNER = 3072
HEADS = 48
HEADDIM = 64
STATE = 128
CONV = 4
SPAN = 256
STEP = 4
CONVCH = 3328
TP = 4
RIM = CONV - 1
LANES = 128
HALF = D_INNER // TP
LOCAL_HEADS = HEADS // TP
PAIRS = LOCAL_HEADS // 2
SIDE = 2 * STATE
COL_SIDE = HALF
COL_DT = HALF + SIDE
COL_GATE = COL_DT + LANES
COLS = COL_GATE + HALF

bf16 = jnp.bfloat16
f32 = jnp.float32
exact_prec = lax.Precision.HIGHEST
norm_eps = 1e-05
adam_eps = 1e-08


def dot(a, b, dims=((1,), (0,)), precision=None):
    return lax.dot_general(a, b, (dims, ((), ())), precision=precision, preferred_element_type=f32)


def unpack_small(small):
    first = D
    second = first + D_INNER
    third = second + CONV * CONVCH
    fourth = third + CONVCH
    fifth = fourth + HEADS
    sixth = fifth + HEADS
    return (
        small[:first],
        small[first:second],
        small[second:third].reshape(CONV, CONVCH),
        small[third:fourth],
        small[fourth:fifth],
        small[fifth:sixth],
        small[sixth:],
    )


def adamw(weight, moment, second, grad, rate, decay):
    moment_new = 0.5 * moment + 0.5 * grad
    second_new = 0.5 * second + 0.5 * grad * grad
    first_hat = moment_new / (1.0 - 0.5**STEP)
    second_hat = second_new / (1.0 - 0.5**STEP)
    weight_new = weight - rate * (first_hat / (jnp.sqrt(second_hat) + adam_eps) + decay * weight)
    return (moment_new, second_new, weight_new)


def pair_cols(cols, h):
    lane = lax.broadcasted_iota(jnp.int32, (cols.shape[0], LANES), 1)
    return jnp.where(lane < HEADDIM, cols[:, h : h + 1], cols[:, h + 1 : h + 2])


def span_rows(c):
    return pl.ds(pl.multiple_of(c * SPAN, SPAN), SPAN)


def span_decay(dt_ref, rate_ref, c):
    dt = dt_ref[span_rows(c), :]
    row = lax.broadcasted_iota(jnp.int32, (SPAN, SPAN), 0)
    col = lax.broadcasted_iota(jnp.int32, (SPAN, SPAN), 1)
    lower = (row >= col).astype(f32)
    return dt, dot(lower, dt * rate_ref[0:1, :], precision=exact_prec)


def state_kernel(spans, x_ref, b_ref, dt_ref, rate_ref, keep_ref, carry_ref, s_ref, dec_ref):
    s_ref[...] = jnp.zeros_like(s_ref)
    dec_ref[...] = jnp.ones_like(dec_ref)

    def body(c, _):
        rows = span_rows(c)
        dt, cum = span_decay(dt_ref, rate_ref, c)
        last = cum[SPAN - 1 : SPAN, :]
        end_weight = jnp.exp(last - cum) * dt * keep_ref[rows, :]
        decay = jnp.exp(last) * carry_ref[pl.ds(c, 1), :]
        dec_ref[...] = dec_ref[...] * decay
        b = b_ref[rows, :]
        for p in range(PAIRS):
            lanes = slice(p * LANES, (p + 1) * LANES)
            xw = (x_ref[rows, lanes].astype(f32) * pair_cols(end_weight, 2 * p)).astype(bf16)
            fresh = dot(b, xw, ((0,), (0,)))
            s_ref[:, lanes] = s_ref[:, lanes] * pair_cols(decay, 2 * p) + fresh
        return 0

    lax.fori_loop(0, spans, body, 0)


def scan_kernel(
    spans, x_ref, b_ref, c_ref, dt_ref, rate_ref, segc_ref, segr_ref, keep_ref, inflow_ref, carry_ref, s_in_ref,
    y_ref, st_ref, s_ref,
):
    s_ref[...] = s_in_ref[...]

    def body(c, _):
        rows = span_rows(c)
        dt, cum = span_decay(dt_ref, rate_ref, c)
        last = cum[SPAN - 1 : SPAN, :]
        end_weight = jnp.exp(last - cum) * dt * keep_ref[rows, :]
        decay = jnp.exp(last) * carry_ref[pl.ds(c, 1), :]
        gain = jnp.exp(cum) * inflow_ref[rows, :]
        back_log = jnp.transpose(cum - jnp.log(dt))
        b = b_ref[rows, :]
        cc = c_ref[rows, :]
        scores = dot(cc, b, ((1,), (1,)))
        row = lax.broadcasted_iota(jnp.int32, (SPAN, SPAN), 0)
        col = lax.broadcasted_iota(jnp.int32, (SPAN, SPAN), 1)
        mask = (row >= col) & (segc_ref[rows, :] == segr_ref[pl.ds(c, 1), :])
        lane = lax.broadcasted_iota(jnp.int32, (SPAN, LANES), 1)
        st_ref[c] = s_ref[...]
        for p in range(PAIRS):
            lanes = slice(p * LANES, (p + 1) * LANES)
            x = x_ref[rows, lanes]
            parts = []
            for h in (2 * p, 2 * p + 1):
                gap = cum[:, h : h + 1] - back_log[h : h + 1, :]
                weights = scores * jnp.exp(jnp.where(mask, gap, -1e30))
                parts.append(dot(weights.astype(bf16), x))
            y = jnp.where(lane < HEADDIM, parts[0], parts[1])
            state = s_ref[:, lanes]
            y = y + dot(cc, state.astype(bf16)) * pair_cols(gain, 2 * p)
            y_ref[rows, lanes] = y
            xw = (x.astype(f32) * pair_cols(end_weight, 2 * p)).astype(bf16)
            s_ref[:, lanes] = state * pair_cols(decay, 2 * p) + dot(b, xw, ((0,), (0,)))
        return 0

    lax.fori_loop(0, spans, body, 0)


def state_back_kernel(spans, dy_ref, c_ref, dt_ref, rate_ref, inflow_ref, carry_ref, s_ref):
    s_ref[...] = jnp.zeros_like(s_ref)

    def body(step, _):
        c = spans - 1 - step
        rows = span_rows(c)
        dt, cum = span_decay(dt_ref, rate_ref, c)
        decay = jnp.exp(cum[SPAN - 1 : SPAN, :]) * carry_ref[pl.ds(c, 1), :]
        gain = jnp.exp(cum) * inflow_ref[rows, :]
        cc = c_ref[rows, :]
        for p in range(PAIRS):
            lanes = slice(p * LANES, (p + 1) * LANES)
            dyg = (dy_ref[rows, lanes].astype(f32) * pair_cols(gain, 2 * p)).astype(bf16)
            s_ref[:, lanes] = s_ref[:, lanes] * pair_cols(decay, 2 * p) + dot(cc, dyg, ((0,), (0,)))
        return 0

    lax.fori_loop(0, spans, body, 0)


def head_sums(values):
    width = values.shape[1]
    chan = lax.broadcasted_iota(jnp.int32, (width, LANES), 0)
    head = lax.broadcasted_iota(jnp.int32, (width, LANES), 1)
    pick = (chan // HEADDIM == head).astype(bf16)
    high = values.astype(bf16)
    low = (values - high.astype(f32)).astype(bf16)
    return dot(high, pick) + dot(low, pick)


def scan_back_kernel(
    spans, x_ref, b_ref, c_ref, dt_ref, ratio_ref, sig_ref, rate_ref, segc_ref, segr_ref, keep_ref, inflow_ref, carry_ref, skip_ref,
    y_ref, st_ref, dy_ref, ds_out_ref,
    dx_ref, db_ref, dc_ref, ddt_ref, drate_ref, dskip_ref,
    ds_ref, prod_ref,
):
    ds_ref[...] = ds_out_ref[...]
    drate_ref[...] = jnp.zeros_like(drate_ref)
    dskip_ref[...] = jnp.zeros_like(dskip_ref)

    def body(step, _):
        c = spans - 1 - step
        rows = span_rows(c)
        dt, cum = span_decay(dt_ref, rate_ref, c)
        last = cum[SPAN - 1 : SPAN, :]
        end_weight = jnp.exp(last - cum) * dt * keep_ref[rows, :]
        decay = jnp.exp(last) * carry_ref[pl.ds(c, 1), :]
        gain = jnp.exp(cum) * inflow_ref[rows, :]
        fore_log = jnp.transpose(cum)
        back_log = cum - jnp.log(dt)
        b = b_ref[rows, :]
        cc = c_ref[rows, :]
        scores = dot(b, cc, ((1,), (1,)))
        row = lax.broadcasted_iota(jnp.int32, (SPAN, SPAN), 0)
        col = lax.broadcasted_iota(jnp.int32, (SPAN, SPAN), 1)
        mask = (col >= row) & (segc_ref[rows, :] == segr_ref[pl.ds(c, 1), :])
        lane = lax.broadcasted_iota(jnp.int32, (SPAN, LANES), 1)
        d_scores = jnp.zeros((SPAN, SPAN), f32)
        db = jnp.zeros((SPAN, STATE), f32)
        dc = jnp.zeros((SPAN, STATE), f32)
        state_row = []
        dx_state_row = []
        for p in range(PAIRS):
            lanes = slice(p * LANES, (p + 1) * LANES)
            x = x_ref[rows, lanes]
            dy = dy_ref[rows, lanes]
            xf = x.astype(f32)
            dyf = dy.astype(f32)
            parts = []
            for k in range(2):
                h = 2 * p + k
                gap = fore_log[h : h + 1, :] - back_log[:, h : h + 1]
                decay_mat = jnp.exp(jnp.where(mask, gap, -1e30))
                weights = (scores * decay_mat).astype(bf16)
                parts.append(dot(weights, dy))
                own = (lane < HEADDIM) if k == 0 else (lane >= HEADDIM)
                d_weights = dot(jnp.where(own, xf, 0.0).astype(bf16), dy, ((1,), (1,)))
                d_scores = d_scores + d_weights * decay_mat
            dx = jnp.where(lane < HEADDIM, parts[0], parts[1])
            dyg = (dyf * pair_cols(gain, 2 * p)).astype(bf16)
            ew = pair_cols(end_weight, 2 * p)
            xw = (xf * ew).astype(bf16)
            state = st_ref[c, :, lanes]
            ds = ds_ref[:, lanes]
            state_b = state.astype(bf16)
            ds_b = ds.astype(bf16)
            dc = dc + dot(dyg, state_b, ((1,), (1,)))
            db = db + dot(xw, ds_b, ((1,), (1,)))
            dx_state = dot(b, ds_b) * ew
            dx = dx + dx_state
            dec = pair_cols(decay, 2 * p)
            state_row.append(jnp.sum(ds * state, axis=0, keepdims=True) * dec)
            dx_state_row.append(jnp.sum(dx_state * xf, axis=0, keepdims=True))
            ds_ref[:, lanes] = ds * dec + dot(cc, dyg, ((0,), (0,)))
            prod_ref[0:SPAN, lanes] = dyf * y_ref[rows, lanes]
            prod_ref[SPAN : 2 * SPAN, lanes] = xf * dx
            dskip_ref[0:1, lanes] += jnp.sum(dyf * xf, axis=0, keepdims=True)
            dx_ref[rows, lanes] = (dx + dyf * skip_ref[0:1, lanes]).astype(bf16)
        d_scores_b = d_scores.astype(bf16)
        db_ref[rows, :] = db + dot(d_scores_b, cc)
        dc_ref[rows, :] = dc + dot(d_scores_b, b, ((0,), (0,)))
        sums = head_sums(prod_ref[...])
        out_sum, in_sum = sums[:SPAN], sums[SPAN:]
        edge = jnp.concatenate(state_row, axis=1) + jnp.concatenate(dx_state_row, axis=1)
        edge_sum = head_sums(jnp.broadcast_to(edge, (8, HALF)))[0:1]
        at_last = lax.broadcasted_iota(jnp.int32, (SPAN, LANES), 0) == SPAN - 1
        d_cum = out_sum - in_sum + jnp.where(at_last, edge_sum, 0.0)
        upper = (col >= row).astype(f32)
        d_log = dot(upper, d_cum, precision=exact_prec)
        drate_ref[0:1, :] += jnp.sum(d_log * dt, axis=0, keepdims=True)
        ddt_ref[rows, :] = d_log * rate_ref[0:1, :] * sig_ref[rows, :] + in_sum * ratio_ref[rows, :]
        return 0

    lax.fori_loop(0, spans, body, 0)


VMEM_LIMIT = 60 * 1024 * 1024


def in_vmem(kernel, out_shape, name, scratch=()):
    return pl.pallas_call(
        kernel,
        out_shape=out_shape,
        scratch_shapes=list(scratch),
        name=name,
        compiler_params=pltpu.CompilerParams(vmem_limit_bytes=VMEM_LIMIT),
    )


def shape(dims, dtype):
    return jax.ShapeDtypeStruct(dims, dtype)


def shift_part(array, by):
    size = lax.axis_size("part")
    pairs = [(i, i + by) for i in range(size) if 0 <= i + by < size]
    return lax.ppermute(array, "part", pairs)


def shards(
    hidden, cotangent, segments, valid, in_w, in_m, in_v, out_w, out_m, out_v, small_w, small_m, small_v,
):
    parts = lax.axis_size("part")
    wt = lax.axis_size("wt")
    part = lax.axis_index("part")
    tp = lax.axis_index("tp")
    own_rows = in_w.shape[0]
    out_rows = out_w.shape[0]
    resid = hidden[0].astype(f32)
    tok_rows = resid.shape[0]
    rows = tok_rows * TP
    spans = rows // SPAN
    seg_all = segments[0]
    pre_gain, norm_gain, conv_weight, conv_bias, dt_shift, a_logs, skips = unpack_small(small_w)

    def own_part(array, width):
        return lax.dynamic_slice_in_dim(array, tp * width, width, array.ndim - 1)

    in_copy = in_w.astype(bf16)
    slices = []
    for j in range(TP):
        slices.append(
            jnp.concatenate(
                [
                    in_copy[:, D_INNER + j * HALF : D_INNER + (j + 1) * HALF],
                    in_copy[:, 2 * D_INNER : 2 * D_INNER + SIDE],
                    in_copy[:, D_INNER + CONVCH + j * LOCAL_HEADS : D_INNER + CONVCH + (j + 1) * LOCAL_HEADS],
                    jnp.zeros((own_rows, LANES - LOCAL_HEADS), bf16),
                    in_copy[:, j * HALF : (j + 1) * HALF],
                ],
                axis=1,
            )
        )
    mine = lax.all_to_all(jnp.stack(slices), "tp", 0, 0, tiled=False)
    w_in = lax.all_gather(mine, ("part", "wt"), axis=0, tiled=False)
    w_in = w_in.reshape(parts, wt, TP, own_rows, COLS).transpose(0, 2, 1, 3, 4).reshape(D, COLS)
    flat = [(i, (i % TP) * parts + i // TP) for i in range(parts * TP)]
    out_mine = lax.ppermute(out_w.astype(bf16), ("part", "tp"), [(b, a) for a, b in flat])
    w_out = lax.all_gather(out_mine, ("part", "wt"), axis=0, tiled=True)

    hidden_all = lax.all_gather(hidden[0], "tp", axis=0, tiled=True)
    back_mix = cotangent[0] * valid[0][:, None].astype(bf16)
    back_all = lax.all_gather(back_mix, "tp", axis=0, tiled=True)

    hid = hidden_all.astype(f32)
    scale_all = lax.rsqrt(jnp.mean(hid * hid, axis=1, keepdims=True) + norm_eps)
    x_normed = (hid * scale_all * pre_gain).astype(bf16)
    projected = dot(x_normed, w_in)
    conv_in = projected[:, :COL_DT].astype(bf16)
    dt_raw = projected[:, COL_DT:COL_GATE].astype(bf16).astype(f32)
    gate_pre = projected[:, COL_GATE:]
    rim_in = shift_part(conv_in[rows - RIM :], 1)
    padded = jnp.concatenate([rim_in, conv_in], axis=0).astype(f32)
    seg_front = jnp.concatenate([jnp.full((RIM,), -1, jnp.int32), seg_all, jnp.full((RIM,), -1, jnp.int32)])
    seg_pad = lax.dynamic_slice_in_dim(seg_front, part * rows, rows + 2 * RIM)
    seg = seg_pad[RIM : RIM + rows]
    masks = [(seg_pad[k : k + rows] == seg).astype(f32)[:, None] for k in range(CONV)]
    taps = jnp.concatenate([own_part(conv_weight[:, :D_INNER], HALF), conv_weight[:, D_INNER:]], axis=1)
    bias = jnp.concatenate([own_part(conv_bias[:D_INNER], HALF), conv_bias[D_INNER:]])
    total = bias[None, :]
    for k in range(CONV):
        total = total + taps[k] * padded[k : k + rows] * masks[k]
    sig_total = jax.nn.sigmoid(total)
    activated = (total * sig_total).astype(bf16)
    x_scan = activated[:, :HALF]
    b_mat = activated[:, HALF : HALF + STATE]
    c_mat = activated[:, HALF + STATE :]

    def head_row(array):
        return jnp.pad(own_part(array, LOCAL_HEADS), (0, LANES - LOCAL_HEADS))

    shift_row = head_row(dt_shift)
    z = dt_raw + shift_row
    dt = jax.nn.softplus(z)
    sig_dt = jax.nn.sigmoid(z)
    ratio = jnp.where(dt > 1e-30, sig_dt / jnp.maximum(dt, 1e-30), 1.0)
    rate_row = -jnp.exp(head_row(a_logs))
    rate8 = jnp.broadcast_to(rate_row, (8, LANES))
    skip_chan = jnp.repeat(own_part(skips, LOCAL_HEADS), HEADDIM)
    skip8 = jnp.broadcast_to(skip_chan, (8, HALF))
    seg_spans = seg.reshape(spans, SPAN)
    seg_last = seg_spans[:, -1]
    seg_before = jnp.concatenate([seg_pad[RIM - 1 : RIM], seg_last[:-1]])
    keep = (seg_spans == seg_last[:, None]).astype(f32).reshape(rows, 1)
    inflow = (seg_spans == seg_before[:, None]).astype(f32).reshape(rows, 1)
    carry = jnp.broadcast_to((seg_last == seg_before).astype(f32)[:, None], (spans, LANES))
    seg_col = seg[:, None]

    state_shape = shape((STATE, HALF), f32)
    s_local, dec_total = in_vmem(
        functools.partial(state_kernel, spans), (state_shape, shape((8, LANES), f32)), "state"
    )(x_scan, b_mat, dt, rate8, keep, carry)
    dec_chan = jnp.repeat(dec_total[0, :LOCAL_HEADS], HEADDIM)
    s_in = jnp.zeros((STATE, HALF), f32)
    for _ in range(parts - 1):
        s_in = shift_part(dec_chan * s_in + s_local, 1)
    y_scan, states = in_vmem(
        functools.partial(scan_kernel, spans),
        (shape((rows, HALF), f32), shape((spans, STATE, HALF), f32)),
        "scan",
        [pltpu.VMEM((STATE, HALF), f32)],
    )(x_scan, b_mat, c_mat, dt, rate8, seg_col, seg_spans, keep, inflow, carry, s_in)
    y_b = (y_scan + skip_chan * x_scan.astype(f32)).astype(bf16).astype(f32)

    gain_own = own_part(norm_gain, HALF)
    sig_gate = jax.nn.sigmoid(gate_pre)
    silu_gate = gate_pre * sig_gate
    gated = y_b * silu_gate
    gate_sq = lax.psum(jnp.sum(gated * gated, axis=1), "tp")
    scale_gate = lax.rsqrt(gate_sq / D_INNER + norm_eps)[:, None]
    normed = (gated * scale_gate * gain_own).astype(bf16)
    mixer = lax.psum_scatter(dot(normed, w_out), "tp", scatter_dimension=0, tiled=True)
    output = (resid + mixer).astype(bf16)
    valid_rows = valid[0].astype(f32)
    res_sq = jnp.sum(valid_rows * jnp.sum(resid * resid, axis=1))
    mix_sq = jnp.sum(valid_rows * jnp.sum(mixer * mixer, axis=1))
    valid_count = jnp.sum(valid_rows)

    d_normed = dot(back_all, w_out, ((1,), (1,)))
    g_out = dot(normed, back_all, ((0,), (0,)))
    g_out = lax.psum_scatter(g_out, ("part", "wt"), scatter_dimension=0, tiled=True)
    g_out = lax.ppermute(g_out, ("part", "tp"), flat)
    d_gain = d_normed * gain_own
    gate_dot = lax.psum(jnp.sum(gated * d_gain, axis=1), "tp")
    d_gated = scale_gate * d_gain - gated * (scale_gate**3 * (gate_dot / D_INNER)[:, None])
    d_norm_gain = jnp.sum(gated * scale_gate * d_normed, axis=0)
    dy = (d_gated * silu_gate).astype(bf16)
    d_gate = d_gated * y_b * (sig_gate * (1.0 + gate_pre * (1.0 - sig_gate)))

    ds_local = in_vmem(functools.partial(state_back_kernel, spans), state_shape, "state_back")(
        dy, c_mat, dt, rate8, inflow, carry
    )
    ds_out = jnp.zeros((STATE, HALF), f32)
    for _ in range(parts - 1):
        ds_out = shift_part(dec_chan * ds_out + ds_local, -1)
    d_x, d_b, d_c, d_dt, d_rate, d_skip = in_vmem(
        functools.partial(scan_back_kernel, spans),
        (
            shape((rows, HALF), bf16),
            shape((rows, STATE), f32),
            shape((rows, STATE), f32),
            shape((rows, LANES), f32),
            shape((8, LANES), f32),
            shape((8, HALF), f32),
        ),
        "scan_back",
        [pltpu.VMEM((STATE, HALF), f32), pltpu.VMEM((2 * SPAN, HALF), f32)],
    )(x_scan, b_mat, c_mat, dt, ratio, sig_dt, rate8, seg_col, seg_spans, keep, inflow, carry, skip8, y_scan, states, dy, ds_out)

    d_total = jnp.concatenate([d_x.astype(f32), d_b, d_c], axis=1) * (sig_total * (1.0 + total * (1.0 - sig_total)))
    rim_back = shift_part(d_total[:RIM], -1)
    d_padded = jnp.concatenate([d_total, rim_back], axis=0)
    d_conv_in = 0.0
    for k in range(CONV):
        later = (seg_pad[2 * RIM - k : 2 * RIM - k + rows] == seg).astype(f32)[:, None]
        d_conv_in = d_conv_in + taps[k] * d_padded[RIM - k : RIM - k + rows] * later
    d_taps = jnp.stack([jnp.sum(d_total * padded[k : k + rows] * masks[k], axis=0) for k in range(CONV)])
    d_bias = jnp.sum(d_total, axis=0)
    d_proj = jnp.concatenate([d_conv_in, d_dt, d_gate], axis=1).astype(bf16)
    d_x_normed = dot(d_proj, w_in, ((1,), (1,)))
    d_x_normed = lax.psum_scatter(d_x_normed, "tp", scatter_dimension=0, tiled=True)
    g_in = dot(x_normed, d_proj, ((0,), (0,)))
    g_in = g_in.reshape(parts, TP, wt, own_rows, COLS).transpose(0, 2, 1, 3, 4).reshape(parts * wt, TP, own_rows, COLS)
    g_in = lax.psum_scatter(g_in, ("part", "wt"), scatter_dimension=0, tiled=False)
    g_in = lax.all_to_all(g_in, "tp", 0, 0, tiled=False)
    g_in = jnp.concatenate(
        [g_in[j, :, COL_GATE:] for j in range(TP)]
        + [g_in[j, :, :HALF] for j in range(TP)]
        + [jnp.sum(g_in[:, :, COL_SIDE:COL_DT], axis=0)]
        + [g_in[j, :, COL_DT : COL_DT + LOCAL_HEADS] for j in range(TP)],
        axis=1,
    )

    scale_own = lax.rsqrt(jnp.mean(resid * resid, axis=1, keepdims=True) + norm_eps)
    d_pre = d_x_normed * pre_gain
    dot_pre = jnp.mean(resid * d_pre, axis=1, keepdims=True)
    grad_hidden = back_mix.astype(f32) + scale_own * d_pre - resid * (scale_own**3 * dot_pre)
    d_pre_gain = jnp.sum(resid * scale_own * d_x_normed, axis=0)

    def placed(values, width):
        spread = (jnp.arange(TP) == tp).astype(f32)[:, None] * values[..., None, :]
        return spread.reshape(*values.shape[:-1], TP * width)

    d_weight = jnp.concatenate([placed(d_taps[:, :HALF], HALF), d_taps[:, HALF:]], axis=1)
    small_grad = jnp.concatenate(
        [
            d_pre_gain,
            placed(d_norm_gain, HALF),
            d_weight.reshape(-1),
            placed(d_bias[:HALF], HALF),
            d_bias[HALF:],
            placed(jnp.sum(d_dt, axis=0)[:LOCAL_HEADS], LOCAL_HEADS),
            placed((d_rate[0] * rate_row)[:LOCAL_HEADS], LOCAL_HEADS),
            placed(jnp.sum(d_skip[0].reshape(LOCAL_HEADS, HEADDIM), axis=1), LOCAL_HEADS),
            jnp.stack([res_sq, mix_sq, valid_count]),
        ]
    )
    small_total = lax.psum(small_grad, ("part", "tp", "wt"))
    res_total, mix_total, count_total = small_total[-3], small_total[-2], small_total[-1]
    in_m_new, in_v_new, in_w_new = adamw(in_w, in_m, in_v, g_in, 0.02, 0.1)
    out_m_new, out_v_new, out_w_new = adamw(out_w, out_m, out_v, g_out, 0.02, 0.1)
    small_m_new, small_v_new, small_w_new = adamw(small_w, small_m, small_v, small_total[:-3], 0.2, 0.0)
    rms = jnp.stack([jnp.sqrt(res_total / (count_total * D)), jnp.sqrt(mix_total / (count_total * D))])
    return (
        output[None], grad_hidden[None], in_m_new, in_v_new, in_w_new, out_m_new, out_v_new, out_w_new,
        small_m_new, small_v_new, small_w_new, rms,
    )


def solution(mesh):
    seq, wt = mesh.shape["seq"], mesh.shape["wt"]
    split = Mesh(mesh.devices.reshape(seq // TP, TP, wt), ("part", "tp", "wt"))
    tokens = ("part", "tp")
    everyone = ("part", "tp", "wt")
    matrix = P(everyone, None)
    stream = P("wt", tokens, None)
    return jax.shard_map(
        shards,
        mesh=split,
        in_specs=(
            stream, stream, P("wt", None), P("wt", tokens), matrix, matrix, matrix, matrix, matrix, matrix, P(), P(), P(),
        ),
        out_specs=(stream, stream, matrix, matrix, matrix, matrix, matrix, matrix, P(), P(), P(), P()),
        check_vma=False,
    )
```

```python
import functools

import jax
import jax.numpy as jnp
from jax import lax
from jax.experimental import pallas as pl
from jax.experimental.pallas import tpu as pltpu
from jax.sharding import Mesh
from jax.sharding import PartitionSpec as P

D = 1536
D_INNER = 3072
HEADS = 48
HEADDIM = 64
STATE = 128
CONV = 4
SPAN = 256
STEP = 4
CONVCH = 3328
TP = 4
RIM = CONV - 1
LANES = 128
HALF = D_INNER // TP
LOCAL_HEADS = HEADS // TP
PAIRS = LOCAL_HEADS // 2
SIDE = 2 * STATE
COL_SIDE = HALF
COL_DT = HALF + SIDE
COL_GATE = COL_DT + LANES
COLS = COL_GATE + HALF

bf16 = jnp.bfloat16
f32 = jnp.float32
exact_prec = lax.Precision.HIGHEST
norm_eps = 1e-05
adam_eps = 1e-08


def dot(a, b, dims=((1,), (0,)), precision=None):
    return lax.dot_general(a, b, (dims, ((), ())), precision=precision, preferred_element_type=f32)


def unpack_small(small):
    first = D
    second = first + D_INNER
    third = second + CONV * CONVCH
    fourth = third + CONVCH
    fifth = fourth + HEADS
    sixth = fifth + HEADS
    return (
        small[:first],
        small[first:second],
        small[second:third].reshape(CONV, CONVCH),
        small[third:fourth],
        small[fourth:fifth],
        small[fifth:sixth],
        small[sixth:],
    )


def adamw(weight, moment, second, grad, rate, decay):
    moment_new = 0.5 * moment + 0.5 * grad
    second_new = 0.5 * second + 0.5 * grad * grad
    first_hat = moment_new / (1.0 - 0.5**STEP)
    second_hat = second_new / (1.0 - 0.5**STEP)
    weight_new = weight - rate * (first_hat / (jnp.sqrt(second_hat) + adam_eps) + decay * weight)
    return (moment_new, second_new, weight_new)


def pair_cols(cols, h):
    lane = lax.broadcasted_iota(jnp.int32, (cols.shape[0], LANES), 1)
    return jnp.where(lane < HEADDIM, cols[:, h : h + 1], cols[:, h + 1 : h + 2])


def span_rows(c):
    return pl.ds(pl.multiple_of(c * SPAN, SPAN), SPAN)


def span_decay(dt_ref, rate_ref, c):
    dt = dt_ref[span_rows(c), :]
    row = lax.broadcasted_iota(jnp.int32, (SPAN, SPAN), 0)
    col = lax.broadcasted_iota(jnp.int32, (SPAN, SPAN), 1)
    lower = (row >= col).astype(f32)
    return dt, dot(lower, dt * rate_ref[0:1, :], precision=exact_prec)


def state_kernel(spans, x_ref, b_ref, dt_ref, rate_ref, keep_ref, carry_ref, s_ref, dec_ref):
    s_ref[...] = jnp.zeros_like(s_ref)
    dec_ref[...] = jnp.ones_like(dec_ref)

    def body(c, _):
        rows = span_rows(c)
        dt, cum = span_decay(dt_ref, rate_ref, c)
        last = cum[SPAN - 1 : SPAN, :]
        end_weight = jnp.exp(last - cum) * dt * keep_ref[rows, :]
        decay = jnp.exp(last) * carry_ref[pl.ds(c, 1), :]
        dec_ref[...] = dec_ref[...] * decay
        b = b_ref[rows, :]
        for p in range(PAIRS):
            lanes = slice(p * LANES, (p + 1) * LANES)
            xw = (x_ref[rows, lanes].astype(f32) * pair_cols(end_weight, 2 * p)).astype(bf16)
            fresh = dot(b, xw, ((0,), (0,)))
            s_ref[:, lanes] = s_ref[:, lanes] * pair_cols(decay, 2 * p) + fresh
        return 0

    lax.fori_loop(0, spans, body, 0)


def scan_kernel(
    spans, x_ref, b_ref, c_ref, dt_ref, rate_ref, segc_ref, segr_ref, keep_ref, inflow_ref, carry_ref, s_in_ref,
    y_ref, st_ref, s_ref,
):
    s_ref[...] = s_in_ref[...]

    def body(c, _):
        rows = span_rows(c)
        dt, cum = span_decay(dt_ref, rate_ref, c)
        last = cum[SPAN - 1 : SPAN, :]
        end_weight = jnp.exp(last - cum) * dt * keep_ref[rows, :]
        decay = jnp.exp(last) * carry_ref[pl.ds(c, 1), :]
        gain = jnp.exp(cum) * inflow_ref[rows, :]
        back_log = jnp.transpose(cum - jnp.log(dt))
        b = b_ref[rows, :]
        cc = c_ref[rows, :]
        scores = dot(cc, b, ((1,), (1,)))
        row = lax.broadcasted_iota(jnp.int32, (SPAN, SPAN), 0)
        col = lax.broadcasted_iota(jnp.int32, (SPAN, SPAN), 1)
        mask = (row >= col) & (segc_ref[rows, :] == segr_ref[pl.ds(c, 1), :])
        lane = lax.broadcasted_iota(jnp.int32, (SPAN, LANES), 1)
        st_ref[c] = s_ref[...]
        for p in range(PAIRS):
            lanes = slice(p * LANES, (p + 1) * LANES)
            x = x_ref[rows, lanes]
            parts = []
            for h in (2 * p, 2 * p + 1):
                gap = cum[:, h : h + 1] - back_log[h : h + 1, :]
                weights = scores * jnp.exp(jnp.where(mask, gap, -1e30))
                parts.append(dot(weights.astype(bf16), x))
            y = jnp.where(lane < HEADDIM, parts[0], parts[1])
            state = s_ref[:, lanes]
            y = y + dot(cc, state.astype(bf16)) * pair_cols(gain, 2 * p)
            y_ref[rows, lanes] = y
            xw = (x.astype(f32) * pair_cols(end_weight, 2 * p)).astype(bf16)
            s_ref[:, lanes] = state * pair_cols(decay, 2 * p) + dot(b, xw, ((0,), (0,)))
        return 0

    lax.fori_loop(0, spans, body, 0)


def state_back_kernel(spans, dy_ref, c_ref, dt_ref, rate_ref, inflow_ref, carry_ref, s_ref):
    s_ref[...] = jnp.zeros_like(s_ref)

    def body(step, _):
        c = spans - 1 - step
        rows = span_rows(c)
        dt, cum = span_decay(dt_ref, rate_ref, c)
        decay = jnp.exp(cum[SPAN - 1 : SPAN, :]) * carry_ref[pl.ds(c, 1), :]
        gain = jnp.exp(cum) * inflow_ref[rows, :]
        cc = c_ref[rows, :]
        for p in range(PAIRS):
            lanes = slice(p * LANES, (p + 1) * LANES)
            dyg = (dy_ref[rows, lanes].astype(f32) * pair_cols(gain, 2 * p)).astype(bf16)
            s_ref[:, lanes] = s_ref[:, lanes] * pair_cols(decay, 2 * p) + dot(cc, dyg, ((0,), (0,)))
        return 0

    lax.fori_loop(0, spans, body, 0)


def head_sums(values):
    width = values.shape[1]
    chan = lax.broadcasted_iota(jnp.int32, (width, LANES), 0)
    head = lax.broadcasted_iota(jnp.int32, (width, LANES), 1)
    pick = (chan // HEADDIM == head).astype(bf16)
    high = values.astype(bf16)
    low = (values - high.astype(f32)).astype(bf16)
    return dot(high, pick) + dot(low, pick)


def scan_back_kernel(
    spans, x_ref, b_ref, c_ref, dt_ref, ratio_ref, sig_ref, rate_ref, segc_ref, segr_ref, keep_ref, inflow_ref, carry_ref, skip_ref,
    y_ref, st_ref, dy_ref, ds_out_ref,
    dx_ref, db_ref, dc_ref, ddt_ref, drate_ref, dskip_ref,
    ds_ref, prod_ref,
):
    ds_ref[...] = ds_out_ref[...]
    drate_ref[...] = jnp.zeros_like(drate_ref)
    dskip_ref[...] = jnp.zeros_like(dskip_ref)

    def body(step, _):
        c = spans - 1 - step
        rows = span_rows(c)
        dt, cum = span_decay(dt_ref, rate_ref, c)
        last = cum[SPAN - 1 : SPAN, :]
        end_weight = jnp.exp(last - cum) * dt * keep_ref[rows, :]
        decay = jnp.exp(last) * carry_ref[pl.ds(c, 1), :]
        gain = jnp.exp(cum) * inflow_ref[rows, :]
        fore_log = jnp.transpose(cum)
        back_log = cum - jnp.log(dt)
        b = b_ref[rows, :]
        cc = c_ref[rows, :]
        scores = dot(b, cc, ((1,), (1,)))
        row = lax.broadcasted_iota(jnp.int32, (SPAN, SPAN), 0)
        col = lax.broadcasted_iota(jnp.int32, (SPAN, SPAN), 1)
        mask = (col >= row) & (segc_ref[rows, :] == segr_ref[pl.ds(c, 1), :])
        lane = lax.broadcasted_iota(jnp.int32, (SPAN, LANES), 1)
        d_scores = jnp.zeros((SPAN, SPAN), f32)
        db = jnp.zeros((SPAN, STATE), f32)
        dc = jnp.zeros((SPAN, STATE), f32)
        state_row = []
        dx_state_row = []
        for p in range(PAIRS):
            lanes = slice(p * LANES, (p + 1) * LANES)
            x = x_ref[rows, lanes]
            dy = dy_ref[rows, lanes]
            xf = x.astype(f32)
            dyf = dy.astype(f32)
            parts = []
            for k in range(2):
                h = 2 * p + k
                gap = fore_log[h : h + 1, :] - back_log[:, h : h + 1]
                decay_mat = jnp.exp(jnp.where(mask, gap, -1e30))
                weights = (scores * decay_mat).astype(bf16)
                parts.append(dot(weights, dy))
                own = (lane < HEADDIM) if k == 0 else (lane >= HEADDIM)
                d_weights = dot(jnp.where(own, xf, 0.0).astype(bf16), dy, ((1,), (1,)))
                d_scores = d_scores + d_weights * decay_mat
            dx = jnp.where(lane < HEADDIM, parts[0], parts[1])
            dyg = (dyf * pair_cols(gain, 2 * p)).astype(bf16)
            ew = pair_cols(end_weight, 2 * p)
            xw = (xf * ew).astype(bf16)
            state = st_ref[c, :, lanes]
            ds = ds_ref[:, lanes]
            state_b = state.astype(bf16)
            ds_b = ds.astype(bf16)
            dc = dc + dot(dyg, state_b, ((1,), (1,)))
            db = db + dot(xw, ds_b, ((1,), (1,)))
            dx_state = dot(b, ds_b) * ew
            dx = dx + dx_state
            dec = pair_cols(decay, 2 * p)
            state_row.append(jnp.sum(ds * state, axis=0, keepdims=True) * dec)
            dx_state_row.append(jnp.sum(dx_state * xf, axis=0, keepdims=True))
            ds_ref[:, lanes] = ds * dec + dot(cc, dyg, ((0,), (0,)))
            prod_ref[0:SPAN, lanes] = dyf * y_ref[rows, lanes]
            prod_ref[SPAN : 2 * SPAN, lanes] = xf * dx
            dskip_ref[0:1, lanes] += jnp.sum(dyf * xf, axis=0, keepdims=True)
            dx_ref[rows, lanes] = (dx + dyf * skip_ref[0:1, lanes]).astype(bf16)
        d_scores_b = d_scores.astype(bf16)
        db_ref[rows, :] = db + dot(d_scores_b, cc)
        dc_ref[rows, :] = dc + dot(d_scores_b, b, ((0,), (0,)))
        sums = head_sums(prod_ref[...])
        out_sum, in_sum = sums[:SPAN], sums[SPAN:]
        edge = jnp.concatenate(state_row, axis=1) + jnp.concatenate(dx_state_row, axis=1)
        edge_sum = head_sums(jnp.broadcast_to(edge, (8, HALF)))[0:1]
        at_last = lax.broadcasted_iota(jnp.int32, (SPAN, LANES), 0) == SPAN - 1
        d_cum = out_sum - in_sum + jnp.where(at_last, edge_sum, 0.0)
        upper = (col >= row).astype(f32)
        d_log = dot(upper, d_cum, precision=exact_prec)
        drate_ref[0:1, :] += jnp.sum(d_log * dt, axis=0, keepdims=True)
        ddt_ref[rows, :] = d_log * rate_ref[0:1, :] * sig_ref[rows, :] + in_sum * ratio_ref[rows, :]
        return 0

    lax.fori_loop(0, spans, body, 0)


MESH = pl.DeviceIdType.MESH
T0, T1, DIAG, CORE, SIDEWAYS, PART = ("t0",), ("t1",), ("t1", "t0"), ("w0",), ("w1",), ("part",)


def place():
    return tuple(lax.axis_index(a) for a in ("part", "t1", "t0", "w1", "w0"))


def across(flips):
    return {a: 1 - lax.axis_index(a) for a in flips}


def greet(neighbours):
    barrier = pltpu.get_barrier_semaphore()
    for flips in neighbours:
        pl.semaphore_signal(barrier, inc=1, device_id=across(flips), device_id_type=MESH)
    pl.semaphore_wait(barrier, len(neighbours))


class Copies:
    def __init__(self, local_sem, send_sem, recv_sem):
        self.local_sem, self.send_sem, self.recv_sem = local_sem, send_sem, recv_sem
        self.sent, self.kept = [], []

    def send(self, src, dst, flips):
        i = len(self.sent)
        copy = pltpu.make_async_remote_copy(
            src_ref=src,
            dst_ref=dst,
            send_sem=self.send_sem.at[i],
            recv_sem=self.recv_sem.at[i],
            device_id=across(flips),
            device_id_type=MESH,
        )
        copy.start()
        self.sent.append(copy)
        return copy

    def keep(self, src, dst):
        copy = pltpu.make_async_copy(src, dst, self.local_sem.at[len(self.kept)])
        copy.start()
        self.kept.append(copy)

    def finish(self):
        for copy in self.sent:
            copy.wait_send()
        for copy in self.kept:
            copy.wait()


def sems(remote, local=1):
    return [
        pltpu.SemaphoreType.DMA((local,)),
        pltpu.SemaphoreType.DMA((remote,)),
        pltpu.SemaphoreType.DMA((remote,)),
    ]


class GroupGather:
    def __init__(self, copies, src, dst):
        _, t1, t0, _, _ = place()
        self.copies, self.dst = copies, dst
        rows = src.shape[0]
        self.halves = [pl.ds(0, rows // 2), pl.ds(rows // 2, rows // 2)]
        copies.keep(src, dst.at[t1, t0])
        self.along_t1 = [copies.send(src.at[h], dst.at[t1, t0, h], T1) for h in self.halves]
        self.along_t0 = [copies.send(src.at[h], dst.at[t1, t0, h], T0) for h in self.halves]

    def hand_on(self):
        _, t1, t0, _, _ = place()
        for k, h in enumerate(self.halves):
            self.along_t1[k].wait_recv()
            block = self.dst.at[1 - t1, t0, h]
            self.along_t0.append(self.copies.send(block, block, T0))

    def finish(self):
        for copy in self.along_t0:
            copy.wait_recv()


class WeightGather:
    def __init__(self, copies, dst, tag):
        self.copies, self.dst, self.tag = copies, dst, tag
        self.by_part, self.by_side, self.by_core = [], [], []

    def at(self, part, w1, w0, block):
        return self.dst.at[(part, *block, w1, w0)]

    def spread(self, src, block):
        p, _, _, w1, w0 = place()
        dst = self.at(p, w1, w0, block)
        self.by_part.append((self.copies.send(src, dst, PART), block))
        self.by_side.append((self.copies.send(src, dst, SIDEWAYS), block))
        self.by_core.append(self.copies.send(src, dst, CORE))

    def pass_core(self, part, w1, block):
        w0 = lax.axis_index("w0")
        here = self.at(part, w1, w0, block)
        self.by_core.append(self.copies.send(here, here, CORE))

    def hand_on(self):
        p, _, _, w1, w0 = place()
        again = []
        for (copy, block), (side, same) in zip(self.by_part, self.by_side):
            side.wait_recv()
            self.pass_core(p, 1 - w1, same)
            copy.wait_recv()
            here = self.at(1 - p, w1, w0, block)
            again.append((self.copies.send(here, here, SIDEWAYS), block))
            self.pass_core(1 - p, w1, block)
        for copy, block in again:
            copy.wait_recv()
            self.pass_core(1 - p, 1 - w1, block)

    def finish(self):
        for copy in self.by_core:
            copy.wait_recv()


def start_kernel(hid_ref, w_ref, h_ref, win_ref, local_sem, send_sem, recv_sem):
    p, t1, t0, w1, w0 = place()
    greet([T0, T1, DIAG, CORE, SIDEWAYS, PART])
    copies = Copies(local_sem, send_sem, recv_sem)
    own = w_ref.at[t1, t0]
    mine = win_ref.at[p, t1, t0, w1, w0]
    weights = WeightGather(copies, win_ref, 0)
    weights.spread(own, (t1, t0))
    swaps = [
        (copies.send(w_ref.at[t1, 1 - t0], mine, T0), (t1, 1 - t0)),
        (copies.send(w_ref.at[1 - t1, t0], mine, T1), (1 - t1, t0)),
        (copies.send(w_ref.at[1 - t1, 1 - t0], mine, DIAG), (1 - t1, 1 - t0)),
    ]
    tokens = GroupGather(copies, hid_ref, h_ref)
    copies.keep(own, mine)
    for copy, block in swaps:
        copy.wait_recv()
        weights.spread(weights.at(p, w1, w0, block), block)
    tokens.hand_on()
    weights.hand_on()
    weights.finish()
    tokens.finish()
    copies.finish()


def group_sum_kernel(v_ref, o_ref, got_ref, local_sem, send_sem, recv_sem):
    greet([T0, T1, DIAG])
    copies = Copies(local_sem, send_sem, recv_sem)
    sent = [copies.send(v_ref, got_ref.at[k], flips) for k, flips in enumerate((T0, T1, DIAG))]
    for copy in sent:
        copy.wait_recv()
    o_ref[...] = v_ref[...] + got_ref[0] + got_ref[1] + got_ref[2]
    copies.finish()


def forward_kernel(
    spans, x_ref, b_ref, c_ref, dt_ref, rate_ref, segc_ref, segr_ref, keep_ref, inflow_ref, carry_ref, cot_ref, out_ref,
    y_ref, st_ref, cum_ref, cots_ref, wout_ref,
    s_ref, pass_ref, got_ref, local_sem, send_sem, recv_sem,
):
    p, _, _, w1, w0 = place()
    greet([T0, T1, CORE, SIDEWAYS, PART])
    copies = Copies(local_sem, send_sem, recv_sem)
    weights = WeightGather(copies, wout_ref, 0)
    weights.spread(out_ref, ())
    copies.keep(out_ref, wout_ref.at[p, w1, w0])
    tokens = GroupGather(copies, cot_ref, cots_ref)
    s_ref[...] = jnp.zeros_like(s_ref)

    def local_states(c, _):
        rows = span_rows(c)
        dt, cum = span_decay(dt_ref, rate_ref, c)
        cum_ref[rows, :] = cum
        last = cum[SPAN - 1 : SPAN, :]
        end_weight = jnp.exp(last - cum) * dt * keep_ref[rows, :]
        decay = jnp.exp(last) * carry_ref[pl.ds(c, 1), :]
        b = b_ref[rows, :]
        st_ref[c] = s_ref[...]
        for q in range(PAIRS):
            lanes = slice(q * LANES, (q + 1) * LANES)
            xw = (x_ref[rows, lanes].astype(f32) * pair_cols(end_weight, 2 * q)).astype(bf16)
            s_ref[:, lanes] = s_ref[:, lanes] * pair_cols(decay, 2 * q) + dot(b, xw, ((0,), (0,)))
        return 0

    lax.fori_loop(0, spans, local_states, 0)
    pass_ref[...] = s_ref[...].astype(bf16)
    state = copies.send(pass_ref, got_ref, PART)
    tokens.hand_on()

    def inside(c, _):
        rows = span_rows(c)
        cum = cum_ref[rows, :]
        back_log = jnp.transpose(cum - jnp.log(dt_ref[rows, :]))
        scores = dot(c_ref[rows, :], b_ref[rows, :], ((1,), (1,)))
        row = lax.broadcasted_iota(jnp.int32, (SPAN, SPAN), 0)
        col = lax.broadcasted_iota(jnp.int32, (SPAN, SPAN), 1)
        mask = (row >= col) & (segc_ref[rows, :] == segr_ref[pl.ds(c, 1), :])
        lane = lax.broadcasted_iota(jnp.int32, (SPAN, LANES), 1)
        for q in range(PAIRS):
            lanes = slice(q * LANES, (q + 1) * LANES)
            x = x_ref[rows, lanes]
            parts = []
            for h in (2 * q, 2 * q + 1):
                gap = cum[:, h : h + 1] - back_log[h : h + 1, :]
                weighted = scores * jnp.exp(jnp.where(mask, gap, -1e30))
                parts.append(dot(weighted.astype(bf16), x))
            y_ref[rows, lanes] = jnp.where(lane < HEADDIM, parts[0], parts[1])
        return 0

    lax.fori_loop(0, spans, inside, 0)
    weights.hand_on()
    state.wait_recv()
    s_ref[...] = got_ref[...].astype(f32) * p.astype(f32)

    def across_spans(c, _):
        rows = span_rows(c)
        cum = cum_ref[rows, :]
        decay = jnp.exp(cum[SPAN - 1 : SPAN, :]) * carry_ref[pl.ds(c, 1), :]
        gain = jnp.exp(cum) * inflow_ref[rows, :]
        cc = c_ref[rows, :]
        for q in range(PAIRS):
            lanes = slice(q * LANES, (q + 1) * LANES)
            entering = s_ref[:, lanes]
            full = st_ref[c, :, lanes] + entering
            st_ref[c, :, lanes] = full
            y_ref[rows, lanes] += dot(cc, full.astype(bf16)) * pair_cols(gain, 2 * q)
            s_ref[:, lanes] = entering * pair_cols(decay, 2 * q)
        return 0

    lax.fori_loop(0, spans, across_spans, 0)
    weights.finish()
    tokens.finish()
    copies.finish()


def backward_kernel(
    spans, x_ref, b_ref, c_ref, dt_ref, ratio_ref, sig_ref, rate_ref, segc_ref, segr_ref, keep_ref, inflow_ref, carry_ref, skip_ref,
    y_ref, st_ref, cum_ref, dy_ref, mix_ref, gout_ref,
    dx_ref, db_ref, dc_ref, ddt_ref, drate_ref, dskip_ref, mixes_ref, g_ref,
    ds_ref, dsl_ref, dyg_ref, dxi_ref, prod_ref, pass_ref, got_ref, core_ref, side_ref, sides_ref, far_ref, fars_ref,
    local_sem, send_sem, recv_sem,
):
    p, t1, t0, w1, w0 = place()
    greet([T0, T1, DIAG, CORE, SIDEWAYS, PART])
    copies = Copies(local_sem, send_sem, recv_sem)
    cores = copies.send(gout_ref.at[:, :, 1 - w0], core_ref, CORE)
    mixes = [
        copies.send(mix_ref.at[t1, 1 - t0], mixes_ref.at[0], T0),
        copies.send(mix_ref.at[1 - t1, t0], mixes_ref.at[1], T1),
        copies.send(mix_ref.at[1 - t1, 1 - t0], mixes_ref.at[2], DIAG),
    ]
    ds_ref[...] = jnp.zeros_like(ds_ref)
    drate_ref[...] = jnp.zeros_like(drate_ref)
    dskip_ref[...] = jnp.zeros_like(dskip_ref)

    def local_states(step, _):
        c = spans - 1 - step
        rows = span_rows(c)
        cum = cum_ref[rows, :]
        decay = jnp.exp(cum[SPAN - 1 : SPAN, :]) * carry_ref[pl.ds(c, 1), :]
        gain = jnp.exp(cum) * inflow_ref[rows, :]
        cc = c_ref[rows, :]
        for q in range(PAIRS):
            lanes = slice(q * LANES, (q + 1) * LANES)
            dyg = (dy_ref[rows, lanes].astype(f32) * pair_cols(gain, 2 * q)).astype(bf16)
            dyg_ref[rows, lanes] = dyg
            ds = ds_ref[:, lanes]
            dsl_ref[c, :, lanes] = ds
            ds_ref[:, lanes] = ds * pair_cols(decay, 2 * q) + dot(cc, dyg, ((0,), (0,)))
        return 0

    lax.fori_loop(0, spans, local_states, 0)
    pass_ref[...] = ds_ref[...].astype(bf16)
    state = copies.send(pass_ref, got_ref, PART)
    cores.wait_recv()
    sides = []
    for k in (0, 1):
        q = 1 - p if k == 0 else p
        side_ref[k] = (gout_ref[q, 1 - w1, w0].astype(f32) + core_ref[q, 1 - w1].astype(f32)).astype(bf16)
        sides.append(copies.send(side_ref.at[k], sides_ref.at[k], SIDEWAYS))

    def inside(c, _):
        rows = span_rows(c)
        cum = cum_ref[rows, :]
        fore_log = jnp.transpose(cum)
        back_log = cum - jnp.log(dt_ref[rows, :])
        b = b_ref[rows, :]
        cc = c_ref[rows, :]
        scores = dot(b, cc, ((1,), (1,)))
        row = lax.broadcasted_iota(jnp.int32, (SPAN, SPAN), 0)
        col = lax.broadcasted_iota(jnp.int32, (SPAN, SPAN), 1)
        mask = (col >= row) & (segc_ref[rows, :] == segr_ref[pl.ds(c, 1), :])
        lane = lax.broadcasted_iota(jnp.int32, (SPAN, LANES), 1)
        d_scores = jnp.zeros((SPAN, SPAN), f32)
        dc = jnp.zeros((SPAN, STATE), f32)
        for q in range(PAIRS):
            lanes = slice(q * LANES, (q + 1) * LANES)
            x = x_ref[rows, lanes]
            dy = dy_ref[rows, lanes]
            xf = x.astype(f32)
            parts = []
            for k in range(2):
                h = 2 * q + k
                gap = fore_log[h : h + 1, :] - back_log[:, h : h + 1]
                decay_mat = jnp.exp(jnp.where(mask, gap, -1e30))
                parts.append(dot((scores * decay_mat).astype(bf16), dy))
                own = (lane < HEADDIM) if k == 0 else (lane >= HEADDIM)
                d_weights = dot(jnp.where(own, xf, 0.0).astype(bf16), dy, ((1,), (1,)))
                d_scores = d_scores + d_weights * decay_mat
            dxi_ref[rows, lanes] = jnp.where(lane < HEADDIM, parts[0], parts[1])
            dc = dc + dot(dyg_ref[rows, lanes], st_ref[c, :, lanes].astype(bf16), ((1,), (1,)))
            dskip_ref[0:1, lanes] += jnp.sum(dy.astype(f32) * xf, axis=0, keepdims=True)
        d_scores_b = d_scores.astype(bf16)
        db_ref[rows, :] = dot(d_scores_b, cc)
        dc_ref[rows, :] = dc + dot(d_scores_b, b, ((0,), (0,)))
        return 0

    lax.fori_loop(0, spans, inside, 0)
    sides[0].wait_recv()
    far_ref[...] = (
        gout_ref[1 - p, w1, w0].astype(f32) + core_ref[1 - p, w1].astype(f32) + sides_ref[0].astype(f32)
    ).astype(bf16)
    far = copies.send(far_ref, fars_ref, PART)
    state.wait_recv()
    ds_ref[...] = got_ref[...].astype(f32) * (1 - p).astype(f32)

    def across_spans(step, _):
        c = spans - 1 - step
        rows = span_rows(c)
        dt = dt_ref[rows, :]
        cum = cum_ref[rows, :]
        last = cum[SPAN - 1 : SPAN, :]
        end_weight = jnp.exp(last - cum) * dt * keep_ref[rows, :]
        decay = jnp.exp(last) * carry_ref[pl.ds(c, 1), :]
        b = b_ref[rows, :]
        db = db_ref[rows, :]
        edges = []
        for q in range(PAIRS):
            lanes = slice(q * LANES, (q + 1) * LANES)
            xf = x_ref[rows, lanes].astype(f32)
            dyf = dy_ref[rows, lanes].astype(f32)
            ew = pair_cols(end_weight, 2 * q)
            dec = pair_cols(decay, 2 * q)
            entering = ds_ref[:, lanes]
            ds = dsl_ref[c, :, lanes] + entering
            ds_ref[:, lanes] = entering * dec
            ds_b = ds.astype(bf16)
            db = db + dot((xf * ew).astype(bf16), ds_b, ((1,), (1,)))
            dx_state = dot(b, ds_b) * ew
            dx = dxi_ref[rows, lanes] + dx_state
            edges.append(
                jnp.sum(ds * st_ref[c, :, lanes], axis=0, keepdims=True) * dec
                + jnp.sum(dx_state * xf, axis=0, keepdims=True)
            )
            prod_ref[0:SPAN, lanes] = dyf * y_ref[rows, lanes]
            prod_ref[SPAN : 2 * SPAN, lanes] = xf * dx
            dx_ref[rows, lanes] = (dx + dyf * skip_ref[0:1, lanes]).astype(bf16)
        db_ref[rows, :] = db
        sums = head_sums(prod_ref[...])
        out_sum, in_sum = sums[:SPAN], sums[SPAN:]
        edge_sum = head_sums(jnp.broadcast_to(jnp.concatenate(edges, axis=1), (8, HALF)))[0:1]
        at_last = lax.broadcasted_iota(jnp.int32, (SPAN, LANES), 0) == SPAN - 1
        d_cum = out_sum - in_sum + jnp.where(at_last, edge_sum, 0.0)
        row = lax.broadcasted_iota(jnp.int32, (SPAN, SPAN), 0)
        col = lax.broadcasted_iota(jnp.int32, (SPAN, SPAN), 1)
        d_log = dot((col >= row).astype(f32), d_cum, precision=exact_prec)
        drate_ref[0:1, :] += jnp.sum(d_log * dt, axis=0, keepdims=True)
        ddt_ref[rows, :] = d_log * rate_ref[0:1, :] * sig_ref[rows, :] + in_sum * ratio_ref[rows, :]
        return 0

    lax.fori_loop(0, spans, across_spans, 0)
    sides[1].wait_recv()
    far.wait_recv()
    g_ref[...] = (
        gout_ref[p, w1, w0].astype(f32)
        + core_ref[p, w1].astype(f32)
        + sides_ref[1].astype(f32)
        + fars_ref[...].astype(f32)
    )
    for copy in mixes:
        copy.wait_recv()
    copies.finish()


def end_kernel(
    dx_ref, g_ref, small_ref,
    dxs_ref, out_ref, total_ref,
    core_ref, side_ref, sides_ref, far_ref, fars_ref, last_ref, lasts_ref, sum_ref, sums_ref,
    local_sem, send_sem, recv_sem,
):
    p, t1, t0, w1, w0 = place()
    greet([T0, T1, DIAG, CORE, SIDEWAYS, PART])
    copies = Copies(local_sem, send_sem, recv_sem)
    blocks = [(t1, t0), (t1, 1 - t0), (1 - t1, t0), (1 - t1, 1 - t0)]
    hops = [None, T0, T1, DIAG]

    def added(q, block, side, mine=None):
        value = g_ref[q, block[0], block[1], side, w0].astype(f32) + core_ref[q, side, block[0], block[1]].astype(f32)
        return value if mine is None else value + mine.astype(f32)

    order = [(1 - p, 1 - w1), (p, 1 - w1), (1 - p, w1), (p, w1)]
    cores = [copies.send(g_ref.at[q, :, :, s, 1 - w0], core_ref.at[q, s], CORE) for q, s in order]
    sums = [small_ref[...]]

    def small_step(k, flips):
        sum_ref[k] = sums[0]
        return copies.send(sum_ref.at[k], sums_ref.at[k], flips)

    def small_end(k, copy):
        copy.wait_recv()
        sums[0] = sums[0] + sums_ref[k]

    small = small_step(0, CORE)
    dxs = [
        copies.send(dx_ref.at[t1, 1 - t0], dxs_ref.at[0], T0),
        copies.send(dx_ref.at[1 - t1, t0], dxs_ref.at[1], T1),
        copies.send(dx_ref.at[1 - t1, 1 - t0], dxs_ref.at[2], DIAG),
    ]
    sides = [[], []]
    for k, q in enumerate((1 - p, p)):
        cores[k].wait_recv()
        for i, block in enumerate(blocks):
            side_ref[k, i] = added(q, block, 1 - w1).astype(bf16)
            sides[k].append(copies.send(side_ref.at[k, i], sides_ref.at[k, i], SIDEWAYS))
    small_end(0, small)
    small = small_step(1, SIDEWAYS)
    cores[2].wait_recv()
    cores[3].wait_recv()
    fars = []
    for i, block in enumerate(blocks):
        sides[0][i].wait_recv()
        far_ref[i] = added(1 - p, block, w1, sides_ref[0, i]).astype(bf16)
        fars.append(copies.send(far_ref.at[i], fars_ref.at[i], PART))
    small_end(1, small)
    small = small_step(2, PART)
    lasts = []
    for i, block in enumerate(blocks):
        sides[1][i].wait_recv()
        fars[i].wait_recv()
        value = added(p, block, w1, sides_ref[1, i]) + fars_ref[i].astype(f32)
        if i == 0:
            out_ref[t1, t0] = value
        else:
            last_ref[i - 1] = value.astype(bf16)
            lasts.append(copies.send(last_ref.at[i - 1], lasts_ref.at[i - 1], hops[i]))
    small_end(2, small)
    small = small_step(3, T0)
    small_end(3, small)
    small = small_step(4, T1)
    for i, block in enumerate(blocks[1:]):
        lasts[i].wait_recv()
        out_ref[block[0], block[1]] = lasts_ref[i].astype(f32)
    small_end(4, small)
    total_ref[...] = sums[0]
    for copy in dxs:
        copy.wait_recv()
    copies.finish()


VMEM_LIMIT = 60 * 1024 * 1024


def in_vmem(kernel, out_shape, name, scratch=()):
    return pl.pallas_call(
        kernel,
        out_shape=out_shape,
        scratch_shapes=list(scratch),
        name=name,
        compiler_params=pltpu.CompilerParams(vmem_limit_bytes=VMEM_LIMIT),
    )


def shape(dims, dtype):
    return jax.ShapeDtypeStruct(dims, dtype)


HBM = pl.BlockSpec(memory_space=pl.ANY)
VMEM = pl.BlockSpec(memory_space=pltpu.VMEM)


def linked(kernel, name, collective_id, in_specs, outs, scratch):
    return pl.pallas_call(
        kernel,
        name=name,
        in_specs=in_specs,
        out_shape=tuple(o for o, _ in outs),
        out_specs=tuple(s for _, s in outs),
        scratch_shapes=scratch,
        compiler_params=pltpu.CompilerParams(
            collective_id=collective_id, has_side_effects=True, vmem_limit_bytes=VMEM_LIMIT
        ),
    )


GROUP = ("t1", "t0")
COPIES = ("part", "w1", "w0")
EVERYONE = ("part", "t1", "t0", "w1", "w0")


def group_sum(values, collective_id):
    size = values.shape[0]
    padded = jnp.pad(values, (0, -size % (8 * LANES))).reshape(-1, LANES)
    box = shape(padded.shape, f32)
    (total,) = linked(
        group_sum_kernel, "group_sum", collective_id, [VMEM], [(box, VMEM)], [pltpu.VMEM((3, *padded.shape), f32), *sems(3)]
    )(padded)
    return total.reshape(-1)[:size]


def shift_part(array, by):
    size = lax.axis_size("part")
    pairs = [(i, i + by) for i in range(size) if 0 <= i + by < size]
    return lax.ppermute(array, "part", pairs)


def shards(
    hidden, cotangent, segments, valid, in_w, in_m, in_v, out_w, out_m, out_v, small_w, small_m, small_v,
):
    parts = lax.axis_size("part")
    wt = lax.axis_size("w1") * lax.axis_size("w0")
    part = lax.axis_index("part")
    tp = lax.axis_index("t1") * 2 + lax.axis_index("t0")
    own_rows = in_w.shape[0]
    out_rows = out_w.shape[0]
    resid = hidden[0].astype(f32)
    tok_rows = resid.shape[0]
    rows = tok_rows * TP
    spans = rows // SPAN
    seg_all = segments[0]
    pre_gain, norm_gain, conv_weight, conv_bias, dt_shift, a_logs, skips = unpack_small(small_w)

    def own_part(array, width):
        return lax.dynamic_slice_in_dim(array, tp * width, width, array.ndim - 1)

    in_copy = in_w.astype(bf16)
    slices = []
    for j in range(TP):
        slices.append(
            jnp.concatenate(
                [
                    in_copy[:, D_INNER + j * HALF : D_INNER + (j + 1) * HALF],
                    in_copy[:, 2 * D_INNER : 2 * D_INNER + SIDE],
                    in_copy[:, D_INNER + CONVCH + j * LOCAL_HEADS : D_INNER + CONVCH + (j + 1) * LOCAL_HEADS],
                    jnp.zeros((own_rows, LANES - LOCAL_HEADS), bf16),
                    in_copy[:, j * HALF : (j + 1) * HALF],
                ],
                axis=1,
            )
        )
    flat = [(i, (i % TP) * parts + i // TP) for i in range(parts * TP)]
    out_mine = lax.ppermute(out_w.astype(bf16), ("part", *GROUP), [(b, a) for a, b in flat])
    back_mix = cotangent[0] * valid[0][:, None].astype(bf16)
    fast = parts == 2 and wt == 4 and own_rows % 16 == 0 and out_rows % 16 == 0 and tok_rows % 32 == 0
    if fast:
        block = (2, 2, tok_rows, D)
        hidden_all, w_in = linked(
            start_kernel, "start", 1, [HBM, HBM],
            [(shape(block, bf16), HBM), (shape((2, 2, 2, 2, 2, own_rows, COLS), bf16), HBM)],
            sems(40, 2),
        )(hidden[0], jnp.stack(slices).reshape(2, 2, own_rows, COLS))
        hidden_all = hidden_all.reshape(rows, D)
        w_in = w_in.reshape(D, COLS)
    else:
        mine = lax.all_to_all(jnp.stack(slices), GROUP, 0, 0, tiled=False)
        w_in = lax.all_gather(mine, COPIES, axis=0, tiled=False)
        w_in = w_in.reshape(parts, wt, TP, own_rows, COLS).transpose(0, 2, 1, 3, 4).reshape(D, COLS)
        w_out = lax.all_gather(out_mine, COPIES, axis=0, tiled=True)
        hidden_all = lax.all_gather(hidden[0], GROUP, axis=0, tiled=True)
        back_all = lax.all_gather(back_mix, GROUP, axis=0, tiled=True)

    hid = hidden_all.astype(f32)
    scale_all = lax.rsqrt(jnp.mean(hid * hid, axis=1, keepdims=True) + norm_eps)
    x_normed = (hid * scale_all * pre_gain).astype(bf16)
    projected = dot(x_normed, w_in)
    conv_in = projected[:, :COL_DT].astype(bf16)
    dt_raw = projected[:, COL_DT:COL_GATE].astype(bf16).astype(f32)
    gate_pre = projected[:, COL_GATE:]
    rim_in = shift_part(conv_in[rows - RIM :], 1)
    padded = jnp.concatenate([rim_in, conv_in], axis=0).astype(f32)
    seg_front = jnp.concatenate([jnp.full((RIM,), -1, jnp.int32), seg_all, jnp.full((RIM,), -1, jnp.int32)])
    seg_pad = lax.dynamic_slice_in_dim(seg_front, part * rows, rows + 2 * RIM)
    seg = seg_pad[RIM : RIM + rows]
    masks = [(seg_pad[k : k + rows] == seg).astype(f32)[:, None] for k in range(CONV)]
    taps = jnp.concatenate([own_part(conv_weight[:, :D_INNER], HALF), conv_weight[:, D_INNER:]], axis=1)
    bias = jnp.concatenate([own_part(conv_bias[:D_INNER], HALF), conv_bias[D_INNER:]])
    total = bias[None, :]
    for k in range(CONV):
        total = total + taps[k] * padded[k : k + rows] * masks[k]
    sig_total = jax.nn.sigmoid(total)
    activated = (total * sig_total).astype(bf16)
    x_scan = activated[:, :HALF]
    b_mat = activated[:, HALF : HALF + STATE]
    c_mat = activated[:, HALF + STATE :]

    def head_row(array):
        return jnp.pad(own_part(array, LOCAL_HEADS), (0, LANES - LOCAL_HEADS))

    shift_row = head_row(dt_shift)
    z = dt_raw + shift_row
    dt = jax.nn.softplus(z)
    sig_dt = jax.nn.sigmoid(z)
    ratio = jnp.where(dt > 1e-30, sig_dt / jnp.maximum(dt, 1e-30), 1.0)
    rate_row = -jnp.exp(head_row(a_logs))
    rate8 = jnp.broadcast_to(rate_row, (8, LANES))
    skip_chan = jnp.repeat(own_part(skips, LOCAL_HEADS), HEADDIM)
    skip8 = jnp.broadcast_to(skip_chan, (8, HALF))
    seg_spans = seg.reshape(spans, SPAN)
    seg_last = seg_spans[:, -1]
    seg_before = jnp.concatenate([seg_pad[RIM - 1 : RIM], seg_last[:-1]])
    keep = (seg_spans == seg_last[:, None]).astype(f32).reshape(rows, 1)
    inflow = (seg_spans == seg_before[:, None]).astype(f32).reshape(rows, 1)
    carry = jnp.broadcast_to((seg_last == seg_before).astype(f32)[:, None], (spans, LANES))
    seg_col = seg[:, None]

    state_shape = shape((STATE, HALF), f32)
    state_buf = pltpu.VMEM((STATE, HALF), f32)
    state_half = pltpu.VMEM((STATE, HALF), bf16)
    if fast:
        y_scan, states, cum, back_all, w_out = linked(
            functools.partial(forward_kernel, spans), "forward", 2, [VMEM] * 10 + [HBM] * 2,
            [
                (shape((rows, HALF), f32), VMEM),
                (shape((spans, STATE, HALF), f32), VMEM),
                (shape((rows, LANES), f32), VMEM),
                (shape(block, bf16), HBM),
                (shape((2, 2, 2, out_rows, D), bf16), HBM),
            ],
            [state_buf, state_half, state_half, *sems(20, 2)],
        )(x_scan, b_mat, c_mat, dt, rate8, seg_col, seg_spans, keep, inflow, carry, back_mix, out_mine)
        back_all = back_all.reshape(rows, D)
        w_out = w_out.reshape(HALF, D)
    else:
        s_local, dec_total = in_vmem(
            functools.partial(state_kernel, spans), (state_shape, shape((8, LANES), f32)), "state"
        )(x_scan, b_mat, dt, rate8, keep, carry)
        dec_chan = jnp.repeat(dec_total[0, :LOCAL_HEADS], HEADDIM)
        s_in = jnp.zeros((STATE, HALF), f32)
        for _ in range(parts - 1):
            s_in = shift_part(dec_chan * s_in + s_local, 1)
        y_scan, states = in_vmem(
            functools.partial(scan_kernel, spans),
            (shape((rows, HALF), f32), shape((spans, STATE, HALF), f32)),
            "scan",
            [pltpu.VMEM((STATE, HALF), f32)],
        )(x_scan, b_mat, c_mat, dt, rate8, seg_col, seg_spans, keep, inflow, carry, s_in)
    y_b = (y_scan + skip_chan * x_scan.astype(f32)).astype(bf16).astype(f32)

    gain_own = own_part(norm_gain, HALF)
    sig_gate = jax.nn.sigmoid(gate_pre)
    silu_gate = gate_pre * sig_gate
    gated = y_b * silu_gate
    gate_sq = jnp.sum(gated * gated, axis=1)
    gate_sq = group_sum(gate_sq, 3) if fast else lax.psum(gate_sq, GROUP)
    scale_gate = lax.rsqrt(gate_sq / D_INNER + norm_eps)[:, None]
    normed = (gated * scale_gate * gain_own).astype(bf16)
    mixer = dot(normed, w_out)

    d_normed = dot(back_all, w_out, ((1,), (1,)))
    g_out = dot(normed, back_all, ((0,), (0,)))
    d_gain = d_normed * gain_own
    gate_dot = jnp.sum(gated * d_gain, axis=1)
    gate_dot = group_sum(gate_dot, 4) if fast else lax.psum(gate_dot, GROUP)
    d_gated = scale_gate * d_gain - gated * (scale_gate**3 * (gate_dot / D_INNER)[:, None])
    d_norm_gain = jnp.sum(gated * scale_gate * d_normed, axis=0)
    dy = (d_gated * silu_gate).astype(bf16)
    d_gate = d_gated * y_b * (sig_gate * (1.0 + gate_pre * (1.0 - sig_gate)))

    scan_outs = (
        shape((rows, HALF), bf16),
        shape((rows, STATE), f32),
        shape((rows, STATE), f32),
        shape((rows, LANES), f32),
        shape((8, LANES), f32),
        shape((8, HALF), f32),
    )

    def own_block(blocks):
        return lax.dynamic_index_in_dim(blocks.reshape(TP, tok_rows, D), tp, 0, keepdims=False).astype(f32)

    if fast:
        mixer = mixer.astype(bf16).reshape(block)
        piece = (out_rows, D)
        d_x, d_b, d_c, d_dt, d_rate, d_skip, mixes, g_out = linked(
            functools.partial(backward_kernel, spans), "backward", 5, [VMEM] * 17 + [HBM, VMEM],
            [*((o, VMEM) for o in scan_outs), (shape((3, tok_rows, D), bf16), HBM), (shape(piece, f32), VMEM)],
            [
                state_buf,
                pltpu.VMEM((spans, STATE, HALF), f32),
                pltpu.VMEM((rows, HALF), bf16),
                pltpu.VMEM((rows, HALF), f32),
                pltpu.VMEM((2 * SPAN, HALF), f32),
                state_half,
                state_half,
                pltpu.VMEM((2, 2, *piece), bf16),
                pltpu.VMEM((2, *piece), bf16),
                pltpu.VMEM((2, *piece), bf16),
                pltpu.VMEM(piece, bf16),
                pltpu.VMEM(piece, bf16),
                *sems(8),
            ],
        )(
            x_scan, b_mat, c_mat, dt, ratio, sig_dt, rate8, seg_col, seg_spans, keep, inflow, carry, skip8,
            y_scan, states, cum, dy, mixer, g_out.astype(bf16).reshape(2, 2, 2, *piece),
        )
        mixer = own_block(mixer) + jnp.sum(mixes.astype(f32), axis=0)
    else:
        ds_local = in_vmem(functools.partial(state_back_kernel, spans), state_shape, "state_back")(
            dy, c_mat, dt, rate8, inflow, carry
        )
        ds_out = jnp.zeros((STATE, HALF), f32)
        for _ in range(parts - 1):
            ds_out = shift_part(dec_chan * ds_out + ds_local, -1)
        d_x, d_b, d_c, d_dt, d_rate, d_skip = in_vmem(
            functools.partial(scan_back_kernel, spans),
            (
                shape((rows, HALF), bf16),
                shape((rows, STATE), f32),
                shape((rows, STATE), f32),
                shape((rows, LANES), f32),
                shape((8, LANES), f32),
                shape((8, HALF), f32),
            ),
            "scan_back",
            [pltpu.VMEM((STATE, HALF), f32), pltpu.VMEM((2 * SPAN, HALF), f32)],
        )(x_scan, b_mat, c_mat, dt, ratio, sig_dt, rate8, seg_col, seg_spans, keep, inflow, carry, skip8, y_scan, states, dy, ds_out)
        mixer = lax.psum_scatter(mixer, GROUP, scatter_dimension=0, tiled=True)
        g_out = lax.psum_scatter(g_out, COPIES, scatter_dimension=0, tiled=True)
    g_out = lax.ppermute(g_out, ("part", *GROUP), flat)
    output = (resid + mixer).astype(bf16)
    valid_rows = valid[0].astype(f32)
    res_sq = jnp.sum(valid_rows * jnp.sum(resid * resid, axis=1))
    mix_sq = jnp.sum(valid_rows * jnp.sum(mixer * mixer, axis=1))
    valid_count = jnp.sum(valid_rows)

    d_total = jnp.concatenate([d_x.astype(f32), d_b, d_c], axis=1) * (sig_total * (1.0 + total * (1.0 - sig_total)))
    rim_back = shift_part(d_total[:RIM], -1)
    d_padded = jnp.concatenate([d_total, rim_back], axis=0)
    d_conv_in = 0.0
    for k in range(CONV):
        later = (seg_pad[2 * RIM - k : 2 * RIM - k + rows] == seg).astype(f32)[:, None]
        d_conv_in = d_conv_in + taps[k] * d_padded[RIM - k : RIM - k + rows] * later
    d_taps = jnp.stack([jnp.sum(d_total * padded[k : k + rows] * masks[k], axis=0) for k in range(CONV)])
    d_bias = jnp.sum(d_total, axis=0)
    d_proj = jnp.concatenate([d_conv_in, d_dt, d_gate], axis=1).astype(bf16)
    d_x_normed = dot(d_proj, w_in, ((1,), (1,)))
    g_in = dot(x_normed, d_proj, ((0,), (0,)))
    d_pre_gain = jnp.sum(hid * scale_all * d_x_normed, axis=0)

    def placed(values, width):
        spread = (jnp.arange(TP) == tp).astype(f32)[:, None] * values[..., None, :]
        return spread.reshape(*values.shape[:-1], TP * width)

    d_weight = jnp.concatenate([placed(d_taps[:, :HALF], HALF), d_taps[:, HALF:]], axis=1)
    small_grad = jnp.concatenate(
        [
            d_pre_gain,
            placed(d_norm_gain, HALF),
            d_weight.reshape(-1),
            placed(d_bias[:HALF], HALF),
            d_bias[HALF:],
            placed(jnp.sum(d_dt, axis=0)[:LOCAL_HEADS], LOCAL_HEADS),
            placed((d_rate[0] * rate_row)[:LOCAL_HEADS], LOCAL_HEADS),
            placed(jnp.sum(d_skip[0].reshape(LOCAL_HEADS, HEADDIM), axis=1), LOCAL_HEADS),
            jnp.stack([res_sq, mix_sq, valid_count]),
        ]
    )
    if fast:
        count = small_grad.shape[0]
        small_box = jnp.pad(small_grad, (0, -count % (8 * LANES))).reshape(-1, LANES)
        piece = (own_rows, COLS)
        halves = pltpu.VMEM((TP, *piece), bf16)
        small_steps = pltpu.VMEM((5, *small_box.shape), f32)
        d_x_normed = d_x_normed.astype(bf16).reshape(block)
        d_xs, g_in, small_total = linked(
            end_kernel, "end", 6, [HBM, VMEM, VMEM],
            [
                (shape((3, tok_rows, D), bf16), HBM),
                (shape((2, 2, *piece), f32), VMEM),
                (shape(small_box.shape, f32), VMEM),
            ],
            [
                pltpu.VMEM((2, 2, 2, 2, *piece), bf16),
                pltpu.VMEM((2, TP, *piece), bf16),
                pltpu.VMEM((2, TP, *piece), bf16),
                halves,
                halves,
                pltpu.VMEM((TP - 1, *piece), bf16),
                pltpu.VMEM((TP - 1, *piece), bf16),
                small_steps,
                small_steps,
                *sems(27),
            ],
        )(d_x_normed, g_in.astype(bf16).reshape(2, 2, 2, 2, 2, *piece), small_box)
        d_x_normed = own_block(d_x_normed) + jnp.sum(d_xs.astype(f32), axis=0)
        g_in = g_in.reshape(TP, *piece)
        small_total = small_total.reshape(-1)[:count]
    else:
        d_x_normed = lax.psum_scatter(d_x_normed, GROUP, scatter_dimension=0, tiled=True)
        g_in = g_in.reshape(parts, TP, wt, own_rows, COLS).transpose(0, 2, 1, 3, 4)
        g_in = g_in.reshape(parts * wt, TP, own_rows, COLS)
        g_in = lax.psum_scatter(g_in, COPIES, scatter_dimension=0, tiled=False)
        g_in = lax.all_to_all(g_in, GROUP, 0, 0, tiled=False)
        small_total = lax.psum(small_grad, EVERYONE)
    g_in = jnp.concatenate(
        [g_in[j, :, COL_GATE:] for j in range(TP)]
        + [g_in[j, :, :HALF] for j in range(TP)]
        + [jnp.sum(g_in[:, :, COL_SIDE:COL_DT], axis=0)]
        + [g_in[j, :, COL_DT : COL_DT + LOCAL_HEADS] for j in range(TP)],
        axis=1,
    )

    scale_own = lax.rsqrt(jnp.mean(resid * resid, axis=1, keepdims=True) + norm_eps)
    d_pre = d_x_normed * pre_gain
    dot_pre = jnp.mean(resid * d_pre, axis=1, keepdims=True)
    grad_hidden = back_mix.astype(f32) + scale_own * d_pre - resid * (scale_own**3 * dot_pre)
    res_total, mix_total, count_total = small_total[-3], small_total[-2], small_total[-1]
    in_m_new, in_v_new, in_w_new = adamw(in_w, in_m, in_v, g_in, 0.02, 0.1)
    out_m_new, out_v_new, out_w_new = adamw(out_w, out_m, out_v, g_out, 0.02, 0.1)
    small_m_new, small_v_new, small_w_new = adamw(small_w, small_m, small_v, small_total[:-3], 0.2, 0.0)
    rms = jnp.stack([jnp.sqrt(res_total / (count_total * D)), jnp.sqrt(mix_total / (count_total * D))])
    return (
        output[None], grad_hidden[None], in_m_new, in_v_new, in_w_new, out_m_new, out_v_new, out_w_new,
        small_m_new, small_v_new, small_w_new, rms,
    )


def solution(mesh):
    seq, wt = mesh.shape["seq"], mesh.shape["wt"]
    split = Mesh(mesh.devices.reshape(seq // TP, 2, 2, wt // 2, 2), EVERYONE)
    streams = ("w1", "w0")
    tokens = ("part", "t1", "t0")
    matrix = P(EVERYONE, None)
    stream = P(streams, tokens, None)
    return jax.shard_map(
        shards,
        mesh=split,
        in_specs=(
            stream, stream, P(streams, None), P(streams, tokens), matrix, matrix, matrix, matrix, matrix, matrix, P(), P(), P(),
        ),
        out_specs=(stream, stream, matrix, matrix, matrix, matrix, matrix, matrix, P(), P(), P(), P()),
        check_vma=False,
    )
```

```python
import functools

import jax
import jax.numpy as jnp
from jax import lax
from jax.experimental import pallas as pl
from jax.experimental.pallas import tpu as pltpu
from jax.sharding import Mesh
from jax.sharding import PartitionSpec as P

D = 1536
D_INNER = 3072
HEADS = 48
HEADDIM = 64
STATE = 128
CONV = 4
SPAN = 256
STEP = 4
CONVCH = 3328
TP = 4
RIM = CONV - 1
LANES = 128
HALF = D_INNER // TP
LOCAL_HEADS = HEADS // TP
PAIRS = LOCAL_HEADS // 2
SIDE = 2 * STATE
COL_SIDE = HALF
COL_DT = HALF + SIDE
COL_GATE = COL_DT + LANES
COLS = COL_GATE + HALF

bf16 = jnp.bfloat16
f32 = jnp.float32
exact_prec = lax.Precision.HIGHEST
norm_eps = 1e-05
adam_eps = 1e-08


def dot(a, b, dims=((1,), (0,)), precision=None):
    return lax.dot_general(a, b, (dims, ((), ())), precision=precision, preferred_element_type=f32)


def unpack_small(small):
    first = D
    second = first + D_INNER
    third = second + CONV * CONVCH
    fourth = third + CONVCH
    fifth = fourth + HEADS
    sixth = fifth + HEADS
    return (
        small[:first],
        small[first:second],
        small[second:third].reshape(CONV, CONVCH),
        small[third:fourth],
        small[fourth:fifth],
        small[fifth:sixth],
        small[sixth:],
    )


def adamw(weight, moment, second, grad, rate, decay):
    moment_new = 0.5 * moment + 0.5 * grad
    second_new = 0.5 * second + 0.5 * grad * grad
    first_hat = moment_new / (1.0 - 0.5**STEP)
    second_hat = second_new / (1.0 - 0.5**STEP)
    weight_new = weight - rate * (first_hat / (jnp.sqrt(second_hat) + adam_eps) + decay * weight)
    return (moment_new, second_new, weight_new)


def pair_cols(cols, h):
    lane = lax.broadcasted_iota(jnp.int32, (cols.shape[0], LANES), 1)
    return jnp.where(lane < HEADDIM, cols[:, h : h + 1], cols[:, h + 1 : h + 2])


def span_rows(c):
    return pl.ds(pl.multiple_of(c * SPAN, SPAN), SPAN)


def span_decay(dt_ref, rate_ref, c, at=0):
    dt = dt_ref[span_rows(c), :]
    row = lax.broadcasted_iota(jnp.int32, (SPAN, SPAN), 0)
    col = lax.broadcasted_iota(jnp.int32, (SPAN, SPAN), 1)
    lower = (row >= col).astype(f32)
    return dt, dot(lower, dt * rate_ref[at : at + 1, :], precision=exact_prec)


def state_kernel(spans, x_ref, b_ref, dt_ref, rate_ref, keep_ref, carry_ref, s_ref, dec_ref):
    s_ref[...] = jnp.zeros_like(s_ref)
    dec_ref[...] = jnp.ones_like(dec_ref)

    def body(c, _):
        rows = span_rows(c)
        dt, cum = span_decay(dt_ref, rate_ref, c)
        last = cum[SPAN - 1 : SPAN, :]
        end_weight = jnp.exp(last - cum) * dt * keep_ref[rows, :]
        decay = jnp.exp(last) * carry_ref[pl.ds(c, 1), :]
        dec_ref[...] = dec_ref[...] * decay
        b = b_ref[rows, :]
        for p in range(PAIRS):
            lanes = slice(p * LANES, (p + 1) * LANES)
            xw = (x_ref[rows, lanes].astype(f32) * pair_cols(end_weight, 2 * p)).astype(bf16)
            fresh = dot(b, xw, ((0,), (0,)))
            s_ref[:, lanes] = s_ref[:, lanes] * pair_cols(decay, 2 * p) + fresh
        return 0

    lax.fori_loop(0, spans, body, 0)


def scan_kernel(
    spans, x_ref, b_ref, c_ref, dt_ref, rate_ref, segc_ref, segr_ref, keep_ref, inflow_ref, carry_ref, s_in_ref,
    y_ref, st_ref, s_ref,
):
    s_ref[...] = s_in_ref[...]

    def body(c, _):
        rows = span_rows(c)
        dt, cum = span_decay(dt_ref, rate_ref, c)
        last = cum[SPAN - 1 : SPAN, :]
        end_weight = jnp.exp(last - cum) * dt * keep_ref[rows, :]
        decay = jnp.exp(last) * carry_ref[pl.ds(c, 1), :]
        gain = jnp.exp(cum) * inflow_ref[rows, :]
        back_log = jnp.transpose(cum - jnp.log(dt))
        b = b_ref[rows, :]
        cc = c_ref[rows, :]
        scores = dot(cc, b, ((1,), (1,)))
        row = lax.broadcasted_iota(jnp.int32, (SPAN, SPAN), 0)
        col = lax.broadcasted_iota(jnp.int32, (SPAN, SPAN), 1)
        mask = (row >= col) & (segc_ref[rows, :] == segr_ref[pl.ds(c, 1), :])
        lane = lax.broadcasted_iota(jnp.int32, (SPAN, LANES), 1)
        st_ref[c] = s_ref[...]
        for p in range(PAIRS):
            lanes = slice(p * LANES, (p + 1) * LANES)
            x = x_ref[rows, lanes]
            parts = []
            for h in (2 * p, 2 * p + 1):
                gap = cum[:, h : h + 1] - back_log[h : h + 1, :]
                weights = scores * jnp.exp(jnp.where(mask, gap, -1e30))
                parts.append(dot(weights.astype(bf16), x))
            y = jnp.where(lane < HEADDIM, parts[0], parts[1])
            state = s_ref[:, lanes]
            y = y + dot(cc, state.astype(bf16)) * pair_cols(gain, 2 * p)
            y_ref[rows, lanes] = y
            xw = (x.astype(f32) * pair_cols(end_weight, 2 * p)).astype(bf16)
            s_ref[:, lanes] = state * pair_cols(decay, 2 * p) + dot(b, xw, ((0,), (0,)))
        return 0

    lax.fori_loop(0, spans, body, 0)


def state_back_kernel(spans, dy_ref, c_ref, dt_ref, rate_ref, inflow_ref, carry_ref, s_ref):
    s_ref[...] = jnp.zeros_like(s_ref)

    def body(step, _):
        c = spans - 1 - step
        rows = span_rows(c)
        dt, cum = span_decay(dt_ref, rate_ref, c)
        decay = jnp.exp(cum[SPAN - 1 : SPAN, :]) * carry_ref[pl.ds(c, 1), :]
        gain = jnp.exp(cum) * inflow_ref[rows, :]
        cc = c_ref[rows, :]
        for p in range(PAIRS):
            lanes = slice(p * LANES, (p + 1) * LANES)
            dyg = (dy_ref[rows, lanes].astype(f32) * pair_cols(gain, 2 * p)).astype(bf16)
            s_ref[:, lanes] = s_ref[:, lanes] * pair_cols(decay, 2 * p) + dot(cc, dyg, ((0,), (0,)))
        return 0

    lax.fori_loop(0, spans, body, 0)


def head_sums(values):
    width = values.shape[1]
    chan = lax.broadcasted_iota(jnp.int32, (width, LANES), 0)
    head = lax.broadcasted_iota(jnp.int32, (width, LANES), 1)
    pick = (chan // HEADDIM == head).astype(bf16)
    high = values.astype(bf16)
    low = (values - high.astype(f32)).astype(bf16)
    return dot(high, pick) + dot(low, pick)


def scan_back_kernel(
    spans, x_ref, b_ref, c_ref, dt_ref, ratio_ref, sig_ref, rate_ref, segc_ref, segr_ref, keep_ref, inflow_ref, carry_ref, skip_ref,
    y_ref, st_ref, dy_ref, ds_out_ref,
    dx_ref, db_ref, dc_ref, ddt_ref, drate_ref, dskip_ref,
    ds_ref, prod_ref,
):
    ds_ref[...] = ds_out_ref[...]
    drate_ref[...] = jnp.zeros_like(drate_ref)
    dskip_ref[...] = jnp.zeros_like(dskip_ref)

    def body(step, _):
        c = spans - 1 - step
        rows = span_rows(c)
        dt, cum = span_decay(dt_ref, rate_ref, c)
        last = cum[SPAN - 1 : SPAN, :]
        end_weight = jnp.exp(last - cum) * dt * keep_ref[rows, :]
        decay = jnp.exp(last) * carry_ref[pl.ds(c, 1), :]
        gain = jnp.exp(cum) * inflow_ref[rows, :]
        fore_log = jnp.transpose(cum)
        back_log = cum - jnp.log(dt)
        b = b_ref[rows, :]
        cc = c_ref[rows, :]
        scores = dot(b, cc, ((1,), (1,)))
        row = lax.broadcasted_iota(jnp.int32, (SPAN, SPAN), 0)
        col = lax.broadcasted_iota(jnp.int32, (SPAN, SPAN), 1)
        mask = (col >= row) & (segc_ref[rows, :] == segr_ref[pl.ds(c, 1), :])
        lane = lax.broadcasted_iota(jnp.int32, (SPAN, LANES), 1)
        d_scores = jnp.zeros((SPAN, SPAN), f32)
        db = jnp.zeros((SPAN, STATE), f32)
        dc = jnp.zeros((SPAN, STATE), f32)
        state_row = []
        dx_state_row = []
        for p in range(PAIRS):
            lanes = slice(p * LANES, (p + 1) * LANES)
            x = x_ref[rows, lanes]
            dy = dy_ref[rows, lanes]
            xf = x.astype(f32)
            dyf = dy.astype(f32)
            parts = []
            for k in range(2):
                h = 2 * p + k
                gap = fore_log[h : h + 1, :] - back_log[:, h : h + 1]
                decay_mat = jnp.exp(jnp.where(mask, gap, -1e30))
                weights = (scores * decay_mat).astype(bf16)
                parts.append(dot(weights, dy))
                own = (lane < HEADDIM) if k == 0 else (lane >= HEADDIM)
                d_weights = dot(jnp.where(own, xf, 0.0).astype(bf16), dy, ((1,), (1,)))
                d_scores = d_scores + d_weights * decay_mat
            dx = jnp.where(lane < HEADDIM, parts[0], parts[1])
            dyg = (dyf * pair_cols(gain, 2 * p)).astype(bf16)
            ew = pair_cols(end_weight, 2 * p)
            xw = (xf * ew).astype(bf16)
            state = st_ref[c, :, lanes]
            ds = ds_ref[:, lanes]
            state_b = state.astype(bf16)
            ds_b = ds.astype(bf16)
            dc = dc + dot(dyg, state_b, ((1,), (1,)))
            db = db + dot(xw, ds_b, ((1,), (1,)))
            dx_state = dot(b, ds_b) * ew
            dx = dx + dx_state
            dec = pair_cols(decay, 2 * p)
            state_row.append(jnp.sum(ds * state, axis=0, keepdims=True) * dec)
            dx_state_row.append(jnp.sum(dx_state * xf, axis=0, keepdims=True))
            ds_ref[:, lanes] = ds * dec + dot(cc, dyg, ((0,), (0,)))
            prod_ref[0:SPAN, lanes] = dyf * y_ref[rows, lanes]
            prod_ref[SPAN : 2 * SPAN, lanes] = xf * dx
            dskip_ref[0:1, lanes] += jnp.sum(dyf * xf, axis=0, keepdims=True)
            dx_ref[rows, lanes] = (dx + dyf * skip_ref[0:1, lanes]).astype(bf16)
        d_scores_b = d_scores.astype(bf16)
        db_ref[rows, :] = db + dot(d_scores_b, cc)
        dc_ref[rows, :] = dc + dot(d_scores_b, b, ((0,), (0,)))
        sums = head_sums(prod_ref[...])
        out_sum, in_sum = sums[:SPAN], sums[SPAN:]
        edge = jnp.concatenate(state_row, axis=1) + jnp.concatenate(dx_state_row, axis=1)
        edge_sum = head_sums(jnp.broadcast_to(edge, (8, HALF)))[0:1]
        at_last = lax.broadcasted_iota(jnp.int32, (SPAN, LANES), 0) == SPAN - 1
        d_cum = out_sum - in_sum + jnp.where(at_last, edge_sum, 0.0)
        upper = (col >= row).astype(f32)
        d_log = dot(upper, d_cum, precision=exact_prec)
        drate_ref[0:1, :] += jnp.sum(d_log * dt, axis=0, keepdims=True)
        ddt_ref[rows, :] = d_log * rate_ref[0:1, :] * sig_ref[rows, :] + in_sum * ratio_ref[rows, :]
        return 0

    lax.fori_loop(0, spans, body, 0)


GROUP = ("t1", "t0")
COPIES = ("part", "w1", "w0")
EVERYONE = ("part", "t1", "t0", "w1", "w0")


VMEM_LIMIT = 60 * 1024 * 1024


def in_vmem(kernel, out_shape, name, scratch=()):
    return pl.pallas_call(
        kernel,
        out_shape=out_shape,
        scratch_shapes=list(scratch),
        name=name,
        compiler_params=pltpu.CompilerParams(vmem_limit_bytes=VMEM_LIMIT),
    )


def shape(dims, dtype):
    return jax.ShapeDtypeStruct(dims, dtype)


def shift_part(array, by):
    size = lax.axis_size("part")
    pairs = [(i, i + by) for i in range(size) if 0 <= i + by < size]
    return lax.ppermute(array, "part", pairs)


def shards_general(
    hidden, cotangent, segments, valid, in_w, in_m, in_v, out_w, out_m, out_v, small_w, small_m, small_v,
):
    parts = lax.axis_size("part")
    wt = lax.axis_size("w1") * lax.axis_size("w0")
    part = lax.axis_index("part")
    tp = lax.axis_index("t1") * 2 + lax.axis_index("t0")
    own_rows = in_w.shape[0]
    out_rows = out_w.shape[0]
    resid = hidden[0].astype(f32)
    tok_rows = resid.shape[0]
    rows = tok_rows * TP
    spans = rows // SPAN
    seg_all = segments[0]
    pre_gain, norm_gain, conv_weight, conv_bias, dt_shift, a_logs, skips = unpack_small(small_w)

    def own_part(array, width):
        return lax.dynamic_slice_in_dim(array, tp * width, width, array.ndim - 1)

    in_copy = in_w.astype(bf16)
    slices = []
    for j in range(TP):
        slices.append(
            jnp.concatenate(
                [
                    in_copy[:, D_INNER + j * HALF : D_INNER + (j + 1) * HALF],
                    in_copy[:, 2 * D_INNER : 2 * D_INNER + SIDE],
                    in_copy[:, D_INNER + CONVCH + j * LOCAL_HEADS : D_INNER + CONVCH + (j + 1) * LOCAL_HEADS],
                    jnp.zeros((own_rows, LANES - LOCAL_HEADS), bf16),
                    in_copy[:, j * HALF : (j + 1) * HALF],
                ],
                axis=1,
            )
        )
    mine = lax.all_to_all(jnp.stack(slices), GROUP, 0, 0, tiled=False)
    w_in = lax.all_gather(mine, COPIES, axis=0, tiled=False)
    w_in = w_in.reshape(parts, wt, TP, own_rows, COLS).transpose(0, 2, 1, 3, 4).reshape(D, COLS)
    flat = [(i, (i % TP) * parts + i // TP) for i in range(parts * TP)]
    out_mine = lax.ppermute(out_w.astype(bf16), ("part", *GROUP), [(b, a) for a, b in flat])
    w_out = lax.all_gather(out_mine, COPIES, axis=0, tiled=True)

    hidden_all = lax.all_gather(hidden[0], GROUP, axis=0, tiled=True)
    back_mix = cotangent[0] * valid[0][:, None].astype(bf16)
    back_all = lax.all_gather(back_mix, GROUP, axis=0, tiled=True)

    hid = hidden_all.astype(f32)
    scale_all = lax.rsqrt(jnp.mean(hid * hid, axis=1, keepdims=True) + norm_eps)
    x_normed = (hid * scale_all * pre_gain).astype(bf16)
    projected = dot(x_normed, w_in)
    conv_in = projected[:, :COL_DT].astype(bf16)
    dt_raw = projected[:, COL_DT:COL_GATE].astype(bf16).astype(f32)
    gate_pre = projected[:, COL_GATE:]
    rim_in = shift_part(conv_in[rows - RIM :], 1)
    padded = jnp.concatenate([rim_in, conv_in], axis=0).astype(f32)
    seg_front = jnp.concatenate([jnp.full((RIM,), -1, jnp.int32), seg_all, jnp.full((RIM,), -1, jnp.int32)])
    seg_pad = lax.dynamic_slice_in_dim(seg_front, part * rows, rows + 2 * RIM)
    seg = seg_pad[RIM : RIM + rows]
    masks = [(seg_pad[k : k + rows] == seg).astype(f32)[:, None] for k in range(CONV)]
    taps = jnp.concatenate([own_part(conv_weight[:, :D_INNER], HALF), conv_weight[:, D_INNER:]], axis=1)
    bias = jnp.concatenate([own_part(conv_bias[:D_INNER], HALF), conv_bias[D_INNER:]])
    total = bias[None, :]
    for k in range(CONV):
        total = total + taps[k] * padded[k : k + rows] * masks[k]
    sig_total = jax.nn.sigmoid(total)
    activated = (total * sig_total).astype(bf16)
    x_scan = activated[:, :HALF]
    b_mat = activated[:, HALF : HALF + STATE]
    c_mat = activated[:, HALF + STATE :]

    def head_row(array):
        return jnp.pad(own_part(array, LOCAL_HEADS), (0, LANES - LOCAL_HEADS))

    shift_row = head_row(dt_shift)
    z = dt_raw + shift_row
    dt = jax.nn.softplus(z)
    sig_dt = jax.nn.sigmoid(z)
    ratio = jnp.where(dt > 1e-30, sig_dt / jnp.maximum(dt, 1e-30), 1.0)
    rate_row = -jnp.exp(head_row(a_logs))
    rate8 = jnp.broadcast_to(rate_row, (8, LANES))
    skip_chan = jnp.repeat(own_part(skips, LOCAL_HEADS), HEADDIM)
    skip8 = jnp.broadcast_to(skip_chan, (8, HALF))
    seg_spans = seg.reshape(spans, SPAN)
    seg_last = seg_spans[:, -1]
    seg_before = jnp.concatenate([seg_pad[RIM - 1 : RIM], seg_last[:-1]])
    keep = (seg_spans == seg_last[:, None]).astype(f32).reshape(rows, 1)
    inflow = (seg_spans == seg_before[:, None]).astype(f32).reshape(rows, 1)
    carry = jnp.broadcast_to((seg_last == seg_before).astype(f32)[:, None], (spans, LANES))
    seg_col = seg[:, None]

    state_shape = shape((STATE, HALF), f32)
    s_local, dec_total = in_vmem(
        functools.partial(state_kernel, spans), (state_shape, shape((8, LANES), f32)), "state"
    )(x_scan, b_mat, dt, rate8, keep, carry)
    dec_chan = jnp.repeat(dec_total[0, :LOCAL_HEADS], HEADDIM)
    s_in = jnp.zeros((STATE, HALF), f32)
    for _ in range(parts - 1):
        s_in = shift_part(dec_chan * s_in + s_local, 1)
    y_scan, states = in_vmem(
        functools.partial(scan_kernel, spans),
        (shape((rows, HALF), f32), shape((spans, STATE, HALF), f32)),
        "scan",
        [pltpu.VMEM((STATE, HALF), f32)],
    )(x_scan, b_mat, c_mat, dt, rate8, seg_col, seg_spans, keep, inflow, carry, s_in)
    y_b = (y_scan + skip_chan * x_scan.astype(f32)).astype(bf16).astype(f32)

    gain_own = own_part(norm_gain, HALF)
    sig_gate = jax.nn.sigmoid(gate_pre)
    silu_gate = gate_pre * sig_gate
    gated = y_b * silu_gate
    gate_sq = lax.psum(jnp.sum(gated * gated, axis=1), GROUP)
    scale_gate = lax.rsqrt(gate_sq / D_INNER + norm_eps)[:, None]
    normed = (gated * scale_gate * gain_own).astype(bf16)
    mixer = lax.psum_scatter(dot(normed, w_out), GROUP, scatter_dimension=0, tiled=True)
    output = (resid + mixer).astype(bf16)
    valid_rows = valid[0].astype(f32)
    res_sq = jnp.sum(valid_rows * jnp.sum(resid * resid, axis=1))
    mix_sq = jnp.sum(valid_rows * jnp.sum(mixer * mixer, axis=1))
    valid_count = jnp.sum(valid_rows)

    d_normed = dot(back_all, w_out, ((1,), (1,)))
    g_out = dot(normed, back_all, ((0,), (0,)))
    g_out = lax.psum_scatter(g_out, COPIES, scatter_dimension=0, tiled=True)
    g_out = lax.ppermute(g_out, ("part", *GROUP), flat)
    d_gain = d_normed * gain_own
    gate_dot = lax.psum(jnp.sum(gated * d_gain, axis=1), GROUP)
    d_gated = scale_gate * d_gain - gated * (scale_gate**3 * (gate_dot / D_INNER)[:, None])
    d_norm_gain = jnp.sum(gated * scale_gate * d_normed, axis=0)
    dy = (d_gated * silu_gate).astype(bf16)
    d_gate = d_gated * y_b * (sig_gate * (1.0 + gate_pre * (1.0 - sig_gate)))

    ds_local = in_vmem(functools.partial(state_back_kernel, spans), state_shape, "state_back")(
        dy, c_mat, dt, rate8, inflow, carry
    )
    ds_out = jnp.zeros((STATE, HALF), f32)
    for _ in range(parts - 1):
        ds_out = shift_part(dec_chan * ds_out + ds_local, -1)
    d_x, d_b, d_c, d_dt, d_rate, d_skip = in_vmem(
        functools.partial(scan_back_kernel, spans),
        (
            shape((rows, HALF), bf16),
            shape((rows, STATE), f32),
            shape((rows, STATE), f32),
            shape((rows, LANES), f32),
            shape((8, LANES), f32),
            shape((8, HALF), f32),
        ),
        "scan_back",
        [pltpu.VMEM((STATE, HALF), f32), pltpu.VMEM((2 * SPAN, HALF), f32)],
    )(x_scan, b_mat, c_mat, dt, ratio, sig_dt, rate8, seg_col, seg_spans, keep, inflow, carry, skip8, y_scan, states, dy, ds_out)

    d_total = jnp.concatenate([d_x.astype(f32), d_b, d_c], axis=1) * (sig_total * (1.0 + total * (1.0 - sig_total)))
    rim_back = shift_part(d_total[:RIM], -1)
    d_padded = jnp.concatenate([d_total, rim_back], axis=0)
    d_conv_in = 0.0
    for k in range(CONV):
        later = (seg_pad[2 * RIM - k : 2 * RIM - k + rows] == seg).astype(f32)[:, None]
        d_conv_in = d_conv_in + taps[k] * d_padded[RIM - k : RIM - k + rows] * later
    d_taps = jnp.stack([jnp.sum(d_total * padded[k : k + rows] * masks[k], axis=0) for k in range(CONV)])
    d_bias = jnp.sum(d_total, axis=0)
    d_proj = jnp.concatenate([d_conv_in, d_dt, d_gate], axis=1).astype(bf16)
    d_x_normed = dot(d_proj, w_in, ((1,), (1,)))
    d_x_normed = lax.psum_scatter(d_x_normed, GROUP, scatter_dimension=0, tiled=True)
    g_in = dot(x_normed, d_proj, ((0,), (0,)))
    g_in = g_in.reshape(parts, TP, wt, own_rows, COLS).transpose(0, 2, 1, 3, 4).reshape(parts * wt, TP, own_rows, COLS)
    g_in = lax.psum_scatter(g_in, COPIES, scatter_dimension=0, tiled=False)
    g_in = lax.all_to_all(g_in, GROUP, 0, 0, tiled=False)
    g_in = jnp.concatenate(
        [g_in[j, :, COL_GATE:] for j in range(TP)]
        + [g_in[j, :, :HALF] for j in range(TP)]
        + [jnp.sum(g_in[:, :, COL_SIDE:COL_DT], axis=0)]
        + [g_in[j, :, COL_DT : COL_DT + LOCAL_HEADS] for j in range(TP)],
        axis=1,
    )

    scale_own = lax.rsqrt(jnp.mean(resid * resid, axis=1, keepdims=True) + norm_eps)
    d_pre = d_x_normed * pre_gain
    dot_pre = jnp.mean(resid * d_pre, axis=1, keepdims=True)
    grad_hidden = back_mix.astype(f32) + scale_own * d_pre - resid * (scale_own**3 * dot_pre)
    d_pre_gain = jnp.sum(resid * scale_own * d_x_normed, axis=0)

    def placed(values, width):
        spread = (jnp.arange(TP) == tp).astype(f32)[:, None] * values[..., None, :]
        return spread.reshape(*values.shape[:-1], TP * width)

    d_weight = jnp.concatenate([placed(d_taps[:, :HALF], HALF), d_taps[:, HALF:]], axis=1)
    small_grad = jnp.concatenate(
        [
            d_pre_gain,
            placed(d_norm_gain, HALF),
            d_weight.reshape(-1),
            placed(d_bias[:HALF], HALF),
            d_bias[HALF:],
            placed(jnp.sum(d_dt, axis=0)[:LOCAL_HEADS], LOCAL_HEADS),
            placed((d_rate[0] * rate_row)[:LOCAL_HEADS], LOCAL_HEADS),
            placed(jnp.sum(d_skip[0].reshape(LOCAL_HEADS, HEADDIM), axis=1), LOCAL_HEADS),
            jnp.stack([res_sq, mix_sq, valid_count]),
        ]
    )
    small_total = lax.psum(small_grad, EVERYONE)
    res_total, mix_total, count_total = small_total[-3], small_total[-2], small_total[-1]
    in_m_new, in_v_new, in_w_new = adamw(in_w, in_m, in_v, g_in, 0.02, 0.1)
    out_m_new, out_v_new, out_w_new = adamw(out_w, out_m, out_v, g_out, 0.02, 0.1)
    small_m_new, small_v_new, small_w_new = adamw(small_w, small_m, small_v, small_total[:-3], 0.2, 0.0)
    rms = jnp.stack([jnp.sqrt(res_total / (count_total * D)), jnp.sqrt(mix_total / (count_total * D))])
    return (
        output[None], grad_hidden[None], in_m_new, in_v_new, in_w_new, out_m_new, out_v_new, out_w_new,
        small_m_new, small_v_new, small_w_new, rms,
    )


MESH = pl.DeviceIdType.MESH
T0, T1, DIAG, CORE, SIDEWAYS, PART = ("t0",), ("t1",), ("t1", "t0"), ("w0",), ("w1",), ("part",)
HOPS = (None, T0, T1, DIAG)
HBM = pl.BlockSpec(memory_space=pl.ANY)
VMEM = pl.BlockSpec(memory_space=pltpu.VMEM)
MAIN = COL_GATE
CHANS = HALF + SIDE
FRONT = 16
TILE = 8
REGION = 48
BOX_GROUP = 16
BOX_SIDE = BOX_GROUP + TP * REGION
BOX_ROWS = BOX_SIDE + 16


def place():
    return tuple(lax.axis_index(a) for a in EVERYONE)


def across(flips):
    return {a: 1 - lax.axis_index(a) for a in flips}


def group_blocks():
    _, t1, t0, _, _ = place()
    return [(t1, t0), (t1, 1 - t0), (1 - t1, t0), (1 - t1, 1 - t0)]


def greet(neighbours):
    barrier = pltpu.get_barrier_semaphore()
    for flips in neighbours:
        pl.semaphore_signal(barrier, inc=1, device_id=across(flips), device_id_type=MESH)
    pl.semaphore_wait(barrier, len(neighbours))


class Copies:
    def __init__(self, local_sem, send_sem, recv_sem):
        self.local_sem, self.send_sem, self.recv_sem = local_sem, send_sem, recv_sem
        self.sent, self.kept = [], []

    def send(self, src, dst, flips):
        i = len(self.sent)
        copy = pltpu.make_async_remote_copy(
            src_ref=src,
            dst_ref=dst,
            send_sem=self.send_sem.at[i],
            recv_sem=self.recv_sem.at[i],
            device_id=across(flips),
            device_id_type=MESH,
        )
        copy.start()
        self.sent.append(copy)
        return copy

    def keep(self, src, dst):
        copy = pltpu.make_async_copy(src, dst, self.local_sem.at[len(self.kept)])
        copy.start()
        self.kept.append(copy)
        return copy

    def finish(self):
        for copy in self.sent:
            copy.wait_send()


def sems(remote, local=1):
    return [
        pltpu.SemaphoreType.DMA((local,)),
        pltpu.SemaphoreType.DMA((remote,)),
        pltpu.SemaphoreType.DMA((remote,)),
    ]


class GroupGather:
    def __init__(self, copies, src, dst):
        self.copies, self.dst = copies, dst
        self.rows = src.shape[0]
        self.halves = (0, self.rows // 2)
        own = group_blocks()[0]
        self.own = copies.keep(src, self.at(own, 0, self.rows))
        size = self.rows // 2
        self.along_t1 = [copies.send(src.at[pl.ds(h, size)], self.at(own, h, size), T1) for h in self.halves]
        self.along_t0 = [copies.send(src.at[pl.ds(h, size)], self.at(own, h, size), T0) for h in self.halves]
        self.diagonal = []

    def at(self, block, first, size):
        return self.dst.at[pl.ds(pl.multiple_of((block[0] * 2 + block[1]) * self.rows + first, size), size)]

    def hand_on(self):
        beside = group_blocks()[2]
        for copy, h in zip(self.along_t1, self.halves):
            copy.wait_recv()
            here = self.at(beside, h, self.rows // 2)
            self.diagonal.append(self.copies.send(here, here, T0))

    def finish(self):
        for copy in self.along_t0 + self.diagonal:
            copy.wait_recv()


class WeightGather:
    def __init__(self, copies, dst, rows, group):
        self.copies, self.dst, self.rows, self.group = copies, dst, rows, group
        self.by_part, self.by_side, self.by_core = [], [], []

    def at(self, part, w1, w0, block):
        index = part
        if self.group:
            index = (index * 2 + block[0]) * 2 + block[1]
        index = (index * 2 + w1) * 2 + w0
        return self.dst.at[pl.ds(pl.multiple_of(index * self.rows, self.rows), self.rows)]

    def mine(self, block):
        p, _, _, w1, w0 = place()
        return self.at(p, w1, w0, block)

    def spread(self, src, block):
        dst = self.mine(block)
        self.by_part.append((self.copies.send(src, dst, PART), block))
        self.by_side.append((self.copies.send(src, dst, SIDEWAYS), block))
        self.by_core.append(self.copies.send(src, dst, CORE))

    def swap(self, src):
        own, *others = group_blocks()
        self.kept = self.copies.keep(src.at[own[0], own[1]], self.mine(own))
        self.spread(src.at[own[0], own[1]], own)
        self.swaps = [
            (self.copies.send(src.at[b[0], b[1]], self.mine(own), flips), b) for b, flips in zip(others, HOPS[1:])
        ]

    def spread_swapped(self):
        for copy, block in self.swaps:
            copy.wait_recv()
            self.spread(self.mine(block), block)

    def pass_core(self, part, w1, block):
        here = self.at(part, w1, lax.axis_index("w0"), block)
        self.by_core.append(self.copies.send(here, here, CORE))

    def hand_on(self):
        p, _, _, w1, w0 = place()
        again = []
        for (copy, block), (side, _) in zip(self.by_part, self.by_side):
            side.wait_recv()
            self.pass_core(p, 1 - w1, block)
            copy.wait_recv()
            here = self.at(1 - p, w1, w0, block)
            again.append((self.copies.send(here, here, SIDEWAYS), block))
            self.pass_core(1 - p, w1, block)
        for copy, block in again:
            copy.wait_recv()
            self.pass_core(1 - p, 1 - w1, block)

    def finish(self):
        for copy in self.by_core:
            copy.wait_recv()


class GradientSum:
    def __init__(self, copies, src, bufs, group):
        self.copies, self.src, self.group = copies, src, group
        self.core, self.side, self.sides, self.far, self.fars = bufs[:5]
        self.last, self.lasts = bufs[5:] if group else (None, None)
        self.blocks = group_blocks() if group else [()]

    def added(self, q, block, side, *more):
        w0 = lax.axis_index("w0")
        value = self.src[(q, *block, side, w0)].astype(f32) + self.core[(q, side, *block)].astype(f32)
        for other in more:
            value = value + other.astype(f32)
        return value

    def cores(self):
        p, _, _, w1, w0 = place()
        every = (slice(None), slice(None)) if self.group else ()
        order = [(1 - p, 1 - w1), (p, 1 - w1), (1 - p, w1), (p, w1)]
        self.core_copies = [
            self.copies.send(self.src.at[(q, *every, s, 1 - w0)], self.core.at[q, s], CORE) for q, s in order
        ]

    def to_sides(self):
        p, _, _, w1, _ = place()
        self.side_copies = [[], []]
        for k, q in enumerate((1 - p, p)):
            self.core_copies[k].wait_recv()
            for i, block in enumerate(self.blocks):
                self.side[k, i] = self.added(q, block, 1 - w1).astype(bf16)
                self.side_copies[k].append(self.copies.send(self.side.at[k, i], self.sides.at[k, i], SIDEWAYS))

    def to_part(self):
        p, _, _, w1, _ = place()
        self.core_copies[2].wait_recv()
        self.core_copies[3].wait_recv()
        self.far_copies = []
        for i, block in enumerate(self.blocks):
            self.side_copies[0][i].wait_recv()
            self.far[i] = self.added(1 - p, block, w1, self.sides[0, i]).astype(bf16)
            self.far_copies.append(self.copies.send(self.far.at[i], self.fars.at[i], PART))

    def total(self, i):
        p, _, _, w1, _ = place()
        self.side_copies[1][i].wait_recv()
        self.far_copies[i].wait_recv()
        return self.added(p, self.blocks[i], w1, self.sides[1, i], self.fars[i])

    def to_group(self, out):
        self.last_copies = []
        for i in (1, 2, 3, 0):
            value = self.total(i)
            if i == 0:
                out[self.blocks[0]] = value
            else:
                self.last[i - 1] = value.astype(bf16)
                self.last_copies.append(self.copies.send(self.last.at[i - 1], self.lasts.at[i - 1], HOPS[i]))

    def finish(self, out):
        for i, copy in enumerate(self.last_copies):
            copy.wait_recv()
            out[self.blocks[i + 1]] = self.lasts[i].astype(f32)


def sum_buffers(rows, cols, group):
    buf = lambda *lead: pltpu.VMEM((*lead, rows, cols), bf16)
    if not group:
        return [buf(2, 2), buf(2, 1), buf(2, 1), buf(1), buf(1)]
    return [buf(2, 2, 2, 2), buf(2, 4), buf(2, 4), buf(4), buf(4), buf(3), buf(3)]


def block_rows(block, size):
    return pl.ds(pl.multiple_of((block[0] * 2 + block[1]) * size, size), size)


def start_kernel(
    hid_ref, w_ref, gain_ref,
    h_ref, xn_ref, win_ref, conv_ref, dtr_ref,
    local_sem, send_sem, recv_sem,
):
    greet([T0, T1, DIAG, CORE, SIDEWAYS, PART])
    copies = Copies(local_sem, send_sem, recv_sem)
    size = hid_ref.shape[0]
    weights = WeightGather(copies, win_ref, w_ref.shape[2], True)
    weights.swap(w_ref)
    tokens = GroupGather(copies, hid_ref, h_ref)
    blocks = group_blocks()

    def norm(block):
        rows = block_rows(block, size)
        hid = h_ref[rows, :].astype(f32)
        scale = lax.rsqrt(jnp.sum(hid * hid, axis=1, keepdims=True) / D + norm_eps)
        xn_ref[rows, :] = (hid * scale * gain_ref[...]).astype(bf16)

    weights.spread_swapped()
    tokens.own.wait()
    norm(blocks[0])
    tokens.hand_on()
    norm(blocks[2])
    weights.hand_on()
    tokens.finish()
    norm(blocks[1])
    norm(blocks[3])
    weights.finish()
    weights.kept.wait()

    def project(c, _):
        rows = span_rows(c)
        xn = xn_ref[rows, :]
        for k in range(CHANS // 256):
            cols = slice(k * 256, (k + 1) * 256)
            conv_ref[rows, cols] = dot(xn, win_ref[:, cols]).astype(bf16)
        dtr_ref[rows, :] = dot(xn, win_ref[:, CHANS:MAIN]).astype(bf16).astype(f32)
        return 0

    lax.fori_loop(0, xn_ref.shape[0] // SPAN, project, 0)
    copies.finish()


def head_lanes(values, back=False):
    first = (lax.axis_index("t1") * 2 + lax.axis_index("t0")) * LOCAL_HEADS
    return pltpu.roll(values, first if back else LANES - first, 1)


def forward_kernel(
    spans, conv_ref, dtr_ref, xn_ref, taps_ref, heads_ref, chans_ref, marks_ref, segc_ref, segr_ref, carry_ref,
    wg_ref, out_ref, cot_ref,
    convp_ref, x_ref, b_ref, c_ref, dsilu_ref, dt_ref, z_ref, cum_ref, y_ref, st_ref, wgate_ref, wout_ref, back_ref,
    normed_ref, mix_ref, dy_ref, dgate_ref, dgain_ref,
    s_ref, pass_ref, got_ref, rim_ref, gated_ref, gate_ref, dn_ref, stat_ref, stats_ref,
    local_sem, send_sem, recv_sem,
):
    p, _, _, _, _ = place()
    greet([T0, T1, DIAG, CORE, SIDEWAYS, PART])
    copies = Copies(local_sem, send_sem, recv_sem)
    rows_all = spans * SPAN
    rim = copies.send(conv_ref.at[pl.ds(rows_all - FRONT, FRONT)], rim_ref, PART)
    gates = WeightGather(copies, wgate_ref, wg_ref.shape[2], True)
    gates.swap(wg_ref)
    outs = WeightGather(copies, wout_ref, out_ref.shape[0], False)
    outs.spread(out_ref, ())
    outs_kept = copies.keep(out_ref, outs.mine(()))
    tokens = GroupGather(copies, cot_ref, back_ref)
    s_ref[...] = jnp.zeros_like(s_ref)
    dgain_ref[...] = jnp.zeros_like(dgain_ref)
    convp_ref[FRONT:, :] = conv_ref[...]
    rim.wait_recv()
    convp_ref[0:FRONT, :] = jnp.where(p == 1, rim_ref[...].astype(f32), 0.0).astype(bf16)
    gates.spread_swapped()

    def convolve(c, _):
        rows = span_rows(c)
        wide = pl.ds(pl.multiple_of(c * SPAN, SPAN), SPAN + FRONT)
        marks = marks_ref[rows, :]
        for k in range(CHANS // LANES):
            lanes = slice(k * LANES, (k + 1) * LANES)
            values = convp_ref[wide, lanes].astype(f32)
            total = taps_ref[CONV : CONV + 1, lanes] + taps_ref[RIM : RIM + 1, lanes] * values[FRONT:]
            for j in range(RIM):
                first = FRONT - RIM + j
                total = total + taps_ref[j : j + 1, lanes] * values[first : first + SPAN] * marks[:, j : j + 1]
            sig = 1.0 / (1.0 + jnp.exp(-total))
            value = (total * sig).astype(bf16)
            dsilu_ref[rows, lanes] = sig * (1.0 + total * (1.0 - sig))
            if k < HALF // LANES:
                x_ref[rows, lanes] = value
            elif k == HALF // LANES:
                b_ref[rows, :] = value
            else:
                c_ref[rows, :] = value
        z = head_lanes(dtr_ref[rows, :]) + heads_ref[0:1, :]
        z_ref[rows, :] = z
        small = jnp.exp(-jnp.abs(z))
        one_more = 1.0 + small
        log_more = jnp.where(one_more == 1.0, small, jnp.log(one_more) * small / jnp.where(one_more == 1.0, 1.0, one_more - 1.0))
        dt_ref[rows, :] = jnp.maximum(z, 0.0) + log_more
        return 0

    lax.fori_loop(0, spans, convolve, 0)

    def local_states(c, _):
        rows = span_rows(c)
        dt, cum = span_decay(dt_ref, heads_ref, c, 1)
        cum_ref[rows, :] = cum
        last = cum[SPAN - 1 : SPAN, :]
        end_weight = jnp.exp(last - cum) * dt * marks_ref[rows, 6:7]
        decay = jnp.exp(last) * carry_ref[pl.ds(c, 1), :]
        b = b_ref[rows, :]
        st_ref[c] = s_ref[...]
        for q in range(PAIRS):
            lanes = slice(q * LANES, (q + 1) * LANES)
            xw = (x_ref[rows, lanes].astype(f32) * pair_cols(end_weight, 2 * q)).astype(bf16)
            s_ref[:, lanes] = s_ref[:, lanes] * pair_cols(decay, 2 * q) + dot(b, xw, ((0,), (0,)))
        return 0

    lax.fori_loop(0, spans, local_states, 0)
    pass_ref[...] = s_ref[...].astype(bf16)
    state = copies.send(pass_ref, got_ref, PART)
    tokens.hand_on()

    def inside(c, _):
        rows = span_rows(c)
        cum = cum_ref[rows, :]
        back_log = jnp.transpose(cum - jnp.log(dt_ref[rows, :]))
        scores = dot(c_ref[rows, :], b_ref[rows, :], ((1,), (1,)))
        row = lax.broadcasted_iota(jnp.int32, (SPAN, SPAN), 0)
        col = lax.broadcasted_iota(jnp.int32, (SPAN, SPAN), 1)
        mask = (row >= col) & (segc_ref[rows, :] == segr_ref[pl.ds(c, 1), :])
        lane = lax.broadcasted_iota(jnp.int32, (SPAN, LANES), 1)
        for q in range(PAIRS):
            lanes = slice(q * LANES, (q + 1) * LANES)
            x = x_ref[rows, lanes]
            parts = []
            for h in (2 * q, 2 * q + 1):
                gap = cum[:, h : h + 1] - back_log[h : h + 1, :]
                weighted = scores * jnp.exp(jnp.where(mask, gap, -1e30))
                parts.append(dot(weighted.astype(bf16), x))
            y_ref[rows, lanes] = jnp.where(lane < HEADDIM, parts[0], parts[1])
        return 0

    lax.fori_loop(0, spans, inside, 0)
    outs.hand_on()
    gates.hand_on()
    state.wait_recv()
    s_ref[...] = got_ref[...].astype(f32) * p.astype(f32)

    def across_spans(c, _):
        rows = span_rows(c)
        cum = cum_ref[rows, :]
        decay = jnp.exp(cum[SPAN - 1 : SPAN, :]) * carry_ref[pl.ds(c, 1), :]
        gain = jnp.exp(cum) * marks_ref[rows, 7:8]
        cc = c_ref[rows, :]
        for q in range(PAIRS):
            lanes = slice(q * LANES, (q + 1) * LANES)
            entering = s_ref[:, lanes]
            full = st_ref[c, :, lanes] + entering
            st_ref[c, :, lanes] = full
            y_ref[rows, lanes] += dot(cc, full.astype(bf16)) * pair_cols(gain, 2 * q)
            s_ref[:, lanes] = entering * pair_cols(decay, 2 * q)
        return 0

    lax.fori_loop(0, spans, across_spans, 0)
    outs.finish()
    outs_kept.wait()
    gates.finish()
    gates.kept.wait()

    def put_stat(k, c, column):
        wide = jnp.transpose(jnp.broadcast_to(column, (SPAN, LANES)))
        stat_ref[k, :, span_rows(c)] = wide[0:TILE, :]

    def exchange(k):
        return [copies.send(stat_ref.at[k], stats_ref.at[k, i], flips) for i, flips in enumerate(HOPS[1:])]

    def get_stat(k, c):
        cols = span_rows(c)
        total = stat_ref[k, :, cols] + stats_ref[k, 0, :, cols] + stats_ref[k, 1, :, cols] + stats_ref[k, 2, :, cols]
        return jnp.transpose(jnp.broadcast_to(total[0:1, :], (LANES, SPAN)))[:, 0:1] / D_INNER

    def values(rows, lanes):
        y_b = (y_ref[rows, lanes] + chans_ref[0:1, lanes] * x_ref[rows, lanes].astype(f32)).astype(bf16).astype(f32)
        gate = gate_ref[rows, lanes]
        sig = 1.0 / (1.0 + jnp.exp(-gate))
        return y_b, gate, sig

    def gating(c, _):
        rows = span_rows(c)
        xn = xn_ref[rows, :]
        total = jnp.zeros((SPAN, 1), f32)
        for k in range(HALF // 256):
            lanes = slice(k * 256, (k + 1) * 256)
            gate_ref[rows, lanes] = dot(xn, wgate_ref[:, lanes])
            y_b, gate, sig = values(rows, lanes)
            gated = y_b * (gate * sig)
            gated_ref[rows, lanes] = gated
            total = total + jnp.sum(gated * gated, axis=1, keepdims=True)
        put_stat(0, c, total)
        return 0

    lax.fori_loop(0, spans, gating, 0)
    squares = exchange(0)
    tokens.finish()
    tokens.own.wait()

    def pull_out(c, _):
        rows = span_rows(c)
        back = back_ref[rows, :]
        total = jnp.zeros((SPAN, 1), f32)
        for k in range(HALF // 256):
            lanes = slice(k * 256, (k + 1) * 256)
            d_normed = dot(back, wout_ref[lanes, :], ((1,), (1,)))
            dn_ref[rows, lanes] = d_normed
            total = total + jnp.sum(gated_ref[rows, lanes] * (d_normed * chans_ref[1:2, lanes]), axis=1, keepdims=True)
        put_stat(1, c, total)
        return 0

    lax.fori_loop(0, spans, pull_out, 0)
    dots = exchange(1)
    for copy in squares:
        copy.wait_recv()

    def push_out(c, _):
        rows = span_rows(c)
        scale = lax.rsqrt(get_stat(0, c) + norm_eps)
        for k in range(HALF // 256):
            lanes = slice(k * 256, (k + 1) * 256)
            scaled = gated_ref[rows, lanes] * scale
            normed_ref[rows, lanes] = (scaled * chans_ref[1:2, lanes]).astype(bf16)
            dgain_ref[0:1, lanes] += jnp.sum(scaled * dn_ref[rows, lanes], axis=0, keepdims=True)
        normed = normed_ref[rows, :]
        for k in range(D // 256):
            cols = slice(k * 256, (k + 1) * 256)
            mix_ref[rows, cols] = dot(normed, wout_ref[:, cols]).astype(bf16)
        return 0

    lax.fori_loop(0, spans, push_out, 0)
    for copy in dots:
        copy.wait_recv()

    def back_gate(c, _):
        rows = span_rows(c)
        scale = lax.rsqrt(get_stat(0, c) + norm_eps)
        pulled = get_stat(1, c) * (scale * scale * scale)
        for k in range(HALF // LANES):
            lanes = slice(k * LANES, (k + 1) * LANES)
            y_b, gate, sig = values(rows, lanes)
            d_gated = scale * (dn_ref[rows, lanes] * chans_ref[1:2, lanes]) - gated_ref[rows, lanes] * pulled
            dy_ref[rows, lanes] = (d_gated * (gate * sig)).astype(bf16)
            dgate_ref[rows, lanes] = (d_gated * y_b * (sig * (1.0 + gate * (1.0 - sig)))).astype(bf16)
        return 0

    lax.fori_loop(0, spans, back_gate, 0)
    copies.finish()


def backward_kernel(
    spans, x_ref, b_ref, c_ref, dt_ref, z_ref, heads_ref, chans_ref, marks_ref, segc_ref, segr_ref, carry_ref,
    y_ref, st_ref, cum_ref, dy_ref, dsilu_ref, convp_ref, taps_ref, normed_ref, back_ref, xn_ref, dgate_ref, mix_ref,
    dmain_ref, hsum_ref, dskip_ref, dtaps_ref, mixes_ref, gout_ref, ggate_ref,
    ds_ref, dsl_ref, dyg_ref, dxi_ref, prod_ref, pass_ref, got_ref, dtot_ref, rims_ref, rimr_ref, db_ref, dc_ref,
    go_ref, gg_ref, *rest,
):
    go_bufs, gg_bufs, (local_sem, send_sem, recv_sem) = rest[:5], rest[5:12], rest[12:]
    p, t1, t0, w1, w0 = place()
    greet([T0, T1, DIAG, CORE, SIDEWAYS, PART])
    copies = Copies(local_sem, send_sem, recv_sem)
    tokens = mixes_ref.shape[1]
    mixes = [
        copies.send(mix_ref.at[block_rows(block, tokens)], mixes_ref.at[i], flips)
        for i, (block, flips) in enumerate(zip(group_blocks()[1:], HOPS[1:]))
    ]
    ds_ref[...] = jnp.zeros_like(ds_ref)
    hsum_ref[...] = jnp.zeros_like(hsum_ref)
    dskip_ref[...] = jnp.zeros_like(dskip_ref)
    dtaps_ref[...] = jnp.zeros_like(dtaps_ref)

    def local_states(step, _):
        c = spans - 1 - step
        rows = span_rows(c)
        cum = cum_ref[rows, :]
        decay = jnp.exp(cum[SPAN - 1 : SPAN, :]) * carry_ref[pl.ds(c, 1), :]
        gain = jnp.exp(cum) * marks_ref[rows, 7:8]
        cc = c_ref[rows, :]
        for q in range(PAIRS):
            lanes = slice(q * LANES, (q + 1) * LANES)
            dyg = (dy_ref[rows, lanes].astype(f32) * pair_cols(gain, 2 * q)).astype(bf16)
            dyg_ref[rows, lanes] = dyg
            ds = ds_ref[:, lanes]
            dsl_ref[c, :, lanes] = ds
            ds_ref[:, lanes] = ds * pair_cols(decay, 2 * q) + dot(cc, dyg, ((0,), (0,)))
        return 0

    lax.fori_loop(0, spans, local_states, 0)
    pass_ref[...] = ds_ref[...].astype(bf16)
    state = copies.send(pass_ref, got_ref, PART)

    out_rows = go_ref.shape[3]
    for q in range(2):
        normed = normed_ref[:, q * HALF // 2 : (q + 1) * HALF // 2]
        for k in range(D // 512):
            cols = slice(k * 512, (k + 1) * 512)
            part = dot(normed, back_ref[:, cols], ((0,), (0,))).astype(bf16)
            go_ref[q, :, :, :, cols] = part.reshape(2, 2, out_rows, 512)
    g_out = GradientSum(copies, go_ref, go_bufs, False)
    g_out.cores()

    own_rows = gg_ref.shape[5]
    width = TP // 2 * 4 * own_rows
    for i in range(4):
        xn = xn_ref[:, i * width : (i + 1) * width]
        part = dot(xn, dgate_ref[...], ((0,), (0,))).astype(bf16)
        gg_ref[i // 2, i % 2] = part.reshape(2, 2, 2, own_rows, HALF)
    g_gate = GradientSum(copies, gg_ref, gg_bufs, True)
    g_gate.cores()
    g_out.to_sides()

    def inside(c, _):
        rows = span_rows(c)
        cum = cum_ref[rows, :]
        fore_log = jnp.transpose(cum)
        back_log = cum - jnp.log(dt_ref[rows, :])
        b = b_ref[rows, :]
        cc = c_ref[rows, :]
        scores = dot(b, cc, ((1,), (1,)))
        row = lax.broadcasted_iota(jnp.int32, (SPAN, SPAN), 0)
        col = lax.broadcasted_iota(jnp.int32, (SPAN, SPAN), 1)
        mask = (col >= row) & (segc_ref[rows, :] == segr_ref[pl.ds(c, 1), :])
        lane = lax.broadcasted_iota(jnp.int32, (SPAN, LANES), 1)
        d_scores = jnp.zeros((SPAN, SPAN), f32)
        dc = jnp.zeros((SPAN, STATE), f32)
        for q in range(PAIRS):
            lanes = slice(q * LANES, (q + 1) * LANES)
            x = x_ref[rows, lanes]
            dy = dy_ref[rows, lanes]
            xf = x.astype(f32)
            parts = []
            for k in range(2):
                h = 2 * q + k
                gap = fore_log[h : h + 1, :] - back_log[:, h : h + 1]
                decay_mat = jnp.exp(jnp.where(mask, gap, -1e30))
                parts.append(dot((scores * decay_mat).astype(bf16), dy))
                own = (lane < HEADDIM) if k == 0 else (lane >= HEADDIM)
                d_weights = dot(jnp.where(own, xf, 0.0).astype(bf16), dy, ((1,), (1,)))
                d_scores = d_scores + d_weights * decay_mat
            dxi_ref[rows, lanes] = jnp.where(lane < HEADDIM, parts[0], parts[1])
            dc = dc + dot(dyg_ref[rows, lanes], st_ref[c, :, lanes].astype(bf16), ((1,), (1,)))
            dskip_ref[0:1, lanes] += jnp.sum(dy.astype(f32) * xf, axis=0, keepdims=True)
        d_scores_b = d_scores.astype(bf16)
        db_ref[rows, :] = dot(d_scores_b, cc)
        dc_ref[rows, :] = dc + dot(d_scores_b, b, ((0,), (0,)))
        return 0

    lax.fori_loop(0, spans, inside, 0)
    g_gate.to_sides()
    g_out.to_part()
    state.wait_recv()
    ds_ref[...] = got_ref[...].astype(f32) * (1 - p).astype(f32)

    def across_spans(step, _):
        c = spans - 1 - step
        rows = span_rows(c)
        dt = dt_ref[rows, :]
        cum = cum_ref[rows, :]
        last = cum[SPAN - 1 : SPAN, :]
        end_weight = jnp.exp(last - cum) * dt * marks_ref[rows, 6:7]
        decay = jnp.exp(last) * carry_ref[pl.ds(c, 1), :]
        b = b_ref[rows, :]
        db = db_ref[rows, :]
        edges = []
        for q in range(PAIRS):
            lanes = slice(q * LANES, (q + 1) * LANES)
            xf = x_ref[rows, lanes].astype(f32)
            dyf = dy_ref[rows, lanes].astype(f32)
            ew = pair_cols(end_weight, 2 * q)
            dec = pair_cols(decay, 2 * q)
            entering = ds_ref[:, lanes]
            ds = dsl_ref[c, :, lanes] + entering
            ds_ref[:, lanes] = entering * dec
            ds_b = ds.astype(bf16)
            db = db + dot((xf * ew).astype(bf16), ds_b, ((1,), (1,)))
            dx_state = dot(b, ds_b) * ew
            dx = dxi_ref[rows, lanes] + dx_state
            edges.append(
                jnp.sum(ds * st_ref[c, :, lanes], axis=0, keepdims=True) * dec
                + jnp.sum(dx_state * xf, axis=0, keepdims=True)
            )
            prod_ref[0:SPAN, lanes] = dyf * y_ref[rows, lanes]
            prod_ref[SPAN : 2 * SPAN, lanes] = xf * dx
            d_x = (dx + dyf * chans_ref[0:1, lanes]).astype(bf16).astype(f32)
            dtot_ref[rows, lanes] = d_x * dsilu_ref[rows, lanes]
        dtot_ref[rows, HALF : HALF + STATE] = db * dsilu_ref[rows, HALF : HALF + STATE]
        dtot_ref[rows, HALF + STATE :] = dc_ref[rows, :] * dsilu_ref[rows, HALF + STATE :]
        sums = head_sums(prod_ref[...])
        out_sum, in_sum = sums[:SPAN], sums[SPAN:]
        edge_sum = head_sums(jnp.broadcast_to(jnp.concatenate(edges, axis=1), (TILE, HALF)))[0:1]
        at_last = lax.broadcasted_iota(jnp.int32, (SPAN, LANES), 0) == SPAN - 1
        d_cum = out_sum - in_sum + jnp.where(at_last, edge_sum, 0.0)
        row = lax.broadcasted_iota(jnp.int32, (SPAN, SPAN), 0)
        col = lax.broadcasted_iota(jnp.int32, (SPAN, SPAN), 1)
        d_log = dot((col >= row).astype(f32), d_cum, precision=exact_prec)
        z = z_ref[rows, :]
        small = jnp.exp(-jnp.abs(z))
        sig = jnp.where(z >= 0.0, 1.0, small) / (1.0 + small)
        ratio = jnp.where(dt > 1e-30, sig / jnp.maximum(dt, 1e-30), 1.0)
        d_dt = d_log * heads_ref[1:2, :] * sig + in_sum * ratio
        hsum_ref[0:1, :] += jnp.sum(d_log * dt, axis=0, keepdims=True)
        hsum_ref[1:2, :] += jnp.sum(d_dt, axis=0, keepdims=True)
        dmain_ref[rows, CHANS:MAIN] = head_lanes(d_dt, back=True).astype(bf16)
        return 0

    lax.fori_loop(0, spans, across_spans, 0)
    rims_ref[...] = dtot_ref[0:TILE, :]
    rim = copies.send(rims_ref, rimr_ref, PART)
    g_gate.to_part()
    rim.wait_recv()
    dtot_ref[pl.ds(spans * SPAN, TILE), :] = jnp.where(p == 0, rimr_ref[...], 0.0)

    def convolve(c, _):
        rows = span_rows(c)
        marks = marks_ref[rows, :]
        fore = pl.ds(pl.multiple_of(c * SPAN, SPAN), SPAN + FRONT)
        hind = pl.ds(pl.multiple_of(c * SPAN, SPAN), SPAN + TILE)
        for k in range(CHANS // LANES):
            lanes = slice(k * LANES, (k + 1) * LANES)
            later = dtot_ref[hind, lanes]
            earlier = convp_ref[fore, lanes].astype(f32)
            own = later[0:SPAN]
            d_conv = taps_ref[RIM : RIM + 1, lanes] * own
            dtaps_ref[RIM : RIM + 1, lanes] += jnp.sum(own * earlier[FRONT:], axis=0, keepdims=True)
            dtaps_ref[CONV : CONV + 1, lanes] += jnp.sum(own, axis=0, keepdims=True)
            for j in range(RIM):
                ahead = RIM - j
                d_conv = d_conv + taps_ref[j : j + 1, lanes] * later[ahead : ahead + SPAN] * marks[:, 3 + j : 4 + j]
                first = FRONT - ahead
                dtaps_ref[j : j + 1, lanes] += jnp.sum(
                    own * earlier[first : first + SPAN] * marks[:, j : j + 1], axis=0, keepdims=True
                )
            dmain_ref[rows, lanes] = d_conv.astype(bf16)
        return 0

    lax.fori_loop(0, spans, convolve, 0)
    gout_ref[...] = g_out.total(0)
    g_gate.to_group(ggate_ref)
    g_gate.finish(ggate_ref)
    for copy in mixes:
        copy.wait_recv()
    copies.finish()


def end_kernel(
    dmain_ref, dgate_ref, win_ref, wgate_ref, xn_ref, h_ref, pre_ref, dgain_ref, dskip_ref, dtaps_ref, hsum_ref,
    mix_ref, mixes_ref, back_ref, valid_ref, ggate_ref, gout_ref,
    inw_ref, inm_ref, inv_ref, outw_ref, outm_ref, outv_ref,
    output_ref, gh_ref, inm_out, inv_out, inw_out, outm_out, outv_out, outw_out, total_ref,
    dxp_ref, dxs_ref, dxo_ref, dpre_ref, gm_ref, gmo_ref, box_ref, boxes_ref, *rest,
):
    gm_bufs, (local_sem, send_sem, recv_sem) = rest[:7], rest[7:]
    p, t1, t0, w1, w0 = place()
    greet([T0, T1, DIAG, CORE, SIDEWAYS, PART])
    copies = Copies(local_sem, send_sem, recv_sem)
    blocks = group_blocks()
    tokens = mixes_ref.shape[1]
    own_rows = gm_ref.shape[5]
    width = 2 * 4 * own_rows

    def grad_piece(q, r):
        first = pl.multiple_of((q * 2 + r) * width, width)
        for k in range(MAIN // 384):
            cols = slice(k * 384, (k + 1) * 384)
            part = dot(xn_ref[:, pl.ds(first, width)], dmain_ref[:, cols], ((0,), (0,))).astype(bf16)
            gm_ref[q, r, :, :, :, :, cols] = part.reshape(2, 2, 2, own_rows, 384)

    lax.fori_loop(0, 4, lambda i, _: (grad_piece(i // 2, i % 2), 0)[1], 0)
    g_main = GradientSum(copies, gm_ref, gm_bufs, True)
    g_main.cores()
    dpre_ref[...] = jnp.zeros_like(dpre_ref)

    def token_grad(block, keep):
        rows = block_rows(block, tokens)
        d_main = dmain_ref[rows, :]
        d_gate = dgate_ref[rows, :]
        hid = h_ref[rows, :].astype(f32)
        scale = lax.rsqrt(jnp.sum(hid * hid, axis=1, keepdims=True) / D + norm_eps)
        for k in range(D // 512):
            cols = slice(k * 512, (k + 1) * 512)
            part = dot(d_main, win_ref[cols, :], ((1,), (1,))) + dot(d_gate, wgate_ref[cols, :], ((1,), (1,)))
            dpre_ref[0:1, cols] += jnp.sum(h_ref[rows, cols].astype(f32) * scale * part, axis=0, keepdims=True)
            if keep:
                dxo_ref[:, cols] = part
            else:
                dxp_ref[rows, cols] = part.astype(bf16)

    dxs = [None] * 3
    for i in (3, 2, 1):
        token_grad(blocks[i], False)
        dxs[i - 1] = copies.send(dxp_ref.at[block_rows(blocks[i], tokens)], dxs_ref.at[i - 1], HOPS[i])
        if i == 3:
            g_main.to_sides()
    token_grad(blocks[0], True)

    own = block_rows(blocks[0], tokens)
    hid = h_ref[own, :].astype(f32)
    mixer = mix_ref[own, :].astype(f32)
    for i in range(3):
        mixer = mixer + mixes_ref[i].astype(f32)
    output_ref[...] = (hid + mixer).astype(bf16)
    valid = valid_ref[...]
    counts = [jnp.sum(valid * jnp.sum(v * v, axis=1, keepdims=True), axis=0, keepdims=True) for v in (hid, mixer)]
    counts.append(jnp.sum(valid, axis=0, keepdims=True))

    box = box_ref.at[0]
    box[...] = jnp.zeros_like(box)
    region = BOX_GROUP + (t1 * 2 + t0) * REGION
    lane = lax.broadcasted_iota(jnp.int32, (1, LANES), 1)
    for k in range(D // LANES):
        box[k : k + 1, :] = dpre_ref[0:1, k * LANES : (k + 1) * LANES]
    for k in range(HALF // LANES):
        lanes = slice(k * LANES, (k + 1) * LANES)
        box[pl.ds(region + k, 1), :] = dgain_ref[0:1, lanes]
        box[pl.ds(region + 6 + k, 1), :] = dskip_ref[0:1, lanes]
        for j in range(CONV + 1):
            box[pl.ds(region + 12 + 6 * j + k, 1), :] = dtaps_ref[j : j + 1, lanes]
    box[pl.ds(region + 42, 1), :] = hsum_ref[0:1, :]
    box[pl.ds(region + 43, 1), :] = hsum_ref[1:2, :]
    for j in range(CONV + 1):
        for k in range(2):
            lanes = slice(HALF + k * LANES, HALF + (k + 1) * LANES)
            box[BOX_SIDE + 2 * j + k : BOX_SIDE + 2 * j + k + 1, :] = dtaps_ref[j : j + 1, lanes]
    scalars = jnp.zeros((1, LANES), f32)
    for k in range(3):
        scalars = jnp.where(lane == k, counts[k], scalars)
    box[BOX_SIDE + 10 : BOX_SIDE + 11, :] = scalars

    def small_step(k, flips):
        return copies.send(box_ref.at[k], boxes_ref.at[k], flips)

    def small_add(k, copy):
        copy.wait_recv()
        if k < 4:
            box_ref[k + 1] = box_ref[k] + boxes_ref[k]
        else:
            total_ref[...] = box_ref[k] + boxes_ref[k]

    def update(refs, outs, rows, cols, grad):
        moment_new, second_new, weight_new = adamw(
            refs[0][rows, cols], refs[1][rows, cols], refs[2][rows, cols], grad, 0.02, 0.1
        )
        outs[0][rows, cols] = moment_new
        outs[1][rows, cols] = second_new
        outs[2][rows, cols] = weight_new

    in_refs, in_outs = (inw_ref, inm_ref, inv_ref), (inm_out, inv_out, inw_out)
    every = slice(None)
    small = small_step(0, CORE)
    g_main.to_part()
    small_add(0, small)
    small = small_step(1, SIDEWAYS)
    update((outw_ref, outm_ref, outv_ref), (outm_out, outv_out, outw_out), every, every, gout_ref[...])
    small_add(1, small)
    small = small_step(2, PART)
    for j in range(TP):
        update(in_refs, in_outs, every, slice(j * HALF, (j + 1) * HALF), ggate_ref[j // 2, j % 2])
    small_add(2, small)
    small = small_step(3, T0)
    for i, copy in enumerate(dxs):
        copy.wait_recv()
        dxo_ref[...] += dxs_ref[i].astype(f32)
    scale = lax.rsqrt(jnp.sum(hid * hid, axis=1, keepdims=True) / D + norm_eps)
    d_pre = dxo_ref[...] * pre_ref[...]
    pulled = jnp.sum(hid * d_pre, axis=1, keepdims=True) / D * (scale * scale * scale)
    gh_ref[...] = back_ref[own, :].astype(f32) + scale * d_pre - hid * pulled
    small_add(3, small)
    small = small_step(4, T1)
    g_main.to_group(gmo_ref)
    small_add(4, small)
    g_main.finish(gmo_ref)
    for j in range(TP):
        update(in_refs, in_outs, every, slice(D_INNER + j * HALF, D_INNER + (j + 1) * HALF), gmo_ref[j // 2, j % 2, :, :HALF])
    rest_grad = gmo_ref[0, 0, :, HALF:] + gmo_ref[0, 1, :, HALF:] + gmo_ref[1, 0, :, HALF:] + gmo_ref[1, 1, :, HALF:]
    update(in_refs, in_outs, every, slice(2 * D_INNER, 2 * D_INNER + SIDE), rest_grad[:, :SIDE])
    update(in_refs, in_outs, every, slice(2 * D_INNER + SIDE, 2 * D_INNER + SIDE + HEADS), rest_grad[:, SIDE : SIDE + HEADS])
    copies.finish()


def linked(kernel, name, collective_id, in_specs, outs, scratch):
    return pl.pallas_call(
        kernel,
        name=name,
        in_specs=in_specs,
        out_shape=tuple(o for o, _ in outs),
        out_specs=tuple(s for _, s in outs),
        scratch_shapes=scratch,
        compiler_params=pltpu.CompilerParams(
            collective_id=collective_id, has_side_effects=True, vmem_limit_bytes=VMEM_LIMIT
        ),
    )


def shards_linked(
    hidden, cotangent, segments, valid, in_w, in_m, in_v, out_w, out_m, out_v, small_w, small_m, small_v,
):
    part, t1, t0, _, _ = place()
    tp = t1 * 2 + t0
    own_rows, out_rows = in_w.shape[0], out_w.shape[0]
    tok_rows = hidden.shape[1]
    rows = tok_rows * TP
    spans = rows // SPAN
    seg_all = segments[0]
    pre_gain, norm_gain, conv_weight, conv_bias, dt_shift, a_logs, skips = unpack_small(small_w)

    def own_part(array, width):
        return lax.dynamic_slice_in_dim(array, tp * width, width, array.ndim - 1)

    in_copy = in_w.astype(bf16)
    side_cols = in_copy[:, 2 * D_INNER : 2 * D_INNER + SIDE]
    dt_cols = jnp.pad(in_copy[:, 2 * D_INNER + SIDE :], ((0, 0), (0, LANES - HEADS)))
    dt_head = jnp.arange(LANES) // LOCAL_HEADS
    w_main = jnp.stack(
        [
            jnp.concatenate(
                [
                    in_copy[:, D_INNER + j * HALF : D_INNER + (j + 1) * HALF],
                    side_cols,
                    jnp.where(dt_head == j, dt_cols, 0),
                ],
                axis=1,
            )
            for j in range(TP)
        ]
    ).reshape(2, 2, own_rows, MAIN)
    w_gate = jnp.stack([in_copy[:, j * HALF : (j + 1) * HALF] for j in range(TP)]).reshape(2, 2, own_rows, HALF)
    flat = [(i, (i % TP) * 2 + i // TP) for i in range(2 * TP)]
    out_mine = lax.ppermute(out_w.astype(bf16), ("part", *GROUP), [(b, a) for a, b in flat])
    back_mix = cotangent[0] * valid[0][:, None].astype(bf16)

    seg_front = jnp.concatenate([jnp.full((RIM,), -1, jnp.int32), seg_all, jnp.full((RIM,), -1, jnp.int32)])
    seg_pad = lax.dynamic_slice_in_dim(seg_front, part * rows, rows + 2 * RIM)
    seg = seg_pad[RIM : RIM + rows]
    seg_spans = seg.reshape(spans, SPAN)
    seg_last = seg_spans[:, -1]
    seg_before = jnp.concatenate([seg_pad[RIM - 1 : RIM], seg_last[:-1]])
    marks = [seg_pad[k : k + rows] == seg for k in range(RIM)]
    marks += [seg_pad[2 * RIM - k : 2 * RIM - k + rows] == seg for k in range(RIM)]
    marks.append(seg == jnp.repeat(seg_last, SPAN))
    marks.append(seg == jnp.repeat(seg_before, SPAN))
    marks = jnp.stack(marks, axis=1).astype(f32)
    carry = jnp.broadcast_to((seg_last == seg_before).astype(f32)[:, None], (spans, LANES))
    seg_col = seg[:, None]

    def both(array):
        return jnp.concatenate([own_part(array[..., :D_INNER], HALF), array[..., D_INNER:]], axis=-1)

    taps = jnp.concatenate([both(conv_weight), both(conv_bias)[None], jnp.zeros((3, CHANS), f32)])
    head_rows = jnp.stack([own_part(dt_shift, LOCAL_HEADS), -jnp.exp(own_part(a_logs, LOCAL_HEADS))])
    head_rows = jnp.pad(head_rows, ((0, 0), (0, LANES - LOCAL_HEADS)))
    rate_row = head_rows[1]
    chans = jnp.stack([jnp.repeat(own_part(skips, LOCAL_HEADS), HEADDIM), own_part(norm_gain, HALF)])

    hidden_all, x_normed, w_in, conv_in, dt_raw = linked(
        start_kernel, "start", 1, [HBM, HBM, VMEM],
        [
            (shape((rows, D), bf16), VMEM),
            (shape((rows, D), bf16), VMEM),
            (shape((D, MAIN), bf16), VMEM),
            (shape((rows, CHANS), bf16), VMEM),
            (shape((rows, LANES), f32), VMEM),
        ],
        sems(40, 2),
    )(hidden[0], w_main, pre_gain[None])

    half = lambda dtype: shape((rows, HALF), dtype)
    lanes = shape((rows, LANES), f32)
    state_buf = pltpu.VMEM((STATE, HALF), f32)
    state_half = pltpu.VMEM((STATE, HALF), bf16)
    half_buf = pltpu.VMEM((rows, HALF), f32)
    (
        conv_pad, x_scan, b_mat, c_mat, dsilu, dt, z, cum, y_scan, states, w_gate, w_out, back_all,
        normed, mix, dy, d_gate, d_gain,
    ) = linked(
        functools.partial(forward_kernel, spans), "forward", 2, [VMEM] * 10 + [HBM] * 3,
        [
            (o, VMEM)
            for o in (
                shape((rows + FRONT, CHANS), bf16),
                half(bf16),
                shape((rows, STATE), bf16),
                shape((rows, STATE), bf16),
                shape((rows, CHANS), f32),
                lanes,
                lanes,
                lanes,
                half(f32),
                shape((spans, STATE, HALF), f32),
                shape((D, HALF), bf16),
                shape((HALF, D), bf16),
                shape((rows, D), bf16),
                half(bf16),
                shape((rows, D), bf16),
                half(bf16),
                half(bf16),
                shape((TILE, HALF), f32),
            )
        ],
        [
            state_buf,
            state_half,
            state_half,
            pltpu.VMEM((FRONT, CHANS), bf16),
            half_buf,
            half_buf,
            half_buf,
            pltpu.VMEM((2, TILE, rows), f32),
            pltpu.VMEM((2, 3, TILE, rows), f32),
            *sems(60, 3),
        ],
    )(conv_in, dt_raw, x_normed, taps, head_rows, chans, marks, seg_col, seg_spans, carry, w_gate, out_mine, back_mix)

    d_main, h_sums, d_skip, d_taps, mixes, g_out, g_gate = linked(
        functools.partial(backward_kernel, spans), "backward", 3, [VMEM] * 23,
        [
            (shape((rows, MAIN), bf16), VMEM),
            (shape((TILE, LANES), f32), VMEM),
            (shape((TILE, HALF), f32), VMEM),
            (shape((TILE, CHANS), f32), VMEM),
            (shape((3, tok_rows, D), bf16), VMEM),
            (shape((out_rows, D), f32), VMEM),
            (shape((2, 2, own_rows, HALF), f32), VMEM),
        ],
        [
            state_buf,
            pltpu.VMEM((spans, STATE, HALF), f32),
            pltpu.VMEM((rows, HALF), bf16),
            half_buf,
            pltpu.VMEM((2 * SPAN, HALF), f32),
            state_half,
            state_half,
            pltpu.VMEM((rows + FRONT, CHANS), f32),
            pltpu.VMEM((TILE, CHANS), f32),
            pltpu.VMEM((TILE, CHANS), f32),
            pltpu.VMEM((rows, STATE), f32),
            pltpu.VMEM((rows, STATE), f32),
            pltpu.VMEM((2, 2, 2, out_rows, D), bf16),
            pltpu.VMEM((2, 2, 2, 2, 2, own_rows, HALF), bf16),
            *sum_buffers(out_rows, D, False),
            *sum_buffers(own_rows, HALF, True),
            *sems(40, 1),
        ],
    )(
        x_scan, b_mat, c_mat, dt, z, head_rows, chans, marks, seg_col, seg_spans, carry, y_scan, states, cum, dy, dsilu,
        conv_pad, taps, normed, back_all, x_normed, d_gate, mix,
    )
    g_out = lax.ppermute(g_out, ("part", *GROUP), flat)

    token_buf = lambda dtype: shape((tok_rows, D), dtype)
    box = (BOX_ROWS, LANES)
    output, grad_hidden, in_m_new, in_v_new, in_w_new, out_m_new, out_v_new, out_w_new, totals = linked(
        end_kernel, "end", 4, [VMEM] * 23,
        [
            (o, VMEM)
            for o in (
                token_buf(bf16),
                token_buf(f32),
                *[shape(in_w.shape, f32)] * 3,
                *[shape(out_w.shape, f32)] * 3,
                shape(box, f32),
            )
        ],
        [
            pltpu.VMEM((rows, D), bf16),
            pltpu.VMEM((3, tok_rows, D), bf16),
            pltpu.VMEM((tok_rows, D), f32),
            pltpu.VMEM((TILE, D), f32),
            pltpu.VMEM((2, 2, 2, 2, 2, own_rows, MAIN), bf16),
            pltpu.VMEM((2, 2, own_rows, MAIN), f32),
            pltpu.VMEM((5, *box), f32),
            pltpu.VMEM((5, *box), f32),
            *sum_buffers(own_rows, MAIN, True),
            *sems(40, 1),
        ],
    )(
        d_main, d_gate, w_in, w_gate, x_normed, hidden_all, pre_gain[None], d_gain, d_skip, d_taps, h_sums, mix, mixes,
        back_all, valid[0][:, None].astype(f32), g_gate, g_out, in_w, in_m, in_v, out_w, out_m, out_v,
    )

    regions = totals[BOX_GROUP:BOX_SIDE].reshape(TP, REGION * LANES)

    def region(first, count):
        return regions[:, first * LANES : (first + count) * LANES]

    sides = totals[BOX_SIDE:].reshape(-1)
    weight_rows = []
    for j in range(CONV + 1):
        weight_rows.append(region(12 + 6 * j, 6).reshape(-1))
        weight_rows.append(sides[2 * j * LANES : 2 * (j + 1) * LANES])
    d_rate = region(42, 1)[:, :LOCAL_HEADS].reshape(-1) * -jnp.exp(a_logs)
    d_shift = region(43, 1)[:, :LOCAL_HEADS].reshape(-1)
    d_skips = jnp.sum(region(6, 6).reshape(HEADS, HEADDIM), axis=1)
    small_grad = jnp.concatenate(
        [totals[: D // LANES].reshape(-1), region(0, 6).reshape(-1), *weight_rows, d_shift, d_rate, d_skips]
    )
    small_m_new, small_v_new, small_w_new = adamw(small_w, small_m, small_v, small_grad, 0.2, 0.0)
    scalars = totals[BOX_SIDE + 10]
    rms = jnp.sqrt(scalars[:2] / (scalars[2] * D))
    return (
        output[None], grad_hidden[None], in_m_new, in_v_new, in_w_new, out_m_new, out_v_new, out_w_new,
        small_m_new, small_v_new, small_w_new, rms,
    )


def solution(mesh):
    seq, wt = mesh.shape["seq"], mesh.shape["wt"]
    split = Mesh(mesh.devices.reshape(seq // TP, 2, 2, wt // 2, 2), EVERYONE)
    streams = ("w1", "w0")
    tokens = ("part", "t1", "t0")
    matrix = P(EVERYONE, None)
    stream = P(streams, tokens, None)
    size = mesh.devices.size
    fits = seq == 2 * TP and wt == 4 and D // size % 16 == 0 and D_INNER // size % 16 == 0
    return jax.shard_map(
        shards_linked if fits else shards_general,
        mesh=split,
        in_specs=(
            stream, stream, P(streams, None), P(streams, tokens), matrix, matrix, matrix, matrix, matrix, matrix, P(), P(), P(),
        ),
        out_specs=(stream, stream, matrix, matrix, matrix, matrix, matrix, matrix, P(), P(), P(), P()),
        check_vma=False,
    )
```

```python
import functools

import jax
import jax.numpy as jnp
from jax import lax
from jax.experimental import pallas as pl
from jax.experimental.pallas import tpu as pltpu
from jax.sharding import Mesh
from jax.sharding import PartitionSpec as P

D = 1536
D_INNER = 3072
HEADS = 48
HEADDIM = 64
STATE = 128
CONV = 4
SPAN = 256
STEP = 4
CONVCH = 3328
TP = 4
RIM = CONV - 1
LANES = 128
HALF = D_INNER // TP
LOCAL_HEADS = HEADS // TP
PAIRS = LOCAL_HEADS // 2
SIDE = 2 * STATE
COL_SIDE = HALF
COL_DT = HALF + SIDE
COL_GATE = COL_DT + LANES
COLS = COL_GATE + HALF

bf16 = jnp.bfloat16
f32 = jnp.float32
exact_prec = lax.Precision.HIGHEST
norm_eps = 1e-05
adam_eps = 1e-08


def dot(a, b, dims=((1,), (0,)), precision=None):
    return lax.dot_general(a, b, (dims, ((), ())), precision=precision, preferred_element_type=f32)


def unpack_small(small):
    first = D
    second = first + D_INNER
    third = second + CONV * CONVCH
    fourth = third + CONVCH
    fifth = fourth + HEADS
    sixth = fifth + HEADS
    return (
        small[:first],
        small[first:second],
        small[second:third].reshape(CONV, CONVCH),
        small[third:fourth],
        small[fourth:fifth],
        small[fifth:sixth],
        small[sixth:],
    )


def adamw(weight, moment, second, grad, rate, decay):
    moment_new = 0.5 * moment + 0.5 * grad
    second_new = 0.5 * second + 0.5 * grad * grad
    first_hat = moment_new / (1.0 - 0.5**STEP)
    second_hat = second_new / (1.0 - 0.5**STEP)
    weight_new = weight - rate * (first_hat / (jnp.sqrt(second_hat) + adam_eps) + decay * weight)
    return (moment_new, second_new, weight_new)


def pair_cols(cols, h):
    lane = lax.broadcasted_iota(jnp.int32, (cols.shape[0], LANES), 1)
    return jnp.where(lane < HEADDIM, cols[:, h : h + 1], cols[:, h + 1 : h + 2])


def span_rows(c):
    return pl.ds(pl.multiple_of(c * SPAN, SPAN), SPAN)


def span_decay(dt_ref, rate_ref, c, at=0):
    dt = dt_ref[span_rows(c), :]
    row = lax.broadcasted_iota(jnp.int32, (SPAN, SPAN), 0)
    col = lax.broadcasted_iota(jnp.int32, (SPAN, SPAN), 1)
    lower = (row >= col).astype(f32)
    return dt, dot(lower, dt * rate_ref[at : at + 1, :], precision=exact_prec)


def state_kernel(spans, x_ref, b_ref, dt_ref, rate_ref, keep_ref, carry_ref, s_ref, dec_ref):
    s_ref[...] = jnp.zeros_like(s_ref)
    dec_ref[...] = jnp.ones_like(dec_ref)

    def body(c, _):
        rows = span_rows(c)
        dt, cum = span_decay(dt_ref, rate_ref, c)
        last = cum[SPAN - 1 : SPAN, :]
        end_weight = jnp.exp(last - cum) * dt * keep_ref[rows, :]
        decay = jnp.exp(last) * carry_ref[pl.ds(c, 1), :]
        dec_ref[...] = dec_ref[...] * decay
        b = b_ref[rows, :]
        for p in range(PAIRS):
            lanes = slice(p * LANES, (p + 1) * LANES)
            xw = (x_ref[rows, lanes].astype(f32) * pair_cols(end_weight, 2 * p)).astype(bf16)
            fresh = dot(b, xw, ((0,), (0,)))
            s_ref[:, lanes] = s_ref[:, lanes] * pair_cols(decay, 2 * p) + fresh
        return 0

    lax.fori_loop(0, spans, body, 0)


def scan_kernel(
    spans, x_ref, b_ref, c_ref, dt_ref, rate_ref, segc_ref, segr_ref, keep_ref, inflow_ref, carry_ref, s_in_ref,
    y_ref, st_ref, s_ref,
):
    s_ref[...] = s_in_ref[...]

    def body(c, _):
        rows = span_rows(c)
        dt, cum = span_decay(dt_ref, rate_ref, c)
        last = cum[SPAN - 1 : SPAN, :]
        end_weight = jnp.exp(last - cum) * dt * keep_ref[rows, :]
        decay = jnp.exp(last) * carry_ref[pl.ds(c, 1), :]
        gain = jnp.exp(cum) * inflow_ref[rows, :]
        back_log = jnp.transpose(cum - jnp.log(dt))
        b = b_ref[rows, :]
        cc = c_ref[rows, :]
        scores = dot(cc, b, ((1,), (1,)))
        row = lax.broadcasted_iota(jnp.int32, (SPAN, SPAN), 0)
        col = lax.broadcasted_iota(jnp.int32, (SPAN, SPAN), 1)
        mask = (row >= col) & (segc_ref[rows, :] == segr_ref[pl.ds(c, 1), :])
        lane = lax.broadcasted_iota(jnp.int32, (SPAN, LANES), 1)
        st_ref[c] = s_ref[...]
        for p in range(PAIRS):
            lanes = slice(p * LANES, (p + 1) * LANES)
            x = x_ref[rows, lanes]
            parts = []
            for h in (2 * p, 2 * p + 1):
                gap = cum[:, h : h + 1] - back_log[h : h + 1, :]
                weights = scores * jnp.exp(jnp.where(mask, gap, -1e30))
                parts.append(dot(weights.astype(bf16), x))
            y = jnp.where(lane < HEADDIM, parts[0], parts[1])
            state = s_ref[:, lanes]
            y = y + dot(cc, state.astype(bf16)) * pair_cols(gain, 2 * p)
            y_ref[rows, lanes] = y
            xw = (x.astype(f32) * pair_cols(end_weight, 2 * p)).astype(bf16)
            s_ref[:, lanes] = state * pair_cols(decay, 2 * p) + dot(b, xw, ((0,), (0,)))
        return 0

    lax.fori_loop(0, spans, body, 0)


def state_back_kernel(spans, dy_ref, c_ref, dt_ref, rate_ref, inflow_ref, carry_ref, s_ref):
    s_ref[...] = jnp.zeros_like(s_ref)

    def body(step, _):
        c = spans - 1 - step
        rows = span_rows(c)
        dt, cum = span_decay(dt_ref, rate_ref, c)
        decay = jnp.exp(cum[SPAN - 1 : SPAN, :]) * carry_ref[pl.ds(c, 1), :]
        gain = jnp.exp(cum) * inflow_ref[rows, :]
        cc = c_ref[rows, :]
        for p in range(PAIRS):
            lanes = slice(p * LANES, (p + 1) * LANES)
            dyg = (dy_ref[rows, lanes].astype(f32) * pair_cols(gain, 2 * p)).astype(bf16)
            s_ref[:, lanes] = s_ref[:, lanes] * pair_cols(decay, 2 * p) + dot(cc, dyg, ((0,), (0,)))
        return 0

    lax.fori_loop(0, spans, body, 0)


def head_sums(values):
    width = values.shape[1]
    chan = lax.broadcasted_iota(jnp.int32, (width, LANES), 0)
    head = lax.broadcasted_iota(jnp.int32, (width, LANES), 1)
    pick = (chan // HEADDIM == head).astype(bf16)
    high = values.astype(bf16)
    low = (values - high.astype(f32)).astype(bf16)
    return dot(high, pick) + dot(low, pick)


def scan_back_kernel(
    spans, x_ref, b_ref, c_ref, dt_ref, ratio_ref, sig_ref, rate_ref, segc_ref, segr_ref, keep_ref, inflow_ref, carry_ref, skip_ref,
    y_ref, st_ref, dy_ref, ds_out_ref,
    dx_ref, db_ref, dc_ref, ddt_ref, drate_ref, dskip_ref,
    ds_ref, prod_ref,
):
    ds_ref[...] = ds_out_ref[...]
    drate_ref[...] = jnp.zeros_like(drate_ref)
    dskip_ref[...] = jnp.zeros_like(dskip_ref)

    def body(step, _):
        c = spans - 1 - step
        rows = span_rows(c)
        dt, cum = span_decay(dt_ref, rate_ref, c)
        last = cum[SPAN - 1 : SPAN, :]
        end_weight = jnp.exp(last - cum) * dt * keep_ref[rows, :]
        decay = jnp.exp(last) * carry_ref[pl.ds(c, 1), :]
        gain = jnp.exp(cum) * inflow_ref[rows, :]
        fore_log = jnp.transpose(cum)
        back_log = cum - jnp.log(dt)
        b = b_ref[rows, :]
        cc = c_ref[rows, :]
        scores = dot(b, cc, ((1,), (1,)))
        row = lax.broadcasted_iota(jnp.int32, (SPAN, SPAN), 0)
        col = lax.broadcasted_iota(jnp.int32, (SPAN, SPAN), 1)
        mask = (col >= row) & (segc_ref[rows, :] == segr_ref[pl.ds(c, 1), :])
        lane = lax.broadcasted_iota(jnp.int32, (SPAN, LANES), 1)
        d_scores = jnp.zeros((SPAN, SPAN), f32)
        db = jnp.zeros((SPAN, STATE), f32)
        dc = jnp.zeros((SPAN, STATE), f32)
        state_row = []
        dx_state_row = []
        for p in range(PAIRS):
            lanes = slice(p * LANES, (p + 1) * LANES)
            x = x_ref[rows, lanes]
            dy = dy_ref[rows, lanes]
            xf = x.astype(f32)
            dyf = dy.astype(f32)
            parts = []
            for k in range(2):
                h = 2 * p + k
                gap = fore_log[h : h + 1, :] - back_log[:, h : h + 1]
                decay_mat = jnp.exp(jnp.where(mask, gap, -1e30))
                weights = (scores * decay_mat).astype(bf16)
                parts.append(dot(weights, dy))
                own = (lane < HEADDIM) if k == 0 else (lane >= HEADDIM)
                d_weights = dot(jnp.where(own, xf, 0.0).astype(bf16), dy, ((1,), (1,)))
                d_scores = d_scores + d_weights * decay_mat
            dx = jnp.where(lane < HEADDIM, parts[0], parts[1])
            dyg = (dyf * pair_cols(gain, 2 * p)).astype(bf16)
            ew = pair_cols(end_weight, 2 * p)
            xw = (xf * ew).astype(bf16)
            state = st_ref[c, :, lanes]
            ds = ds_ref[:, lanes]
            state_b = state.astype(bf16)
            ds_b = ds.astype(bf16)
            dc = dc + dot(dyg, state_b, ((1,), (1,)))
            db = db + dot(xw, ds_b, ((1,), (1,)))
            dx_state = dot(b, ds_b) * ew
            dx = dx + dx_state
            dec = pair_cols(decay, 2 * p)
            state_row.append(jnp.sum(ds * state, axis=0, keepdims=True) * dec)
            dx_state_row.append(jnp.sum(dx_state * xf, axis=0, keepdims=True))
            ds_ref[:, lanes] = ds * dec + dot(cc, dyg, ((0,), (0,)))
            prod_ref[0:SPAN, lanes] = dyf * y_ref[rows, lanes]
            prod_ref[SPAN : 2 * SPAN, lanes] = xf * dx
            dskip_ref[0:1, lanes] += jnp.sum(dyf * xf, axis=0, keepdims=True)
            dx_ref[rows, lanes] = (dx + dyf * skip_ref[0:1, lanes]).astype(bf16)
        d_scores_b = d_scores.astype(bf16)
        db_ref[rows, :] = db + dot(d_scores_b, cc)
        dc_ref[rows, :] = dc + dot(d_scores_b, b, ((0,), (0,)))
        sums = head_sums(prod_ref[...])
        out_sum, in_sum = sums[:SPAN], sums[SPAN:]
        edge = jnp.concatenate(state_row, axis=1) + jnp.concatenate(dx_state_row, axis=1)
        edge_sum = head_sums(jnp.broadcast_to(edge, (8, HALF)))[0:1]
        at_last = lax.broadcasted_iota(jnp.int32, (SPAN, LANES), 0) == SPAN - 1
        d_cum = out_sum - in_sum + jnp.where(at_last, edge_sum, 0.0)
        upper = (col >= row).astype(f32)
        d_log = dot(upper, d_cum, precision=exact_prec)
        drate_ref[0:1, :] += jnp.sum(d_log * dt, axis=0, keepdims=True)
        ddt_ref[rows, :] = d_log * rate_ref[0:1, :] * sig_ref[rows, :] + in_sum * ratio_ref[rows, :]
        return 0

    lax.fori_loop(0, spans, body, 0)


GROUP = ("t1", "t0")
COPIES = ("part", "w1", "w0")
EVERYONE = ("part", "t1", "t0", "w1", "w0")


VMEM_LIMIT = 60 * 1024 * 1024


def in_vmem(kernel, out_shape, name, scratch=()):
    return pl.pallas_call(
        kernel,
        out_shape=out_shape,
        scratch_shapes=list(scratch),
        name=name,
        compiler_params=pltpu.CompilerParams(vmem_limit_bytes=VMEM_LIMIT),
    )


def shape(dims, dtype):
    return jax.ShapeDtypeStruct(dims, dtype)


def shift_part(array, by):
    size = lax.axis_size("part")
    pairs = [(i, i + by) for i in range(size) if 0 <= i + by < size]
    return lax.ppermute(array, "part", pairs)


def shards_general(
    hidden, cotangent, segments, valid, in_w, in_m, in_v, out_w, out_m, out_v, small_w, small_m, small_v,
):
    parts = lax.axis_size("part")
    wt = lax.axis_size("w1") * lax.axis_size("w0")
    part = lax.axis_index("part")
    tp = lax.axis_index("t1") * 2 + lax.axis_index("t0")
    own_rows = in_w.shape[0]
    out_rows = out_w.shape[0]
    resid = hidden[0].astype(f32)
    tok_rows = resid.shape[0]
    rows = tok_rows * TP
    spans = rows // SPAN
    seg_all = segments[0]
    pre_gain, norm_gain, conv_weight, conv_bias, dt_shift, a_logs, skips = unpack_small(small_w)

    def own_part(array, width):
        return lax.dynamic_slice_in_dim(array, tp * width, width, array.ndim - 1)

    in_copy = in_w.astype(bf16)
    slices = []
    for j in range(TP):
        slices.append(
            jnp.concatenate(
                [
                    in_copy[:, D_INNER + j * HALF : D_INNER + (j + 1) * HALF],
                    in_copy[:, 2 * D_INNER : 2 * D_INNER + SIDE],
                    in_copy[:, D_INNER + CONVCH + j * LOCAL_HEADS : D_INNER + CONVCH + (j + 1) * LOCAL_HEADS],
                    jnp.zeros((own_rows, LANES - LOCAL_HEADS), bf16),
                    in_copy[:, j * HALF : (j + 1) * HALF],
                ],
                axis=1,
            )
        )
    mine = lax.all_to_all(jnp.stack(slices), GROUP, 0, 0, tiled=False)
    w_in = lax.all_gather(mine, COPIES, axis=0, tiled=False)
    w_in = w_in.reshape(parts, wt, TP, own_rows, COLS).transpose(0, 2, 1, 3, 4).reshape(D, COLS)
    flat = [(i, (i % TP) * parts + i // TP) for i in range(parts * TP)]
    out_mine = lax.ppermute(out_w.astype(bf16), ("part", *GROUP), [(b, a) for a, b in flat])
    w_out = lax.all_gather(out_mine, COPIES, axis=0, tiled=True)

    hidden_all = lax.all_gather(hidden[0], GROUP, axis=0, tiled=True)
    back_mix = cotangent[0] * valid[0][:, None].astype(bf16)
    back_all = lax.all_gather(back_mix, GROUP, axis=0, tiled=True)

    hid = hidden_all.astype(f32)
    scale_all = lax.rsqrt(jnp.mean(hid * hid, axis=1, keepdims=True) + norm_eps)
    x_normed = (hid * scale_all * pre_gain).astype(bf16)
    projected = dot(x_normed, w_in)
    conv_in = projected[:, :COL_DT].astype(bf16)
    dt_raw = projected[:, COL_DT:COL_GATE].astype(bf16).astype(f32)
    gate_pre = projected[:, COL_GATE:]
    rim_in = shift_part(conv_in[rows - RIM :], 1)
    padded = jnp.concatenate([rim_in, conv_in], axis=0).astype(f32)
    seg_front = jnp.concatenate([jnp.full((RIM,), -1, jnp.int32), seg_all, jnp.full((RIM,), -1, jnp.int32)])
    seg_pad = lax.dynamic_slice_in_dim(seg_front, part * rows, rows + 2 * RIM)
    seg = seg_pad[RIM : RIM + rows]
    masks = [(seg_pad[k : k + rows] == seg).astype(f32)[:, None] for k in range(CONV)]
    taps = jnp.concatenate([own_part(conv_weight[:, :D_INNER], HALF), conv_weight[:, D_INNER:]], axis=1)
    bias = jnp.concatenate([own_part(conv_bias[:D_INNER], HALF), conv_bias[D_INNER:]])
    total = bias[None, :]
    for k in range(CONV):
        total = total + taps[k] * padded[k : k + rows] * masks[k]
    sig_total = jax.nn.sigmoid(total)
    activated = (total * sig_total).astype(bf16)
    x_scan = activated[:, :HALF]
    b_mat = activated[:, HALF : HALF + STATE]
    c_mat = activated[:, HALF + STATE :]

    def head_row(array):
        return jnp.pad(own_part(array, LOCAL_HEADS), (0, LANES - LOCAL_HEADS))

    shift_row = head_row(dt_shift)
    z = dt_raw + shift_row
    dt = jax.nn.softplus(z)
    sig_dt = jax.nn.sigmoid(z)
    ratio = jnp.where(dt > 1e-30, sig_dt / jnp.maximum(dt, 1e-30), 1.0)
    rate_row = -jnp.exp(head_row(a_logs))
    rate8 = jnp.broadcast_to(rate_row, (8, LANES))
    skip_chan = jnp.repeat(own_part(skips, LOCAL_HEADS), HEADDIM)
    skip8 = jnp.broadcast_to(skip_chan, (8, HALF))
    seg_spans = seg.reshape(spans, SPAN)
    seg_last = seg_spans[:, -1]
    seg_before = jnp.concatenate([seg_pad[RIM - 1 : RIM], seg_last[:-1]])
    keep = (seg_spans == seg_last[:, None]).astype(f32).reshape(rows, 1)
    inflow = (seg_spans == seg_before[:, None]).astype(f32).reshape(rows, 1)
    carry = jnp.broadcast_to((seg_last == seg_before).astype(f32)[:, None], (spans, LANES))
    seg_col = seg[:, None]

    state_shape = shape((STATE, HALF), f32)
    s_local, dec_total = in_vmem(
        functools.partial(state_kernel, spans), (state_shape, shape((8, LANES), f32)), "state"
    )(x_scan, b_mat, dt, rate8, keep, carry)
    dec_chan = jnp.repeat(dec_total[0, :LOCAL_HEADS], HEADDIM)
    s_in = jnp.zeros((STATE, HALF), f32)
    for _ in range(parts - 1):
        s_in = shift_part(dec_chan * s_in + s_local, 1)
    y_scan, states = in_vmem(
        functools.partial(scan_kernel, spans),
        (shape((rows, HALF), f32), shape((spans, STATE, HALF), f32)),
        "scan",
        [pltpu.VMEM((STATE, HALF), f32)],
    )(x_scan, b_mat, c_mat, dt, rate8, seg_col, seg_spans, keep, inflow, carry, s_in)
    y_b = (y_scan + skip_chan * x_scan.astype(f32)).astype(bf16).astype(f32)

    gain_own = own_part(norm_gain, HALF)
    sig_gate = jax.nn.sigmoid(gate_pre)
    silu_gate = gate_pre * sig_gate
    gated = y_b * silu_gate
    gate_sq = lax.psum(jnp.sum(gated * gated, axis=1), GROUP)
    scale_gate = lax.rsqrt(gate_sq / D_INNER + norm_eps)[:, None]
    normed = (gated * scale_gate * gain_own).astype(bf16)
    mixer = lax.psum_scatter(dot(normed, w_out), GROUP, scatter_dimension=0, tiled=True)
    output = (resid + mixer).astype(bf16)
    valid_rows = valid[0].astype(f32)
    res_sq = jnp.sum(valid_rows * jnp.sum(resid * resid, axis=1))
    mix_sq = jnp.sum(valid_rows * jnp.sum(mixer * mixer, axis=1))
    valid_count = jnp.sum(valid_rows)

    d_normed = dot(back_all, w_out, ((1,), (1,)))
    g_out = dot(normed, back_all, ((0,), (0,)))
    g_out = lax.psum_scatter(g_out, COPIES, scatter_dimension=0, tiled=True)
    g_out = lax.ppermute(g_out, ("part", *GROUP), flat)
    d_gain = d_normed * gain_own
    gate_dot = lax.psum(jnp.sum(gated * d_gain, axis=1), GROUP)
    d_gated = scale_gate * d_gain - gated * (scale_gate**3 * (gate_dot / D_INNER)[:, None])
    d_norm_gain = jnp.sum(gated * scale_gate * d_normed, axis=0)
    dy = (d_gated * silu_gate).astype(bf16)
    d_gate = d_gated * y_b * (sig_gate * (1.0 + gate_pre * (1.0 - sig_gate)))

    ds_local = in_vmem(functools.partial(state_back_kernel, spans), state_shape, "state_back")(
        dy, c_mat, dt, rate8, inflow, carry
    )
    ds_out = jnp.zeros((STATE, HALF), f32)
    for _ in range(parts - 1):
        ds_out = shift_part(dec_chan * ds_out + ds_local, -1)
    d_x, d_b, d_c, d_dt, d_rate, d_skip = in_vmem(
        functools.partial(scan_back_kernel, spans),
        (
            shape((rows, HALF), bf16),
            shape((rows, STATE), f32),
            shape((rows, STATE), f32),
            shape((rows, LANES), f32),
            shape((8, LANES), f32),
            shape((8, HALF), f32),
        ),
        "scan_back",
        [pltpu.VMEM((STATE, HALF), f32), pltpu.VMEM((2 * SPAN, HALF), f32)],
    )(x_scan, b_mat, c_mat, dt, ratio, sig_dt, rate8, seg_col, seg_spans, keep, inflow, carry, skip8, y_scan, states, dy, ds_out)

    d_total = jnp.concatenate([d_x.astype(f32), d_b, d_c], axis=1) * (sig_total * (1.0 + total * (1.0 - sig_total)))
    rim_back = shift_part(d_total[:RIM], -1)
    d_padded = jnp.concatenate([d_total, rim_back], axis=0)
    d_conv_in = 0.0
    for k in range(CONV):
        later = (seg_pad[2 * RIM - k : 2 * RIM - k + rows] == seg).astype(f32)[:, None]
        d_conv_in = d_conv_in + taps[k] * d_padded[RIM - k : RIM - k + rows] * later
    d_taps = jnp.stack([jnp.sum(d_total * padded[k : k + rows] * masks[k], axis=0) for k in range(CONV)])
    d_bias = jnp.sum(d_total, axis=0)
    d_proj = jnp.concatenate([d_conv_in, d_dt, d_gate], axis=1).astype(bf16)
    d_x_normed = dot(d_proj, w_in, ((1,), (1,)))
    d_x_normed = lax.psum_scatter(d_x_normed, GROUP, scatter_dimension=0, tiled=True)
    g_in = dot(x_normed, d_proj, ((0,), (0,)))
    g_in = g_in.reshape(parts, TP, wt, own_rows, COLS).transpose(0, 2, 1, 3, 4).reshape(parts * wt, TP, own_rows, COLS)
    g_in = lax.psum_scatter(g_in, COPIES, scatter_dimension=0, tiled=False)
    g_in = lax.all_to_all(g_in, GROUP, 0, 0, tiled=False)
    g_in = jnp.concatenate(
        [g_in[j, :, COL_GATE:] for j in range(TP)]
        + [g_in[j, :, :HALF] for j in range(TP)]
        + [jnp.sum(g_in[:, :, COL_SIDE:COL_DT], axis=0)]
        + [g_in[j, :, COL_DT : COL_DT + LOCAL_HEADS] for j in range(TP)],
        axis=1,
    )

    scale_own = lax.rsqrt(jnp.mean(resid * resid, axis=1, keepdims=True) + norm_eps)
    d_pre = d_x_normed * pre_gain
    dot_pre = jnp.mean(resid * d_pre, axis=1, keepdims=True)
    grad_hidden = back_mix.astype(f32) + scale_own * d_pre - resid * (scale_own**3 * dot_pre)
    d_pre_gain = jnp.sum(resid * scale_own * d_x_normed, axis=0)

    def placed(values, width):
        spread = (jnp.arange(TP) == tp).astype(f32)[:, None] * values[..., None, :]
        return spread.reshape(*values.shape[:-1], TP * width)

    d_weight = jnp.concatenate([placed(d_taps[:, :HALF], HALF), d_taps[:, HALF:]], axis=1)
    small_grad = jnp.concatenate(
        [
            d_pre_gain,
            placed(d_norm_gain, HALF),
            d_weight.reshape(-1),
            placed(d_bias[:HALF], HALF),
            d_bias[HALF:],
            placed(jnp.sum(d_dt, axis=0)[:LOCAL_HEADS], LOCAL_HEADS),
            placed((d_rate[0] * rate_row)[:LOCAL_HEADS], LOCAL_HEADS),
            placed(jnp.sum(d_skip[0].reshape(LOCAL_HEADS, HEADDIM), axis=1), LOCAL_HEADS),
            jnp.stack([res_sq, mix_sq, valid_count]),
        ]
    )
    small_total = lax.psum(small_grad, EVERYONE)
    res_total, mix_total, count_total = small_total[-3], small_total[-2], small_total[-1]
    in_m_new, in_v_new, in_w_new = adamw(in_w, in_m, in_v, g_in, 0.02, 0.1)
    out_m_new, out_v_new, out_w_new = adamw(out_w, out_m, out_v, g_out, 0.02, 0.1)
    small_m_new, small_v_new, small_w_new = adamw(small_w, small_m, small_v, small_total[:-3], 0.2, 0.0)
    rms = jnp.stack([jnp.sqrt(res_total / (count_total * D)), jnp.sqrt(mix_total / (count_total * D))])
    return (
        output[None], grad_hidden[None], in_m_new, in_v_new, in_w_new, out_m_new, out_v_new, out_w_new,
        small_m_new, small_v_new, small_w_new, rms,
    )


MESH = pl.DeviceIdType.MESH
T0, T1, DIAG, CORE, SIDEWAYS, PART = ("t0",), ("t1",), ("t1", "t0"), ("w0",), ("w1",), ("part",)
SIDE_CORE = ("w1", "w0")
HOPS = (None, T0, T1, DIAG)
HBM = pl.BlockSpec(memory_space=pl.ANY)
VMEM = pl.BlockSpec(memory_space=pltpu.VMEM)
MAIN = COL_GATE
CHANS = HALF + SIDE
FRONT = 16
TILE = 8
QUARTER = HALF // 2
NORM_ROW = D // LANES
TAP_ROW = NORM_ROW + D_INNER // LANES
TAP_ROWS = CONVCH // LANES
HEAD_ROW = TAP_ROW + (CONV + 1) * TAP_ROWS
SMALL_ROWS = HEAD_ROW + 2
BOX_ROWS = SMALL_ROWS + 8


def place():
    return tuple(lax.axis_index(a) for a in EVERYONE)


def across(flips):
    return {a: 1 - lax.axis_index(a) for a in flips}


def group_blocks():
    _, t1, t0, _, _ = place()
    return [(t1, t0), (t1, 1 - t0), (1 - t1, t0), (1 - t1, 1 - t0)]


def greet(neighbours):
    barrier = pltpu.get_barrier_semaphore()
    for flips in neighbours:
        pl.semaphore_signal(barrier, inc=1, device_id=across(flips), device_id_type=MESH)
    pl.semaphore_wait(barrier, len(neighbours))


class Copies:
    def __init__(self, local_sem, send_sem, recv_sem):
        self.local_sem, self.send_sem, self.recv_sem = local_sem, send_sem, recv_sem
        self.sent, self.kept = [], []

    def send(self, src, dst, flips):
        i = len(self.sent)
        copy = pltpu.make_async_remote_copy(
            src_ref=src,
            dst_ref=dst,
            send_sem=self.send_sem.at[i],
            recv_sem=self.recv_sem.at[i],
            device_id=across(flips),
            device_id_type=MESH,
        )
        copy.start()
        self.sent.append(copy)
        return copy

    def keep(self, src, dst):
        copy = pltpu.make_async_copy(src, dst, self.local_sem.at[len(self.kept)])
        copy.start()
        self.kept.append(copy)
        return copy

    def finish(self):
        for copy in self.sent:
            copy.wait_send()


def sems(remote, local=1):
    return [
        pltpu.SemaphoreType.DMA((local,)),
        pltpu.SemaphoreType.DMA((remote,)),
        pltpu.SemaphoreType.DMA((remote,)),
    ]


class GroupGather:
    def __init__(self, copies, src, dst):
        self.copies, self.dst = copies, dst
        self.rows = src.shape[0]
        self.halves = (0, self.rows // 2)
        own = group_blocks()[0]
        self.own = copies.keep(src, self.at(own, 0, self.rows))
        size = self.rows // 2
        self.along_t1 = [copies.send(src.at[pl.ds(h, size)], self.at(own, h, size), T1) for h in self.halves]
        self.along_t0 = [copies.send(src.at[pl.ds(h, size)], self.at(own, h, size), T0) for h in self.halves]
        self.diagonal = []

    def at(self, block, first, size):
        return self.dst.at[pl.ds(pl.multiple_of((block[0] * 2 + block[1]) * self.rows + first, size), size)]

    def hand_on(self):
        beside = group_blocks()[2]
        for copy, h in zip(self.along_t1, self.halves):
            copy.wait_recv()
            here = self.at(beside, h, self.rows // 2)
            self.diagonal.append(self.copies.send(here, here, T0))

    def finish(self):
        for copy in self.along_t0 + self.diagonal:
            copy.wait_recv()


class WeightGather:
    def __init__(self, copies, dst, rows, group):
        self.copies, self.dst, self.rows, self.group = copies, dst, rows, group
        self.by_part, self.by_side, self.by_core = [], [], []

    def at(self, part, w1, w0, block):
        index = part
        if self.group:
            index = (index * 2 + block[0]) * 2 + block[1]
        index = (index * 2 + w1) * 2 + w0
        return self.dst.at[pl.ds(pl.multiple_of(index * self.rows, self.rows), self.rows)]

    def mine(self, block):
        p, _, _, w1, w0 = place()
        return self.at(p, w1, w0, block)

    def spread(self, src, block):
        dst = self.mine(block)
        self.by_part.append((self.copies.send(src, dst, PART), block))
        self.by_side.append((self.copies.send(src, dst, SIDEWAYS), block))
        self.by_core.append(self.copies.send(src, dst, CORE))

    def swap(self, src):
        own, *others = group_blocks()
        self.kept = self.copies.keep(src.at[own[0], own[1]], self.mine(own))
        self.spread(src.at[own[0], own[1]], own)
        self.swaps = [
            (self.copies.send(src.at[b[0], b[1]], self.mine(own), flips), b) for b, flips in zip(others, HOPS[1:])
        ]

    def spread_swapped(self):
        for copy, block in self.swaps:
            copy.wait_recv()
            self.spread(self.mine(block), block)

    def pass_core(self, part, w1, block):
        here = self.at(part, w1, lax.axis_index("w0"), block)
        self.by_core.append(self.copies.send(here, here, CORE))

    def hand_on(self):
        p, _, _, w1, w0 = place()
        again = []
        for (copy, block), (side, _) in zip(self.by_part, self.by_side):
            side.wait_recv()
            self.pass_core(p, 1 - w1, block)
            copy.wait_recv()
            here = self.at(1 - p, w1, w0, block)
            again.append((self.copies.send(here, here, SIDEWAYS), block))
            self.pass_core(1 - p, w1, block)
        for copy, block in again:
            copy.wait_recv()
            self.pass_core(1 - p, 1 - w1, block)

    def finish(self):
        for copy in self.by_core:
            copy.wait_recv()


class GradientSum:
    def __init__(self, copies, src, bufs, group):
        self.copies, self.src, self.group = copies, src, group
        self.core, self.side, self.sides, self.far, self.fars = bufs[:5]
        self.last, self.lasts = bufs[5:] if group else (None, None)
        self.blocks = group_blocks() if group else [()]

    def added(self, q, block, side, *more):
        w0 = lax.axis_index("w0")
        value = self.src[(q, *block, side, w0)].astype(f32) + self.core[(q, side, *block)].astype(f32)
        for other in more:
            value = value + other.astype(f32)
        return value

    def cores(self):
        p, _, _, w1, w0 = place()
        every = (slice(None), slice(None)) if self.group else ()
        order = [(1 - p, 1 - w1), (p, 1 - w1), (1 - p, w1), (p, w1)]
        self.core_copies = [
            self.copies.send(self.src.at[(q, *every, s, 1 - w0)], self.core.at[q, s], CORE) for q, s in order
        ]

    def to_sides(self):
        p, _, _, w1, _ = place()
        self.side_copies = [[], []]
        for k, q in enumerate((1 - p, p)):
            self.core_copies[k].wait_recv()
            for i, block in enumerate(self.blocks):
                self.side[k, i] = self.added(q, block, 1 - w1).astype(bf16)
                self.side_copies[k].append(self.copies.send(self.side.at[k, i], self.sides.at[k, i], SIDEWAYS))

    def to_part(self):
        p, _, _, w1, _ = place()
        self.core_copies[2].wait_recv()
        self.core_copies[3].wait_recv()
        self.far_copies = []
        for i, block in enumerate(self.blocks):
            self.side_copies[0][i].wait_recv()
            self.far[i] = self.added(1 - p, block, w1, self.sides[0, i]).astype(bf16)
            self.far_copies.append(self.copies.send(self.far.at[i], self.fars.at[i], PART))

    def total(self, i):
        p, _, _, w1, _ = place()
        self.side_copies[1][i].wait_recv()
        self.far_copies[i].wait_recv()
        return self.added(p, self.blocks[i], w1, self.sides[1, i], self.fars[i])

    def to_group(self, out):
        self.last_copies = []
        for i in (1, 2, 3, 0):
            value = self.total(i)
            if i == 0:
                out[self.blocks[0]] = value
            else:
                self.last[i - 1] = value.astype(bf16)
                self.last_copies.append(self.copies.send(self.last.at[i - 1], self.lasts.at[i - 1], HOPS[i]))

    def finish(self, out):
        for i, copy in enumerate(self.last_copies):
            copy.wait_recv()
            out[self.blocks[i + 1]] = self.lasts[i].astype(f32)


class GroupScatter:
    def __init__(self, copies, src, bufs):
        self.copies, self.src = copies, src
        self.here, self.pass_on, self.joined, self.last = bufs
        self.rows = self.here.shape[0]

    def block(self, i):
        return block_rows(group_blocks()[i], self.rows)

    def to_t0(self, i):
        copy = self.copies.send(self.src.at[self.block(i)], self.here if i == 1 else self.pass_on, T0)
        if i == 1:
            self.own_copy = copy
        else:
            self.pass_copy = copy

    def to_t1(self):
        self.pass_copy.wait_recv()
        self.joined[...] = (self.src[self.block(2), :].astype(f32) + self.pass_on[...].astype(f32)).astype(bf16)
        self.last_copy = self.copies.send(self.joined, self.last, T1)

    def finish(self):
        self.own_copy.wait_recv()
        self.last_copy.wait_recv()
        return self.here[...].astype(f32) + self.last[...].astype(f32)


def scatter_buffers(rows):
    return [pltpu.VMEM((rows, D), bf16)] * 4


def sum_buffers(rows, cols, group):
    buf = lambda *lead: pltpu.VMEM((*lead, rows, cols), bf16)
    if not group:
        return [buf(2, 2), buf(2, 1), buf(2, 1), buf(1), buf(1)]
    return [buf(2, 2, 2, 2), buf(2, 4), buf(2, 4), buf(4), buf(4), buf(3), buf(3)]


def block_rows(block, size):
    return pl.ds(pl.multiple_of((block[0] * 2 + block[1]) * size, size), size)


def lane_of(h):
    return h if h < LOCAL_HEADS // 2 else h + HEADS // 2 - LOCAL_HEADS // 2


def own_pair(cols, h):
    lane = lax.broadcasted_iota(jnp.int32, (cols.shape[0], LANES), 1)
    first, second = lane_of(h), lane_of(h + 1)
    return jnp.where(lane < HEADDIM, cols[:, first : first + 1], cols[:, second : second + 1])


def own_sums(values):
    width = values.shape[1]
    head = lax.broadcasted_iota(jnp.int32, (width, LANES), 0) // HEADDIM
    lane = lax.broadcasted_iota(jnp.int32, (width, LANES), 1)
    pick = (jnp.where(head < LOCAL_HEADS // 2, head, head + lane_of(LOCAL_HEADS) - LOCAL_HEADS) == lane).astype(bf16)
    high = values.astype(bf16)
    low = (values - high.astype(f32)).astype(bf16)
    return dot(high, pick) + dot(low, pick)


def head_lanes(values, back=False):
    first = (lax.axis_index("t1") * 2 + lax.axis_index("t0")) * (LOCAL_HEADS // 2)
    return pltpu.roll(values, first if back else LANES - first, 1)


def own_row(first, k):
    tp = lax.axis_index("t1") * 2 + lax.axis_index("t0")
    third = QUARTER // LANES
    return pl.ds(first + (k // third) * (D_INNER // 2 // LANES) + tp * third + k % third, 1)


def own_chans(j):
    return [slice(first + j * QUARTER, first + (j + 1) * QUARTER) for first in (0, D_INNER // 2)]


def forward_kernel(
    spans, hid_ref, inw_ref, outw_ref, cot_ref, valid_ref, small_ref, segc_ref, segr_ref,
    h_ref, xn_ref, win_ref, convp_ref, x_ref, b_ref, c_ref, dsilu_ref, dt_ref, z_ref, cum_ref, y_ref, st_ref,
    wgate_ref, wout_ref, back_ref, normed_ref, mix_ref, dy_ref, dgate_ref, dgain_ref, taps_ref, heads_ref, chans_ref,
    marks_ref, carry_ref,
    wm_ref, wg_ref, wo_ref, cotv_ref, s_ref, pass_ref, got_ref, rim_ref, gated_ref, gate_ref, dn_ref, stat_ref, stats_ref,
    local_sem, send_sem, recv_sem,
):
    p, _, _, _, _ = place()
    rows_all = spans * SPAN
    tokens = hid_ref.shape[0]
    lane = lax.broadcasted_iota(jnp.int32, (1, LANES), 1)

    for j in range(TP):
        at = (j // 2, j % 2)
        for k, chans in enumerate(own_chans(j)):
            wg_ref[(*at, slice(None), slice(k * QUARTER, (k + 1) * QUARTER))] = inw_ref[:, chans].astype(bf16)
            scan = slice(D_INNER + chans.start, D_INNER + chans.stop)
            wm_ref[(*at, slice(None), slice(k * QUARTER, (k + 1) * QUARTER))] = inw_ref[:, scan].astype(bf16)
        wm_ref[(*at, slice(None), slice(HALF, CHANS))] = inw_ref[:, 2 * D_INNER : 2 * D_INNER + SIDE].astype(bf16)
        dt_cols = jnp.concatenate(
            [inw_ref[:, 2 * D_INNER + SIDE :], jnp.zeros((inw_ref.shape[0], LANES - HEADS), f32)], axis=1
        )
        dt_own = (lane % (HEADS // 2) // (LOCAL_HEADS // 2) == j) & (lane < HEADS)
        wm_ref[(*at, slice(None), slice(CHANS, MAIN))] = jnp.where(dt_own, dt_cols, 0.0).astype(bf16)
    wo_ref[...] = outw_ref[...].astype(bf16)
    cotv_ref[...] = (cot_ref[...].astype(f32) * valid_ref[...]).astype(bf16)

    greet([T0, T1, DIAG, CORE, SIDEWAYS, PART])
    copies = Copies(local_sem, send_sem, recv_sem)
    mains = WeightGather(copies, win_ref, wm_ref.shape[2], True)
    mains.swap(wm_ref)
    hids = GroupGather(copies, hid_ref, h_ref)

    for k in range(HALF // LANES):
        lanes = slice(k * LANES, (k + 1) * LANES)
        chans_ref[1:2, lanes] = small_ref[own_row(NORM_ROW, k), :]
        for j in range(CONV + 1):
            taps_ref[j : j + 1, lanes] = small_ref[own_row(TAP_ROW + TAP_ROWS * j, k), :]
    for k in range(SIDE // LANES):
        lanes = slice(HALF + k * LANES, HALF + (k + 1) * LANES)
        for j in range(CONV + 1):
            row = TAP_ROW + TAP_ROWS * j + D_INNER // LANES + k
            taps_ref[j : j + 1, lanes] = small_ref[row : row + 1, :]
    head_row = jnp.broadcast_to(small_ref[HEAD_ROW : HEAD_ROW + 1, :], (TILE, LANES))
    next_row = jnp.broadcast_to(small_ref[HEAD_ROW + 1 : HEAD_ROW + 2, :], (TILE, LANES))
    a_log = pltpu.roll(head_row, LANES - HEADS, 1)
    lane8 = lax.broadcasted_iota(jnp.int32, (TILE, LANES), 1)
    spill = LANES - 2 * HEADS
    skip = jnp.where(lane8 < spill, pltpu.roll(head_row, spill, 1), pltpu.roll(next_row, spill, 1))
    own = lane8 < HEADS
    heads_ref[0:1, :] = head_lanes(jnp.where(own, head_row, 0.0))[0:1]
    heads_ref[1:2, :] = -jnp.exp(head_lanes(jnp.where(own, a_log, 0.0))[0:1])
    skip = head_lanes(jnp.where(own, skip, 0.0))[0:1]
    for q in range(PAIRS):
        chans_ref[0:1, q * LANES : (q + 1) * LANES] = own_pair(skip, 2 * q)

    def mark(c, _):
        rows = span_rows(c)
        seg = segc_ref[pl.ds(pl.multiple_of(c * SPAN, SPAN), SPAN + 2 * FRONT), :]
        here = seg[FRONT : FRONT + SPAN]
        last = seg[FRONT + SPAN - 1 : FRONT + SPAN]
        before = seg[FRONT - 1 : FRONT]
        cols = [seg[FRONT - RIM + k : FRONT - RIM + k + SPAN] == here for k in range(RIM)]
        cols += [seg[FRONT + RIM - k : FRONT + RIM - k + SPAN] == here for k in range(RIM)]
        cols += [here == last, here == before]
        lane_m = lax.broadcasted_iota(jnp.int32, (SPAN, TILE), 1)
        marks = jnp.zeros((SPAN, TILE), f32)
        for k, col in enumerate(cols):
            marks = jnp.where(lane_m == k, jnp.where(col, 1.0, 0.0), marks)
        marks_ref[rows, :] = marks
        carry_ref[pl.ds(c, 1), :] = jnp.broadcast_to(jnp.where(last == before, 1.0, 0.0), (1, LANES))
        return 0

    lax.fori_loop(0, spans, mark, 0)
    blocks = group_blocks()

    def norm(block):
        rows = block_rows(block, tokens)
        hid = h_ref[rows, :].astype(f32)
        scale = lax.rsqrt(jnp.sum(hid * hid, axis=1, keepdims=True) / D + norm_eps)
        for k in range(D // LANES):
            lanes = slice(k * LANES, (k + 1) * LANES)
            xn_ref[rows, lanes] = (h_ref[rows, lanes].astype(f32) * scale * small_ref[k : k + 1, :]).astype(bf16)

    mains.spread_swapped()
    hids.own.wait()
    norm(blocks[0])
    gates = WeightGather(copies, wgate_ref, wg_ref.shape[2], True)
    gates.swap(wg_ref)
    hids.hand_on()
    norm(blocks[2])
    mains.hand_on()
    gates.spread_swapped()
    hids.finish()
    norm(blocks[1])
    norm(blocks[3])
    cots = GroupGather(copies, cotv_ref, back_ref)
    outs = WeightGather(copies, wout_ref, wo_ref.shape[0], False)
    outs.spread(wo_ref, ())
    outs_kept = copies.keep(wo_ref, outs.mine(()))
    mains.finish()
    mains.kept.wait()

    def project(c, _):
        rows = span_rows(c)
        xn = xn_ref[rows, :]
        at = pl.ds(pl.multiple_of(FRONT + c * SPAN, FRONT), SPAN)
        for k in range(CHANS // 256):
            cols = slice(k * 256, (k + 1) * 256)
            convp_ref[at, cols] = dot(xn, win_ref[:, cols]).astype(bf16)
        dt_raw = dot(xn, win_ref[:, CHANS:MAIN]).astype(bf16).astype(f32)
        z = head_lanes(dt_raw) + heads_ref[0:1, :]
        z_ref[rows, :] = z
        small = jnp.exp(-jnp.abs(z))
        one_more = 1.0 + small
        is_one = one_more == 1.0
        log_more = jnp.where(is_one, small, jnp.log(one_more) * small / jnp.where(is_one, 1.0, one_more - 1.0))
        dt_ref[rows, :] = jnp.maximum(z, 0.0) + log_more
        return 0

    lax.fori_loop(0, spans, project, 0)
    rim = copies.send(convp_ref.at[pl.ds(rows_all, FRONT)], rim_ref, PART)
    gates.hand_on()
    s_ref[...] = jnp.zeros_like(s_ref)
    dgain_ref[...] = jnp.zeros_like(dgain_ref)
    rim.wait_recv()
    convp_ref[0:FRONT, :] = jnp.where(p == 1, rim_ref[...].astype(f32), 0.0).astype(bf16)

    def convolve(c, _):
        rows = span_rows(c)
        wide = pl.ds(pl.multiple_of(c * SPAN, SPAN), SPAN + FRONT)
        marks = marks_ref[rows, :]
        for k in range(CHANS // LANES):
            lanes = slice(k * LANES, (k + 1) * LANES)
            values = convp_ref[wide, lanes].astype(f32)
            total = taps_ref[CONV : CONV + 1, lanes] + taps_ref[RIM : RIM + 1, lanes] * values[FRONT:]
            for j in range(RIM):
                first = FRONT - RIM + j
                total = total + taps_ref[j : j + 1, lanes] * values[first : first + SPAN] * marks[:, j : j + 1]
            sig = 1.0 / (1.0 + jnp.exp(-total))
            value = (total * sig).astype(bf16)
            dsilu_ref[rows, lanes] = sig * (1.0 + total * (1.0 - sig))
            if k < HALF // LANES:
                x_ref[rows, lanes] = value
            elif k == HALF // LANES:
                b_ref[rows, :] = value
            else:
                c_ref[rows, :] = value
        return 0

    lax.fori_loop(0, spans, convolve, 0)

    def local_states(c, _):
        rows = span_rows(c)
        dt, cum = span_decay(dt_ref, heads_ref, c, 1)
        cum_ref[rows, :] = cum
        last = cum[SPAN - 1 : SPAN, :]
        end_weight = jnp.exp(last - cum) * dt * marks_ref[rows, 6:7]
        decay = jnp.exp(last) * carry_ref[pl.ds(c, 1), :]
        b = b_ref[rows, :]
        st_ref[c] = s_ref[...]
        for q in range(PAIRS):
            lanes = slice(q * LANES, (q + 1) * LANES)
            xw = (x_ref[rows, lanes].astype(f32) * own_pair(end_weight, 2 * q)).astype(bf16)
            s_ref[:, lanes] = s_ref[:, lanes] * own_pair(decay, 2 * q) + dot(b, xw, ((0,), (0,)))
        return 0

    lax.fori_loop(0, spans, local_states, 0)
    pass_ref[...] = s_ref[...].astype(bf16)
    state = copies.send(pass_ref, got_ref, PART)
    cots.hand_on()

    def inside(c, _):
        rows = span_rows(c)
        cum = cum_ref[rows, :]
        back_log = jnp.transpose(cum - jnp.log(dt_ref[rows, :]))
        scores = dot(c_ref[rows, :], b_ref[rows, :], ((1,), (1,)))
        row = lax.broadcasted_iota(jnp.int32, (SPAN, SPAN), 0)
        col = lax.broadcasted_iota(jnp.int32, (SPAN, SPAN), 1)
        mask = (row >= col) & (segc_ref[pl.ds(pl.multiple_of(FRONT + c * SPAN, FRONT), SPAN), :] == segr_ref[pl.ds(c, 1), :])
        lane = lax.broadcasted_iota(jnp.int32, (SPAN, LANES), 1)
        for q in range(PAIRS):
            lanes = slice(q * LANES, (q + 1) * LANES)
            x = x_ref[rows, lanes]
            parts = []
            for h in (lane_of(2 * q), lane_of(2 * q + 1)):
                gap = cum[:, h : h + 1] - back_log[h : h + 1, :]
                weighted = scores * jnp.exp(jnp.where(mask, gap, -1e30))
                parts.append(dot(weighted.astype(bf16), x))
            y_ref[rows, lanes] = jnp.where(lane < HEADDIM, parts[0], parts[1])
        return 0

    lax.fori_loop(0, spans, inside, 0)
    outs.hand_on()
    state.wait_recv()
    s_ref[...] = got_ref[...].astype(f32) * p.astype(f32)

    def across_spans(c, _):
        rows = span_rows(c)
        cum = cum_ref[rows, :]
        decay = jnp.exp(cum[SPAN - 1 : SPAN, :]) * carry_ref[pl.ds(c, 1), :]
        gain = jnp.exp(cum) * marks_ref[rows, 7:8]
        cc = c_ref[rows, :]
        for q in range(PAIRS):
            lanes = slice(q * LANES, (q + 1) * LANES)
            entering = s_ref[:, lanes]
            full = st_ref[c, :, lanes] + entering
            st_ref[c, :, lanes] = full
            y_ref[rows, lanes] += dot(cc, full.astype(bf16)) * own_pair(gain, 2 * q)
            s_ref[:, lanes] = entering * own_pair(decay, 2 * q)
        return 0

    lax.fori_loop(0, spans, across_spans, 0)
    gates.finish()
    gates.kept.wait()

    def put_stat(k, c, column):
        wide = jnp.transpose(jnp.broadcast_to(column, (SPAN, LANES)))
        stat_ref[k, :, span_rows(c)] = wide[0:TILE, :]

    def exchange(k):
        return [copies.send(stat_ref.at[k], stats_ref.at[k, i], flips) for i, flips in enumerate(HOPS[1:])]

    def get_stat(k, c):
        cols = span_rows(c)
        total = stat_ref[k, :, cols] + stats_ref[k, 0, :, cols] + stats_ref[k, 1, :, cols] + stats_ref[k, 2, :, cols]
        return jnp.transpose(jnp.broadcast_to(total[0:1, :], (LANES, SPAN)))[:, 0:1] / D_INNER

    def values(rows, lanes):
        y_b = (y_ref[rows, lanes] + chans_ref[0:1, lanes] * x_ref[rows, lanes].astype(f32)).astype(bf16).astype(f32)
        gate = gate_ref[rows, lanes]
        sig = 1.0 / (1.0 + jnp.exp(-gate))
        return y_b, gate, sig

    def gating(c, _):
        rows = span_rows(c)
        xn = xn_ref[rows, :]
        total = jnp.zeros((SPAN, 1), f32)
        for k in range(HALF // 256):
            lanes = slice(k * 256, (k + 1) * 256)
            gate_ref[rows, lanes] = dot(xn, wgate_ref[:, lanes])
            y_b, gate, sig = values(rows, lanes)
            gated = y_b * (gate * sig)
            gated_ref[rows, lanes] = gated
            total = total + jnp.sum(gated * gated, axis=1, keepdims=True)
        put_stat(0, c, total)
        return 0

    lax.fori_loop(0, spans, gating, 0)
    squares = exchange(0)
    cots.finish()
    cots.own.wait()
    outs.finish()
    outs_kept.wait()

    def pull_out(c, _):
        rows = span_rows(c)
        back = back_ref[rows, :]
        total = jnp.zeros((SPAN, 1), f32)
        for k in range(HALF // 256):
            lanes = slice(k * 256, (k + 1) * 256)
            d_normed = dot(back, wout_ref[lanes, :], ((1,), (1,)))
            dn_ref[rows, lanes] = d_normed
            total = total + jnp.sum(gated_ref[rows, lanes] * (d_normed * chans_ref[1:2, lanes]), axis=1, keepdims=True)
        put_stat(1, c, total)
        return 0

    lax.fori_loop(0, spans, pull_out, 0)
    dots = exchange(1)
    for copy in squares:
        copy.wait_recv()

    def push_out(c, _):
        rows = span_rows(c)
        scale = lax.rsqrt(get_stat(0, c) + norm_eps)
        for k in range(HALF // 256):
            lanes = slice(k * 256, (k + 1) * 256)
            scaled = gated_ref[rows, lanes] * scale
            normed_ref[rows, lanes] = (scaled * chans_ref[1:2, lanes]).astype(bf16)
            dgain_ref[0:1, lanes] += jnp.sum(scaled * dn_ref[rows, lanes], axis=0, keepdims=True)
        normed = normed_ref[rows, :]
        for k in range(D // 256):
            cols = slice(k * 256, (k + 1) * 256)
            mix_ref[rows, cols] = dot(normed, wout_ref[:, cols]).astype(bf16)
        return 0

    lax.fori_loop(0, spans, push_out, 0)
    for copy in dots:
        copy.wait_recv()

    def back_gate(c, _):
        rows = span_rows(c)
        scale = lax.rsqrt(get_stat(0, c) + norm_eps)
        pulled = get_stat(1, c) * (scale * scale * scale)
        for k in range(HALF // LANES):
            lanes = slice(k * LANES, (k + 1) * LANES)
            y_b, gate, sig = values(rows, lanes)
            d_gated = scale * (dn_ref[rows, lanes] * chans_ref[1:2, lanes]) - gated_ref[rows, lanes] * pulled
            dy_ref[rows, lanes] = (d_gated * (gate * sig)).astype(bf16)
            dgate_ref[rows, lanes] = (d_gated * y_b * (sig * (1.0 + gate * (1.0 - sig)))).astype(bf16)
        return 0

    lax.fori_loop(0, spans, back_gate, 0)
    copies.finish()


def backward_kernel(
    spans, x_ref, b_ref, c_ref, dt_ref, z_ref, heads_ref, chans_ref, marks_ref, segc_ref, segr_ref, carry_ref,
    y_ref, st_ref, cum_ref, dy_ref, dsilu_ref, convp_ref, taps_ref, normed_ref, back_ref, xn_ref, dgate_ref, mix_ref,
    dmain_ref, hsum_ref, dtaps_ref, mixer_ref, gout_ref, ggate_ref,
    ds_ref, dsl_ref, dyg_ref, dxi_ref, prod_ref, pass_ref, got_ref, dtot_ref, rims_ref, rimr_ref, db_ref, dc_ref,
    dskip_ref, go_ref, gg_ref, *rest,
):
    go_bufs, gg_bufs, mix_bufs, (local_sem, send_sem, recv_sem) = rest[:5], rest[5:12], rest[12:16], rest[16:]
    p, t1, t0, w1, w0 = place()
    greet([T0, T1, DIAG, CORE, SIDEWAYS, PART])
    copies = Copies(local_sem, send_sem, recv_sem)
    mixes = GroupScatter(copies, mix_ref, mix_bufs)
    mixes.to_t0(3)
    mixes.to_t0(1)
    ds_ref[...] = jnp.zeros_like(ds_ref)
    hsum_ref[...] = jnp.zeros_like(hsum_ref)
    dskip_ref[...] = jnp.zeros_like(dskip_ref)
    dtaps_ref[...] = jnp.zeros_like(dtaps_ref)

    def local_states(step, _):
        c = spans - 1 - step
        rows = span_rows(c)
        cum = cum_ref[rows, :]
        decay = jnp.exp(cum[SPAN - 1 : SPAN, :]) * carry_ref[pl.ds(c, 1), :]
        gain = jnp.exp(cum) * marks_ref[rows, 7:8]
        cc = c_ref[rows, :]
        for q in range(PAIRS):
            lanes = slice(q * LANES, (q + 1) * LANES)
            dyg = (dy_ref[rows, lanes].astype(f32) * own_pair(gain, 2 * q)).astype(bf16)
            dyg_ref[rows, lanes] = dyg
            ds = ds_ref[:, lanes]
            dsl_ref[c, :, lanes] = ds
            ds_ref[:, lanes] = ds * own_pair(decay, 2 * q) + dot(cc, dyg, ((0,), (0,)))
        return 0

    lax.fori_loop(0, spans, local_states, 0)
    pass_ref[...] = ds_ref[...].astype(bf16)
    state = copies.send(pass_ref, got_ref, PART)

    out_rows = go_ref.shape[3]
    for q in range(2):
        normed = normed_ref[:, q * HALF // 2 : (q + 1) * HALF // 2]
        for k in range(D // 512):
            cols = slice(k * 512, (k + 1) * 512)
            part = dot(normed, back_ref[:, cols], ((0,), (0,))).astype(bf16)
            go_ref[q, :, :, :, cols] = part.reshape(2, 2, out_rows, 512)
    g_out = GradientSum(copies, go_ref, go_bufs, False)
    g_out.cores()

    own_rows = gg_ref.shape[5]
    width = TP // 2 * 4 * own_rows
    for i in range(4):
        xn = xn_ref[:, i * width : (i + 1) * width]
        part = dot(xn, dgate_ref[...], ((0,), (0,))).astype(bf16)
        gg_ref[i // 2, i % 2] = part.reshape(2, 2, 2, own_rows, HALF)
    g_gate = GradientSum(copies, gg_ref, gg_bufs, True)
    g_gate.cores()
    g_out.to_sides()

    def inside(c, _):
        rows = span_rows(c)
        cum = cum_ref[rows, :]
        fore_log = jnp.transpose(cum)
        back_log = cum - jnp.log(dt_ref[rows, :])
        b = b_ref[rows, :]
        cc = c_ref[rows, :]
        scores = dot(b, cc, ((1,), (1,)))
        row = lax.broadcasted_iota(jnp.int32, (SPAN, SPAN), 0)
        col = lax.broadcasted_iota(jnp.int32, (SPAN, SPAN), 1)
        mask = (col >= row) & (segc_ref[rows, :] == segr_ref[pl.ds(c, 1), :])
        lane = lax.broadcasted_iota(jnp.int32, (SPAN, LANES), 1)
        d_scores = jnp.zeros((SPAN, SPAN), f32)
        dc = jnp.zeros((SPAN, STATE), f32)
        for q in range(PAIRS):
            lanes = slice(q * LANES, (q + 1) * LANES)
            x = x_ref[rows, lanes]
            dy = dy_ref[rows, lanes]
            xf = x.astype(f32)
            parts = []
            for k in range(2):
                h = lane_of(2 * q + k)
                gap = fore_log[h : h + 1, :] - back_log[:, h : h + 1]
                decay_mat = jnp.exp(jnp.where(mask, gap, -1e30))
                parts.append(dot((scores * decay_mat).astype(bf16), dy))
                own = (lane < HEADDIM) if k == 0 else (lane >= HEADDIM)
                d_weights = dot(jnp.where(own, xf, 0.0).astype(bf16), dy, ((1,), (1,)))
                d_scores = d_scores + d_weights * decay_mat
            dxi_ref[rows, lanes] = jnp.where(lane < HEADDIM, parts[0], parts[1])
            dc = dc + dot(dyg_ref[rows, lanes], st_ref[c, :, lanes].astype(bf16), ((1,), (1,)))
            dskip_ref[0:1, lanes] += jnp.sum(dy.astype(f32) * xf, axis=0, keepdims=True)
        d_scores_b = d_scores.astype(bf16)
        db_ref[rows, :] = dot(d_scores_b, cc)
        dc_ref[rows, :] = dc + dot(d_scores_b, b, ((0,), (0,)))
        return 0

    lax.fori_loop(0, spans, inside, 0)
    mixes.to_t1()
    g_gate.to_sides()
    g_out.to_part()
    state.wait_recv()
    ds_ref[...] = got_ref[...].astype(f32) * (1 - p).astype(f32)

    def across_spans(step, _):
        c = spans - 1 - step
        rows = span_rows(c)
        dt = dt_ref[rows, :]
        cum = cum_ref[rows, :]
        last = cum[SPAN - 1 : SPAN, :]
        end_weight = jnp.exp(last - cum) * dt * marks_ref[rows, 6:7]
        decay = jnp.exp(last) * carry_ref[pl.ds(c, 1), :]
        b = b_ref[rows, :]
        db = db_ref[rows, :]
        edges = []
        for q in range(PAIRS):
            lanes = slice(q * LANES, (q + 1) * LANES)
            xf = x_ref[rows, lanes].astype(f32)
            dyf = dy_ref[rows, lanes].astype(f32)
            ew = own_pair(end_weight, 2 * q)
            dec = own_pair(decay, 2 * q)
            entering = ds_ref[:, lanes]
            ds = dsl_ref[c, :, lanes] + entering
            ds_ref[:, lanes] = entering * dec
            ds_b = ds.astype(bf16)
            db = db + dot((xf * ew).astype(bf16), ds_b, ((1,), (1,)))
            dx_state = dot(b, ds_b) * ew
            dx = dxi_ref[rows, lanes] + dx_state
            edges.append(
                jnp.sum(ds * st_ref[c, :, lanes], axis=0, keepdims=True) * dec
                + jnp.sum(dx_state * xf, axis=0, keepdims=True)
            )
            prod_ref[0:SPAN, lanes] = dyf * y_ref[rows, lanes]
            prod_ref[SPAN : 2 * SPAN, lanes] = xf * dx
            d_x = (dx + dyf * chans_ref[0:1, lanes]).astype(bf16).astype(f32)
            dtot_ref[rows, lanes] = d_x * dsilu_ref[rows, lanes]
        dtot_ref[rows, HALF : HALF + STATE] = db * dsilu_ref[rows, HALF : HALF + STATE]
        dtot_ref[rows, HALF + STATE :] = dc_ref[rows, :] * dsilu_ref[rows, HALF + STATE :]
        sums = own_sums(prod_ref[...])
        out_sum, in_sum = sums[:SPAN], sums[SPAN:]
        edge_sum = own_sums(jnp.broadcast_to(jnp.concatenate(edges, axis=1), (TILE, HALF)))[0:1]
        at_last = lax.broadcasted_iota(jnp.int32, (SPAN, LANES), 0) == SPAN - 1
        d_cum = out_sum - in_sum + jnp.where(at_last, edge_sum, 0.0)
        row = lax.broadcasted_iota(jnp.int32, (SPAN, SPAN), 0)
        col = lax.broadcasted_iota(jnp.int32, (SPAN, SPAN), 1)
        d_log = dot((col >= row).astype(f32), d_cum, precision=exact_prec)
        z = z_ref[rows, :]
        small = jnp.exp(-jnp.abs(z))
        sig = jnp.where(z >= 0.0, 1.0, small) / (1.0 + small)
        ratio = jnp.where(dt > 1e-30, sig / jnp.maximum(dt, 1e-30), 1.0)
        d_dt = d_log * heads_ref[1:2, :] * sig + in_sum * ratio
        hsum_ref[0:1, :] += jnp.sum(d_log * dt, axis=0, keepdims=True)
        hsum_ref[1:2, :] += jnp.sum(d_dt, axis=0, keepdims=True)
        dmain_ref[rows, CHANS:MAIN] = head_lanes(d_dt, back=True).astype(bf16)
        return 0

    lax.fori_loop(0, spans, across_spans, 0)
    rims_ref[...] = dtot_ref[0:TILE, :]
    rim = copies.send(rims_ref, rimr_ref, PART)
    g_gate.to_part()
    rim.wait_recv()
    dtot_ref[pl.ds(spans * SPAN, TILE), :] = jnp.where(p == 0, rimr_ref[...], 0.0)

    def convolve(c, _):
        rows = span_rows(c)
        marks = marks_ref[rows, :]
        fore = pl.ds(pl.multiple_of(c * SPAN, SPAN), SPAN + FRONT)
        hind = pl.ds(pl.multiple_of(c * SPAN, SPAN), SPAN + TILE)
        for k in range(CHANS // LANES):
            lanes = slice(k * LANES, (k + 1) * LANES)
            later = dtot_ref[hind, lanes]
            earlier = convp_ref[fore, lanes].astype(f32)
            own = later[0:SPAN]
            d_conv = taps_ref[RIM : RIM + 1, lanes] * own
            dtaps_ref[RIM : RIM + 1, lanes] += jnp.sum(own * earlier[FRONT:], axis=0, keepdims=True)
            dtaps_ref[CONV : CONV + 1, lanes] += jnp.sum(own, axis=0, keepdims=True)
            for j in range(RIM):
                ahead = RIM - j
                d_conv = d_conv + taps_ref[j : j + 1, lanes] * later[ahead : ahead + SPAN] * marks[:, 3 + j : 4 + j]
                first = FRONT - ahead
                dtaps_ref[j : j + 1, lanes] += jnp.sum(
                    own * earlier[first : first + SPAN] * marks[:, j : j + 1], axis=0, keepdims=True
                )
            dmain_ref[rows, lanes] = d_conv.astype(bf16)
        return 0

    lax.fori_loop(0, spans, convolve, 0)
    gout_ref[...] = g_out.total(0)
    g_gate.to_group(ggate_ref)
    g_gate.finish(ggate_ref)
    mixer_ref[...] = mix_ref[mixes.block(0), :].astype(f32) + mixes.finish()
    skips = own_sums(dskip_ref[...])
    hsum_ref[0:1, :] = hsum_ref[0:1, :] * heads_ref[1:2, :]
    hsum_ref[2:3, :] = skips[0:1, :]
    hsum_ref[...] = head_lanes(hsum_ref[...], back=True)
    copies.finish()


def end_kernel(
    dmain_ref, dgate_ref, win_ref, wgate_ref, xn_ref, h_ref, pre_ref, dgain_ref, dtaps_ref, hsum_ref,
    mixer_ref, back_ref, valid_ref, ggate_ref, gout_ref,
    inw_ref, inm_ref, inv_ref, outw_ref, outm_ref, outv_ref, small_ref, smallm_ref, smallv_ref,
    output_ref, gh_ref, inm_out, inv_out, inw_out, outm_out, outv_out, outw_out, smallm_out, smallv_out, smallw_out, rms_ref,
    dxp_ref, dxo_ref, dpre_ref, gm_ref, gmo_ref, box_ref, boxes_ref, *rest,
):
    gm_bufs, dx_bufs, (local_sem, send_sem, recv_sem) = rest[:7], rest[7:11], rest[11:]
    p, t1, t0, w1, w0 = place()
    greet([T0, T1, DIAG, CORE, SIDEWAYS, SIDE_CORE, PART])
    copies = Copies(local_sem, send_sem, recv_sem)
    blocks = group_blocks()
    tokens = mixer_ref.shape[0]
    own_rows = gm_ref.shape[5]
    width = 2 * 4 * own_rows

    def grad_piece(q, r):
        first = pl.multiple_of((q * 2 + r) * width, width)
        for k in range(MAIN // 384):
            cols = slice(k * 384, (k + 1) * 384)
            part = dot(xn_ref[:, pl.ds(first, width)], dmain_ref[:, cols], ((0,), (0,))).astype(bf16)
            gm_ref[q, r, :, :, :, :, cols] = part.reshape(2, 2, 2, own_rows, 384)

    lax.fori_loop(0, 4, lambda i, _: (grad_piece(i // 2, i % 2), 0)[1], 0)
    g_main = GradientSum(copies, gm_ref, gm_bufs, True)
    g_main.cores()
    dpre_ref[...] = jnp.zeros_like(dpre_ref)

    def token_grad(block, keep):
        rows = block_rows(block, tokens)
        d_main = dmain_ref[rows, :]
        d_gate = dgate_ref[rows, :]
        hid = h_ref[rows, :].astype(f32)
        scale = lax.rsqrt(jnp.sum(hid * hid, axis=1, keepdims=True) / D + norm_eps)
        for k in range(D // 512):
            cols = slice(k * 512, (k + 1) * 512)
            part = dot(d_main, win_ref[cols, :], ((1,), (1,))) + dot(d_gate, wgate_ref[cols, :], ((1,), (1,)))
            dpre_ref[0:1, cols] += jnp.sum(h_ref[rows, cols].astype(f32) * scale * part, axis=0, keepdims=True)
            if keep:
                dxo_ref[:, cols] = part
            else:
                dxp_ref[rows, cols] = part.astype(bf16)

    dxs = GroupScatter(copies, dxp_ref, dx_bufs)
    token_grad(blocks[3], False)
    dxs.to_t0(3)
    g_main.to_sides()
    token_grad(blocks[1], False)
    dxs.to_t0(1)
    token_grad(blocks[2], False)
    token_grad(blocks[0], True)

    own = block_rows(blocks[0], tokens)
    hid = h_ref[own, :].astype(f32)
    mixer = mixer_ref[...]
    output_ref[...] = (hid + mixer).astype(bf16)
    valid = valid_ref[...]
    counts = [jnp.sum(valid * jnp.sum(v * v, axis=1, keepdims=True), axis=0, keepdims=True) for v in (hid, mixer)]
    counts.append(jnp.sum(valid, axis=0, keepdims=True))

    box = box_ref.at[0]
    box[...] = jnp.zeros_like(box)
    lane = lax.broadcasted_iota(jnp.int32, (1, LANES), 1)
    for k in range(D // LANES):
        box[k : k + 1, :] = dpre_ref[0:1, k * LANES : (k + 1) * LANES]
    for k in range(HALF // LANES):
        lanes = slice(k * LANES, (k + 1) * LANES)
        box[own_row(NORM_ROW, k), :] = dgain_ref[0:1, lanes]
        for j in range(CONV + 1):
            box[own_row(TAP_ROW + TAP_ROWS * j, k), :] = dtaps_ref[j : j + 1, lanes]
    for k in range(SIDE // LANES):
        lanes = slice(HALF + k * LANES, HALF + (k + 1) * LANES)
        for j in range(CONV + 1):
            row = TAP_ROW + TAP_ROWS * j + D_INNER // LANES + k
            box[row : row + 1, :] = dtaps_ref[j : j + 1, lanes]
    lane8 = lax.broadcasted_iota(jnp.int32, (TILE, LANES), 1)
    sums = jnp.where(lane8 < HEADS, hsum_ref[...], 0.0)
    d_rate, d_shift, d_skip = (jnp.broadcast_to(sums[k : k + 1], (TILE, LANES)) for k in range(3))
    spill = LANES - 2 * HEADS
    joined = d_shift + pltpu.roll(d_rate, HEADS, 1) + jnp.where(lane8 >= 2 * HEADS, pltpu.roll(d_skip, 2 * HEADS, 1), 0.0)
    box[HEAD_ROW : HEAD_ROW + 1, :] = joined[0:1]
    box[HEAD_ROW + 1 : HEAD_ROW + 2, :] = jnp.where(lane8 < HEADS - spill, pltpu.roll(d_skip, LANES - spill, 1), 0.0)[0:1]
    scalars = jnp.zeros((1, LANES), f32)
    for k in range(3):
        scalars = jnp.where(lane == k, counts[k], scalars)
    box[SMALL_ROWS : SMALL_ROWS + 1, :] = scalars

    def small_step(k, hops):
        return [copies.send(box_ref.at[k], boxes_ref.at[k, i], flips) for i, flips in enumerate(hops)]

    def small_add(k, sent):
        total = box_ref[k]
        for i, copy in enumerate(sent):
            copy.wait_recv()
            total = total + boxes_ref[k, i]
        box_ref[k + 1] = total

    def update(refs, outs, rows, cols, grad):
        moment_new, second_new, weight_new = adamw(
            refs[0][rows, cols], refs[1][rows, cols], refs[2][rows, cols], grad, 0.02, 0.1
        )
        outs[0][rows, cols] = moment_new
        outs[1][rows, cols] = second_new
        outs[2][rows, cols] = weight_new

    in_refs, in_outs = (inw_ref, inm_ref, inv_ref), (inm_out, inv_out, inw_out)
    every = slice(None)
    small = small_step(0, (CORE, SIDEWAYS, SIDE_CORE))
    dxs.to_t1()
    g_main.to_part()
    small_add(0, small)
    small = small_step(1, (T0, T1, DIAG))
    update((outw_ref, outm_ref, outv_ref), (outm_out, outv_out, outw_out), every, every, gout_ref[...])
    for j in range(TP):
        for k, chans in enumerate(own_chans(j)):
            update(in_refs, in_outs, every, chans, ggate_ref[j // 2, j % 2, :, k * QUARTER : (k + 1) * QUARTER])
    small_add(1, small)
    small = small_step(2, (PART,))
    g_main.to_group(gmo_ref)
    dx = dxo_ref[...] + dxs.finish()
    scale = lax.rsqrt(jnp.sum(hid * hid, axis=1, keepdims=True) / D + norm_eps)
    d_pre = dx * pre_ref[...]
    pulled = jnp.sum(hid * d_pre, axis=1, keepdims=True) / D * (scale * scale * scale)
    gh_ref[...] = back_ref[own, :].astype(f32) + scale * d_pre - hid * pulled
    small_add(2, small)
    small_rows = slice(0, SMALL_ROWS)
    moment_new, second_new, weight_new = adamw(
        small_ref[...], smallm_ref[...], smallv_ref[...], box_ref[3, small_rows], 0.2, 0.0
    )
    smallm_out[...] = moment_new
    smallv_out[...] = second_new
    smallw_out[...] = weight_new
    totals = box_ref[3, SMALL_ROWS:]
    rms_ref[...] = jnp.sqrt(totals / (totals[0:1, 2:3] * D))
    g_main.finish(gmo_ref)
    for j in range(TP):
        for k, chans in enumerate(own_chans(j)):
            cols = slice(D_INNER + chans.start, D_INNER + chans.stop)
            update(in_refs, in_outs, every, cols, gmo_ref[j // 2, j % 2, :, k * QUARTER : (k + 1) * QUARTER])
    rest_grad = gmo_ref[0, 0, :, HALF:] + gmo_ref[0, 1, :, HALF:] + gmo_ref[1, 0, :, HALF:] + gmo_ref[1, 1, :, HALF:]
    update(in_refs, in_outs, every, slice(2 * D_INNER, 2 * D_INNER + SIDE), rest_grad[:, :SIDE])
    update(in_refs, in_outs, every, slice(2 * D_INNER + SIDE, 2 * D_INNER + SIDE + HEADS), rest_grad[:, SIDE : SIDE + HEADS])
    copies.finish()


def linked(kernel, name, collective_id, in_specs, outs, scratch):
    return pl.pallas_call(
        kernel,
        name=name,
        in_specs=in_specs,
        out_shape=tuple(o for o, _ in outs),
        out_specs=tuple(s for _, s in outs),
        scratch_shapes=scratch,
        compiler_params=pltpu.CompilerParams(
            collective_id=collective_id, has_side_effects=True, vmem_limit_bytes=VMEM_LIMIT
        ),
    )


def shards_linked(
    hidden, cotangent, segments, valid, in_w, in_m, in_v, out_w, out_m, out_v, small_w, small_m, small_v,
):
    part = lax.axis_index("part")
    own_rows, out_rows = in_w.shape[0], out_w.shape[0]
    tok_rows = hidden.shape[1]
    rows = tok_rows * TP
    spans = rows // SPAN
    edge = jnp.full((FRONT,), -1, jnp.int32)
    seg_wide = lax.dynamic_slice_in_dim(jnp.concatenate([edge, segments[0], edge]), part * rows, rows + 2 * FRONT)
    seg_spans = seg_wide[FRONT : FRONT + rows].reshape(spans, SPAN)
    valid_col = valid[0].astype(f32)[:, None]
    small_size = small_w.shape[0]

    def small_box(array):
        return jnp.pad(array, (0, SMALL_ROWS * LANES - small_size)).reshape(SMALL_ROWS, LANES)

    small_w, small_m, small_v = small_box(small_w), small_box(small_m), small_box(small_v)
    pre_row = small_w[:NORM_ROW].reshape(1, D)

    half = lambda dtype: shape((rows, HALF), dtype)
    wide = shape((rows, D), bf16)
    lanes = shape((rows, LANES), f32)
    side = shape((rows, STATE), bf16)
    state_buf = pltpu.VMEM((STATE, HALF), f32)
    state_half = pltpu.VMEM((STATE, HALF), bf16)
    half_buf = pltpu.VMEM((rows, HALF), f32)
    forward_outs = (
        wide,
        wide,
        shape((D, MAIN), bf16),
        shape((rows + FRONT, CHANS), bf16),
        half(bf16),
        side,
        side,
        shape((rows, CHANS), f32),
        lanes,
        lanes,
        lanes,
        half(f32),
        shape((spans, STATE, HALF), f32),
        shape((D, HALF), bf16),
        shape((HALF, D), bf16),
        wide,
        half(bf16),
        wide,
        half(bf16),
        half(bf16),
        shape((TILE, HALF), f32),
        shape((TILE, CHANS), f32),
        shape((TILE, LANES), f32),
        shape((TILE, HALF), f32),
        shape((rows, TILE), f32),
        shape((spans, LANES), f32),
    )
    (
        hidden_all, x_normed, w_in, conv_pad, x_scan, b_mat, c_mat, dsilu, dt, z, cum, y_scan, states, w_gate, w_out, back_all,
        normed, mix, dy, d_gate, d_gain, taps, head_rows, chans, marks, carry,
    ) = linked(
        functools.partial(forward_kernel, spans), "forward", 1, [VMEM] * 8, [(o, VMEM) for o in forward_outs],
        [
            pltpu.VMEM((2, 2, own_rows, MAIN), bf16),
            pltpu.VMEM((2, 2, own_rows, HALF), bf16),
            pltpu.VMEM((out_rows, D), bf16),
            pltpu.VMEM((tok_rows, D), bf16),
            state_buf,
            state_half,
            state_half,
            pltpu.VMEM((FRONT, CHANS), bf16),
            half_buf,
            half_buf,
            half_buf,
            pltpu.VMEM((2, TILE, rows), f32),
            pltpu.VMEM((2, 3, TILE, rows), f32),
            *sems(120, 6),
        ],
    )(hidden[0], in_w, out_w, cotangent[0], valid_col, small_w, seg_wide[:, None], seg_spans)

    d_main, h_sums, d_taps, mixer, g_out, g_gate = linked(
        functools.partial(backward_kernel, spans), "backward", 2, [VMEM] * 23,
        [
            (o, VMEM)
            for o in (
                shape((rows, MAIN), bf16),
                shape((TILE, LANES), f32),
                shape((TILE, CHANS), f32),
                shape((tok_rows, D), f32),
                shape((out_rows, D), f32),
                shape((2, 2, own_rows, HALF), f32),
            )
        ],
        [
            state_buf,
            pltpu.VMEM((spans, STATE, HALF), f32),
            pltpu.VMEM((rows, HALF), bf16),
            half_buf,
            pltpu.VMEM((2 * SPAN, HALF), f32),
            state_half,
            state_half,
            pltpu.VMEM((rows + FRONT, CHANS), f32),
            pltpu.VMEM((TILE, CHANS), f32),
            pltpu.VMEM((TILE, CHANS), f32),
            pltpu.VMEM((rows, STATE), f32),
            pltpu.VMEM((rows, STATE), f32),
            pltpu.VMEM((TILE, HALF), f32),
            pltpu.VMEM((2, 2, 2, out_rows, D), bf16),
            pltpu.VMEM((2, 2, 2, 2, 2, own_rows, HALF), bf16),
            *sum_buffers(out_rows, D, False),
            *sum_buffers(own_rows, HALF, True),
            *scatter_buffers(tok_rows),
            *sems(40, 1),
        ],
    )(
        x_scan, b_mat, c_mat, dt, z, head_rows, chans, marks, seg_wide[FRONT : FRONT + rows, None], seg_spans, carry, y_scan, states,
        cum, dy, dsilu, conv_pad, taps, normed, back_all, x_normed, d_gate, mix,
    )

    small_shape = shape((SMALL_ROWS, LANES), f32)
    (
        output, grad_hidden, in_m_new, in_v_new, in_w_new, out_m_new, out_v_new, out_w_new,
        small_m_new, small_v_new, small_w_new, rms,
    ) = linked(
        end_kernel, "end", 3, [VMEM] * 24,
        [
            (o, VMEM)
            for o in (
                shape((tok_rows, D), bf16),
                shape((tok_rows, D), f32),
                *[shape(in_w.shape, f32)] * 3,
                *[shape(out_w.shape, f32)] * 3,
                *[small_shape] * 3,
                shape((TILE, LANES), f32),
            )
        ],
        [
            pltpu.VMEM((rows, D), bf16),
            pltpu.VMEM((tok_rows, D), f32),
            pltpu.VMEM((TILE, D), f32),
            pltpu.VMEM((2, 2, 2, 2, 2, own_rows, MAIN), bf16),
            pltpu.VMEM((2, 2, own_rows, MAIN), f32),
            pltpu.VMEM((4, BOX_ROWS, LANES), f32),
            pltpu.VMEM((3, 3, BOX_ROWS, LANES), f32),
            *sum_buffers(own_rows, MAIN, True),
            *scatter_buffers(tok_rows),
            *sems(40, 1),
        ],
    )(
        d_main, d_gate, w_in, w_gate, x_normed, hidden_all, pre_row, d_gain, d_taps, h_sums, mixer, back_all, valid_col, g_gate, g_out,
        in_w, in_m, in_v, out_w, out_m, out_v, small_w, small_m, small_v,
    )
    small_m_new, small_v_new, small_w_new = (
        array.reshape(-1)[:small_size] for array in (small_m_new, small_v_new, small_w_new)
    )
    return (
        output[None], grad_hidden[None], in_m_new, in_v_new, in_w_new, out_m_new, out_v_new, out_w_new,
        small_m_new, small_v_new, small_w_new, rms[0, :2],
    )


def solution(mesh):
    seq, wt = mesh.shape["seq"], mesh.shape["wt"]
    split = Mesh(mesh.devices.reshape(seq // TP, 2, 2, wt // 2, 2), EVERYONE)
    streams = ("w1", "w0")
    tokens = ("part", "t1", "t0")
    matrix = P(EVERYONE, None)
    stream = P(streams, tokens, None)
    size = mesh.devices.size
    fits = seq == 2 * TP and wt == 4 and D // size % 16 == 0 and D_INNER // size % 16 == 0
    return jax.shard_map(
        shards_linked if fits else shards_general,
        mesh=split,
        in_specs=(
            stream, stream, P(streams, None), P(streams, tokens), matrix, matrix, matrix, matrix, matrix, matrix, P(), P(), P(),
        ),
        out_specs=(stream, stream, matrix, matrix, matrix, matrix, matrix, matrix, P(), P(), P(), P()),
        check_vma=False,
    )
```

```python
import functools

import jax
import jax.numpy as jnp
from jax import lax
from jax.experimental import pallas as pl
from jax.experimental.pallas import tpu as pltpu
from jax.sharding import Mesh
from jax.sharding import PartitionSpec as P

D = 1536
D_INNER = 3072
HEADS = 48
HEADDIM = 64
STATE = 128
CONV = 4
SPAN = 256
STEP = 4
CONVCH = 3328
TP = 4
RIM = CONV - 1
LANES = 128
HALF = D_INNER // TP
LOCAL_HEADS = HEADS // TP
PAIRS = LOCAL_HEADS // 2
SIDE = 2 * STATE
COL_SIDE = HALF
COL_DT = HALF + SIDE
COL_GATE = COL_DT + LANES
COLS = COL_GATE + HALF

bf16 = jnp.bfloat16
f32 = jnp.float32
exact_prec = lax.Precision.HIGHEST
norm_eps = 1e-05
adam_eps = 1e-08


def dot(a, b, dims=((1,), (0,)), precision=None):
    return lax.dot_general(a, b, (dims, ((), ())), precision=precision, preferred_element_type=f32)


def unpack_small(small):
    first = D
    second = first + D_INNER
    third = second + CONV * CONVCH
    fourth = third + CONVCH
    fifth = fourth + HEADS
    sixth = fifth + HEADS
    return (
        small[:first],
        small[first:second],
        small[second:third].reshape(CONV, CONVCH),
        small[third:fourth],
        small[fourth:fifth],
        small[fifth:sixth],
        small[sixth:],
    )


def adamw(weight, moment, second, grad, rate, decay):
    moment_new = 0.5 * moment + 0.5 * grad
    second_new = 0.5 * second + 0.5 * grad * grad
    first_hat = moment_new / (1.0 - 0.5**STEP)
    second_hat = second_new / (1.0 - 0.5**STEP)
    weight_new = weight - rate * (first_hat / (jnp.sqrt(second_hat) + adam_eps) + decay * weight)
    return (moment_new, second_new, weight_new)


def pair_cols(cols, h):
    lane = lax.broadcasted_iota(jnp.int32, (cols.shape[0], LANES), 1)
    return jnp.where(lane < HEADDIM, cols[:, h : h + 1], cols[:, h + 1 : h + 2])


def span_rows(c):
    return pl.ds(pl.multiple_of(c * SPAN, SPAN), SPAN)


def span_decay(dt_ref, rate_ref, c, at=0):
    dt = dt_ref[span_rows(c), :]
    row = lax.broadcasted_iota(jnp.int32, (SPAN, SPAN), 0)
    col = lax.broadcasted_iota(jnp.int32, (SPAN, SPAN), 1)
    lower = (row >= col).astype(f32)
    return dt, dot(lower, dt * rate_ref[at : at + 1, :], precision=exact_prec)


def state_kernel(spans, x_ref, b_ref, dt_ref, rate_ref, keep_ref, carry_ref, s_ref, dec_ref):
    s_ref[...] = jnp.zeros_like(s_ref)
    dec_ref[...] = jnp.ones_like(dec_ref)

    def body(c, _):
        rows = span_rows(c)
        dt, cum = span_decay(dt_ref, rate_ref, c)
        last = cum[SPAN - 1 : SPAN, :]
        end_weight = jnp.exp(last - cum) * dt * keep_ref[rows, :]
        decay = jnp.exp(last) * carry_ref[pl.ds(c, 1), :]
        dec_ref[...] = dec_ref[...] * decay
        b = b_ref[rows, :]
        for p in range(PAIRS):
            lanes = slice(p * LANES, (p + 1) * LANES)
            xw = (x_ref[rows, lanes].astype(f32) * pair_cols(end_weight, 2 * p)).astype(bf16)
            fresh = dot(b, xw, ((0,), (0,)))
            s_ref[:, lanes] = s_ref[:, lanes] * pair_cols(decay, 2 * p) + fresh
        return 0

    lax.fori_loop(0, spans, body, 0)


def scan_kernel(
    spans, x_ref, b_ref, c_ref, dt_ref, rate_ref, segc_ref, segr_ref, keep_ref, inflow_ref, carry_ref, s_in_ref,
    y_ref, st_ref, s_ref,
):
    s_ref[...] = s_in_ref[...]

    def body(c, _):
        rows = span_rows(c)
        dt, cum = span_decay(dt_ref, rate_ref, c)
        last = cum[SPAN - 1 : SPAN, :]
        end_weight = jnp.exp(last - cum) * dt * keep_ref[rows, :]
        decay = jnp.exp(last) * carry_ref[pl.ds(c, 1), :]
        gain = jnp.exp(cum) * inflow_ref[rows, :]
        back_log = jnp.transpose(cum - jnp.log(dt))
        b = b_ref[rows, :]
        cc = c_ref[rows, :]
        scores = dot(cc, b, ((1,), (1,)))
        row = lax.broadcasted_iota(jnp.int32, (SPAN, SPAN), 0)
        col = lax.broadcasted_iota(jnp.int32, (SPAN, SPAN), 1)
        mask = (row >= col) & (segc_ref[rows, :] == segr_ref[pl.ds(c, 1), :])
        lane = lax.broadcasted_iota(jnp.int32, (SPAN, LANES), 1)
        st_ref[c] = s_ref[...]
        for p in range(PAIRS):
            lanes = slice(p * LANES, (p + 1) * LANES)
            x = x_ref[rows, lanes]
            parts = []
            for h in (2 * p, 2 * p + 1):
                gap = cum[:, h : h + 1] - back_log[h : h + 1, :]
                weights = scores * jnp.exp(jnp.where(mask, gap, -1e30))
                parts.append(dot(weights.astype(bf16), x))
            y = jnp.where(lane < HEADDIM, parts[0], parts[1])
            state = s_ref[:, lanes]
            y = y + dot(cc, state.astype(bf16)) * pair_cols(gain, 2 * p)
            y_ref[rows, lanes] = y
            xw = (x.astype(f32) * pair_cols(end_weight, 2 * p)).astype(bf16)
            s_ref[:, lanes] = state * pair_cols(decay, 2 * p) + dot(b, xw, ((0,), (0,)))
        return 0

    lax.fori_loop(0, spans, body, 0)


def state_back_kernel(spans, dy_ref, c_ref, dt_ref, rate_ref, inflow_ref, carry_ref, s_ref):
    s_ref[...] = jnp.zeros_like(s_ref)

    def body(step, _):
        c = spans - 1 - step
        rows = span_rows(c)
        dt, cum = span_decay(dt_ref, rate_ref, c)
        decay = jnp.exp(cum[SPAN - 1 : SPAN, :]) * carry_ref[pl.ds(c, 1), :]
        gain = jnp.exp(cum) * inflow_ref[rows, :]
        cc = c_ref[rows, :]
        for p in range(PAIRS):
            lanes = slice(p * LANES, (p + 1) * LANES)
            dyg = (dy_ref[rows, lanes].astype(f32) * pair_cols(gain, 2 * p)).astype(bf16)
            s_ref[:, lanes] = s_ref[:, lanes] * pair_cols(decay, 2 * p) + dot(cc, dyg, ((0,), (0,)))
        return 0

    lax.fori_loop(0, spans, body, 0)


def head_sums(values):
    width = values.shape[1]
    chan = lax.broadcasted_iota(jnp.int32, (width, LANES), 0)
    head = lax.broadcasted_iota(jnp.int32, (width, LANES), 1)
    pick = (chan // HEADDIM == head).astype(bf16)
    high = values.astype(bf16)
    low = (values - high.astype(f32)).astype(bf16)
    return dot(high, pick) + dot(low, pick)


def scan_back_kernel(
    spans, x_ref, b_ref, c_ref, dt_ref, ratio_ref, sig_ref, rate_ref, segc_ref, segr_ref, keep_ref, inflow_ref, carry_ref, skip_ref,
    y_ref, st_ref, dy_ref, ds_out_ref,
    dx_ref, db_ref, dc_ref, ddt_ref, drate_ref, dskip_ref,
    ds_ref, prod_ref,
):
    ds_ref[...] = ds_out_ref[...]
    drate_ref[...] = jnp.zeros_like(drate_ref)
    dskip_ref[...] = jnp.zeros_like(dskip_ref)

    def body(step, _):
        c = spans - 1 - step
        rows = span_rows(c)
        dt, cum = span_decay(dt_ref, rate_ref, c)
        last = cum[SPAN - 1 : SPAN, :]
        end_weight = jnp.exp(last - cum) * dt * keep_ref[rows, :]
        decay = jnp.exp(last) * carry_ref[pl.ds(c, 1), :]
        gain = jnp.exp(cum) * inflow_ref[rows, :]
        fore_log = jnp.transpose(cum)
        back_log = cum - jnp.log(dt)
        b = b_ref[rows, :]
        cc = c_ref[rows, :]
        scores = dot(b, cc, ((1,), (1,)))
        row = lax.broadcasted_iota(jnp.int32, (SPAN, SPAN), 0)
        col = lax.broadcasted_iota(jnp.int32, (SPAN, SPAN), 1)
        mask = (col >= row) & (segc_ref[rows, :] == segr_ref[pl.ds(c, 1), :])
        lane = lax.broadcasted_iota(jnp.int32, (SPAN, LANES), 1)
        d_scores = jnp.zeros((SPAN, SPAN), f32)
        db = jnp.zeros((SPAN, STATE), f32)
        dc = jnp.zeros((SPAN, STATE), f32)
        state_row = []
        dx_state_row = []
        for p in range(PAIRS):
            lanes = slice(p * LANES, (p + 1) * LANES)
            x = x_ref[rows, lanes]
            dy = dy_ref[rows, lanes]
            xf = x.astype(f32)
            dyf = dy.astype(f32)
            parts = []
            for k in range(2):
                h = 2 * p + k
                gap = fore_log[h : h + 1, :] - back_log[:, h : h + 1]
                decay_mat = jnp.exp(jnp.where(mask, gap, -1e30))
                weights = (scores * decay_mat).astype(bf16)
                parts.append(dot(weights, dy))
                own = (lane < HEADDIM) if k == 0 else (lane >= HEADDIM)
                d_weights = dot(jnp.where(own, xf, 0.0).astype(bf16), dy, ((1,), (1,)))
                d_scores = d_scores + d_weights * decay_mat
            dx = jnp.where(lane < HEADDIM, parts[0], parts[1])
            dyg = (dyf * pair_cols(gain, 2 * p)).astype(bf16)
            ew = pair_cols(end_weight, 2 * p)
            xw = (xf * ew).astype(bf16)
            state = st_ref[c, :, lanes]
            ds = ds_ref[:, lanes]
            state_b = state.astype(bf16)
            ds_b = ds.astype(bf16)
            dc = dc + dot(dyg, state_b, ((1,), (1,)))
            db = db + dot(xw, ds_b, ((1,), (1,)))
            dx_state = dot(b, ds_b) * ew
            dx = dx + dx_state
            dec = pair_cols(decay, 2 * p)
            state_row.append(jnp.sum(ds * state, axis=0, keepdims=True) * dec)
            dx_state_row.append(jnp.sum(dx_state * xf, axis=0, keepdims=True))
            ds_ref[:, lanes] = ds * dec + dot(cc, dyg, ((0,), (0,)))
            prod_ref[0:SPAN, lanes] = dyf * y_ref[rows, lanes]
            prod_ref[SPAN : 2 * SPAN, lanes] = xf * dx
            dskip_ref[0:1, lanes] += jnp.sum(dyf * xf, axis=0, keepdims=True)
            dx_ref[rows, lanes] = (dx + dyf * skip_ref[0:1, lanes]).astype(bf16)
        d_scores_b = d_scores.astype(bf16)
        db_ref[rows, :] = db + dot(d_scores_b, cc)
        dc_ref[rows, :] = dc + dot(d_scores_b, b, ((0,), (0,)))
        sums = head_sums(prod_ref[...])
        out_sum, in_sum = sums[:SPAN], sums[SPAN:]
        edge = jnp.concatenate(state_row, axis=1) + jnp.concatenate(dx_state_row, axis=1)
        edge_sum = head_sums(jnp.broadcast_to(edge, (8, HALF)))[0:1]
        at_last = lax.broadcasted_iota(jnp.int32, (SPAN, LANES), 0) == SPAN - 1
        d_cum = out_sum - in_sum + jnp.where(at_last, edge_sum, 0.0)
        upper = (col >= row).astype(f32)
        d_log = dot(upper, d_cum, precision=exact_prec)
        drate_ref[0:1, :] += jnp.sum(d_log * dt, axis=0, keepdims=True)
        ddt_ref[rows, :] = d_log * rate_ref[0:1, :] * sig_ref[rows, :] + in_sum * ratio_ref[rows, :]
        return 0

    lax.fori_loop(0, spans, body, 0)


GROUP = ("t1", "t0")
COPIES = ("part", "w1", "w0")
EVERYONE = ("part", "t1", "t0", "w1", "w0")


VMEM_LIMIT = 63 * 1024 * 1024


def in_vmem(kernel, out_shape, name, scratch=()):
    return pl.pallas_call(
        kernel,
        out_shape=out_shape,
        scratch_shapes=list(scratch),
        name=name,
        compiler_params=pltpu.CompilerParams(vmem_limit_bytes=VMEM_LIMIT),
    )


def shape(dims, dtype):
    return jax.ShapeDtypeStruct(dims, dtype)


def shift_part(array, by):
    size = lax.axis_size("part")
    pairs = [(i, i + by) for i in range(size) if 0 <= i + by < size]
    return lax.ppermute(array, "part", pairs)


def shards_general(
    hidden, cotangent, segments, valid, in_w, in_m, in_v, out_w, out_m, out_v, small_w, small_m, small_v,
):
    parts = lax.axis_size("part")
    wt = lax.axis_size("w1") * lax.axis_size("w0")
    part = lax.axis_index("part")
    tp = lax.axis_index("t1") * 2 + lax.axis_index("t0")
    own_rows = in_w.shape[0]
    out_rows = out_w.shape[0]
    resid = hidden[0].astype(f32)
    tok_rows = resid.shape[0]
    rows = tok_rows * TP
    spans = rows // SPAN
    seg_all = segments[0]
    pre_gain, norm_gain, conv_weight, conv_bias, dt_shift, a_logs, skips = unpack_small(small_w)

    def own_part(array, width):
        return lax.dynamic_slice_in_dim(array, tp * width, width, array.ndim - 1)

    in_copy = in_w.astype(bf16)
    slices = []
    for j in range(TP):
        slices.append(
            jnp.concatenate(
                [
                    in_copy[:, D_INNER + j * HALF : D_INNER + (j + 1) * HALF],
                    in_copy[:, 2 * D_INNER : 2 * D_INNER + SIDE],
                    in_copy[:, D_INNER + CONVCH + j * LOCAL_HEADS : D_INNER + CONVCH + (j + 1) * LOCAL_HEADS],
                    jnp.zeros((own_rows, LANES - LOCAL_HEADS), bf16),
                    in_copy[:, j * HALF : (j + 1) * HALF],
                ],
                axis=1,
            )
        )
    mine = lax.all_to_all(jnp.stack(slices), GROUP, 0, 0, tiled=False)
    w_in = lax.all_gather(mine, COPIES, axis=0, tiled=False)
    w_in = w_in.reshape(parts, wt, TP, own_rows, COLS).transpose(0, 2, 1, 3, 4).reshape(D, COLS)
    flat = [(i, (i % TP) * parts + i // TP) for i in range(parts * TP)]
    out_mine = lax.ppermute(out_w.astype(bf16), ("part", *GROUP), [(b, a) for a, b in flat])
    w_out = lax.all_gather(out_mine, COPIES, axis=0, tiled=True)

    hidden_all = lax.all_gather(hidden[0], GROUP, axis=0, tiled=True)
    back_mix = cotangent[0] * valid[0][:, None].astype(bf16)
    back_all = lax.all_gather(back_mix, GROUP, axis=0, tiled=True)

    hid = hidden_all.astype(f32)
    scale_all = lax.rsqrt(jnp.mean(hid * hid, axis=1, keepdims=True) + norm_eps)
    x_normed = (hid * scale_all * pre_gain).astype(bf16)
    projected = dot(x_normed, w_in)
    conv_in = projected[:, :COL_DT].astype(bf16)
    dt_raw = projected[:, COL_DT:COL_GATE].astype(bf16).astype(f32)
    gate_pre = projected[:, COL_GATE:]
    rim_in = shift_part(conv_in[rows - RIM :], 1)
    padded = jnp.concatenate([rim_in, conv_in], axis=0).astype(f32)
    seg_front = jnp.concatenate([jnp.full((RIM,), -1, jnp.int32), seg_all, jnp.full((RIM,), -1, jnp.int32)])
    seg_pad = lax.dynamic_slice_in_dim(seg_front, part * rows, rows + 2 * RIM)
    seg = seg_pad[RIM : RIM + rows]
    masks = [(seg_pad[k : k + rows] == seg).astype(f32)[:, None] for k in range(CONV)]
    taps = jnp.concatenate([own_part(conv_weight[:, :D_INNER], HALF), conv_weight[:, D_INNER:]], axis=1)
    bias = jnp.concatenate([own_part(conv_bias[:D_INNER], HALF), conv_bias[D_INNER:]])
    total = bias[None, :]
    for k in range(CONV):
        total = total + taps[k] * padded[k : k + rows] * masks[k]
    sig_total = jax.nn.sigmoid(total)
    activated = (total * sig_total).astype(bf16)
    x_scan = activated[:, :HALF]
    b_mat = activated[:, HALF : HALF + STATE]
    c_mat = activated[:, HALF + STATE :]

    def head_row(array):
        return jnp.pad(own_part(array, LOCAL_HEADS), (0, LANES - LOCAL_HEADS))

    shift_row = head_row(dt_shift)
    z = dt_raw + shift_row
    dt = jax.nn.softplus(z)
    sig_dt = jax.nn.sigmoid(z)
    ratio = jnp.where(dt > 1e-30, sig_dt / jnp.maximum(dt, 1e-30), 1.0)
    rate_row = -jnp.exp(head_row(a_logs))
    rate8 = jnp.broadcast_to(rate_row, (8, LANES))
    skip_chan = jnp.repeat(own_part(skips, LOCAL_HEADS), HEADDIM)
    skip8 = jnp.broadcast_to(skip_chan, (8, HALF))
    seg_spans = seg.reshape(spans, SPAN)
    seg_last = seg_spans[:, -1]
    seg_before = jnp.concatenate([seg_pad[RIM - 1 : RIM], seg_last[:-1]])
    keep = (seg_spans == seg_last[:, None]).astype(f32).reshape(rows, 1)
    inflow = (seg_spans == seg_before[:, None]).astype(f32).reshape(rows, 1)
    carry = jnp.broadcast_to((seg_last == seg_before).astype(f32)[:, None], (spans, LANES))
    seg_col = seg[:, None]

    state_shape = shape((STATE, HALF), f32)
    s_local, dec_total = in_vmem(
        functools.partial(state_kernel, spans), (state_shape, shape((8, LANES), f32)), "state"
    )(x_scan, b_mat, dt, rate8, keep, carry)
    dec_chan = jnp.repeat(dec_total[0, :LOCAL_HEADS], HEADDIM)
    s_in = jnp.zeros((STATE, HALF), f32)
    for _ in range(parts - 1):
        s_in = shift_part(dec_chan * s_in + s_local, 1)
    y_scan, states = in_vmem(
        functools.partial(scan_kernel, spans),
        (shape((rows, HALF), f32), shape((spans, STATE, HALF), f32)),
        "scan",
        [pltpu.VMEM((STATE, HALF), f32)],
    )(x_scan, b_mat, c_mat, dt, rate8, seg_col, seg_spans, keep, inflow, carry, s_in)
    y_b = (y_scan + skip_chan * x_scan.astype(f32)).astype(bf16).astype(f32)

    gain_own = own_part(norm_gain, HALF)
    sig_gate = jax.nn.sigmoid(gate_pre)
    silu_gate = gate_pre * sig_gate
    gated = y_b * silu_gate
    gate_sq = lax.psum(jnp.sum(gated * gated, axis=1), GROUP)
    scale_gate = lax.rsqrt(gate_sq / D_INNER + norm_eps)[:, None]
    normed = (gated * scale_gate * gain_own).astype(bf16)
    mixer = lax.psum_scatter(dot(normed, w_out), GROUP, scatter_dimension=0, tiled=True)
    output = (resid + mixer).astype(bf16)
    valid_rows = valid[0].astype(f32)
    res_sq = jnp.sum(valid_rows * jnp.sum(resid * resid, axis=1))
    mix_sq = jnp.sum(valid_rows * jnp.sum(mixer * mixer, axis=1))
    valid_count = jnp.sum(valid_rows)

    d_normed = dot(back_all, w_out, ((1,), (1,)))
    g_out = dot(normed, back_all, ((0,), (0,)))
    g_out = lax.psum_scatter(g_out, COPIES, scatter_dimension=0, tiled=True)
    g_out = lax.ppermute(g_out, ("part", *GROUP), flat)
    d_gain = d_normed * gain_own
    gate_dot = lax.psum(jnp.sum(gated * d_gain, axis=1), GROUP)
    d_gated = scale_gate * d_gain - gated * (scale_gate**3 * (gate_dot / D_INNER)[:, None])
    d_norm_gain = jnp.sum(gated * scale_gate * d_normed, axis=0)
    dy = (d_gated * silu_gate).astype(bf16)
    d_gate = d_gated * y_b * (sig_gate * (1.0 + gate_pre * (1.0 - sig_gate)))

    ds_local = in_vmem(functools.partial(state_back_kernel, spans), state_shape, "state_back")(
        dy, c_mat, dt, rate8, inflow, carry
    )
    ds_out = jnp.zeros((STATE, HALF), f32)
    for _ in range(parts - 1):
        ds_out = shift_part(dec_chan * ds_out + ds_local, -1)
    d_x, d_b, d_c, d_dt, d_rate, d_skip = in_vmem(
        functools.partial(scan_back_kernel, spans),
        (
            shape((rows, HALF), bf16),
            shape((rows, STATE), f32),
            shape((rows, STATE), f32),
            shape((rows, LANES), f32),
            shape((8, LANES), f32),
            shape((8, HALF), f32),
        ),
        "scan_back",
        [pltpu.VMEM((STATE, HALF), f32), pltpu.VMEM((2 * SPAN, HALF), f32)],
    )(x_scan, b_mat, c_mat, dt, ratio, sig_dt, rate8, seg_col, seg_spans, keep, inflow, carry, skip8, y_scan, states, dy, ds_out)

    d_total = jnp.concatenate([d_x.astype(f32), d_b, d_c], axis=1) * (sig_total * (1.0 + total * (1.0 - sig_total)))
    rim_back = shift_part(d_total[:RIM], -1)
    d_padded = jnp.concatenate([d_total, rim_back], axis=0)
    d_conv_in = 0.0
    for k in range(CONV):
        later = (seg_pad[2 * RIM - k : 2 * RIM - k + rows] == seg).astype(f32)[:, None]
        d_conv_in = d_conv_in + taps[k] * d_padded[RIM - k : RIM - k + rows] * later
    d_taps = jnp.stack([jnp.sum(d_total * padded[k : k + rows] * masks[k], axis=0) for k in range(CONV)])
    d_bias = jnp.sum(d_total, axis=0)
    d_proj = jnp.concatenate([d_conv_in, d_dt, d_gate], axis=1).astype(bf16)
    d_x_normed = dot(d_proj, w_in, ((1,), (1,)))
    d_x_normed = lax.psum_scatter(d_x_normed, GROUP, scatter_dimension=0, tiled=True)
    g_in = dot(x_normed, d_proj, ((0,), (0,)))
    g_in = g_in.reshape(parts, TP, wt, own_rows, COLS).transpose(0, 2, 1, 3, 4).reshape(parts * wt, TP, own_rows, COLS)
    g_in = lax.psum_scatter(g_in, COPIES, scatter_dimension=0, tiled=False)
    g_in = lax.all_to_all(g_in, GROUP, 0, 0, tiled=False)
    g_in = jnp.concatenate(
        [g_in[j, :, COL_GATE:] for j in range(TP)]
        + [g_in[j, :, :HALF] for j in range(TP)]
        + [jnp.sum(g_in[:, :, COL_SIDE:COL_DT], axis=0)]
        + [g_in[j, :, COL_DT : COL_DT + LOCAL_HEADS] for j in range(TP)],
        axis=1,
    )

    scale_own = lax.rsqrt(jnp.mean(resid * resid, axis=1, keepdims=True) + norm_eps)
    d_pre = d_x_normed * pre_gain
    dot_pre = jnp.mean(resid * d_pre, axis=1, keepdims=True)
    grad_hidden = back_mix.astype(f32) + scale_own * d_pre - resid * (scale_own**3 * dot_pre)
    d_pre_gain = jnp.sum(resid * scale_own * d_x_normed, axis=0)

    def placed(values, width):
        spread = (jnp.arange(TP) == tp).astype(f32)[:, None] * values[..., None, :]
        return spread.reshape(*values.shape[:-1], TP * width)

    d_weight = jnp.concatenate([placed(d_taps[:, :HALF], HALF), d_taps[:, HALF:]], axis=1)
    small_grad = jnp.concatenate(
        [
            d_pre_gain,
            placed(d_norm_gain, HALF),
            d_weight.reshape(-1),
            placed(d_bias[:HALF], HALF),
            d_bias[HALF:],
            placed(jnp.sum(d_dt, axis=0)[:LOCAL_HEADS], LOCAL_HEADS),
            placed((d_rate[0] * rate_row)[:LOCAL_HEADS], LOCAL_HEADS),
            placed(jnp.sum(d_skip[0].reshape(LOCAL_HEADS, HEADDIM), axis=1), LOCAL_HEADS),
            jnp.stack([res_sq, mix_sq, valid_count]),
        ]
    )
    small_total = lax.psum(small_grad, EVERYONE)
    res_total, mix_total, count_total = small_total[-3], small_total[-2], small_total[-1]
    in_m_new, in_v_new, in_w_new = adamw(in_w, in_m, in_v, g_in, 0.02, 0.1)
    out_m_new, out_v_new, out_w_new = adamw(out_w, out_m, out_v, g_out, 0.02, 0.1)
    small_m_new, small_v_new, small_w_new = adamw(small_w, small_m, small_v, small_total[:-3], 0.2, 0.0)
    rms = jnp.stack([jnp.sqrt(res_total / (count_total * D)), jnp.sqrt(mix_total / (count_total * D))])
    return (
        output[None], grad_hidden[None], in_m_new, in_v_new, in_w_new, out_m_new, out_v_new, out_w_new,
        small_m_new, small_v_new, small_w_new, rms,
    )


MESH = pl.DeviceIdType.MESH
T0, T1, DIAG, CORE, SIDEWAYS, PART = ("t0",), ("t1",), ("t1", "t0"), ("w0",), ("w1",), ("part",)
SIDE_CORE = ("w1", "w0")
HOPS = (None, T0, T1, DIAG)
HBM = pl.BlockSpec(memory_space=pl.ANY)
VMEM = pl.BlockSpec(memory_space=pltpu.VMEM)
MAIN = COL_GATE
CHANS = HALF + SIDE
FRONT = 16
TILE = 8
QUARTER = HALF // 2
NORM_ROW = D // LANES
TAP_ROW = NORM_ROW + D_INNER // LANES
TAP_ROWS = CONVCH // LANES
HEAD_ROW = TAP_ROW + (CONV + 1) * TAP_ROWS
SMALL_ROWS = HEAD_ROW + 2
BOX_ROWS = SMALL_ROWS + 8
OWN_NORM = NORM_ROW
OWN_TAP = OWN_NORM + HALF // LANES
OWN_SIDE = OWN_TAP + (CONV + 1) * (HALF // LANES)
OWN_HEAD = OWN_SIDE + (CONV + 1) * (SIDE // LANES)
OWN_SUMS = OWN_HEAD + 3
OWN_ROWS = 64


def place():
    return tuple(lax.axis_index(a) for a in EVERYONE)


def across(flips):
    return {a: 1 - lax.axis_index(a) for a in flips}


def group_blocks():
    _, t1, t0, _, _ = place()
    return [(t1, t0), (t1, 1 - t0), (1 - t1, t0), (1 - t1, 1 - t0)]


def greet(neighbours):
    barrier = pltpu.get_barrier_semaphore()
    for flips in neighbours:
        pl.semaphore_signal(barrier, inc=1, device_id=across(flips), device_id_type=MESH)


def greeted(neighbours):
    pl.semaphore_wait(pltpu.get_barrier_semaphore(), len(neighbours))


class Copies:
    def __init__(self, local_sem, send_sem, recv_sem):
        self.local_sem, self.send_sem, self.recv_sem = local_sem, send_sem, recv_sem
        self.sent, self.kept, self.in_flight, self.on_device = 0, 0, [], []

    def send(self, src, dst, flips):
        copy = pltpu.make_async_remote_copy(
            src_ref=src,
            dst_ref=dst,
            send_sem=self.send_sem.at[self.sent],
            recv_sem=self.recv_sem.at[self.sent],
            device_id=across(flips),
            device_id_type=MESH,
        )
        copy.start()
        self.sent += 1
        self.in_flight.append(copy)
        return copy

    def keep(self, src, dst):
        copy = pltpu.make_async_copy(src, dst, self.local_sem.at[self.kept])
        copy.start()
        self.kept += 1
        self.on_device.append(copy)
        return copy

    def settle(self, copy):
        copy.wait()
        self.on_device = [other for other in self.on_device if other is not copy]

    def drain(self):
        for copy in self.in_flight:
            copy.wait_send()
        for copy in self.on_device:
            copy.wait()
        self.in_flight, self.on_device = [], []


def sems(remote, local=1):
    return [
        pltpu.SemaphoreType.DMA((local,)),
        pltpu.SemaphoreType.DMA((remote,)),
        pltpu.SemaphoreType.DMA((remote,)),
    ]


class GroupGather:
    def __init__(self, copies, src, dst):
        self.copies, self.dst = copies, dst
        self.rows = src.shape[0]
        self.halves = (0, self.rows // 2)
        own = group_blocks()[0]
        self.own = copies.keep(src, self.at(own, 0, self.rows))
        size = self.rows // 2
        self.along_t1 = [copies.send(src.at[pl.ds(h, size)], self.at(own, h, size), T1) for h in self.halves]
        self.along_t0 = [copies.send(src.at[pl.ds(h, size)], self.at(own, h, size), T0) for h in self.halves]
        self.diagonal = []

    def at(self, block, first, size):
        return self.dst.at[pl.ds(pl.multiple_of((block[0] * 2 + block[1]) * self.rows + first, size), size)]

    def hand_on(self):
        beside = group_blocks()[2]
        for copy, h in zip(self.along_t1, self.halves):
            copy.wait_recv()
            here = self.at(beside, h, self.rows // 2)
            self.diagonal.append(self.copies.send(here, here, T0))

    def finish(self):
        for copy in self.along_t0 + self.diagonal:
            copy.wait_recv()


class WeightGather:
    def __init__(self, copies, dst, rows, group):
        self.copies, self.dst, self.rows, self.group = copies, dst, rows, group
        self.by_part, self.by_side, self.by_core = [], [], []

    def at(self, part, w1, w0, block):
        index = part
        if self.group:
            index = (index * 2 + block[0]) * 2 + block[1]
        index = (index * 2 + w1) * 2 + w0
        return self.dst.at[pl.ds(pl.multiple_of(index * self.rows, self.rows), self.rows)]

    def mine(self, block):
        p, _, _, w1, w0 = place()
        return self.at(p, w1, w0, block)

    def spread(self, src, block):
        dst = self.mine(block)
        self.by_part.append((self.copies.send(src, dst, PART), block))
        self.by_side.append((self.copies.send(src, dst, SIDEWAYS), block))
        self.by_core.append(self.copies.send(src, dst, CORE))

    def swap(self, src):
        own, *others = group_blocks()
        self.swaps = [
            (self.copies.send(src.at[b[0], b[1]], self.mine(own), flips), b) for b, flips in zip(others, HOPS[1:])
        ]
        self.kept = self.copies.keep(src.at[own[0], own[1]], self.mine(own))
        self.spread(src.at[own[0], own[1]], own)

    def spread_swapped(self):
        for copy, block in self.swaps:
            copy.wait_recv()
            self.spread(self.mine(block), block)

    def pass_core(self, part, w1, block):
        here = self.at(part, w1, lax.axis_index("w0"), block)
        self.by_core.append(self.copies.send(here, here, CORE))

    def hand_on(self):
        p, _, _, w1, w0 = place()
        again = []
        for (copy, block), (side, _) in zip(self.by_part, self.by_side):
            side.wait_recv()
            self.pass_core(p, 1 - w1, block)
            copy.wait_recv()
            here = self.at(1 - p, w1, w0, block)
            again.append((self.copies.send(here, here, SIDEWAYS), block))
            self.pass_core(1 - p, w1, block)
        for copy, block in again:
            copy.wait_recv()
            self.pass_core(1 - p, 1 - w1, block)

    def finish(self):
        for copy in self.by_core:
            copy.wait_recv()


class GradientSum:
    def __init__(self, copies, src, rows, bufs, group):
        self.copies, self.src, self.rows, self.group = copies, src, rows, group
        self.core, self.side, self.sides, self.far, self.fars = bufs[:5]
        self.last, self.lasts = bufs[5:] if group else (None, None)
        self.blocks = group_blocks() if group else [()]
        self.order = (1, 2, 3, 0) if group else (0,)
        self.cols = pl.ds(0, self.core.shape[-1])
        p, _, _, w1, _ = place()
        self.parts, self.sides_of = (1 - p, p), (1 - w1, w1)
        self.core_copies, self.side_copies, self.far_copies, self.last_copies = {}, {}, {}, {}

    def at(self, q, block, side, w0):
        index = q
        if self.group:
            index = (index * 2 + block[0]) * 2 + block[1]
        index = (index * 2 + side) * 2 + w0
        return pl.ds(pl.multiple_of(index * self.rows, self.rows), self.rows)

    def added(self, k, i, j, *more):
        q, block, side = self.parts[k], self.blocks[i], self.sides_of[j]
        self.core_copies[k, i, j].wait_recv()
        value = self.src[self.at(q, block, side, lax.axis_index("w0")), self.cols].astype(f32)
        value = value + self.core[(q, side, *block)].astype(f32)
        for other in more:
            value = value + other.astype(f32)
        return value

    def cores(self, k):
        w0 = lax.axis_index("w0")
        for j in range(2):
            for i in self.order:
                q, block, side = self.parts[k], self.blocks[i], self.sides_of[j]
                src = self.src.at[self.at(q, block, side, 1 - w0), self.cols]
                self.core_copies[k, i, j] = self.copies.send(src, self.core.at[(q, side, *block)], CORE)

    def to_sides(self, k):
        for i in self.order:
            self.side[k, i] = self.added(k, i, 0).astype(bf16)
            self.side_copies[k, i] = self.copies.send(self.side.at[k, i], self.sides.at[k, i], SIDEWAYS)

    def to_part(self):
        for i in self.order:
            self.side_copies[0, i].wait_recv()
            self.far[i] = self.added(0, i, 1, self.sides[0, i]).astype(bf16)
            self.far_copies[i] = self.copies.send(self.far.at[i], self.fars.at[i], PART)

    def total(self, i):
        self.side_copies[1, i].wait_recv()
        self.far_copies[i].wait_recv()
        return self.added(1, i, 1, self.sides[1, i], self.fars[i])

    def to_group(self):
        self.sums = {}
        for i in self.order:
            value = self.total(i)
            if i == 0:
                self.sums[0] = value
            else:
                self.last[i - 1] = value.astype(bf16)
                self.last_copies[i] = self.copies.send(self.last.at[i - 1], self.lasts.at[i - 1], HOPS[i])

    def finish(self):
        for i, copy in self.last_copies.items():
            copy.wait_recv()
            self.sums[i] = self.lasts[i - 1].astype(f32)


class GroupScatter:
    def __init__(self, copies, src, bufs):
        self.copies, self.src = copies, src
        self.here, self.pass_on, self.joined, self.last = bufs
        self.rows = self.here.shape[0]

    def block(self, i):
        return block_rows(group_blocks()[i], self.rows)

    def to_t0(self, i):
        copy = self.copies.send(self.src.at[self.block(i)], self.here if i == 1 else self.pass_on, T0)
        if i == 1:
            self.own_copy = copy
        else:
            self.pass_copy = copy

    def to_t1(self):
        self.pass_copy.wait_recv()
        self.joined[...] = (self.src[self.block(2), :].astype(f32) + self.pass_on[...].astype(f32)).astype(bf16)
        self.last_copy = self.copies.send(self.joined, self.last, T1)

    def finish(self):
        self.own_copy.wait_recv()
        self.last_copy.wait_recv()
        return self.here[...].astype(f32) + self.last[...].astype(f32)


def scatter_buffers(rows):
    return [pltpu.VMEM((rows, D), bf16)] * 4


def sum_buffers(rows, cols, group):
    buf = lambda *lead: pltpu.VMEM((*lead, rows, cols), bf16)
    if not group:
        return [buf(2, 2), buf(2, 1), buf(2, 1), buf(1), buf(1)]
    return [buf(2, 2, 2, 2), buf(2, 4), buf(2, 4), buf(4), buf(4), buf(3), buf(3)]


def block_rows(block, size):
    return pl.ds(pl.multiple_of((block[0] * 2 + block[1]) * size, size), size)


def lane_of(h):
    return h if h < LOCAL_HEADS // 2 else h + HEADS // 2 - LOCAL_HEADS // 2


def own_pair(cols, h):
    lane = lax.broadcasted_iota(jnp.int32, (cols.shape[0], LANES), 1)
    first, second = lane_of(h), lane_of(h + 1)
    return jnp.where(lane < HEADDIM, cols[:, first : first + 1], cols[:, second : second + 1])


def own_sums(values):
    width = values.shape[1]
    head = lax.broadcasted_iota(jnp.int32, (width, LANES), 0) // HEADDIM
    lane = lax.broadcasted_iota(jnp.int32, (width, LANES), 1)
    pick = (jnp.where(head < LOCAL_HEADS // 2, head, head + lane_of(LOCAL_HEADS) - LOCAL_HEADS) == lane).astype(bf16)
    high = values.astype(bf16)
    low = (values - high.astype(f32)).astype(bf16)
    return dot(high, pick) + dot(low, pick)


def head_lanes(values, back=False):
    first = (lax.axis_index("t1") * 2 + lax.axis_index("t0")) * (LOCAL_HEADS // 2)
    return pltpu.roll(values, first if back else LANES - first, 1)


def own_row(first, k):
    tp = lax.axis_index("t1") * 2 + lax.axis_index("t0")
    third = QUARTER // LANES
    return pl.ds(first + (k // third) * (D_INNER // 2 // LANES) + tp * third + k % third, 1)


def own_chans(j):
    return [slice(first + j * QUARTER, first + (j + 1) * QUARTER) for first in (0, D_INNER // 2)]


NEIGHBOURS = (T0, T1, DIAG, CORE, SIDEWAYS, PART)


def main_kernel(
    spans, hid_ref, inw_hbm, outw_hbm, inside_ref, cot_ref, valid_ref, small_ref, segc_ref, segr_ref,
    h_out, xn_out, win_out, wgate_out, dgate_out, dmain_out, cotv_out, mixer_out, ggate_out, own_ref, gout_ref,
    h_ref, xn_ref, win_ref, convp_ref, x_ref, b_ref, c_ref, dtot_ref, dt_ref, z_ref, cum_ref, y_ref, st_ref,
    wgate_ref, wout_ref, back_ref, normed_ref, mix_ref, dy_ref, dgate_ref, dmain_ref, dgain_ref, taps_ref, heads_ref, chans_ref,
    marks_ref, carry_ref, wm_ref, wg_ref, wo_ref, cotv_ref, s_ref, pass_ref, got_ref, rim_ref, gated_ref, gate_ref, dn_ref,
    stat_ref, stats_ref, dyg_ref, passb_ref, gotb_ref, rims_ref, rimr_ref, db_ref, dc_ref, hsum_ref, dskip_ref, dtaps_ref,
    *rest,
):
    go_bufs, gg_bufs, mix_bufs, (local_sem, send_sem, recv_sem) = rest[:5], rest[5:12], rest[12:16], rest[16:]
    greet(NEIGHBOURS)
    p, _, _, _, _ = place()
    rows_all = spans * SPAN
    tokens = hid_ref.shape[0]
    own_rows, out_rows = inw_hbm.shape[0], outw_hbm.shape[0]
    lane = lax.broadcasted_iota(jnp.int32, (1, LANES), 1)
    dxi_ref, prod_ref = gated_ref, gate_ref

    copies = Copies(local_sem, send_sem, recv_sem)
    loads = [
        copies.keep(inw_hbm.at[:, pl.ds(k * HALF, HALF)], gate_ref.at[pl.ds(k * own_rows, own_rows)])
        for k in range(2 * D_INNER // HALF)
    ]
    loads += [
        copies.keep(outw_hbm.at[:, pl.ds(k * HALF, HALF)], dn_ref.at[pl.ds(k * out_rows, out_rows)]) for k in range(D // HALF)
    ]
    cotv_ref[...] = (cot_ref[...].astype(f32) * valid_ref[...]).astype(bf16)

    side = inside_ref[...]
    dt_cols = jnp.concatenate([side[:, SIDE:], jnp.zeros((own_rows, LANES - HEADS), f32)], axis=1)
    for copy in loads:
        copies.settle(copy)

    def master(first):
        return gate_ref[first // HALF * own_rows : (first // HALF + 1) * own_rows, first % HALF : first % HALF + QUARTER]

    for j in range(TP):
        at = (j // 2, j % 2)
        for k, chans in enumerate(own_chans(j)):
            part = slice(k * QUARTER, (k + 1) * QUARTER)
            wg_ref[(*at, slice(None), part)] = master(chans.start).astype(bf16)
            wm_ref[(*at, slice(None), part)] = master(D_INNER + chans.start).astype(bf16)
        wm_ref[(*at, slice(None), slice(HALF, CHANS))] = side[:, :SIDE].astype(bf16)
        dt_own = (lane % (HEADS // 2) // (LOCAL_HEADS // 2) == j) & (lane < HEADS)
        wm_ref[(*at, slice(None), slice(CHANS, MAIN))] = jnp.where(dt_own, dt_cols, 0.0).astype(bf16)
    for k in range(D // HALF):
        wo_ref[:, k * HALF : (k + 1) * HALF] = dn_ref[k * out_rows : (k + 1) * out_rows, :].astype(bf16)

    greeted(NEIGHBOURS)
    mains = WeightGather(copies, win_ref, wm_ref.shape[2], True)
    mains.swap(wm_ref)
    hids = GroupGather(copies, hid_ref, h_ref)
    copies.keep(cotv_ref, cotv_out)

    for k in range(HALF // LANES):
        lanes = slice(k * LANES, (k + 1) * LANES)
        chans_ref[1:2, lanes] = small_ref[own_row(NORM_ROW, k), :]
        for j in range(CONV + 1):
            taps_ref[j : j + 1, lanes] = small_ref[own_row(TAP_ROW + TAP_ROWS * j, k), :]
    for k in range(SIDE // LANES):
        lanes = slice(HALF + k * LANES, HALF + (k + 1) * LANES)
        for j in range(CONV + 1):
            row = TAP_ROW + TAP_ROWS * j + D_INNER // LANES + k
            taps_ref[j : j + 1, lanes] = small_ref[row : row + 1, :]
    head_row = jnp.broadcast_to(small_ref[HEAD_ROW : HEAD_ROW + 1, :], (TILE, LANES))
    next_row = jnp.broadcast_to(small_ref[HEAD_ROW + 1 : HEAD_ROW + 2, :], (TILE, LANES))
    a_log = pltpu.roll(head_row, LANES - HEADS, 1)
    lane8 = lax.broadcasted_iota(jnp.int32, (TILE, LANES), 1)
    spill = LANES - 2 * HEADS
    skip = jnp.where(lane8 < spill, pltpu.roll(head_row, spill, 1), pltpu.roll(next_row, spill, 1))
    own = lane8 < HEADS
    heads_ref[0:1, :] = head_lanes(jnp.where(own, head_row, 0.0))[0:1]
    heads_ref[1:2, :] = -jnp.exp(head_lanes(jnp.where(own, a_log, 0.0))[0:1])
    skip = head_lanes(jnp.where(own, skip, 0.0))[0:1]
    for q in range(PAIRS):
        chans_ref[0:1, q * LANES : (q + 1) * LANES] = own_pair(skip, 2 * q)

    def mark(c, _):
        rows = span_rows(c)
        seg = segc_ref[pl.ds(pl.multiple_of(c * SPAN, SPAN), SPAN + 2 * FRONT), :]
        here = seg[FRONT : FRONT + SPAN]
        last = seg[FRONT + SPAN - 1 : FRONT + SPAN]
        before = seg[FRONT - 1 : FRONT]
        cols = [seg[FRONT - RIM + k : FRONT - RIM + k + SPAN] == here for k in range(RIM)]
        cols += [seg[FRONT + RIM - k : FRONT + RIM - k + SPAN] == here for k in range(RIM)]
        cols += [here == last, here == before]
        lane_m = lax.broadcasted_iota(jnp.int32, (SPAN, TILE), 1)
        marks = jnp.zeros((SPAN, TILE), f32)
        for k, col in enumerate(cols):
            marks = jnp.where(lane_m == k, jnp.where(col, 1.0, 0.0), marks)
        marks_ref[rows, :] = marks
        carry_ref[pl.ds(c, 1), :] = jnp.broadcast_to(jnp.where(last == before, 1.0, 0.0), (1, LANES))
        return 0

    lax.fori_loop(0, spans, mark, 0)
    blocks = group_blocks()

    def norm(block):
        rows = block_rows(block, tokens)
        hid = h_ref[rows, :].astype(f32)
        scale = lax.rsqrt(jnp.sum(hid * hid, axis=1, keepdims=True) / D + norm_eps)
        for k in range(D // LANES):
            lanes = slice(k * LANES, (k + 1) * LANES)
            xn_ref[rows, lanes] = (h_ref[rows, lanes].astype(f32) * scale * small_ref[k : k + 1, :]).astype(bf16)

    mains.spread_swapped()
    copies.settle(hids.own)
    norm(blocks[0])
    gates = WeightGather(copies, wgate_ref, wg_ref.shape[2], True)
    gates.swap(wg_ref)
    hids.hand_on()
    norm(blocks[2])
    mains.hand_on()
    gates.spread_swapped()
    hids.finish()
    norm(blocks[1])
    norm(blocks[3])
    copies.keep(h_ref, h_out)
    copies.keep(xn_ref, xn_out)
    cots = GroupGather(copies, cotv_ref, back_ref)
    outs = WeightGather(copies, wout_ref, wo_ref.shape[0], False)
    outs.spread(wo_ref, ())
    outs_kept = copies.keep(wo_ref, outs.mine(()))
    mains.finish()
    copies.settle(mains.kept)
    copies.keep(win_ref, win_out)

    def project(c, _):
        rows = span_rows(c)
        xn = xn_ref[rows, :]
        at = pl.ds(pl.multiple_of(FRONT + c * SPAN, FRONT), SPAN)
        for k in range(CHANS // 256):
            cols = slice(k * 256, (k + 1) * 256)
            convp_ref[at, cols] = dot(xn, win_ref[:, cols]).astype(bf16)
        dt_raw = dot(xn, win_ref[:, CHANS:MAIN]).astype(bf16).astype(f32)
        z = head_lanes(dt_raw) + heads_ref[0:1, :]
        z_ref[rows, :] = z
        small = jnp.exp(-jnp.abs(z))
        one_more = 1.0 + small
        is_one = one_more == 1.0
        log_more = jnp.where(is_one, small, jnp.log(one_more) * small / jnp.where(is_one, 1.0, one_more - 1.0))
        dt_ref[rows, :] = jnp.maximum(z, 0.0) + log_more
        return 0

    lax.fori_loop(0, spans, project, 0)
    rim = copies.send(convp_ref.at[pl.ds(rows_all, FRONT)], rim_ref, PART)
    gates.hand_on()
    s_ref[...] = jnp.zeros_like(s_ref)
    dgain_ref[...] = jnp.zeros_like(dgain_ref)
    rim.wait_recv()
    convp_ref[0:FRONT, :] = jnp.where(p == 1, rim_ref[...].astype(f32), 0.0).astype(bf16)

    def convolve(c, _):
        rows = span_rows(c)
        wide = pl.ds(pl.multiple_of(c * SPAN, SPAN), SPAN + FRONT)
        marks = marks_ref[rows, :]
        for k in range(CHANS // LANES):
            lanes = slice(k * LANES, (k + 1) * LANES)
            values = convp_ref[wide, lanes].astype(f32)
            total = taps_ref[CONV : CONV + 1, lanes] + taps_ref[RIM : RIM + 1, lanes] * values[FRONT:]
            for j in range(RIM):
                first = FRONT - RIM + j
                total = total + taps_ref[j : j + 1, lanes] * values[first : first + SPAN] * marks[:, j : j + 1]
            sig = 1.0 / (1.0 + jnp.exp(-total))
            value = (total * sig).astype(bf16)
            dtot_ref[rows, lanes] = sig * (1.0 + total * (1.0 - sig))
            if k < HALF // LANES:
                x_ref[rows, lanes] = value
            elif k == HALF // LANES:
                b_ref[rows, :] = value
            else:
                c_ref[rows, :] = value
        return 0

    lax.fori_loop(0, spans, convolve, 0)

    def local_states(c, _):
        rows = span_rows(c)
        dt, cum = span_decay(dt_ref, heads_ref, c, 1)
        cum_ref[rows, :] = cum
        last = cum[SPAN - 1 : SPAN, :]
        end_weight = jnp.exp(last - cum) * dt * marks_ref[rows, 6:7]
        decay = jnp.exp(last) * carry_ref[pl.ds(c, 1), :]
        b = b_ref[rows, :]
        st_ref[c] = s_ref[...]
        for q in range(PAIRS):
            lanes = slice(q * LANES, (q + 1) * LANES)
            xw = (x_ref[rows, lanes].astype(f32) * own_pair(end_weight, 2 * q)).astype(bf16)
            s_ref[:, lanes] = s_ref[:, lanes] * own_pair(decay, 2 * q) + dot(b, xw, ((0,), (0,)))
        return 0

    lax.fori_loop(0, spans, local_states, 0)
    pass_ref[...] = s_ref[...].astype(bf16)
    state = copies.send(pass_ref, got_ref, PART)
    cots.hand_on()

    def inside(c, _):
        rows = span_rows(c)
        cum = cum_ref[rows, :]
        back_log = jnp.transpose(cum - jnp.log(dt_ref[rows, :]))
        scores = dot(c_ref[rows, :], b_ref[rows, :], ((1,), (1,)))
        row = lax.broadcasted_iota(jnp.int32, (SPAN, SPAN), 0)
        col = lax.broadcasted_iota(jnp.int32, (SPAN, SPAN), 1)
        mask = (row >= col) & (segc_ref[pl.ds(pl.multiple_of(FRONT + c * SPAN, FRONT), SPAN), :] == segr_ref[pl.ds(c, 1), :])
        lane = lax.broadcasted_iota(jnp.int32, (SPAN, LANES), 1)
        for q in range(PAIRS):
            lanes = slice(q * LANES, (q + 1) * LANES)
            x = x_ref[rows, lanes]
            parts = []
            for h in (lane_of(2 * q), lane_of(2 * q + 1)):
                gap = cum[:, h : h + 1] - back_log[h : h + 1, :]
                weighted = scores * jnp.exp(jnp.where(mask, gap, -1e30))
                parts.append(dot(weighted.astype(bf16), x))
            y_ref[rows, lanes] = jnp.where(lane < HEADDIM, parts[0], parts[1])
        return 0

    lax.fori_loop(0, spans, inside, 0)
    outs.hand_on()
    state.wait_recv()
    s_ref[...] = got_ref[...].astype(f32) * p.astype(f32)

    def across_spans(c, _):
        rows = span_rows(c)
        cum = cum_ref[rows, :]
        decay = jnp.exp(cum[SPAN - 1 : SPAN, :]) * carry_ref[pl.ds(c, 1), :]
        gain = jnp.exp(cum) * marks_ref[rows, 7:8]
        cc = c_ref[rows, :]
        for q in range(PAIRS):
            lanes = slice(q * LANES, (q + 1) * LANES)
            entering = s_ref[:, lanes]
            full = st_ref[c, :, lanes] + entering
            st_ref[c, :, lanes] = full
            y_ref[rows, lanes] += dot(cc, full.astype(bf16)) * own_pair(gain, 2 * q)
            s_ref[:, lanes] = entering * own_pair(decay, 2 * q)
        return 0

    lax.fori_loop(0, spans, across_spans, 0)
    gates.finish()
    copies.settle(gates.kept)
    copies.keep(wgate_ref, wgate_out)

    def put_stat(k, c, column):
        wide = jnp.transpose(jnp.broadcast_to(column, (SPAN, LANES)))
        stat_ref[k, :, span_rows(c)] = wide[0:TILE, :]

    def exchange(k):
        return [copies.send(stat_ref.at[k], stats_ref.at[k, i], flips) for i, flips in enumerate(HOPS[1:])]

    def get_stat(k, c):
        cols = span_rows(c)
        total = stat_ref[k, :, cols] + stats_ref[k, 0, :, cols] + stats_ref[k, 1, :, cols] + stats_ref[k, 2, :, cols]
        return jnp.transpose(jnp.broadcast_to(total[0:1, :], (LANES, SPAN)))[:, 0:1] / D_INNER

    def values(rows, lanes):
        y_b = (y_ref[rows, lanes] + chans_ref[0:1, lanes] * x_ref[rows, lanes].astype(f32)).astype(bf16).astype(f32)
        gate = gate_ref[rows, lanes]
        sig = 1.0 / (1.0 + jnp.exp(-gate))
        return y_b, gate, sig

    def gating(c, _):
        rows = span_rows(c)
        xn = xn_ref[rows, :]
        total = jnp.zeros((SPAN, 1), f32)
        for k in range(HALF // 256):
            lanes = slice(k * 256, (k + 1) * 256)
            gate_ref[rows, lanes] = dot(xn, wgate_ref[:, lanes])
            y_b, gate, sig = values(rows, lanes)
            gated = y_b * (gate * sig)
            gated_ref[rows, lanes] = gated
            total = total + jnp.sum(gated * gated, axis=1, keepdims=True)
        put_stat(0, c, total)
        return 0

    lax.fori_loop(0, spans, gating, 0)
    squares = exchange(0)
    cots.finish()
    copies.settle(cots.own)
    outs.finish()
    copies.settle(outs_kept)

    def pull_out(c, _):
        rows = span_rows(c)
        back = back_ref[rows, :]
        total = jnp.zeros((SPAN, 1), f32)
        for k in range(HALF // 256):
            lanes = slice(k * 256, (k + 1) * 256)
            d_normed = dot(back, wout_ref[lanes, :], ((1,), (1,)))
            dn_ref[rows, lanes] = d_normed
            total = total + jnp.sum(gated_ref[rows, lanes] * (d_normed * chans_ref[1:2, lanes]), axis=1, keepdims=True)
        put_stat(1, c, total)
        return 0

    lax.fori_loop(0, spans, pull_out, 0)
    dots = exchange(1)
    for copy in squares:
        copy.wait_recv()

    def push_out(c, _):
        rows = span_rows(c)
        scale = lax.rsqrt(get_stat(0, c) + norm_eps)
        for k in range(HALF // 256):
            lanes = slice(k * 256, (k + 1) * 256)
            scaled = gated_ref[rows, lanes] * scale
            normed_ref[rows, lanes] = (scaled * chans_ref[1:2, lanes]).astype(bf16)
            dgain_ref[0:1, lanes] += jnp.sum(scaled * dn_ref[rows, lanes], axis=0, keepdims=True)
        normed = normed_ref[rows, :]
        for k in range(D // 256):
            cols = slice(k * 256, (k + 1) * 256)
            mix_ref[rows, cols] = dot(normed, wout_ref[:, cols]).astype(bf16)
        return 0

    lax.fori_loop(0, spans, push_out, 0)
    copies.drain()
    mixes = GroupScatter(copies, mix_ref, mix_bufs)
    mixes.to_t0(3)
    mixes.to_t0(1)
    for q in range(2):
        normed = normed_ref[:, q * HALF // 2 : (q + 1) * HALF // 2]
        for k in range(D // 512):
            cols = slice(k * 512, (k + 1) * 512)
            wout_ref[q * HALF // 2 : (q + 1) * HALF // 2, cols] = dot(normed, back_ref[:, cols], ((0,), (0,))).astype(bf16)
    g_out = GradientSum(copies, wout_ref, out_rows, go_bufs, False)
    g_out.cores(0)
    g_out.cores(1)
    for copy in dots:
        copy.wait_recv()

    def back_gate(c, _):
        rows = span_rows(c)
        scale = lax.rsqrt(get_stat(0, c) + norm_eps)
        pulled = get_stat(1, c) * (scale * scale * scale)
        for k in range(HALF // LANES):
            lanes = slice(k * LANES, (k + 1) * LANES)
            y_b, gate, sig = values(rows, lanes)
            d_gated = scale * (dn_ref[rows, lanes] * chans_ref[1:2, lanes]) - gated_ref[rows, lanes] * pulled
            dy_ref[rows, lanes] = (d_gated * (gate * sig)).astype(bf16)
            dgate_ref[rows, lanes] = (d_gated * y_b * (sig * (1.0 + gate * (1.0 - sig)))).astype(bf16)
        return 0

    lax.fori_loop(0, spans, back_gate, 0)
    copies.keep(dgate_ref, dgate_out)
    g_out.to_sides(0)
    s_ref[...] = jnp.zeros_like(s_ref)
    hsum_ref[...] = jnp.zeros_like(hsum_ref)
    dskip_ref[...] = jnp.zeros_like(dskip_ref)
    dtaps_ref[...] = jnp.zeros_like(dtaps_ref)

    def local_states(step, _):
        c = spans - 1 - step
        rows = span_rows(c)
        cum = cum_ref[rows, :]
        decay = jnp.exp(cum[SPAN - 1 : SPAN, :]) * carry_ref[pl.ds(c, 1), :]
        gain = jnp.exp(cum) * marks_ref[rows, 7:8]
        cc = c_ref[rows, :]
        for q in range(PAIRS):
            lanes = slice(q * LANES, (q + 1) * LANES)
            dyg = (dy_ref[rows, lanes].astype(f32) * own_pair(gain, 2 * q)).astype(bf16)
            dyg_ref[rows, lanes] = dyg
            ds = s_ref[:, lanes]
            dn_ref[pl.ds(pl.multiple_of(c * STATE, STATE), STATE), lanes] = ds
            s_ref[:, lanes] = ds * own_pair(decay, 2 * q) + dot(cc, dyg, ((0,), (0,)))
        return 0

    lax.fori_loop(0, spans, local_states, 0)
    passb_ref[...] = s_ref[...].astype(bf16)
    state = copies.send(passb_ref, gotb_ref, PART)

    width = D // 4
    g_gate = GradientSum(copies, win_ref, own_rows, gg_bufs, True)

    def gate_gradient(far):
        for half in range(2):
            first = pl.multiple_of(((1 - p if far else p) * 2 + half) * width, width)
            piece = dot(xn_ref[:, pl.ds(first, width)], dgate_ref[...], ((0,), (0,)))
            win_ref[pl.ds(first, width), 0:HALF] = piece.astype(bf16)

    gate_gradient(True)
    g_gate.cores(0)
    gate_gradient(False)
    g_gate.cores(1)
    g_out.to_sides(1)
    g_gate.to_sides(0)

    def inside(c, _):
        rows = span_rows(c)
        cum = cum_ref[rows, :]
        fore_log = jnp.transpose(cum)
        back_log = cum - jnp.log(dt_ref[rows, :])
        b = b_ref[rows, :]
        cc = c_ref[rows, :]
        scores = dot(b, cc, ((1,), (1,)))
        row = lax.broadcasted_iota(jnp.int32, (SPAN, SPAN), 0)
        col = lax.broadcasted_iota(jnp.int32, (SPAN, SPAN), 1)
        mask = (col >= row) & (segc_ref[pl.ds(pl.multiple_of(FRONT + c * SPAN, FRONT), SPAN), :] == segr_ref[pl.ds(c, 1), :])
        lane = lax.broadcasted_iota(jnp.int32, (SPAN, LANES), 1)
        d_scores = jnp.zeros((SPAN, SPAN), f32)
        dc = jnp.zeros((SPAN, STATE), f32)
        for q in range(PAIRS):
            lanes = slice(q * LANES, (q + 1) * LANES)
            x = x_ref[rows, lanes]
            dy = dy_ref[rows, lanes]
            xf = x.astype(f32)
            parts = []
            for k in range(2):
                h = lane_of(2 * q + k)
                gap = fore_log[h : h + 1, :] - back_log[:, h : h + 1]
                decay_mat = jnp.exp(jnp.where(mask, gap, -1e30))
                parts.append(dot((scores * decay_mat).astype(bf16), dy))
                own = (lane < HEADDIM) if k == 0 else (lane >= HEADDIM)
                d_weights = dot(jnp.where(own, xf, 0.0).astype(bf16), dy, ((1,), (1,)))
                d_scores = d_scores + d_weights * decay_mat
            dxi_ref[rows, lanes] = jnp.where(lane < HEADDIM, parts[0], parts[1])
            dc = dc + dot(dyg_ref[rows, lanes], st_ref[c, :, lanes].astype(bf16), ((1,), (1,)))
            dskip_ref[0:1, lanes] += jnp.sum(dy.astype(f32) * xf, axis=0, keepdims=True)
        d_scores_b = d_scores.astype(bf16)
        db_ref[rows, :] = dot(d_scores_b, cc)
        dc_ref[rows, :] = dc + dot(d_scores_b, b, ((0,), (0,)))
        return 0

    lax.fori_loop(0, spans, inside, 0)
    g_out.to_part()
    g_gate.to_sides(1)
    mixes.to_t1()
    state.wait_recv()
    s_ref[...] = gotb_ref[...].astype(f32) * (1 - p).astype(f32)

    def across_spans(step, _):
        c = spans - 1 - step
        rows = span_rows(c)
        dt = dt_ref[rows, :]
        cum = cum_ref[rows, :]
        last = cum[SPAN - 1 : SPAN, :]
        end_weight = jnp.exp(last - cum) * dt * marks_ref[rows, 6:7]
        decay = jnp.exp(last) * carry_ref[pl.ds(c, 1), :]
        b = b_ref[rows, :]
        db = db_ref[rows, :]
        edges = []
        for q in range(PAIRS):
            lanes = slice(q * LANES, (q + 1) * LANES)
            xf = x_ref[rows, lanes].astype(f32)
            dyf = dy_ref[rows, lanes].astype(f32)
            ew = own_pair(end_weight, 2 * q)
            dec = own_pair(decay, 2 * q)
            entering = s_ref[:, lanes]
            ds = dn_ref[pl.ds(pl.multiple_of(c * STATE, STATE), STATE), lanes] + entering
            s_ref[:, lanes] = entering * dec
            ds_b = ds.astype(bf16)
            db = db + dot((xf * ew).astype(bf16), ds_b, ((1,), (1,)))
            dx_state = dot(b, ds_b) * ew
            dx = dxi_ref[rows, lanes] + dx_state
            edges.append(
                jnp.sum(ds * st_ref[c, :, lanes], axis=0, keepdims=True) * dec
                + jnp.sum(dx_state * xf, axis=0, keepdims=True)
            )
            prod_ref[0:SPAN, lanes] = dyf * y_ref[rows, lanes]
            prod_ref[SPAN : 2 * SPAN, lanes] = xf * dx
            d_x = (dx + dyf * chans_ref[0:1, lanes]).astype(bf16).astype(f32)
            dtot_ref[rows, lanes] = d_x * dtot_ref[rows, lanes]
        dtot_ref[rows, HALF : HALF + STATE] = db * dtot_ref[rows, HALF : HALF + STATE]
        dtot_ref[rows, HALF + STATE :] = dc_ref[rows, :] * dtot_ref[rows, HALF + STATE :]
        sums = own_sums(prod_ref[0 : 2 * SPAN, :])
        out_sum, in_sum = sums[:SPAN], sums[SPAN:]
        edge_sum = own_sums(jnp.broadcast_to(jnp.concatenate(edges, axis=1), (TILE, HALF)))[0:1]
        at_last = lax.broadcasted_iota(jnp.int32, (SPAN, LANES), 0) == SPAN - 1
        d_cum = out_sum - in_sum + jnp.where(at_last, edge_sum, 0.0)
        row = lax.broadcasted_iota(jnp.int32, (SPAN, SPAN), 0)
        col = lax.broadcasted_iota(jnp.int32, (SPAN, SPAN), 1)
        d_log = dot((col >= row).astype(f32), d_cum, precision=exact_prec)
        z = z_ref[rows, :]
        small = jnp.exp(-jnp.abs(z))
        sig = jnp.where(z >= 0.0, 1.0, small) / (1.0 + small)
        ratio = jnp.where(dt > 1e-30, sig / jnp.maximum(dt, 1e-30), 1.0)
        d_dt = d_log * heads_ref[1:2, :] * sig + in_sum * ratio
        hsum_ref[0:1, :] += jnp.sum(d_log * dt, axis=0, keepdims=True)
        hsum_ref[1:2, :] += jnp.sum(d_dt, axis=0, keepdims=True)
        dmain_ref[rows, CHANS:MAIN] = head_lanes(d_dt, back=True).astype(bf16)
        return 0

    lax.fori_loop(0, spans, across_spans, 0)
    rims_ref[...] = dtot_ref[0:TILE, :]
    rim = copies.send(rims_ref, rimr_ref, PART)
    g_gate.to_part()
    rim.wait_recv()
    dtot_ref[pl.ds(spans * SPAN, TILE), :] = jnp.where(p == 0, rimr_ref[...], 0.0)

    def convolve(c, _):
        rows = span_rows(c)
        marks = marks_ref[rows, :]
        fore = pl.ds(pl.multiple_of(c * SPAN, SPAN), SPAN + FRONT)
        hind = pl.ds(pl.multiple_of(c * SPAN, SPAN), SPAN + TILE)
        for k in range(CHANS // LANES):
            lanes = slice(k * LANES, (k + 1) * LANES)
            later = dtot_ref[hind, lanes]
            earlier = convp_ref[fore, lanes].astype(f32)
            own = later[0:SPAN]
            d_conv = taps_ref[RIM : RIM + 1, lanes] * own
            dtaps_ref[RIM : RIM + 1, lanes] += jnp.sum(own * earlier[FRONT:], axis=0, keepdims=True)
            dtaps_ref[CONV : CONV + 1, lanes] += jnp.sum(own, axis=0, keepdims=True)
            for j in range(RIM):
                ahead = RIM - j
                d_conv = d_conv + taps_ref[j : j + 1, lanes] * later[ahead : ahead + SPAN] * marks[:, 3 + j : 4 + j]
                first = FRONT - ahead
                dtaps_ref[j : j + 1, lanes] += jnp.sum(
                    own * earlier[first : first + SPAN] * marks[:, j : j + 1], axis=0, keepdims=True
                )
            dmain_ref[rows, lanes] = d_conv.astype(bf16)
        return 0

    lax.fori_loop(0, spans, convolve, 0)
    copies.keep(dmain_ref, dmain_out)

    own_ref[...] = jnp.zeros_like(own_ref)
    for k in range(HALF // LANES):
        lanes = slice(k * LANES, (k + 1) * LANES)
        own_ref[OWN_NORM + k : OWN_NORM + k + 1, :] = dgain_ref[0:1, lanes]
        for j in range(CONV + 1):
            row = OWN_TAP + j * (HALF // LANES) + k
            own_ref[row : row + 1, :] = dtaps_ref[j : j + 1, lanes]
    for k in range(SIDE // LANES):
        lanes = slice(HALF + k * LANES, HALF + (k + 1) * LANES)
        for j in range(CONV + 1):
            row = OWN_SIDE + j * (SIDE // LANES) + k
            own_ref[row : row + 1, :] = dtaps_ref[j : j + 1, lanes]
    hsum_ref[0:1, :] = hsum_ref[0:1, :] * heads_ref[1:2, :]
    hsum_ref[2:3, :] = own_sums(dskip_ref[...])[0:1, :]
    lane8 = lax.broadcasted_iota(jnp.int32, (TILE, LANES), 1)
    own_ref[OWN_HEAD : OWN_HEAD + 3, :] = jnp.where(lane8 < HEADS, head_lanes(hsum_ref[...], back=True), 0.0)[0:3]

    gout_ref[...] = g_out.total(0)
    mixer = mix_ref[mixes.block(0), :].astype(f32) + mixes.finish()
    for k in range(D // HALF):
        kept = pl.ds(spans * STATE + k * tokens, tokens)
        dn_ref[kept, :] = mixer[:, k * HALF : (k + 1) * HALF]
        copies.keep(dn_ref.at[kept], mixer_out.at[:, pl.ds(k * HALF, HALF)])
    hid = h_ref[mixes.block(0), :].astype(f32)
    valid = valid_ref[...]
    counts = [jnp.sum(valid * jnp.sum(v * v, axis=1, keepdims=True), axis=0, keepdims=True) for v in (hid, mixer)]
    counts.append(jnp.sum(valid, axis=0, keepdims=True))
    scalars = jnp.zeros((1, LANES), f32)
    for k in range(3):
        scalars = jnp.where(lane == k, counts[k], scalars)
    own_ref[OWN_SUMS : OWN_SUMS + 1, :] = scalars
    g_gate.to_group()
    g_gate.finish()
    for i, block in enumerate(blocks):
        kept = pl.ds(2 * SPAN + i * own_rows, own_rows)
        gate_ref[kept, :] = g_gate.sums[i]
        copies.keep(gate_ref.at[kept], ggate_out.at[block[0], block[1]])
    copies.drain()


def end_kernel(
    dmain_hbm, dgate_hbm, win_hbm, wgate_hbm, xn_hbm, h_hbm, own_ref,
    dx_ref, gmo_ref, total_ref,
    dmain_ref, dgate_ref, win_ref, wgate_ref, xn_ref, h_ref, dxp_ref, dpre_ref, gm_ref, box_ref, boxes_ref, *rest,
):
    gm_bufs, dx_bufs, (local_sem, send_sem, recv_sem) = rest[:7], rest[7:11], rest[11:]
    neighbours = (*NEIGHBOURS, SIDE_CORE)
    greet(neighbours)
    p, t1, t0, _, _ = place()
    copies = Copies(local_sem, send_sem, recv_sem)
    got_main = copies.keep(dmain_hbm, dmain_ref)
    got_xn = copies.keep(xn_hbm, xn_ref)
    others = [
        copies.keep(src, dst)
        for src, dst in ((win_hbm, win_ref), (wgate_hbm, wgate_ref), (dgate_hbm, dgate_ref), (h_hbm, h_ref))
    ]
    blocks = group_blocks()
    tokens = dx_ref.shape[0]
    own_rows = gmo_ref.shape[2]
    width = D // 4
    dpre_ref[...] = jnp.zeros_like(dpre_ref)

    def grad_half(far):
        part = 1 - p if far else p

        def piece(i, _):
            first = pl.multiple_of((part * 2 + i) * width, width)
            xn = xn_ref[:, pl.ds(first, width)]
            for k in range(MAIN // 384):
                cols = slice(k * 384, (k + 1) * 384)
                gm_ref[pl.ds(first, width), cols] = dot(xn, dmain_ref[:, cols], ((0,), (0,))).astype(bf16)
            return 0

        lax.fori_loop(0, 2, piece, 0)

    def token_grad(block, keep):
        rows = block_rows(block, tokens)
        d_main = dmain_ref[rows, :]
        d_gate = dgate_ref[rows, :]
        hid = h_ref[rows, :].astype(f32)
        scale = lax.rsqrt(jnp.sum(hid * hid, axis=1, keepdims=True) / D + norm_eps)
        for k in range(D // 512):
            cols = slice(k * 512, (k + 1) * 512)
            part = dot(d_main, win_ref[cols, :], ((1,), (1,))) + dot(d_gate, wgate_ref[cols, :], ((1,), (1,)))
            dpre_ref[0:1, cols] += jnp.sum(h_ref[rows, cols].astype(f32) * scale * part, axis=0, keepdims=True)
            if keep:
                dx_ref[:, cols] = part
            else:
                dxp_ref[rows, cols] = part.astype(bf16)

    copies.settle(got_main)
    copies.settle(got_xn)
    grad_half(True)
    greeted(neighbours)
    g_main = GradientSum(copies, gm_ref, own_rows, gm_bufs, True)
    g_main.cores(0)
    for copy in others:
        copies.settle(copy)
    dxs = GroupScatter(copies, dxp_ref, dx_bufs)
    token_grad(blocks[3], False)
    dxs.to_t0(3)
    g_main.to_sides(0)
    grad_half(False)
    g_main.cores(1)
    token_grad(blocks[1], False)
    dxs.to_t0(1)
    g_main.to_sides(1)
    token_grad(blocks[2], False)
    g_main.to_part()
    token_grad(blocks[0], True)
    box_ref[0] = own_ref[...]
    for k in range(D // LANES):
        box_ref[0, k : k + 1, :] = dpre_ref[0:1, k * LANES : (k + 1) * LANES]

    def small_step(k, hops):
        return [copies.send(box_ref.at[k], boxes_ref.at[k, i], flips) for i, flips in enumerate(hops)]

    def small_add(k, sent):
        total = box_ref[k]
        for i, copy in enumerate(sent):
            copy.wait_recv()
            total = total + boxes_ref[k, i]
        box_ref[k + 1] = total

    small = small_step(0, (CORE, SIDEWAYS, SIDE_CORE))
    dxs.to_t1()
    small_add(0, small)
    small = small_step(1, (PART,))
    small_add(1, small)
    small = small_step(2, (T0, T1, DIAG))
    g_main.to_group()
    dx_ref[...] += dxs.finish()
    small_add(2, small)
    total_ref[...] = jnp.zeros_like(total_ref)
    total_ref[0:NORM_ROW, :] = box_ref[3, 0:NORM_ROW]
    third = QUARTER // LANES
    runs = [(OWN_NORM, NORM_ROW)]
    runs += [(OWN_TAP + j * 2 * third, TAP_ROW + j * TAP_ROWS) for j in range(CONV + 1)]
    for i, block in enumerate(blocks):
        source = box_ref.at[2] if i == 0 else boxes_ref.at[2, i - 1]
        place_at = (block[0] * 2 + block[1]) * third
        for own, first in runs:
            for k in range(2 * third):
                row = first + k // third * (D_INNER // 2 // LANES) + place_at + k % third
                total_ref[pl.ds(row, 1), :] = source[own + k : own + k + 1, :]
    for j in range(CONV + 1):
        row, own = TAP_ROW + TAP_ROWS * j + D_INNER // LANES, OWN_SIDE + j * (SIDE // LANES)
        total_ref[row : row + SIDE // LANES, :] = box_ref[3, own : own + SIDE // LANES]
    lane8 = lax.broadcasted_iota(jnp.int32, (TILE, LANES), 1)
    d_rate, d_shift, d_skip = (
        jnp.broadcast_to(box_ref[3, OWN_HEAD + k : OWN_HEAD + k + 1], (TILE, LANES)) for k in range(3)
    )
    spill = LANES - 2 * HEADS
    joined = d_shift + pltpu.roll(d_rate, HEADS, 1) + jnp.where(lane8 >= 2 * HEADS, pltpu.roll(d_skip, 2 * HEADS, 1), 0.0)
    total_ref[HEAD_ROW : HEAD_ROW + 1, :] = joined[0:1]
    spilled = jnp.where(lane8 < HEADS - spill, pltpu.roll(d_skip, LANES - spill, 1), 0.0)
    total_ref[HEAD_ROW + 1 : HEAD_ROW + 2, :] = spilled[0:1]
    total_ref[SMALL_ROWS : SMALL_ROWS + 1, :] = box_ref[3, OWN_SUMS : OWN_SUMS + 1]
    g_main.finish()
    for i, block in enumerate(blocks):
        gmo_ref[block[0], block[1]] = g_main.sums[i]
    copies.drain()


def update_kernel(
    hid_ref, mixer_ref, dx_ref, back_ref, pre_ref, gmain_ref, ggate_ref, gout_ref, total_ref,
    inw_ref, inm_ref, inv_ref, outw_ref, outm_ref, outv_ref, small_ref, smallm_ref, smallv_ref,
    output_ref, gh_ref, inm_out, inv_out, inw_out, outm_out, outv_out, outw_out, smallm_out, smallv_out, smallw_out, rms_ref,
):
    hid = hid_ref[...].astype(f32)
    output_ref[...] = (hid + mixer_ref[...]).astype(bf16)
    scale = lax.rsqrt(jnp.sum(hid * hid, axis=1, keepdims=True) / D + norm_eps)
    d_pre = dx_ref[...] * pre_ref[...]
    pulled = jnp.sum(hid * d_pre, axis=1, keepdims=True) / D * (scale * scale * scale)
    gh_ref[...] = back_ref[...].astype(f32) + scale * d_pre - hid * pulled

    def update(refs, outs, cols, grad, rate=0.02, decay=0.1):
        weight, moment, second = (ref[:, cols] for ref in refs)
        for out, value in zip(outs, adamw(weight, moment, second, grad, rate, decay)):
            out[:, cols] = value

    every = slice(None)
    update((outw_ref, outm_ref, outv_ref), (outm_out, outv_out, outw_out), every, gout_ref[...])
    in_refs, in_outs = (inw_ref, inm_ref, inv_ref), (inm_out, inv_out, inw_out)
    for j in range(TP):
        for k, chans in enumerate(own_chans(j)):
            part = slice(k * QUARTER, (k + 1) * QUARTER)
            update(in_refs, in_outs, chans, ggate_ref[j // 2, j % 2, :, part])
            scan = slice(D_INNER + chans.start, D_INNER + chans.stop)
            update(in_refs, in_outs, scan, gmain_ref[j // 2, j % 2, :, part])
    rest_grad = gmain_ref[0, 0, :, HALF:] + gmain_ref[0, 1, :, HALF:] + gmain_ref[1, 0, :, HALF:] + gmain_ref[1, 1, :, HALF:]
    first = 2 * D_INNER
    update(in_refs, in_outs, slice(first, first + SIDE), rest_grad[:, :SIDE])
    update(in_refs, in_outs, slice(first + SIDE, first + SIDE + HEADS), rest_grad[:, SIDE : SIDE + HEADS])

    @pl.when(pl.program_id(0) == 0)
    def _():
        update(
            (small_ref, smallm_ref, smallv_ref), (smallm_out, smallv_out, smallw_out), every, total_ref[0:SMALL_ROWS, :], 0.2, 0.0
        )
        totals = total_ref[SMALL_ROWS:, :]
        rms_ref[...] = jnp.sqrt(totals / (totals[0:1, 2:3] * D))


def linked(kernel, name, collective_id, in_specs, outs, scratch):
    return pl.pallas_call(
        kernel,
        name=name,
        in_specs=in_specs,
        out_shape=tuple(o for o, _ in outs),
        out_specs=tuple(s for _, s in outs),
        scratch_shapes=scratch,
        compiler_params=pltpu.CompilerParams(
            collective_id=collective_id, has_side_effects=True, vmem_limit_bytes=VMEM_LIMIT
        ),
    )


def shards_linked(
    hidden, cotangent, segments, valid, in_w, in_m, in_v, out_w, out_m, out_v, small_w, small_m, small_v,
):
    part = lax.axis_index("part")
    own_rows, out_rows = in_w.shape[0], out_w.shape[0]
    tok_rows = hidden.shape[1]
    rows = tok_rows * TP
    spans = rows // SPAN
    edge = jnp.full((FRONT,), -1, jnp.int32)
    seg_wide = lax.dynamic_slice_in_dim(jnp.concatenate([edge, segments[0], edge]), part * rows, rows + 2 * FRONT)
    seg_spans = seg_wide[FRONT : FRONT + rows].reshape(spans, SPAN)
    valid_col = valid[0].astype(f32)[:, None]
    small_size = small_w.shape[0]

    def small_box(array):
        return jnp.pad(array, (0, SMALL_ROWS * LANES - small_size)).reshape(SMALL_ROWS, LANES)

    small_w, small_m, small_v = small_box(small_w), small_box(small_m), small_box(small_v)
    pre_row = small_w[:NORM_ROW].reshape(1, D)

    wide = (rows, D)
    half = (rows, HALF)
    lanes = (rows, LANES)
    side = (rows, STATE)
    state = (STATE, HALF)
    main_outs = (
        (shape(wide, bf16), HBM),
        (shape(wide, bf16), HBM),
        (shape((D, MAIN), bf16), HBM),
        (shape((D, HALF), bf16), HBM),
        (shape(half, bf16), HBM),
        (shape((rows, MAIN), bf16), HBM),
        (shape((tok_rows, D), bf16), HBM),
        (shape((tok_rows, D), f32), HBM),
        (shape((2, 2, own_rows, HALF), f32), HBM),
        (shape((OWN_ROWS, LANES), f32), VMEM),
        (shape((out_rows, D), f32), VMEM),
    )
    main_scratch = (
        (wide, bf16),
        (wide, bf16),
        ((D, MAIN), bf16),
        ((rows + FRONT, CHANS), bf16),
        (half, bf16),
        (side, bf16),
        (side, bf16),
        ((rows + FRONT, CHANS), f32),
        (lanes, f32),
        (lanes, f32),
        (lanes, f32),
        (half, f32),
        ((spans, *state), f32),
        ((D, HALF), bf16),
        ((HALF, D), bf16),
        (wide, bf16),
        (half, bf16),
        (wide, bf16),
        (half, bf16),
        (half, bf16),
        ((rows, MAIN), bf16),
        ((TILE, HALF), f32),
        ((TILE, CHANS), f32),
        ((TILE, LANES), f32),
        ((TILE, HALF), f32),
        ((rows, TILE), f32),
        ((spans, LANES), f32),
        ((2, 2, own_rows, MAIN), bf16),
        ((2, 2, own_rows, HALF), bf16),
        ((out_rows, D), bf16),
        ((tok_rows, D), bf16),
        (state, f32),
        (state, bf16),
        (state, bf16),
        ((FRONT, CHANS), bf16),
        (half, f32),
        (half, f32),
        (half, f32),
        ((2, TILE, rows), f32),
        ((2, 3, TILE, rows), f32),
        (half, bf16),
        (state, bf16),
        (state, bf16),
        ((TILE, CHANS), f32),
        ((TILE, CHANS), f32),
        (side, f32),
        (side, f32),
        ((TILE, LANES), f32),
        ((TILE, HALF), f32),
        ((TILE, CHANS), f32),
    )
    hidden_all, x_normed, w_in, w_gate, d_gate, d_main, back_own, mixer, g_gate, own_small, g_out = linked(
        functools.partial(main_kernel, spans), "main", 1, [*[HBM] * 3, *[VMEM] * 6], main_outs,
        [
            *[pltpu.VMEM(dims, dtype) for dims, dtype in main_scratch],
            *sum_buffers(out_rows, D, False),
            *sum_buffers(own_rows, HALF, True),
            *scatter_buffers(tok_rows),
            *sems(160, 32),
        ],
    )(hidden[0], in_w, out_w, in_w[:, 2 * D_INNER :], cotangent[0], valid_col, small_w, seg_wide[:, None], seg_spans)

    d_x_normed, g_main, totals = linked(
        end_kernel, "end", 2, [*[HBM] * 6, VMEM],
        [
            (shape((tok_rows, D), f32), VMEM),
            (shape((2, 2, own_rows, MAIN), f32), VMEM),
            (shape((BOX_ROWS, LANES), f32), VMEM),
        ],
        [
            pltpu.VMEM((rows, MAIN), bf16),
            pltpu.VMEM(half, bf16),
            pltpu.VMEM((D, MAIN), bf16),
            pltpu.VMEM((D, HALF), bf16),
            pltpu.VMEM(wide, bf16),
            pltpu.VMEM(wide, bf16),
            pltpu.VMEM(wide, bf16),
            pltpu.VMEM((TILE, D), f32),
            pltpu.VMEM((D, MAIN), bf16),
            pltpu.VMEM((4, OWN_ROWS, LANES), f32),
            pltpu.VMEM((3, 3, OWN_ROWS, LANES), f32),
            *sum_buffers(own_rows, MAIN, True),
            *scatter_buffers(tok_rows),
            *sems(60, 6),
        ],
    )(d_main, d_gate, w_in, w_gate, x_normed, hidden_all, own_small)

    steps = own_rows // TILE

    def cut(dims, axis=0):
        block = tuple(size // steps if k == axis else size for k, size in enumerate(dims))
        return pl.BlockSpec(block, lambda i: tuple(i if k == axis else 0 for k in range(len(dims))))

    def fixed(dims):
        return pl.BlockSpec(dims, lambda i: (0, 0))

    tokens, matrix_in, matrix_out, small_dims = (tok_rows, D), in_w.shape, out_w.shape, (SMALL_ROWS, LANES)
    out_dims = [tokens] * 2 + [matrix_in] * 3 + [matrix_out] * 3
    (
        output, grad_hidden, in_m_new, in_v_new, in_w_new, out_m_new, out_v_new, out_w_new,
        small_m_new, small_v_new, small_w_new, rms,
    ) = pl.pallas_call(
        update_kernel,
        name="update",
        grid=(steps,),
        in_specs=[
            *[cut(tokens)] * 4,
            fixed((1, D)),
            cut(g_main.shape, 2),
            cut(g_gate.shape, 2),
            cut(matrix_out),
            fixed((BOX_ROWS, LANES)),
            *[cut(matrix_in)] * 3,
            *[cut(matrix_out)] * 3,
            *[fixed(small_dims)] * 3,
        ],
        out_shape=[
            *[shape(dims, bf16 if k == 0 else f32) for k, dims in enumerate(out_dims)],
            *[shape(small_dims, f32)] * 3,
            shape((TILE, LANES), f32),
        ],
        out_specs=[*[cut(dims) for dims in out_dims], *[fixed(small_dims)] * 3, fixed((TILE, LANES))],
        compiler_params=pltpu.CompilerParams(vmem_limit_bytes=VMEM_LIMIT),
    )(
        hidden[0], mixer, d_x_normed, back_own, pre_row, g_main, g_gate, g_out, totals,
        in_w, in_m, in_v, out_w, out_m, out_v, small_w, small_m, small_v,
    )
    small_m_new, small_v_new, small_w_new = (
        array.reshape(-1)[:small_size] for array in (small_m_new, small_v_new, small_w_new)
    )
    return (
        output[None], grad_hidden[None], in_m_new, in_v_new, in_w_new, out_m_new, out_v_new, out_w_new,
        small_m_new, small_v_new, small_w_new, rms[0, :2],
    )


def solution(mesh):
    seq, wt = mesh.shape["seq"], mesh.shape["wt"]
    split = Mesh(mesh.devices.reshape(seq // TP, 2, 2, wt // 2, 2), EVERYONE)
    streams = ("w1", "w0")
    tokens = ("part", "t1", "t0")
    matrix = P(EVERYONE, None)
    stream = P(streams, tokens, None)
    size = mesh.devices.size
    fits = seq == 2 * TP and wt == 4 and D // size % 16 == 0 and D_INNER // size % 16 == 0
    return jax.shard_map(
        shards_linked if fits else shards_general,
        mesh=split,
        in_specs=(
            stream, stream, P(streams, None), P(streams, tokens), matrix, matrix, matrix, matrix, matrix, matrix, P(), P(), P(),
        ),
        out_specs=(stream, stream, matrix, matrix, matrix, matrix, matrix, matrix, P(), P(), P(), P()),
        check_vma=False,
    )
```

```python
import functools

import jax
import jax.numpy as jnp
from jax import lax
from jax.experimental import pallas as pl
from jax.experimental.pallas import tpu as pltpu
from jax.sharding import Mesh
from jax.sharding import PartitionSpec as P

D = 1536
D_INNER = 3072
HEADS = 48
HEADDIM = 64
STATE = 128
CONV = 4
SPAN = 256
STEP = 4
CONVCH = 3328
TP = 4
RIM = CONV - 1
LANES = 128
HALF = D_INNER // TP
LOCAL_HEADS = HEADS // TP
PAIRS = LOCAL_HEADS // 2
SIDE = 2 * STATE
COL_SIDE = HALF
COL_DT = HALF + SIDE
COL_GATE = COL_DT + LANES
COLS = COL_GATE + HALF

bf16 = jnp.bfloat16
f32 = jnp.float32
exact_prec = lax.Precision.HIGHEST
norm_eps = 1e-05
adam_eps = 1e-08


def dot(a, b, dims=((1,), (0,)), precision=None):
    return lax.dot_general(a, b, (dims, ((), ())), precision=precision, preferred_element_type=f32)


def unpack_small(small):
    first = D
    second = first + D_INNER
    third = second + CONV * CONVCH
    fourth = third + CONVCH
    fifth = fourth + HEADS
    sixth = fifth + HEADS
    return (
        small[:first],
        small[first:second],
        small[second:third].reshape(CONV, CONVCH),
        small[third:fourth],
        small[fourth:fifth],
        small[fifth:sixth],
        small[sixth:],
    )


def adamw(weight, moment, second, grad, rate, decay):
    moment_new = 0.5 * moment + 0.5 * grad
    second_new = 0.5 * second + 0.5 * grad * grad
    first_hat = moment_new / (1.0 - 0.5**STEP)
    second_hat = second_new / (1.0 - 0.5**STEP)
    weight_new = weight - rate * (first_hat / (jnp.sqrt(second_hat) + adam_eps) + decay * weight)
    return (moment_new, second_new, weight_new)


def pair_cols(cols, h):
    lane = lax.broadcasted_iota(jnp.int32, (cols.shape[0], LANES), 1)
    return jnp.where(lane < HEADDIM, cols[:, h : h + 1], cols[:, h + 1 : h + 2])


def span_rows(c):
    return pl.ds(pl.multiple_of(c * SPAN, SPAN), SPAN)


def span_decay(dt_ref, rate_ref, c, at=0):
    dt = dt_ref[span_rows(c), :]
    row = lax.broadcasted_iota(jnp.int32, (SPAN, SPAN), 0)
    col = lax.broadcasted_iota(jnp.int32, (SPAN, SPAN), 1)
    lower = (row >= col).astype(f32)
    return dt, dot(lower, dt * rate_ref[at : at + 1, :], precision=exact_prec)


def state_kernel(spans, x_ref, b_ref, dt_ref, rate_ref, keep_ref, carry_ref, s_ref, dec_ref):
    s_ref[...] = jnp.zeros_like(s_ref)
    dec_ref[...] = jnp.ones_like(dec_ref)

    def body(c, _):
        rows = span_rows(c)
        dt, cum = span_decay(dt_ref, rate_ref, c)
        last = cum[SPAN - 1 : SPAN, :]
        end_weight = jnp.exp(last - cum) * dt * keep_ref[rows, :]
        decay = jnp.exp(last) * carry_ref[pl.ds(c, 1), :]
        dec_ref[...] = dec_ref[...] * decay
        b = b_ref[rows, :]
        for p in range(PAIRS):
            lanes = slice(p * LANES, (p + 1) * LANES)
            xw = (x_ref[rows, lanes].astype(f32) * pair_cols(end_weight, 2 * p)).astype(bf16)
            fresh = dot(b, xw, ((0,), (0,)))
            s_ref[:, lanes] = s_ref[:, lanes] * pair_cols(decay, 2 * p) + fresh
        return 0

    lax.fori_loop(0, spans, body, 0)


def scan_kernel(
    spans, x_ref, b_ref, c_ref, dt_ref, rate_ref, segc_ref, segr_ref, keep_ref, inflow_ref, carry_ref, s_in_ref,
    y_ref, st_ref, s_ref,
):
    s_ref[...] = s_in_ref[...]

    def body(c, _):
        rows = span_rows(c)
        dt, cum = span_decay(dt_ref, rate_ref, c)
        last = cum[SPAN - 1 : SPAN, :]
        end_weight = jnp.exp(last - cum) * dt * keep_ref[rows, :]
        decay = jnp.exp(last) * carry_ref[pl.ds(c, 1), :]
        gain = jnp.exp(cum) * inflow_ref[rows, :]
        back_log = jnp.transpose(cum - jnp.log(dt))
        b = b_ref[rows, :]
        cc = c_ref[rows, :]
        scores = dot(cc, b, ((1,), (1,)))
        row = lax.broadcasted_iota(jnp.int32, (SPAN, SPAN), 0)
        col = lax.broadcasted_iota(jnp.int32, (SPAN, SPAN), 1)
        mask = (row >= col) & (segc_ref[rows, :] == segr_ref[pl.ds(c, 1), :])
        lane = lax.broadcasted_iota(jnp.int32, (SPAN, LANES), 1)
        st_ref[c] = s_ref[...]
        for p in range(PAIRS):
            lanes = slice(p * LANES, (p + 1) * LANES)
            x = x_ref[rows, lanes]
            parts = []
            for h in (2 * p, 2 * p + 1):
                gap = cum[:, h : h + 1] - back_log[h : h + 1, :]
                weights = scores * jnp.exp(jnp.where(mask, gap, -1e30))
                parts.append(dot(weights.astype(bf16), x))
            y = jnp.where(lane < HEADDIM, parts[0], parts[1])
            state = s_ref[:, lanes]
            y = y + dot(cc, state.astype(bf16)) * pair_cols(gain, 2 * p)
            y_ref[rows, lanes] = y
            xw = (x.astype(f32) * pair_cols(end_weight, 2 * p)).astype(bf16)
            s_ref[:, lanes] = state * pair_cols(decay, 2 * p) + dot(b, xw, ((0,), (0,)))
        return 0

    lax.fori_loop(0, spans, body, 0)


def state_back_kernel(spans, dy_ref, c_ref, dt_ref, rate_ref, inflow_ref, carry_ref, s_ref):
    s_ref[...] = jnp.zeros_like(s_ref)

    def body(step, _):
        c = spans - 1 - step
        rows = span_rows(c)
        dt, cum = span_decay(dt_ref, rate_ref, c)
        decay = jnp.exp(cum[SPAN - 1 : SPAN, :]) * carry_ref[pl.ds(c, 1), :]
        gain = jnp.exp(cum) * inflow_ref[rows, :]
        cc = c_ref[rows, :]
        for p in range(PAIRS):
            lanes = slice(p * LANES, (p + 1) * LANES)
            dyg = (dy_ref[rows, lanes].astype(f32) * pair_cols(gain, 2 * p)).astype(bf16)
            s_ref[:, lanes] = s_ref[:, lanes] * pair_cols(decay, 2 * p) + dot(cc, dyg, ((0,), (0,)))
        return 0

    lax.fori_loop(0, spans, body, 0)


def head_sums(values):
    width = values.shape[1]
    chan = lax.broadcasted_iota(jnp.int32, (width, LANES), 0)
    head = lax.broadcasted_iota(jnp.int32, (width, LANES), 1)
    pick = (chan // HEADDIM == head).astype(bf16)
    high = values.astype(bf16)
    low = (values - high.astype(f32)).astype(bf16)
    return dot(high, pick) + dot(low, pick)


def scan_back_kernel(
    spans, x_ref, b_ref, c_ref, dt_ref, ratio_ref, sig_ref, rate_ref, segc_ref, segr_ref, keep_ref, inflow_ref, carry_ref, skip_ref,
    y_ref, st_ref, dy_ref, ds_out_ref,
    dx_ref, db_ref, dc_ref, ddt_ref, drate_ref, dskip_ref,
    ds_ref, prod_ref,
):
    ds_ref[...] = ds_out_ref[...]
    drate_ref[...] = jnp.zeros_like(drate_ref)
    dskip_ref[...] = jnp.zeros_like(dskip_ref)

    def body(step, _):
        c = spans - 1 - step
        rows = span_rows(c)
        dt, cum = span_decay(dt_ref, rate_ref, c)
        last = cum[SPAN - 1 : SPAN, :]
        end_weight = jnp.exp(last - cum) * dt * keep_ref[rows, :]
        decay = jnp.exp(last) * carry_ref[pl.ds(c, 1), :]
        gain = jnp.exp(cum) * inflow_ref[rows, :]
        fore_log = jnp.transpose(cum)
        back_log = cum - jnp.log(dt)
        b = b_ref[rows, :]
        cc = c_ref[rows, :]
        scores = dot(b, cc, ((1,), (1,)))
        row = lax.broadcasted_iota(jnp.int32, (SPAN, SPAN), 0)
        col = lax.broadcasted_iota(jnp.int32, (SPAN, SPAN), 1)
        mask = (col >= row) & (segc_ref[rows, :] == segr_ref[pl.ds(c, 1), :])
        lane = lax.broadcasted_iota(jnp.int32, (SPAN, LANES), 1)
        d_scores = jnp.zeros((SPAN, SPAN), f32)
        db = jnp.zeros((SPAN, STATE), f32)
        dc = jnp.zeros((SPAN, STATE), f32)
        state_row = []
        dx_state_row = []
        for p in range(PAIRS):
            lanes = slice(p * LANES, (p + 1) * LANES)
            x = x_ref[rows, lanes]
            dy = dy_ref[rows, lanes]
            xf = x.astype(f32)
            dyf = dy.astype(f32)
            parts = []
            for k in range(2):
                h = 2 * p + k
                gap = fore_log[h : h + 1, :] - back_log[:, h : h + 1]
                decay_mat = jnp.exp(jnp.where(mask, gap, -1e30))
                weights = (scores * decay_mat).astype(bf16)
                parts.append(dot(weights, dy))
                own = (lane < HEADDIM) if k == 0 else (lane >= HEADDIM)
                d_weights = dot(jnp.where(own, xf, 0.0).astype(bf16), dy, ((1,), (1,)))
                d_scores = d_scores + d_weights * decay_mat
            dx = jnp.where(lane < HEADDIM, parts[0], parts[1])
            dyg = (dyf * pair_cols(gain, 2 * p)).astype(bf16)
            ew = pair_cols(end_weight, 2 * p)
            xw = (xf * ew).astype(bf16)
            state = st_ref[c, :, lanes]
            ds = ds_ref[:, lanes]
            state_b = state.astype(bf16)
            ds_b = ds.astype(bf16)
            dc = dc + dot(dyg, state_b, ((1,), (1,)))
            db = db + dot(xw, ds_b, ((1,), (1,)))
            dx_state = dot(b, ds_b) * ew
            dx = dx + dx_state
            dec = pair_cols(decay, 2 * p)
            state_row.append(jnp.sum(ds * state, axis=0, keepdims=True) * dec)
            dx_state_row.append(jnp.sum(dx_state * xf, axis=0, keepdims=True))
            ds_ref[:, lanes] = ds * dec + dot(cc, dyg, ((0,), (0,)))
            prod_ref[0:SPAN, lanes] = dyf * y_ref[rows, lanes]
            prod_ref[SPAN : 2 * SPAN, lanes] = xf * dx
            dskip_ref[0:1, lanes] += jnp.sum(dyf * xf, axis=0, keepdims=True)
            dx_ref[rows, lanes] = (dx + dyf * skip_ref[0:1, lanes]).astype(bf16)
        d_scores_b = d_scores.astype(bf16)
        db_ref[rows, :] = db + dot(d_scores_b, cc)
        dc_ref[rows, :] = dc + dot(d_scores_b, b, ((0,), (0,)))
        sums = head_sums(prod_ref[...])
        out_sum, in_sum = sums[:SPAN], sums[SPAN:]
        edge = jnp.concatenate(state_row, axis=1) + jnp.concatenate(dx_state_row, axis=1)
        edge_sum = head_sums(jnp.broadcast_to(edge, (8, HALF)))[0:1]
        at_last = lax.broadcasted_iota(jnp.int32, (SPAN, LANES), 0) == SPAN - 1
        d_cum = out_sum - in_sum + jnp.where(at_last, edge_sum, 0.0)
        upper = (col >= row).astype(f32)
        d_log = dot(upper, d_cum, precision=exact_prec)
        drate_ref[0:1, :] += jnp.sum(d_log * dt, axis=0, keepdims=True)
        ddt_ref[rows, :] = d_log * rate_ref[0:1, :] * sig_ref[rows, :] + in_sum * ratio_ref[rows, :]
        return 0

    lax.fori_loop(0, spans, body, 0)


GROUP = ("t1", "t0")
COPIES = ("part", "w1", "w0")
EVERYONE = ("part", "t1", "t0", "w1", "w0")


VMEM_LIMIT = 63 * 1024 * 1024


def in_vmem(kernel, out_shape, name, scratch=()):
    return pl.pallas_call(
        kernel,
        out_shape=out_shape,
        scratch_shapes=list(scratch),
        name=name,
        compiler_params=pltpu.CompilerParams(vmem_limit_bytes=VMEM_LIMIT),
    )


def shape(dims, dtype):
    return jax.ShapeDtypeStruct(dims, dtype)


def shift_part(array, by):
    size = lax.axis_size("part")
    pairs = [(i, i + by) for i in range(size) if 0 <= i + by < size]
    return lax.ppermute(array, "part", pairs)


def shards_general(
    hidden, cotangent, segments, valid, in_w, in_m, in_v, out_w, out_m, out_v, small_w, small_m, small_v,
):
    parts = lax.axis_size("part")
    wt = lax.axis_size("w1") * lax.axis_size("w0")
    part = lax.axis_index("part")
    tp = lax.axis_index("t1") * 2 + lax.axis_index("t0")
    own_rows = in_w.shape[0]
    out_rows = out_w.shape[0]
    resid = hidden[0].astype(f32)
    tok_rows = resid.shape[0]
    rows = tok_rows * TP
    spans = rows // SPAN
    seg_all = segments[0]
    pre_gain, norm_gain, conv_weight, conv_bias, dt_shift, a_logs, skips = unpack_small(small_w)

    def own_part(array, width):
        return lax.dynamic_slice_in_dim(array, tp * width, width, array.ndim - 1)

    in_copy = in_w.astype(bf16)
    slices = []
    for j in range(TP):
        slices.append(
            jnp.concatenate(
                [
                    in_copy[:, D_INNER + j * HALF : D_INNER + (j + 1) * HALF],
                    in_copy[:, 2 * D_INNER : 2 * D_INNER + SIDE],
                    in_copy[:, D_INNER + CONVCH + j * LOCAL_HEADS : D_INNER + CONVCH + (j + 1) * LOCAL_HEADS],
                    jnp.zeros((own_rows, LANES - LOCAL_HEADS), bf16),
                    in_copy[:, j * HALF : (j + 1) * HALF],
                ],
                axis=1,
            )
        )
    mine = lax.all_to_all(jnp.stack(slices), GROUP, 0, 0, tiled=False)
    w_in = lax.all_gather(mine, COPIES, axis=0, tiled=False)
    w_in = w_in.reshape(parts, wt, TP, own_rows, COLS).transpose(0, 2, 1, 3, 4).reshape(D, COLS)
    flat = [(i, (i % TP) * parts + i // TP) for i in range(parts * TP)]
    out_mine = lax.ppermute(out_w.astype(bf16), ("part", *GROUP), [(b, a) for a, b in flat])
    w_out = lax.all_gather(out_mine, COPIES, axis=0, tiled=True)

    hidden_all = lax.all_gather(hidden[0], GROUP, axis=0, tiled=True)
    back_mix = cotangent[0] * valid[0][:, None].astype(bf16)
    back_all = lax.all_gather(back_mix, GROUP, axis=0, tiled=True)

    hid = hidden_all.astype(f32)
    scale_all = lax.rsqrt(jnp.mean(hid * hid, axis=1, keepdims=True) + norm_eps)
    x_normed = (hid * scale_all * pre_gain).astype(bf16)
    projected = dot(x_normed, w_in)
    conv_in = projected[:, :COL_DT].astype(bf16)
    dt_raw = projected[:, COL_DT:COL_GATE].astype(bf16).astype(f32)
    gate_pre = projected[:, COL_GATE:]
    rim_in = shift_part(conv_in[rows - RIM :], 1)
    padded = jnp.concatenate([rim_in, conv_in], axis=0).astype(f32)
    seg_front = jnp.concatenate([jnp.full((RIM,), -1, jnp.int32), seg_all, jnp.full((RIM,), -1, jnp.int32)])
    seg_pad = lax.dynamic_slice_in_dim(seg_front, part * rows, rows + 2 * RIM)
    seg = seg_pad[RIM : RIM + rows]
    masks = [(seg_pad[k : k + rows] == seg).astype(f32)[:, None] for k in range(CONV)]
    taps = jnp.concatenate([own_part(conv_weight[:, :D_INNER], HALF), conv_weight[:, D_INNER:]], axis=1)
    bias = jnp.concatenate([own_part(conv_bias[:D_INNER], HALF), conv_bias[D_INNER:]])
    total = bias[None, :]
    for k in range(CONV):
        total = total + taps[k] * padded[k : k + rows] * masks[k]
    sig_total = jax.nn.sigmoid(total)
    activated = (total * sig_total).astype(bf16)
    x_scan = activated[:, :HALF]
    b_mat = activated[:, HALF : HALF + STATE]
    c_mat = activated[:, HALF + STATE :]

    def head_row(array):
        return jnp.pad(own_part(array, LOCAL_HEADS), (0, LANES - LOCAL_HEADS))

    shift_row = head_row(dt_shift)
    z = dt_raw + shift_row
    dt = jax.nn.softplus(z)
    sig_dt = jax.nn.sigmoid(z)
    ratio = jnp.where(dt > 1e-30, sig_dt / jnp.maximum(dt, 1e-30), 1.0)
    rate_row = -jnp.exp(head_row(a_logs))
    rate8 = jnp.broadcast_to(rate_row, (8, LANES))
    skip_chan = jnp.repeat(own_part(skips, LOCAL_HEADS), HEADDIM)
    skip8 = jnp.broadcast_to(skip_chan, (8, HALF))
    seg_spans = seg.reshape(spans, SPAN)
    seg_last = seg_spans[:, -1]
    seg_before = jnp.concatenate([seg_pad[RIM - 1 : RIM], seg_last[:-1]])
    keep = (seg_spans == seg_last[:, None]).astype(f32).reshape(rows, 1)
    inflow = (seg_spans == seg_before[:, None]).astype(f32).reshape(rows, 1)
    carry = jnp.broadcast_to((seg_last == seg_before).astype(f32)[:, None], (spans, LANES))
    seg_col = seg[:, None]

    state_shape = shape((STATE, HALF), f32)
    s_local, dec_total = in_vmem(
        functools.partial(state_kernel, spans), (state_shape, shape((8, LANES), f32)), "state"
    )(x_scan, b_mat, dt, rate8, keep, carry)
    dec_chan = jnp.repeat(dec_total[0, :LOCAL_HEADS], HEADDIM)
    s_in = jnp.zeros((STATE, HALF), f32)
    for _ in range(parts - 1):
        s_in = shift_part(dec_chan * s_in + s_local, 1)
    y_scan, states = in_vmem(
        functools.partial(scan_kernel, spans),
        (shape((rows, HALF), f32), shape((spans, STATE, HALF), f32)),
        "scan",
        [pltpu.VMEM((STATE, HALF), f32)],
    )(x_scan, b_mat, c_mat, dt, rate8, seg_col, seg_spans, keep, inflow, carry, s_in)
    y_b = (y_scan + skip_chan * x_scan.astype(f32)).astype(bf16).astype(f32)

    gain_own = own_part(norm_gain, HALF)
    sig_gate = jax.nn.sigmoid(gate_pre)
    silu_gate = gate_pre * sig_gate
    gated = y_b * silu_gate
    gate_sq = lax.psum(jnp.sum(gated * gated, axis=1), GROUP)
    scale_gate = lax.rsqrt(gate_sq / D_INNER + norm_eps)[:, None]
    normed = (gated * scale_gate * gain_own).astype(bf16)
    mixer = lax.psum_scatter(dot(normed, w_out), GROUP, scatter_dimension=0, tiled=True)
    output = (resid + mixer).astype(bf16)
    valid_rows = valid[0].astype(f32)
    res_sq = jnp.sum(valid_rows * jnp.sum(resid * resid, axis=1))
    mix_sq = jnp.sum(valid_rows * jnp.sum(mixer * mixer, axis=1))
    valid_count = jnp.sum(valid_rows)

    d_normed = dot(back_all, w_out, ((1,), (1,)))
    g_out = dot(normed, back_all, ((0,), (0,)))
    g_out = lax.psum_scatter(g_out, COPIES, scatter_dimension=0, tiled=True)
    g_out = lax.ppermute(g_out, ("part", *GROUP), flat)
    d_gain = d_normed * gain_own
    gate_dot = lax.psum(jnp.sum(gated * d_gain, axis=1), GROUP)
    d_gated = scale_gate * d_gain - gated * (scale_gate**3 * (gate_dot / D_INNER)[:, None])
    d_norm_gain = jnp.sum(gated * scale_gate * d_normed, axis=0)
    dy = (d_gated * silu_gate).astype(bf16)
    d_gate = d_gated * y_b * (sig_gate * (1.0 + gate_pre * (1.0 - sig_gate)))

    ds_local = in_vmem(functools.partial(state_back_kernel, spans), state_shape, "state_back")(
        dy, c_mat, dt, rate8, inflow, carry
    )
    ds_out = jnp.zeros((STATE, HALF), f32)
    for _ in range(parts - 1):
        ds_out = shift_part(dec_chan * ds_out + ds_local, -1)
    d_x, d_b, d_c, d_dt, d_rate, d_skip = in_vmem(
        functools.partial(scan_back_kernel, spans),
        (
            shape((rows, HALF), bf16),
            shape((rows, STATE), f32),
            shape((rows, STATE), f32),
            shape((rows, LANES), f32),
            shape((8, LANES), f32),
            shape((8, HALF), f32),
        ),
        "scan_back",
        [pltpu.VMEM((STATE, HALF), f32), pltpu.VMEM((2 * SPAN, HALF), f32)],
    )(x_scan, b_mat, c_mat, dt, ratio, sig_dt, rate8, seg_col, seg_spans, keep, inflow, carry, skip8, y_scan, states, dy, ds_out)

    d_total = jnp.concatenate([d_x.astype(f32), d_b, d_c], axis=1) * (sig_total * (1.0 + total * (1.0 - sig_total)))
    rim_back = shift_part(d_total[:RIM], -1)
    d_padded = jnp.concatenate([d_total, rim_back], axis=0)
    d_conv_in = 0.0
    for k in range(CONV):
        later = (seg_pad[2 * RIM - k : 2 * RIM - k + rows] == seg).astype(f32)[:, None]
        d_conv_in = d_conv_in + taps[k] * d_padded[RIM - k : RIM - k + rows] * later
    d_taps = jnp.stack([jnp.sum(d_total * padded[k : k + rows] * masks[k], axis=0) for k in range(CONV)])
    d_bias = jnp.sum(d_total, axis=0)
    d_proj = jnp.concatenate([d_conv_in, d_dt, d_gate], axis=1).astype(bf16)
    d_x_normed = dot(d_proj, w_in, ((1,), (1,)))
    d_x_normed = lax.psum_scatter(d_x_normed, GROUP, scatter_dimension=0, tiled=True)
    g_in = dot(x_normed, d_proj, ((0,), (0,)))
    g_in = g_in.reshape(parts, TP, wt, own_rows, COLS).transpose(0, 2, 1, 3, 4).reshape(parts * wt, TP, own_rows, COLS)
    g_in = lax.psum_scatter(g_in, COPIES, scatter_dimension=0, tiled=False)
    g_in = lax.all_to_all(g_in, GROUP, 0, 0, tiled=False)
    g_in = jnp.concatenate(
        [g_in[j, :, COL_GATE:] for j in range(TP)]
        + [g_in[j, :, :HALF] for j in range(TP)]
        + [jnp.sum(g_in[:, :, COL_SIDE:COL_DT], axis=0)]
        + [g_in[j, :, COL_DT : COL_DT + LOCAL_HEADS] for j in range(TP)],
        axis=1,
    )

    scale_own = lax.rsqrt(jnp.mean(resid * resid, axis=1, keepdims=True) + norm_eps)
    d_pre = d_x_normed * pre_gain
    dot_pre = jnp.mean(resid * d_pre, axis=1, keepdims=True)
    grad_hidden = back_mix.astype(f32) + scale_own * d_pre - resid * (scale_own**3 * dot_pre)
    d_pre_gain = jnp.sum(resid * scale_own * d_x_normed, axis=0)

    def placed(values, width):
        spread = (jnp.arange(TP) == tp).astype(f32)[:, None] * values[..., None, :]
        return spread.reshape(*values.shape[:-1], TP * width)

    d_weight = jnp.concatenate([placed(d_taps[:, :HALF], HALF), d_taps[:, HALF:]], axis=1)
    small_grad = jnp.concatenate(
        [
            d_pre_gain,
            placed(d_norm_gain, HALF),
            d_weight.reshape(-1),
            placed(d_bias[:HALF], HALF),
            d_bias[HALF:],
            placed(jnp.sum(d_dt, axis=0)[:LOCAL_HEADS], LOCAL_HEADS),
            placed((d_rate[0] * rate_row)[:LOCAL_HEADS], LOCAL_HEADS),
            placed(jnp.sum(d_skip[0].reshape(LOCAL_HEADS, HEADDIM), axis=1), LOCAL_HEADS),
            jnp.stack([res_sq, mix_sq, valid_count]),
        ]
    )
    small_total = lax.psum(small_grad, EVERYONE)
    res_total, mix_total, count_total = small_total[-3], small_total[-2], small_total[-1]
    in_m_new, in_v_new, in_w_new = adamw(in_w, in_m, in_v, g_in, 0.02, 0.1)
    out_m_new, out_v_new, out_w_new = adamw(out_w, out_m, out_v, g_out, 0.02, 0.1)
    small_m_new, small_v_new, small_w_new = adamw(small_w, small_m, small_v, small_total[:-3], 0.2, 0.0)
    rms = jnp.stack([jnp.sqrt(res_total / (count_total * D)), jnp.sqrt(mix_total / (count_total * D))])
    return (
        output[None], grad_hidden[None], in_m_new, in_v_new, in_w_new, out_m_new, out_v_new, out_w_new,
        small_m_new, small_v_new, small_w_new, rms,
    )


MESH = pl.DeviceIdType.MESH
T0, T1, DIAG, CORE, SIDEWAYS, PART = ("t0",), ("t1",), ("t1", "t0"), ("w0",), ("w1",), ("part",)
SIDE_CORE = ("w1", "w0")
HOPS = (None, T0, T1, DIAG)
HBM = pl.BlockSpec(memory_space=pl.ANY)
VMEM = pl.BlockSpec(memory_space=pltpu.VMEM)
MAIN = COL_GATE
CHANS = HALF + SIDE
FRONT = 16
TILE = 8
QUARTER = HALF // 2
NORM_ROW = D // LANES
TAP_ROW = NORM_ROW + D_INNER // LANES
TAP_ROWS = CONVCH // LANES
HEAD_ROW = TAP_ROW + (CONV + 1) * TAP_ROWS
SMALL_ROWS = HEAD_ROW + 2
BOX_ROWS = SMALL_ROWS + 8
OWN_NORM = NORM_ROW
OWN_TAP = OWN_NORM + HALF // LANES
OWN_SIDE = OWN_TAP + (CONV + 1) * (HALF // LANES)
OWN_HEAD = OWN_SIDE + (CONV + 1) * (SIDE // LANES)
OWN_SUMS = OWN_HEAD + 3
OWN_ROWS = 64


def place():
    return tuple(lax.axis_index(a) for a in EVERYONE)


def across(flips):
    return {a: 1 - lax.axis_index(a) for a in flips}


def group_blocks():
    _, t1, t0, _, _ = place()
    return [(t1, t0), (t1, 1 - t0), (1 - t1, t0), (1 - t1, 1 - t0)]


def greet(neighbours):
    barrier = pltpu.get_barrier_semaphore()
    for flips in neighbours:
        pl.semaphore_signal(barrier, inc=1, device_id=across(flips), device_id_type=MESH)


def greeted(neighbours):
    pl.semaphore_wait(pltpu.get_barrier_semaphore(), len(neighbours))


class Copies:
    def __init__(self, local_sem, send_sem, recv_sem):
        self.local_sem, self.send_sem, self.recv_sem = local_sem, send_sem, recv_sem
        self.sent, self.kept, self.in_flight, self.on_device = 0, 0, [], []

    def send(self, src, dst, flips):
        copy = pltpu.make_async_remote_copy(
            src_ref=src,
            dst_ref=dst,
            send_sem=self.send_sem.at[self.sent],
            recv_sem=self.recv_sem.at[self.sent],
            device_id=across(flips),
            device_id_type=MESH,
        )
        copy.start()
        self.sent += 1
        self.in_flight.append(copy)
        return copy

    def keep(self, src, dst):
        copy = pltpu.make_async_copy(src, dst, self.local_sem.at[self.kept])
        copy.start()
        self.kept += 1
        self.on_device.append(copy)
        return copy

    def settle(self, copy):
        copy.wait()
        self.on_device = [other for other in self.on_device if other is not copy]

    def left(self, copies):
        for copy in copies:
            copy.wait_send()
            self.in_flight = [other for other in self.in_flight if other is not copy]

    def drain(self):
        for copy in self.in_flight:
            copy.wait_send()
        for copy in self.on_device:
            copy.wait()
        self.in_flight, self.on_device = [], []


def sems(remote, local=1):
    return [
        pltpu.SemaphoreType.DMA((local,)),
        pltpu.SemaphoreType.DMA((remote,)),
        pltpu.SemaphoreType.DMA((remote,)),
    ]


class GroupGather:
    def __init__(self, copies, src, dst):
        self.copies, self.dst = copies, dst
        self.rows = src.shape[0]
        self.halves = (0, self.rows // 2)
        own = group_blocks()[0]
        self.own = copies.keep(src, self.at(own, 0, self.rows))
        size = self.rows // 2
        self.along_t1 = [copies.send(src.at[pl.ds(h, size)], self.at(own, h, size), T1) for h in self.halves]
        self.along_t0 = [copies.send(src.at[pl.ds(h, size)], self.at(own, h, size), T0) for h in self.halves]
        self.diagonal = []

    def at(self, block, first, size):
        return self.dst.at[pl.ds(pl.multiple_of((block[0] * 2 + block[1]) * self.rows + first, size), size)]

    def hand_on(self):
        beside = group_blocks()[2]
        for copy, h in zip(self.along_t1, self.halves):
            copy.wait_recv()
            here = self.at(beside, h, self.rows // 2)
            self.diagonal.append(self.copies.send(here, here, T0))

    def finish(self):
        for copy in self.along_t0 + self.diagonal:
            copy.wait_recv()


class WeightGather:
    def __init__(self, copies, dst, rows, group):
        self.copies, self.dst, self.rows, self.group = copies, dst, rows, group
        self.by_part, self.by_side, self.by_core = [], [], []

    def at(self, part, w1, w0, block):
        index = part
        if self.group:
            index = (index * 2 + block[0]) * 2 + block[1]
        index = (index * 2 + w1) * 2 + w0
        return self.dst.at[pl.ds(pl.multiple_of(index * self.rows, self.rows), self.rows)]

    def mine(self, block):
        p, _, _, w1, w0 = place()
        return self.at(p, w1, w0, block)

    def spread(self, src, block):
        dst = self.mine(block)
        self.by_part.append((self.copies.send(src, dst, PART), block))
        self.by_side.append((self.copies.send(src, dst, SIDEWAYS), block))
        self.by_core.append(self.copies.send(src, dst, CORE))

    def swap(self, src):
        own, *others = group_blocks()

        def slice_of(block):
            return src.at[block_rows(block, self.rows)]

        self.swaps = [(self.copies.send(slice_of(b), self.mine(own), flips), b) for b, flips in zip(others, HOPS[1:])]
        self.kept = self.copies.keep(slice_of(own), self.mine(own))
        self.spread(slice_of(own), own)

    def spread_swapped(self):
        for copy, block in self.swaps:
            copy.wait_recv()
            self.spread(self.mine(block), block)

    def pass_core(self, part, w1, block):
        here = self.at(part, w1, lax.axis_index("w0"), block)
        self.by_core.append(self.copies.send(here, here, CORE))

    def hand_on(self):
        p, _, _, w1, w0 = place()
        self.again = []
        for (copy, block), (side, _) in zip(self.by_part, self.by_side):
            side.wait_recv()
            self.pass_core(p, 1 - w1, block)
            copy.wait_recv()
            here = self.at(1 - p, w1, w0, block)
            self.again.append((self.copies.send(here, here, SIDEWAYS), block))
            self.pass_core(1 - p, w1, block)

    def hand_on_last(self):
        p, _, _, w1, _ = place()
        for copy, block in self.again:
            copy.wait_recv()
            self.pass_core(1 - p, 1 - w1, block)

    def finish(self):
        for copy in self.by_core:
            copy.wait_recv()


class GradientSum:
    def __init__(self, copies, srcs, rows, bufs, group):
        self.copies, self.srcs, self.rows, self.group = copies, srcs, rows, group
        self.core, self.sides, self.fars = bufs[:3]
        self.lasts = bufs[3] if group else None
        self.blocks = group_blocks() if group else [()]
        self.order = (1, 2, 3, 0) if group else (0,)
        p, _, _, w1, _ = place()
        self.parts, self.sides_of = (1 - p, p), (1 - w1, w1)
        self.core_copies, self.side_copies, self.far_copies, self.last_copies = {}, {}, {}, {}

    def at(self, block, side, w0):
        index = block[0] * 2 + block[1] if self.group else 0
        index = (index * 2 + side) * 2 + w0
        return pl.ds(pl.multiple_of(index * self.rows, self.rows), self.rows)

    def place(self, i, j):
        return self.at(self.blocks[i], self.sides_of[j], lax.axis_index("w0"))

    def pass_on(self, k, i, j, value, dst, flips):
        here = self.place(i, j)
        self.srcs[k][here, :] = value.astype(bf16)
        return self.copies.send(self.srcs[k].at[here], dst, flips)

    def added(self, k, i, j, *more):
        q, block, side = self.parts[k], self.blocks[i], self.sides_of[j]
        self.core_copies[k, i, j].wait_recv()
        value = self.srcs[k][self.place(i, j), :].astype(f32)
        value = value + self.core[(q, side, *block)].astype(f32)
        for other in more:
            value = value + other.astype(f32)
        return value

    def cores(self, k):
        w0 = lax.axis_index("w0")
        for j in range(2):
            for i in self.order:
                q, block, side = self.parts[k], self.blocks[i], self.sides_of[j]
                src = self.srcs[k].at[self.at(block, side, 1 - w0)]
                self.core_copies[k, i, j] = self.copies.send(src, self.core.at[(q, side, *block)], CORE)

    def left(self):
        for copies in (self.core_copies, self.side_copies, self.far_copies, self.last_copies):
            self.copies.left(copies.values())

    def to_sides(self, k):
        for i in self.order:
            self.side_copies[k, i] = self.pass_on(k, i, 0, self.added(k, i, 0), self.sides.at[k, i], SIDEWAYS)

    def to_part(self, which=None):
        for i in self.order if which is None else which:
            self.side_copies[0, i].wait_recv()
            value = self.added(0, i, 1, self.sides[0, i])
            self.far_copies[i] = self.pass_on(0, i, 1, value, self.fars.at[i], PART)

    def total(self, i):
        self.side_copies[1, i].wait_recv()
        self.far_copies[i].wait_recv()
        return self.added(1, i, 1, self.sides[1, i], self.fars[i])

    def to_group(self, store):
        for i in self.order:
            value = self.total(i)
            if i == 0:
                store(0, value)
            else:
                self.last_copies[i] = self.pass_on(1, i, 1, value, self.lasts.at[i - 1], HOPS[i])

    def finish(self, store):
        for i, copy in self.last_copies.items():
            copy.wait_recv()
            store(i, self.lasts[i - 1].astype(f32))


class GroupScatter:
    def __init__(self, copies, src, bufs):
        self.copies, self.src = copies, src
        self.here, self.pass_on, self.last = bufs
        self.rows = self.here.shape[0]

    def block(self, i):
        return block_rows(group_blocks()[i], self.rows)

    def left(self):
        self.copies.left([self.own_copy, self.pass_copy])

    def to_t0(self, i):
        copy = self.copies.send(self.src.at[self.block(i)], self.here if i == 1 else self.pass_on, T0)
        if i == 1:
            self.own_copy = copy
        else:
            self.pass_copy = copy

    def to_t1(self):
        self.pass_copy.wait_recv()
        here = self.block(2)
        self.src[here, :] = (self.src[here, :].astype(f32) + self.pass_on[...].astype(f32)).astype(bf16)
        self.last_copy = self.copies.send(self.src.at[here], self.last, T1)

    def finish(self):
        self.own_copy.wait_recv()
        self.last_copy.wait_recv()
        return self.here[...].astype(f32) + self.last[...].astype(f32)


def scatter_buffers(rows):
    return [pltpu.VMEM((rows, D), bf16)] * 3


def sum_buffers(rows, cols, group):
    buf = lambda *lead: pltpu.VMEM((*lead, rows, cols), bf16)
    if not group:
        return [buf(2, 2), buf(2, 1), buf(1)]
    return [buf(2, 2, 2, 2), buf(2, 4), buf(4), buf(3)]


def block_rows(block, size):
    return pl.ds(pl.multiple_of((block[0] * 2 + block[1]) * size, size), size)


def lane_of(h):
    return h if h < LOCAL_HEADS // 2 else h + HEADS // 2 - LOCAL_HEADS // 2


def own_pair(cols, h):
    lane = lax.broadcasted_iota(jnp.int32, (cols.shape[0], LANES), 1)
    first, second = lane_of(h), lane_of(h + 1)
    return jnp.where(lane < HEADDIM, cols[:, first : first + 1], cols[:, second : second + 1])


def own_sums(values):
    width = values.shape[1]
    head = lax.broadcasted_iota(jnp.int32, (width, LANES), 0) // HEADDIM
    lane = lax.broadcasted_iota(jnp.int32, (width, LANES), 1)
    pick = (jnp.where(head < LOCAL_HEADS // 2, head, head + lane_of(LOCAL_HEADS) - LOCAL_HEADS) == lane).astype(bf16)
    high = values.astype(bf16)
    low = (values - high.astype(f32)).astype(bf16)
    return dot(high, pick) + dot(low, pick)


def head_lanes(values, back=False):
    first = (lax.axis_index("t1") * 2 + lax.axis_index("t0")) * (LOCAL_HEADS // 2)
    return pltpu.roll(values, first if back else LANES - first, 1)


def own_row(first, k):
    tp = lax.axis_index("t1") * 2 + lax.axis_index("t0")
    third = QUARTER // LANES
    return pl.ds(first + (k // third) * (D_INNER // 2 // LANES) + tp * third + k % third, 1)


def own_chans(j):
    return [slice(first + j * QUARTER, first + (j + 1) * QUARTER) for first in (0, D_INNER // 2)]


EVERY_NEIGHBOUR = (T0, T1, DIAG, CORE, SIDEWAYS, SIDE_CORE, PART)


def main_kernel(
    spans, hid_ref, inw_hbm, outw_hbm, cot_hbm, inside_ref, valid_ref, small_ref, segc_ref, segr_ref,
    cotv_out, mixer_out, ggate_out, gmain_out, dx_out, gout_out, total_ref,
    h_ref, xn_ref, win_ref, convp_ref, x_ref, b_ref, c_ref, dtot_ref, dt_ref, z_ref, cum_ref, y_ref, st_ref,
    wgate_ref, wout_ref, back_ref, normed_ref, mix_ref, dy_ref, dgate_ref, dmain_ref, dgain_ref, taps_ref, heads_ref, chans_ref,
    marks_ref, carry_ref, s_ref, pass_ref, got_ref, rim_ref, gated_ref, gate_ref, dn_ref,
    stat_ref, stats_ref, dyg_ref, passb_ref, gotb_ref, rims_ref, rimr_ref, hsum_ref, dskip_ref, dtaps_ref,
    dpre_ref, box_ref, boxes_ref, gm_ref,
    *rest,
):
    go_bufs, gg_bufs, gm_bufs, mix_bufs, dx_bufs = rest[:3], rest[3:7], rest[7:11], rest[11:14], rest[14:17]
    local_sem, send_sem, recv_sem = rest[17:]
    greet(EVERY_NEIGHBOUR)
    p, _, _, _, _ = place()
    rows_all = spans * SPAN
    tokens = hid_ref.shape[0]
    own_rows, out_rows = inw_hbm.shape[0], outw_hbm.shape[0]
    lane = lax.broadcasted_iota(jnp.int32, (1, LANES), 1)
    wm_ref = dmain_ref.at[pl.ds(0, TP * own_rows)]
    wg_ref = dgate_ref.at[pl.ds(0, TP * own_rows)]
    wo_ref = mix_ref.at[pl.ds(0, out_rows)]
    cotv_ref = mix_ref.at[pl.ds(tokens, tokens)]
    dxi_ref, prod_ref = gated_ref, gate_ref

    def side_at(c, which):
        return (slice(spans * STATE, spans * STATE + SPAN), pl.ds(pl.multiple_of((which * spans + c) * STATE, STATE), STATE))


    copies = Copies(local_sem, send_sem, recv_sem)
    loads = [
        copies.keep(inw_hbm.at[:, pl.ds(k * HALF, HALF)], gate_ref.at[pl.ds(k * own_rows, own_rows)])
        for k in range(2 * D_INNER // HALF)
    ]
    loads += [
        copies.keep(outw_hbm.at[:, pl.ds(k * HALF, HALF)], dn_ref.at[pl.ds(k * out_rows, out_rows)]) for k in range(D // HALF)
    ]
    loads.append(copies.keep(cot_hbm, cotv_ref))

    side = inside_ref[...]
    dt_cols = jnp.concatenate([side[:, SIDE:], jnp.zeros((own_rows, LANES - HEADS), f32)], axis=1)
    for copy in loads:
        copies.settle(copy)
    cotv_ref[...] = (cotv_ref[...].astype(f32) * valid_ref[...]).astype(bf16)

    def master(first):
        return gate_ref[first // HALF * own_rows : (first // HALF + 1) * own_rows, first % HALF : first % HALF + QUARTER]

    for j in range(TP):
        at = slice(j * own_rows, (j + 1) * own_rows)
        for k, chans in enumerate(own_chans(j)):
            part = slice(k * QUARTER, (k + 1) * QUARTER)
            wg_ref[at, part] = master(chans.start).astype(bf16)
            wm_ref[at, part] = master(D_INNER + chans.start).astype(bf16)
        wm_ref[at, HALF:CHANS] = side[:, :SIDE].astype(bf16)
        dt_own = (lane % (HEADS // 2) // (LOCAL_HEADS // 2) == j) & (lane < HEADS)
        wm_ref[at, CHANS:MAIN] = jnp.where(dt_own, dt_cols, 0.0).astype(bf16)
    for k in range(D // HALF):
        wo_ref[:, k * HALF : (k + 1) * HALF] = dn_ref[k * out_rows : (k + 1) * out_rows, :].astype(bf16)

    greeted(EVERY_NEIGHBOUR)
    mains = WeightGather(copies, win_ref, own_rows, True)
    mains.swap(wm_ref)
    hids = GroupGather(copies, hid_ref, h_ref)
    copies.keep(cotv_ref, cotv_out)

    for k in range(HALF // LANES):
        lanes = slice(k * LANES, (k + 1) * LANES)
        chans_ref[1:2, lanes] = small_ref[own_row(NORM_ROW, k), :]
        for j in range(CONV + 1):
            taps_ref[j : j + 1, lanes] = small_ref[own_row(TAP_ROW + TAP_ROWS * j, k), :]
    for k in range(SIDE // LANES):
        lanes = slice(HALF + k * LANES, HALF + (k + 1) * LANES)
        for j in range(CONV + 1):
            row = TAP_ROW + TAP_ROWS * j + D_INNER // LANES + k
            taps_ref[j : j + 1, lanes] = small_ref[row : row + 1, :]
    head_row = jnp.broadcast_to(small_ref[HEAD_ROW : HEAD_ROW + 1, :], (TILE, LANES))
    next_row = jnp.broadcast_to(small_ref[HEAD_ROW + 1 : HEAD_ROW + 2, :], (TILE, LANES))
    a_log = pltpu.roll(head_row, LANES - HEADS, 1)
    lane8 = lax.broadcasted_iota(jnp.int32, (TILE, LANES), 1)
    spill = LANES - 2 * HEADS
    skip = jnp.where(lane8 < spill, pltpu.roll(head_row, spill, 1), pltpu.roll(next_row, spill, 1))
    own = lane8 < HEADS
    heads_ref[0:1, :] = head_lanes(jnp.where(own, head_row, 0.0))[0:1]
    heads_ref[1:2, :] = -jnp.exp(head_lanes(jnp.where(own, a_log, 0.0))[0:1])
    skip = head_lanes(jnp.where(own, skip, 0.0))[0:1]
    for q in range(PAIRS):
        chans_ref[0:1, q * LANES : (q + 1) * LANES] = own_pair(skip, 2 * q)

    def mark(c, _):
        rows = span_rows(c)
        seg = segc_ref[pl.ds(pl.multiple_of(c * SPAN, SPAN), SPAN + 2 * FRONT), :]
        here = seg[FRONT : FRONT + SPAN]
        last = seg[FRONT + SPAN - 1 : FRONT + SPAN]
        before = seg[FRONT - 1 : FRONT]
        cols = [seg[FRONT - RIM + k : FRONT - RIM + k + SPAN] == here for k in range(RIM)]
        cols += [seg[FRONT + RIM - k : FRONT + RIM - k + SPAN] == here for k in range(RIM)]
        cols += [here == last, here == before]
        lane_m = lax.broadcasted_iota(jnp.int32, (SPAN, TILE), 1)
        marks = jnp.zeros((SPAN, TILE), f32)
        for k, col in enumerate(cols):
            marks = jnp.where(lane_m == k, jnp.where(col, 1.0, 0.0), marks)
        marks_ref[rows, :] = marks
        carry_ref[pl.ds(c, 1), :] = jnp.broadcast_to(jnp.where(last == before, 1.0, 0.0), (1, LANES))
        return 0

    lax.fori_loop(0, spans, mark, 0)
    blocks = group_blocks()

    def norm(block):
        rows = block_rows(block, tokens)
        hid = h_ref[rows, :].astype(f32)
        scale = lax.rsqrt(jnp.sum(hid * hid, axis=1, keepdims=True) / D + norm_eps)
        for k in range(D // LANES):
            lanes = slice(k * LANES, (k + 1) * LANES)
            xn_ref[rows, lanes] = (h_ref[rows, lanes].astype(f32) * scale * small_ref[k : k + 1, :]).astype(bf16)

    mains.spread_swapped()
    copies.settle(hids.own)
    norm(blocks[0])
    gates = WeightGather(copies, wgate_ref, own_rows, True)
    gates.swap(wg_ref)
    hids.hand_on()
    norm(blocks[2])
    mains.hand_on()
    gates.spread_swapped()
    hids.finish()
    norm(blocks[1])
    norm(blocks[3])
    mains.hand_on_last()
    cots = GroupGather(copies, cotv_ref, back_ref)
    outs = WeightGather(copies, wout_ref, out_rows, False)
    outs.spread(wo_ref, ())
    outs_kept = copies.keep(wo_ref, outs.mine(()))
    mains.finish()
    copies.settle(mains.kept)

    def project(c, _):
        rows = span_rows(c)
        xn = xn_ref[rows, :]
        at = pl.ds(pl.multiple_of(FRONT + c * SPAN, FRONT), SPAN)
        for k in range(CHANS // 256):
            cols = slice(k * 256, (k + 1) * 256)
            convp_ref[at, cols] = dot(xn, win_ref[:, cols]).astype(bf16)
        dt_raw = dot(xn, win_ref[:, CHANS:MAIN]).astype(bf16).astype(f32)
        z = head_lanes(dt_raw) + heads_ref[0:1, :]
        z_ref[rows, :] = z
        small = jnp.exp(-jnp.abs(z))
        one_more = 1.0 + small
        is_one = one_more == 1.0
        log_more = jnp.where(is_one, small, jnp.log(one_more) * small / jnp.where(is_one, 1.0, one_more - 1.0))
        dt_ref[rows, :] = jnp.maximum(z, 0.0) + log_more
        return 0

    lax.fori_loop(0, spans, project, 0)
    rim = copies.send(convp_ref.at[pl.ds(rows_all, FRONT)], rim_ref, PART)
    gates.hand_on()
    s_ref[...] = jnp.zeros_like(s_ref)
    dgain_ref[...] = jnp.zeros_like(dgain_ref)

    def convolve(c, _):
        rows = span_rows(c)
        wide = pl.ds(pl.multiple_of(c * SPAN, SPAN), SPAN + FRONT)
        marks = marks_ref[rows, :]
        for k in range(CHANS // LANES):
            lanes = slice(k * LANES, (k + 1) * LANES)
            values = convp_ref[wide, lanes].astype(f32)
            total = taps_ref[CONV : CONV + 1, lanes] + taps_ref[RIM : RIM + 1, lanes] * values[FRONT:]
            for j in range(RIM):
                first = FRONT - RIM + j
                total = total + taps_ref[j : j + 1, lanes] * values[first : first + SPAN] * marks[:, j : j + 1]
            sig = 1.0 / (1.0 + jnp.exp(-total))
            value = (total * sig).astype(bf16)
            dtot_ref[rows, lanes] = sig * (1.0 + total * (1.0 - sig))
            if k < HALF // LANES:
                x_ref[rows, lanes] = value
            elif k == HALF // LANES:
                b_ref[rows, :] = value
            else:
                c_ref[rows, :] = value
        return 0

    lax.fori_loop(1, spans, convolve, 0)
    rim.wait_recv()
    convp_ref[0:FRONT, :] = jnp.where(p == 1, rim_ref[...].astype(f32), 0.0).astype(bf16)
    lax.fori_loop(0, 1, convolve, 0)
    gates.hand_on_last()

    def local_states(c, _):
        rows = span_rows(c)
        dt, cum = span_decay(dt_ref, heads_ref, c, 1)
        cum_ref[rows, :] = cum
        last = cum[SPAN - 1 : SPAN, :]
        end_weight = jnp.exp(last - cum) * dt * marks_ref[rows, 6:7]
        decay = jnp.exp(last) * carry_ref[pl.ds(c, 1), :]
        b = b_ref[rows, :]
        st_ref[c] = s_ref[...]
        for q in range(PAIRS):
            lanes = slice(q * LANES, (q + 1) * LANES)
            xw = (x_ref[rows, lanes].astype(f32) * own_pair(end_weight, 2 * q)).astype(bf16)
            s_ref[:, lanes] = s_ref[:, lanes] * own_pair(decay, 2 * q) + dot(b, xw, ((0,), (0,)))
        return 0

    lax.fori_loop(0, spans, local_states, 0)
    pass_ref[...] = s_ref[...].astype(bf16)
    state = copies.send(pass_ref, got_ref, PART)
    cots.hand_on()
    outs.hand_on()

    def inside(c, _):
        rows = span_rows(c)
        cum = cum_ref[rows, :]
        back_log = jnp.transpose(cum - jnp.log(dt_ref[rows, :]))
        scores = dot(c_ref[rows, :], b_ref[rows, :], ((1,), (1,)))
        row = lax.broadcasted_iota(jnp.int32, (SPAN, SPAN), 0)
        col = lax.broadcasted_iota(jnp.int32, (SPAN, SPAN), 1)
        mask = (row >= col) & (segc_ref[pl.ds(pl.multiple_of(FRONT + c * SPAN, FRONT), SPAN), :] == segr_ref[pl.ds(c, 1), :])
        lane = lax.broadcasted_iota(jnp.int32, (SPAN, LANES), 1)
        for q in range(PAIRS):
            lanes = slice(q * LANES, (q + 1) * LANES)
            x = x_ref[rows, lanes]
            parts = []
            for h in (lane_of(2 * q), lane_of(2 * q + 1)):
                gap = cum[:, h : h + 1] - back_log[h : h + 1, :]
                weighted = scores * jnp.exp(jnp.where(mask, gap, -1e30))
                parts.append(dot(weighted.astype(bf16), x))
            y_ref[rows, lanes] = jnp.where(lane < HEADDIM, parts[0], parts[1])
        return 0

    lax.fori_loop(0, spans, inside, 0)
    state.wait_recv()
    s_ref[...] = got_ref[...].astype(f32) * p.astype(f32)

    def across_spans(c, _):
        rows = span_rows(c)
        cum = cum_ref[rows, :]
        decay = jnp.exp(cum[SPAN - 1 : SPAN, :]) * carry_ref[pl.ds(c, 1), :]
        gain = jnp.exp(cum) * marks_ref[rows, 7:8]
        cc = c_ref[rows, :]
        for q in range(PAIRS):
            lanes = slice(q * LANES, (q + 1) * LANES)
            entering = s_ref[:, lanes]
            full = st_ref[c, :, lanes] + entering
            st_ref[c, :, lanes] = full
            y_ref[rows, lanes] += dot(cc, full.astype(bf16)) * own_pair(gain, 2 * q)
            s_ref[:, lanes] = entering * own_pair(decay, 2 * q)
        return 0

    lax.fori_loop(0, spans, across_spans, 0)
    gates.finish()
    copies.settle(gates.kept)

    def put_stat(k, c, column):
        wide = jnp.transpose(jnp.broadcast_to(column, (SPAN, LANES)))
        stat_ref[k, :, span_rows(c)] = wide[0:TILE, :]

    def exchange(k):
        return [copies.send(stat_ref.at[k], stats_ref.at[k, i], flips) for i, flips in enumerate(HOPS[1:])]

    def get_stat(k, c):
        cols = span_rows(c)
        total = stat_ref[k, :, cols] + stats_ref[k, 0, :, cols] + stats_ref[k, 1, :, cols] + stats_ref[k, 2, :, cols]
        return jnp.transpose(jnp.broadcast_to(total[0:1, :], (LANES, SPAN)))[:, 0:1] / D_INNER

    def values(rows, lanes):
        y_b = (y_ref[rows, lanes] + chans_ref[0:1, lanes] * x_ref[rows, lanes].astype(f32)).astype(bf16).astype(f32)
        gate = gate_ref[rows, lanes]
        sig = 1.0 / (1.0 + jnp.exp(-gate))
        return y_b, gate, sig

    def gating(c, _):
        rows = span_rows(c)
        xn = xn_ref[rows, :]
        total = jnp.zeros((SPAN, 1), f32)
        for k in range(HALF // 256):
            lanes = slice(k * 256, (k + 1) * 256)
            gate_ref[rows, lanes] = dot(xn, wgate_ref[:, lanes])
            y_b, gate, sig = values(rows, lanes)
            gated = y_b * (gate * sig)
            gated_ref[rows, lanes] = gated
            total = total + jnp.sum(gated * gated, axis=1, keepdims=True)
        put_stat(0, c, total)
        return 0

    lax.fori_loop(0, spans, gating, 0)
    outs.hand_on_last()
    squares = exchange(0)
    cots.finish()
    copies.settle(cots.own)
    outs.finish()
    copies.settle(outs_kept)

    def pull_out(c, _):
        rows = span_rows(c)
        back = back_ref[rows, :]
        total = jnp.zeros((SPAN, 1), f32)
        for k in range(HALF // 256):
            lanes = slice(k * 256, (k + 1) * 256)
            d_normed = dot(back, wout_ref[lanes, :], ((1,), (1,)))
            dn_ref[rows, lanes] = d_normed
            total = total + jnp.sum(gated_ref[rows, lanes] * (d_normed * chans_ref[1:2, lanes]), axis=1, keepdims=True)
        put_stat(1, c, total)
        return 0

    lax.fori_loop(0, spans, pull_out, 0)
    for copy in squares:
        copy.wait_recv()
    dots = exchange(1)

    def push_out(c, _):
        rows = span_rows(c)
        scale = lax.rsqrt(get_stat(0, c) + norm_eps)
        for k in range(HALF // 256):
            lanes = slice(k * 256, (k + 1) * 256)
            scaled = gated_ref[rows, lanes] * scale
            normed_ref[rows, lanes] = (scaled * chans_ref[1:2, lanes]).astype(bf16)
            dgain_ref[0:1, lanes] += jnp.sum(scaled * dn_ref[rows, lanes], axis=0, keepdims=True)
        normed = normed_ref[rows, :]
        for k in range(D // 256):
            cols = slice(k * 256, (k + 1) * 256)
            mix_ref[rows, cols] = dot(normed, wout_ref[:, cols]).astype(bf16)
        return 0

    copies.drain()
    lax.fori_loop(0, spans, push_out, 0)
    mixes = GroupScatter(copies, mix_ref, mix_bufs)
    mixes.to_t0(3)
    mixes.to_t0(1)
    for q in range(2):
        normed = normed_ref[:, q * HALF // 2 : (q + 1) * HALF // 2]
        for k in range(D // 512):
            cols = slice(k * 512, (k + 1) * 512)
            wout_ref[q * HALF // 2 : (q + 1) * HALF // 2, cols] = dot(normed, back_ref[:, cols], ((0,), (0,))).astype(bf16)
    go_halves = [wout_ref.at[pl.ds(pl.multiple_of(q * (HALF // 2), HALF // 2), HALF // 2)] for q in (1 - p, p)]
    g_out = GradientSum(copies, go_halves, out_rows, go_bufs, False)
    g_out.cores(0)
    g_out.cores(1)
    for copy in dots:
        copy.wait_recv()

    def back_gate(c, _):
        rows = span_rows(c)
        scale = lax.rsqrt(get_stat(0, c) + norm_eps)
        pulled = get_stat(1, c) * (scale * scale * scale)
        for k in range(HALF // LANES):
            lanes = slice(k * LANES, (k + 1) * LANES)
            y_b, gate, sig = values(rows, lanes)
            d_gated = scale * (dn_ref[rows, lanes] * chans_ref[1:2, lanes]) - gated_ref[rows, lanes] * pulled
            dy_ref[rows, lanes] = (d_gated * (gate * sig)).astype(bf16)
            dgate_ref[rows, lanes] = (d_gated * y_b * (sig * (1.0 + gate * (1.0 - sig)))).astype(bf16)
        return 0

    lax.fori_loop(0, spans, back_gate, 0)
    g_out.to_sides(0)
    s_ref[...] = jnp.zeros_like(s_ref)
    hsum_ref[...] = jnp.zeros_like(hsum_ref)
    dskip_ref[...] = jnp.zeros_like(dskip_ref)
    dtaps_ref[...] = jnp.zeros_like(dtaps_ref)

    def local_states(step, _):
        c = spans - 1 - step
        rows = span_rows(c)
        cum = cum_ref[rows, :]
        decay = jnp.exp(cum[SPAN - 1 : SPAN, :]) * carry_ref[pl.ds(c, 1), :]
        gain = jnp.exp(cum) * marks_ref[rows, 7:8]
        cc = c_ref[rows, :]
        for q in range(PAIRS):
            lanes = slice(q * LANES, (q + 1) * LANES)
            dyg = (dy_ref[rows, lanes].astype(f32) * own_pair(gain, 2 * q)).astype(bf16)
            dyg_ref[rows, lanes] = dyg
            ds = s_ref[:, lanes]
            dn_ref[pl.ds(pl.multiple_of(c * STATE, STATE), STATE), lanes] = ds
            s_ref[:, lanes] = ds * own_pair(decay, 2 * q) + dot(cc, dyg, ((0,), (0,)))
        return 0

    lax.fori_loop(0, spans, local_states, 0)
    passb_ref[...] = s_ref[...].astype(bf16)
    state = copies.send(passb_ref, gotb_ref, PART)

    width = D // 4
    gg_halves = [back_ref.at[:, pl.ds(k * HALF, HALF)] for k in range(2)]
    g_gate = GradientSum(copies, gg_halves, own_rows, gg_bufs, True)

    def gate_gradient(far):
        for half in range(2):
            first = pl.multiple_of(((1 - p if far else p) * 2 + half) * width, width)
            piece = dot(xn_ref[:, pl.ds(first, width)], dgate_ref[...], ((0,), (0,)))
            gg_halves[0 if far else 1][half * width : (half + 1) * width, :] = piece.astype(bf16)

    gate_gradient(True)
    g_gate.cores(0)
    gate_gradient(False)
    g_gate.cores(1)
    g_gate.to_sides(0)
    g_out.to_part()
    g_out.to_sides(1)
    g_gate.to_sides(1)

    def inside(c, _):
        rows = span_rows(c)
        cum = cum_ref[rows, :]
        fore_log = jnp.transpose(cum)
        back_log = cum - jnp.log(dt_ref[rows, :])
        b = b_ref[rows, :]
        cc = c_ref[rows, :]
        scores = dot(b, cc, ((1,), (1,)))
        row = lax.broadcasted_iota(jnp.int32, (SPAN, SPAN), 0)
        col = lax.broadcasted_iota(jnp.int32, (SPAN, SPAN), 1)
        mask = (col >= row) & (segc_ref[pl.ds(pl.multiple_of(FRONT + c * SPAN, FRONT), SPAN), :] == segr_ref[pl.ds(c, 1), :])
        lane = lax.broadcasted_iota(jnp.int32, (SPAN, LANES), 1)
        d_scores = jnp.zeros((SPAN, SPAN), f32)
        dc = jnp.zeros((SPAN, STATE), f32)
        for q in range(PAIRS):
            lanes = slice(q * LANES, (q + 1) * LANES)
            x = x_ref[rows, lanes]
            dy = dy_ref[rows, lanes]
            xf = x.astype(f32)
            parts = []
            for k in range(2):
                h = lane_of(2 * q + k)
                gap = fore_log[h : h + 1, :] - back_log[:, h : h + 1]
                decay_mat = jnp.exp(jnp.where(mask, gap, -1e30))
                parts.append(dot((scores * decay_mat).astype(bf16), dy))
                own = (lane < HEADDIM) if k == 0 else (lane >= HEADDIM)
                d_weights = dot(jnp.where(own, xf, 0.0).astype(bf16), dy, ((1,), (1,)))
                d_scores = d_scores + d_weights * decay_mat
            dxi_ref[rows, lanes] = jnp.where(lane < HEADDIM, parts[0], parts[1])
            dc = dc + dot(dyg_ref[rows, lanes], st_ref[c, :, lanes].astype(bf16), ((1,), (1,)))
            dskip_ref[0:1, lanes] += jnp.sum(dy.astype(f32) * xf, axis=0, keepdims=True)
        d_scores_b = d_scores.astype(bf16)
        dn_ref[side_at(c, 0)] = dot(d_scores_b, cc)
        dn_ref[side_at(c, 1)] = dc + dot(d_scores_b, b, ((0,), (0,)))
        return 0

    lax.fori_loop(0, spans, inside, 0)
    mixes.to_t1()
    state.wait_recv()
    s_ref[...] = gotb_ref[...].astype(f32) * (1 - p).astype(f32)

    def across_spans(step, _):
        c = spans - 1 - step
        rows = span_rows(c)
        dt = dt_ref[rows, :]
        cum = cum_ref[rows, :]
        last = cum[SPAN - 1 : SPAN, :]
        end_weight = jnp.exp(last - cum) * dt * marks_ref[rows, 6:7]
        decay = jnp.exp(last) * carry_ref[pl.ds(c, 1), :]
        b = b_ref[rows, :]
        db = dn_ref[side_at(c, 0)]
        edges = []
        for q in range(PAIRS):
            lanes = slice(q * LANES, (q + 1) * LANES)
            xf = x_ref[rows, lanes].astype(f32)
            dyf = dy_ref[rows, lanes].astype(f32)
            ew = own_pair(end_weight, 2 * q)
            dec = own_pair(decay, 2 * q)
            entering = s_ref[:, lanes]
            ds = dn_ref[pl.ds(pl.multiple_of(c * STATE, STATE), STATE), lanes] + entering
            s_ref[:, lanes] = entering * dec
            ds_b = ds.astype(bf16)
            db = db + dot((xf * ew).astype(bf16), ds_b, ((1,), (1,)))
            dx_state = dot(b, ds_b) * ew
            dx = dxi_ref[rows, lanes] + dx_state
            edges.append(
                jnp.sum(ds * st_ref[c, :, lanes], axis=0, keepdims=True) * dec
                + jnp.sum(dx_state * xf, axis=0, keepdims=True)
            )
            prod_ref[0:SPAN, lanes] = dyf * y_ref[rows, lanes]
            prod_ref[SPAN : 2 * SPAN, lanes] = xf * dx
            d_x = (dx + dyf * chans_ref[0:1, lanes]).astype(bf16).astype(f32)
            dtot_ref[rows, lanes] = d_x * dtot_ref[rows, lanes]
        dtot_ref[rows, HALF : HALF + STATE] = db * dtot_ref[rows, HALF : HALF + STATE]
        dtot_ref[rows, HALF + STATE :] = dn_ref[side_at(c, 1)] * dtot_ref[rows, HALF + STATE :]
        sums = own_sums(prod_ref[0 : 2 * SPAN, :])
        out_sum, in_sum = sums[:SPAN], sums[SPAN:]
        edge_sum = own_sums(jnp.broadcast_to(jnp.concatenate(edges, axis=1), (TILE, HALF)))[0:1]
        at_last = lax.broadcasted_iota(jnp.int32, (SPAN, LANES), 0) == SPAN - 1
        d_cum = out_sum - in_sum + jnp.where(at_last, edge_sum, 0.0)
        row = lax.broadcasted_iota(jnp.int32, (SPAN, SPAN), 0)
        col = lax.broadcasted_iota(jnp.int32, (SPAN, SPAN), 1)
        d_log = dot((col >= row).astype(f32), d_cum, precision=exact_prec)
        z = z_ref[rows, :]
        small = jnp.exp(-jnp.abs(z))
        sig = jnp.where(z >= 0.0, 1.0, small) / (1.0 + small)
        ratio = jnp.where(dt > 1e-30, sig / jnp.maximum(dt, 1e-30), 1.0)
        d_dt = d_log * heads_ref[1:2, :] * sig + in_sum * ratio
        hsum_ref[0:1, :] += jnp.sum(d_log * dt, axis=0, keepdims=True)
        hsum_ref[1:2, :] += jnp.sum(d_dt, axis=0, keepdims=True)
        dmain_ref[rows, CHANS:MAIN] = head_lanes(d_dt, back=True).astype(bf16)
        return 0

    lax.fori_loop(0, spans, across_spans, 0)
    rims_ref[...] = dtot_ref[0:TILE, :]
    rim = copies.send(rims_ref, rimr_ref, PART)
    g_gate.to_part()

    def convolve(c, _):
        rows = span_rows(c)
        marks = marks_ref[rows, :]
        fore = pl.ds(pl.multiple_of(c * SPAN, SPAN), SPAN + FRONT)
        hind = pl.ds(pl.multiple_of(c * SPAN, SPAN), SPAN + TILE)
        for k in range(CHANS // LANES):
            lanes = slice(k * LANES, (k + 1) * LANES)
            later = dtot_ref[hind, lanes]
            earlier = convp_ref[fore, lanes].astype(f32)
            own = later[0:SPAN]
            d_conv = taps_ref[RIM : RIM + 1, lanes] * own
            dtaps_ref[RIM : RIM + 1, lanes] += jnp.sum(own * earlier[FRONT:], axis=0, keepdims=True)
            dtaps_ref[CONV : CONV + 1, lanes] += jnp.sum(own, axis=0, keepdims=True)
            for j in range(RIM):
                ahead = RIM - j
                d_conv = d_conv + taps_ref[j : j + 1, lanes] * later[ahead : ahead + SPAN] * marks[:, 3 + j : 4 + j]
                first = FRONT - ahead
                dtaps_ref[j : j + 1, lanes] += jnp.sum(
                    own * earlier[first : first + SPAN] * marks[:, j : j + 1], axis=0, keepdims=True
                )
            dmain_ref[rows, lanes] = d_conv.astype(bf16)
        return 0

    lax.fori_loop(0, spans - 1, convolve, 0)
    rim.wait_recv()
    dtot_ref[pl.ds(spans * SPAN, TILE), :] = jnp.where(p == 0, rimr_ref[...], 0.0)
    lax.fori_loop(spans - 1, spans, convolve, 0)

    mixes.left()
    dpre_ref[...] = jnp.zeros_like(dpre_ref)

    def token_grad(block, keep):
        rows = block_rows(block, tokens)
        d_main = dmain_ref[rows, :]
        d_gate = dgate_ref[rows, :]
        hid = h_ref[rows, :].astype(f32)
        scale = lax.rsqrt(jnp.sum(hid * hid, axis=1, keepdims=True) / D + norm_eps)
        for k in range(D // 256):
            cols = slice(k * 256, (k + 1) * 256)
            part = dot(d_main, win_ref[cols, :], ((1,), (1,))) + dot(d_gate, wgate_ref[cols, :], ((1,), (1,)))
            dpre_ref[0:1, cols] += jnp.sum(h_ref[rows, cols].astype(f32) * scale * part, axis=0, keepdims=True)
            if keep:
                first = k * 256 // HALF * tokens
                y_ref[first : first + tokens, k * 256 % HALF : k * 256 % HALF + 256] = part
            else:
                mix_ref[rows, cols] = part.astype(bf16)

    def store_gate(i, value):
        kept = pl.ds(2 * SPAN + i * own_rows, own_rows)
        gate_ref[kept, :] = value
        copies.keep(gate_ref.at[kept], ggate_out.at[blocks[i][0], blocks[i][1]])

    def store_main(i, value):
        for first, count in ((0, HALF), (HALF, MAIN - HALF)):
            kept = pl.ds((first // HALF * TP + i) * own_rows, own_rows)
            gated_ref[kept, 0:count] = value[:, first : first + count]
            copies.keep(
                gated_ref.at[kept, pl.ds(0, count)], gmain_out.at[blocks[i][0], blocks[i][1], :, pl.ds(first, count)]
            )

    total = g_out.total(0)
    for k in range(D // HALF):
        kept = pl.ds(2 * TP * own_rows + k * out_rows, out_rows)
        gated_ref[kept, :] = total[:, k * HALF : (k + 1) * HALF]
        copies.keep(gated_ref.at[kept], gout_out.at[:, pl.ds(k * HALF, HALF)])
    g_out.left()
    gm_halves = [wout_ref.at[:, pl.ds(0, MAIN)], gm_ref]

    def grad_half(far):
        part = 1 - p if far else p
        out = gm_halves[0 if far else 1]

        def piece(i, _):
            xn = xn_ref[:, pl.ds(pl.multiple_of((part * 2 + i) * width, width), width)]
            rows = pl.ds(pl.multiple_of(i * width, width), width)
            for k in range(MAIN // 384):
                cols = slice(k * 384, (k + 1) * 384)
                out[rows, cols] = dot(xn, dmain_ref[:, cols], ((0,), (0,))).astype(bf16)
            return 0

        lax.fori_loop(0, 2, piece, 0)

    grad_half(True)
    g_main = GradientSum(copies, gm_halves, own_rows, gm_bufs, True)
    g_main.cores(0)
    dxs = GroupScatter(copies, mix_ref, dx_bufs)
    token_grad(blocks[3], False)
    dxs.to_t0(3)
    g_main.to_sides(0)
    token_grad(blocks[1], False)
    dxs.to_t0(1)
    grad_half(False)
    g_main.cores(1)
    g_main.to_part((1,))
    g_gate.to_group(store_gate)
    g_main.to_part((2,))
    g_main.to_sides(1)
    g_main.to_part((3,))

    mixer = mix_ref[mixes.block(0), :].astype(f32) + mixes.finish()
    copies.left([mixes.last_copy])
    for k in range(D // HALF):
        kept = pl.ds(spans * STATE + k * tokens, tokens)
        dn_ref[kept, :] = mixer[:, k * HALF : (k + 1) * HALF]
        copies.keep(dn_ref.at[kept], mixer_out.at[:, pl.ds(k * HALF, HALF)])
    hid = h_ref[mixes.block(0), :].astype(f32)
    valid = valid_ref[...]
    counts = [jnp.sum(valid * jnp.sum(v * v, axis=1, keepdims=True), axis=0, keepdims=True) for v in (hid, mixer)]
    counts.append(jnp.sum(valid, axis=0, keepdims=True))
    scalars = jnp.zeros((1, LANES), f32)
    for k in range(3):
        scalars = jnp.where(lane == k, counts[k], scalars)
    box = box_ref.at[0]
    box[...] = jnp.zeros_like(box)
    box[OWN_SUMS : OWN_SUMS + 1, :] = scalars

    token_grad(blocks[2], False)
    g_main.to_part((0,))
    dxs.to_t1()
    token_grad(blocks[0], True)

    for k in range(D // LANES):
        box[k : k + 1, :] = dpre_ref[0:1, k * LANES : (k + 1) * LANES]
    for k in range(HALF // LANES):
        lanes = slice(k * LANES, (k + 1) * LANES)
        box[OWN_NORM + k : OWN_NORM + k + 1, :] = dgain_ref[0:1, lanes]
        for j in range(CONV + 1):
            row = OWN_TAP + j * (HALF // LANES) + k
            box[row : row + 1, :] = dtaps_ref[j : j + 1, lanes]
    for k in range(SIDE // LANES):
        lanes = slice(HALF + k * LANES, HALF + (k + 1) * LANES)
        for j in range(CONV + 1):
            row = OWN_SIDE + j * (SIDE // LANES) + k
            box[row : row + 1, :] = dtaps_ref[j : j + 1, lanes]
    hsum_ref[0:1, :] = hsum_ref[0:1, :] * heads_ref[1:2, :]
    hsum_ref[2:3, :] = own_sums(dskip_ref[...])[0:1, :]
    lane8 = lax.broadcasted_iota(jnp.int32, (TILE, LANES), 1)
    box[OWN_HEAD : OWN_HEAD + 3, :] = jnp.where(lane8 < HEADS, head_lanes(hsum_ref[...], back=True), 0.0)[0:3]

    def small_step(k, hops):
        return [copies.send(box_ref.at[k], boxes_ref.at[k, i], flips) for i, flips in enumerate(hops)]

    def small_add(k, sent):
        total = box_ref[k]
        for i, copy in enumerate(sent):
            copy.wait_recv()
            total = total + boxes_ref[k, i]
        box_ref[k + 1] = total

    small = small_step(0, (CORE, SIDEWAYS, SIDE_CORE))
    g_gate.finish(store_gate)
    small_add(0, small)
    small = small_step(1, (PART,))
    small_add(1, small)
    small = small_step(2, (T0, T1, DIAG))
    g_main.to_group(store_main)
    dx = dxs.finish()
    for k in range(D // HALF):
        kept = pl.ds(k * tokens, tokens)
        y_ref[kept, :] += dx[:, k * HALF : (k + 1) * HALF]
        copies.keep(y_ref.at[kept], dx_out.at[:, pl.ds(k * HALF, HALF)])
    small_add(2, small)
    total_ref[...] = jnp.zeros_like(total_ref)
    total_ref[0:NORM_ROW, :] = box_ref[3, 0:NORM_ROW]
    third = QUARTER // LANES
    runs = [(OWN_NORM, NORM_ROW)]
    runs += [(OWN_TAP + j * 2 * third, TAP_ROW + j * TAP_ROWS) for j in range(CONV + 1)]
    for i, block in enumerate(blocks):
        source = box_ref.at[2] if i == 0 else boxes_ref.at[2, i - 1]
        place_at = (block[0] * 2 + block[1]) * third
        for own, first in runs:
            for k in range(2 * third):
                row = first + k // third * (D_INNER // 2 // LANES) + place_at + k % third
                total_ref[pl.ds(row, 1), :] = source[own + k : own + k + 1, :]
    for j in range(CONV + 1):
        row, own = TAP_ROW + TAP_ROWS * j + D_INNER // LANES, OWN_SIDE + j * (SIDE // LANES)
        total_ref[row : row + SIDE // LANES, :] = box_ref[3, own : own + SIDE // LANES]
    d_rate, d_shift, d_skip = (
        jnp.broadcast_to(box_ref[3, OWN_HEAD + k : OWN_HEAD + k + 1], (TILE, LANES)) for k in range(3)
    )
    spill = LANES - 2 * HEADS
    joined = d_shift + pltpu.roll(d_rate, HEADS, 1) + jnp.where(lane8 >= 2 * HEADS, pltpu.roll(d_skip, 2 * HEADS, 1), 0.0)
    total_ref[HEAD_ROW : HEAD_ROW + 1, :] = joined[0:1]
    spilled = jnp.where(lane8 < HEADS - spill, pltpu.roll(d_skip, LANES - spill, 1), 0.0)
    total_ref[HEAD_ROW + 1 : HEAD_ROW + 2, :] = spilled[0:1]
    total_ref[SMALL_ROWS : SMALL_ROWS + 1, :] = box_ref[3, OWN_SUMS : OWN_SUMS + 1]
    g_main.finish(store_main)
    copies.drain()


def update_kernel(
    hid_ref, mixer_ref, dx_ref, back_ref, pre_ref, gmain_ref, ggate_ref, gout_ref, total_ref,
    inw_ref, inm_ref, inv_ref, outw_ref, outm_ref, outv_ref, small_ref, smallm_ref, smallv_ref,
    output_ref, gh_ref, inm_out, inv_out, inw_out, outm_out, outv_out, outw_out, smallm_out, smallv_out, smallw_out, rms_ref,
):
    hid = hid_ref[...].astype(f32)
    output_ref[...] = (hid + mixer_ref[...]).astype(bf16)
    scale = lax.rsqrt(jnp.sum(hid * hid, axis=1, keepdims=True) / D + norm_eps)
    d_pre = dx_ref[...] * pre_ref[...]
    pulled = jnp.sum(hid * d_pre, axis=1, keepdims=True) / D * (scale * scale * scale)
    gh_ref[...] = back_ref[...].astype(f32) + scale * d_pre - hid * pulled

    def update(refs, outs, cols, grad, rate=0.02, decay=0.1):
        weight, moment, second = (ref[:, cols] for ref in refs)
        for out, value in zip(outs, adamw(weight, moment, second, grad, rate, decay)):
            out[:, cols] = value

    every = slice(None)
    update((outw_ref, outm_ref, outv_ref), (outm_out, outv_out, outw_out), every, gout_ref[...])
    in_refs, in_outs = (inw_ref, inm_ref, inv_ref), (inm_out, inv_out, inw_out)
    for j in range(TP):
        for k, chans in enumerate(own_chans(j)):
            part = slice(k * QUARTER, (k + 1) * QUARTER)
            update(in_refs, in_outs, chans, ggate_ref[j // 2, j % 2, :, part])
            scan = slice(D_INNER + chans.start, D_INNER + chans.stop)
            update(in_refs, in_outs, scan, gmain_ref[j // 2, j % 2, :, part])
    rest_grad = gmain_ref[0, 0, :, HALF:] + gmain_ref[0, 1, :, HALF:] + gmain_ref[1, 0, :, HALF:] + gmain_ref[1, 1, :, HALF:]
    first = 2 * D_INNER
    update(in_refs, in_outs, slice(first, first + SIDE), rest_grad[:, :SIDE])
    update(in_refs, in_outs, slice(first + SIDE, first + SIDE + HEADS), rest_grad[:, SIDE : SIDE + HEADS])

    @pl.when(pl.program_id(0) == 0)
    def _():
        update(
            (small_ref, smallm_ref, smallv_ref), (smallm_out, smallv_out, smallw_out), every, total_ref[0:SMALL_ROWS, :], 0.2, 0.0
        )
        totals = total_ref[SMALL_ROWS:, :]
        rms_ref[...] = jnp.sqrt(totals / (totals[0:1, 2:3] * D))


def linked(kernel, name, collective_id, in_specs, outs, scratch):
    return pl.pallas_call(
        kernel,
        name=name,
        in_specs=in_specs,
        out_shape=tuple(o for o, _ in outs),
        out_specs=tuple(s for _, s in outs),
        scratch_shapes=scratch,
        compiler_params=pltpu.CompilerParams(
            collective_id=collective_id, has_side_effects=True, vmem_limit_bytes=VMEM_LIMIT
        ),
    )


def shards_linked(
    hidden, cotangent, segments, valid, in_w, in_m, in_v, out_w, out_m, out_v, small_w, small_m, small_v,
):
    part = lax.axis_index("part")
    own_rows, out_rows = in_w.shape[0], out_w.shape[0]
    tok_rows = hidden.shape[1]
    rows = tok_rows * TP
    spans = rows // SPAN
    edge = jnp.full((FRONT,), -1, jnp.int32)
    seg_wide = lax.dynamic_slice_in_dim(jnp.concatenate([edge, segments[0], edge]), part * rows, rows + 2 * FRONT)
    seg_spans = seg_wide[FRONT : FRONT + rows].reshape(spans, SPAN)
    valid_col = valid[0].astype(f32)[:, None]
    small_size = small_w.shape[0]

    def small_box(array):
        return jnp.pad(array, (0, SMALL_ROWS * LANES - small_size)).reshape(SMALL_ROWS, LANES)

    small_w, small_m, small_v = small_box(small_w), small_box(small_m), small_box(small_v)
    pre_row = small_w[:NORM_ROW].reshape(1, D)

    wide = (rows, D)
    half = (rows, HALF)
    lanes = (rows, LANES)
    side = (rows, STATE)
    state = (STATE, HALF)
    main_outs = (
        (shape((tok_rows, D), bf16), HBM),
        (shape((tok_rows, D), f32), HBM),
        (shape((2, 2, own_rows, HALF), f32), HBM),
        (shape((2, 2, own_rows, MAIN), f32), HBM),
        (shape((tok_rows, D), f32), HBM),
        (shape((out_rows, D), f32), HBM),
        (shape((BOX_ROWS, LANES), f32), VMEM),
    )
    main_scratch = (
        (wide, bf16),
        (wide, bf16),
        ((D, MAIN), bf16),
        ((rows + FRONT, CHANS), bf16),
        (half, bf16),
        (side, bf16),
        (side, bf16),
        ((rows + FRONT, CHANS), f32),
        (lanes, f32),
        (lanes, f32),
        (lanes, f32),
        (half, f32),
        ((spans, *state), f32),
        ((D, HALF), bf16),
        ((HALF, D), bf16),
        (wide, bf16),
        (half, bf16),
        (wide, bf16),
        (half, bf16),
        (half, bf16),
        ((rows, MAIN), bf16),
        ((TILE, HALF), f32),
        ((TILE, CHANS), f32),
        ((TILE, LANES), f32),
        ((TILE, HALF), f32),
        ((rows, TILE), f32),
        ((spans, LANES), f32),
        (state, f32),
        (state, bf16),
        (state, bf16),
        ((FRONT, CHANS), bf16),
        (half, f32),
        (half, f32),
        (half, f32),
        ((2, TILE, rows), f32),
        ((2, 3, TILE, rows), f32),
        (half, bf16),
        (state, bf16),
        (state, bf16),
        ((TILE, CHANS), f32),
        ((TILE, CHANS), f32),
        ((TILE, LANES), f32),
        ((TILE, HALF), f32),
        ((TILE, CHANS), f32),
        ((TILE, D), f32),
        ((4, OWN_ROWS, LANES), f32),
        ((3, 3, OWN_ROWS, LANES), f32),
        ((D // 2, MAIN), bf16),
    )
    back_own, mixer, g_gate, g_main, d_x_normed, g_out, totals = linked(
        functools.partial(main_kernel, spans), "main", 1, [*[HBM] * 4, *[VMEM] * 5], main_outs,
        [
            *[pltpu.VMEM(dims, dtype) for dims, dtype in main_scratch],
            *sum_buffers(out_rows, D, False),
            *sum_buffers(own_rows, HALF, True),
            *sum_buffers(own_rows, MAIN, True),
            *scatter_buffers(tok_rows),
            *scatter_buffers(tok_rows),
            *sems(200, 48),
        ],
    )(hidden[0], in_w, out_w, cotangent[0], in_w[:, 2 * D_INNER :], valid_col, small_w, seg_wide[:, None], seg_spans)

    steps = own_rows // TILE

    def cut(dims, axis=0):
        block = tuple(size // steps if k == axis else size for k, size in enumerate(dims))
        return pl.BlockSpec(block, lambda i: tuple(i if k == axis else 0 for k in range(len(dims))))

    def fixed(dims):
        return pl.BlockSpec(dims, lambda i: (0, 0))

    tokens, matrix_in, matrix_out, small_dims = (tok_rows, D), in_w.shape, out_w.shape, (SMALL_ROWS, LANES)
    out_dims = [tokens] * 2 + [matrix_in] * 3 + [matrix_out] * 3
    (
        output, grad_hidden, in_m_new, in_v_new, in_w_new, out_m_new, out_v_new, out_w_new,
        small_m_new, small_v_new, small_w_new, rms,
    ) = pl.pallas_call(
        update_kernel,
        name="update",
        grid=(steps,),
        in_specs=[
            *[cut(tokens)] * 4,
            fixed((1, D)),
            cut(g_main.shape, 2),
            cut(g_gate.shape, 2),
            cut(matrix_out),
            fixed((BOX_ROWS, LANES)),
            *[cut(matrix_in)] * 3,
            *[cut(matrix_out)] * 3,
            *[fixed(small_dims)] * 3,
        ],
        out_shape=[
            *[shape(dims, bf16 if k == 0 else f32) for k, dims in enumerate(out_dims)],
            *[shape(small_dims, f32)] * 3,
            shape((TILE, LANES), f32),
        ],
        out_specs=[*[cut(dims) for dims in out_dims], *[fixed(small_dims)] * 3, fixed((TILE, LANES))],
        compiler_params=pltpu.CompilerParams(vmem_limit_bytes=VMEM_LIMIT),
    )(
        hidden[0], mixer, d_x_normed, back_own, pre_row, g_main, g_gate, g_out, totals,
        in_w, in_m, in_v, out_w, out_m, out_v, small_w, small_m, small_v,
    )
    small_m_new, small_v_new, small_w_new = (
        array.reshape(-1)[:small_size] for array in (small_m_new, small_v_new, small_w_new)
    )
    return (
        output[None], grad_hidden[None], in_m_new, in_v_new, in_w_new, out_m_new, out_v_new, out_w_new,
        small_m_new, small_v_new, small_w_new, rms[0, :2],
    )


def solution(mesh):
    seq, wt = mesh.shape["seq"], mesh.shape["wt"]
    split = Mesh(mesh.devices.reshape(seq // TP, 2, 2, wt // 2, 2), EVERYONE)
    streams = ("w1", "w0")
    tokens = ("part", "t1", "t0")
    matrix = P(EVERYONE, None)
    stream = P(streams, tokens, None)
    size = mesh.devices.size
    fits = seq == 2 * TP and wt == 4 and D // size % 16 == 0 and D_INNER // size % 16 == 0
    return jax.shard_map(
        shards_linked if fits else shards_general,
        mesh=split,
        in_specs=(
            stream, stream, P(streams, None), P(streams, tokens), matrix, matrix, matrix, matrix, matrix, matrix, P(), P(), P(),
        ),
        out_specs=(stream, stream, matrix, matrix, matrix, matrix, matrix, matrix, P(), P(), P(), P()),
        check_vma=False,
    )
```

```python
import functools

import jax
import jax.numpy as jnp
from jax import lax
from jax.experimental import pallas as pl
from jax.experimental.pallas import tpu as pltpu
from jax.sharding import Mesh
from jax.sharding import PartitionSpec as P

D = 1536
D_INNER = 3072
HEADS = 48
HEADDIM = 64
STATE = 128
CONV = 4
SPAN = 256
STEP = 4
CONVCH = 3328
TP = 4
RIM = CONV - 1
LANES = 128
HALF = D_INNER // TP
LOCAL_HEADS = HEADS // TP
PAIRS = LOCAL_HEADS // 2
SIDE = 2 * STATE
COL_SIDE = HALF
COL_DT = HALF + SIDE
COL_GATE = COL_DT + LANES
COLS = COL_GATE + HALF

bf16 = jnp.bfloat16
f32 = jnp.float32
exact_prec = lax.Precision.HIGHEST
norm_eps = 1e-05
adam_eps = 1e-08


def dot(a, b, dims=((1,), (0,)), precision=None):
    return lax.dot_general(a, b, (dims, ((), ())), precision=precision, preferred_element_type=f32)


def unpack_small(small):
    first = D
    second = first + D_INNER
    third = second + CONV * CONVCH
    fourth = third + CONVCH
    fifth = fourth + HEADS
    sixth = fifth + HEADS
    return (
        small[:first],
        small[first:second],
        small[second:third].reshape(CONV, CONVCH),
        small[third:fourth],
        small[fourth:fifth],
        small[fifth:sixth],
        small[sixth:],
    )


def adamw(weight, moment, second, grad, rate, decay):
    moment_new = 0.5 * moment + 0.5 * grad
    second_new = 0.5 * second + 0.5 * grad * grad
    first_hat = moment_new / (1.0 - 0.5**STEP)
    second_hat = second_new / (1.0 - 0.5**STEP)
    weight_new = weight - rate * (first_hat / (jnp.sqrt(second_hat) + adam_eps) + decay * weight)
    return (moment_new, second_new, weight_new)


def pair_cols(cols, h):
    lane = lax.broadcasted_iota(jnp.int32, (cols.shape[0], LANES), 1)
    return jnp.where(lane < HEADDIM, cols[:, h : h + 1], cols[:, h + 1 : h + 2])


def span_rows(c):
    return pl.ds(pl.multiple_of(c * SPAN, SPAN), SPAN)


def span_decay(dt_ref, rate_ref, c, at=0):
    dt = dt_ref[span_rows(c), :]
    row = lax.broadcasted_iota(jnp.int32, (SPAN, SPAN), 0)
    col = lax.broadcasted_iota(jnp.int32, (SPAN, SPAN), 1)
    lower = (row >= col).astype(f32)
    return dt, dot(lower, dt * rate_ref[at : at + 1, :], precision=exact_prec)


def state_kernel(spans, x_ref, b_ref, dt_ref, rate_ref, keep_ref, carry_ref, s_ref, dec_ref):
    s_ref[...] = jnp.zeros_like(s_ref)
    dec_ref[...] = jnp.ones_like(dec_ref)

    def body(c, _):
        rows = span_rows(c)
        dt, cum = span_decay(dt_ref, rate_ref, c)
        last = cum[SPAN - 1 : SPAN, :]
        end_weight = jnp.exp(last - cum) * dt * keep_ref[rows, :]
        decay = jnp.exp(last) * carry_ref[pl.ds(c, 1), :]
        dec_ref[...] = dec_ref[...] * decay
        b = b_ref[rows, :]
        for p in range(PAIRS):
            lanes = slice(p * LANES, (p + 1) * LANES)
            xw = (x_ref[rows, lanes].astype(f32) * pair_cols(end_weight, 2 * p)).astype(bf16)
            fresh = dot(b, xw, ((0,), (0,)))
            s_ref[:, lanes] = s_ref[:, lanes] * pair_cols(decay, 2 * p) + fresh
        return 0

    lax.fori_loop(0, spans, body, 0)


def scan_kernel(
    spans, x_ref, b_ref, c_ref, dt_ref, rate_ref, segc_ref, segr_ref, keep_ref, inflow_ref, carry_ref, s_in_ref,
    y_ref, st_ref, s_ref,
):
    s_ref[...] = s_in_ref[...]

    def body(c, _):
        rows = span_rows(c)
        dt, cum = span_decay(dt_ref, rate_ref, c)
        last = cum[SPAN - 1 : SPAN, :]
        end_weight = jnp.exp(last - cum) * dt * keep_ref[rows, :]
        decay = jnp.exp(last) * carry_ref[pl.ds(c, 1), :]
        gain = jnp.exp(cum) * inflow_ref[rows, :]
        back_log = jnp.transpose(cum - jnp.log(dt))
        b = b_ref[rows, :]
        cc = c_ref[rows, :]
        scores = dot(cc, b, ((1,), (1,)))
        row = lax.broadcasted_iota(jnp.int32, (SPAN, SPAN), 0)
        col = lax.broadcasted_iota(jnp.int32, (SPAN, SPAN), 1)
        mask = (row >= col) & (segc_ref[rows, :] == segr_ref[pl.ds(c, 1), :])
        lane = lax.broadcasted_iota(jnp.int32, (SPAN, LANES), 1)
        st_ref[c] = s_ref[...]
        for p in range(PAIRS):
            lanes = slice(p * LANES, (p + 1) * LANES)
            x = x_ref[rows, lanes]
            parts = []
            for h in (2 * p, 2 * p + 1):
                gap = cum[:, h : h + 1] - back_log[h : h + 1, :]
                weights = scores * jnp.exp(jnp.where(mask, gap, -1e30))
                parts.append(dot(weights.astype(bf16), x))
            y = jnp.where(lane < HEADDIM, parts[0], parts[1])
            state = s_ref[:, lanes]
            y = y + dot(cc, state.astype(bf16)) * pair_cols(gain, 2 * p)
            y_ref[rows, lanes] = y
            xw = (x.astype(f32) * pair_cols(end_weight, 2 * p)).astype(bf16)
            s_ref[:, lanes] = state * pair_cols(decay, 2 * p) + dot(b, xw, ((0,), (0,)))
        return 0

    lax.fori_loop(0, spans, body, 0)


def state_back_kernel(spans, dy_ref, c_ref, dt_ref, rate_ref, inflow_ref, carry_ref, s_ref):
    s_ref[...] = jnp.zeros_like(s_ref)

    def body(step, _):
        c = spans - 1 - step
        rows = span_rows(c)
        dt, cum = span_decay(dt_ref, rate_ref, c)
        decay = jnp.exp(cum[SPAN - 1 : SPAN, :]) * carry_ref[pl.ds(c, 1), :]
        gain = jnp.exp(cum) * inflow_ref[rows, :]
        cc = c_ref[rows, :]
        for p in range(PAIRS):
            lanes = slice(p * LANES, (p + 1) * LANES)
            dyg = (dy_ref[rows, lanes].astype(f32) * pair_cols(gain, 2 * p)).astype(bf16)
            s_ref[:, lanes] = s_ref[:, lanes] * pair_cols(decay, 2 * p) + dot(cc, dyg, ((0,), (0,)))
        return 0

    lax.fori_loop(0, spans, body, 0)


def head_sums(values):
    width = values.shape[1]
    chan = lax.broadcasted_iota(jnp.int32, (width, LANES), 0)
    head = lax.broadcasted_iota(jnp.int32, (width, LANES), 1)
    pick = (chan // HEADDIM == head).astype(bf16)
    high = values.astype(bf16)
    low = (values - high.astype(f32)).astype(bf16)
    return dot(high, pick) + dot(low, pick)


def scan_back_kernel(
    spans, x_ref, b_ref, c_ref, dt_ref, ratio_ref, sig_ref, rate_ref, segc_ref, segr_ref, keep_ref, inflow_ref, carry_ref, skip_ref,
    y_ref, st_ref, dy_ref, ds_out_ref,
    dx_ref, db_ref, dc_ref, ddt_ref, drate_ref, dskip_ref,
    ds_ref, prod_ref,
):
    ds_ref[...] = ds_out_ref[...]
    drate_ref[...] = jnp.zeros_like(drate_ref)
    dskip_ref[...] = jnp.zeros_like(dskip_ref)

    def body(step, _):
        c = spans - 1 - step
        rows = span_rows(c)
        dt, cum = span_decay(dt_ref, rate_ref, c)
        last = cum[SPAN - 1 : SPAN, :]
        end_weight = jnp.exp(last - cum) * dt * keep_ref[rows, :]
        decay = jnp.exp(last) * carry_ref[pl.ds(c, 1), :]
        gain = jnp.exp(cum) * inflow_ref[rows, :]
        fore_log = jnp.transpose(cum)
        back_log = cum - jnp.log(dt)
        b = b_ref[rows, :]
        cc = c_ref[rows, :]
        scores = dot(b, cc, ((1,), (1,)))
        row = lax.broadcasted_iota(jnp.int32, (SPAN, SPAN), 0)
        col = lax.broadcasted_iota(jnp.int32, (SPAN, SPAN), 1)
        mask = (col >= row) & (segc_ref[rows, :] == segr_ref[pl.ds(c, 1), :])
        lane = lax.broadcasted_iota(jnp.int32, (SPAN, LANES), 1)
        d_scores = jnp.zeros((SPAN, SPAN), f32)
        db = jnp.zeros((SPAN, STATE), f32)
        dc = jnp.zeros((SPAN, STATE), f32)
        state_row = []
        dx_state_row = []
        for p in range(PAIRS):
            lanes = slice(p * LANES, (p + 1) * LANES)
            x = x_ref[rows, lanes]
            dy = dy_ref[rows, lanes]
            xf = x.astype(f32)
            dyf = dy.astype(f32)
            parts = []
            for k in range(2):
                h = 2 * p + k
                gap = fore_log[h : h + 1, :] - back_log[:, h : h + 1]
                decay_mat = jnp.exp(jnp.where(mask, gap, -1e30))
                weights = (scores * decay_mat).astype(bf16)
                parts.append(dot(weights, dy))
                own = (lane < HEADDIM) if k == 0 else (lane >= HEADDIM)
                d_weights = dot(jnp.where(own, xf, 0.0).astype(bf16), dy, ((1,), (1,)))
                d_scores = d_scores + d_weights * decay_mat
            dx = jnp.where(lane < HEADDIM, parts[0], parts[1])
            dyg = (dyf * pair_cols(gain, 2 * p)).astype(bf16)
            ew = pair_cols(end_weight, 2 * p)
            xw = (xf * ew).astype(bf16)
            state = st_ref[c, :, lanes]
            ds = ds_ref[:, lanes]
            state_b = state.astype(bf16)
            ds_b = ds.astype(bf16)
            dc = dc + dot(dyg, state_b, ((1,), (1,)))
            db = db + dot(xw, ds_b, ((1,), (1,)))
            dx_state = dot(b, ds_b) * ew
            dx = dx + dx_state
            dec = pair_cols(decay, 2 * p)
            state_row.append(jnp.sum(ds * state, axis=0, keepdims=True) * dec)
            dx_state_row.append(jnp.sum(dx_state * xf, axis=0, keepdims=True))
            ds_ref[:, lanes] = ds * dec + dot(cc, dyg, ((0,), (0,)))
            prod_ref[0:SPAN, lanes] = dyf * y_ref[rows, lanes]
            prod_ref[SPAN : 2 * SPAN, lanes] = xf * dx
            dskip_ref[0:1, lanes] += jnp.sum(dyf * xf, axis=0, keepdims=True)
            dx_ref[rows, lanes] = (dx + dyf * skip_ref[0:1, lanes]).astype(bf16)
        d_scores_b = d_scores.astype(bf16)
        db_ref[rows, :] = db + dot(d_scores_b, cc)
        dc_ref[rows, :] = dc + dot(d_scores_b, b, ((0,), (0,)))
        sums = head_sums(prod_ref[...])
        out_sum, in_sum = sums[:SPAN], sums[SPAN:]
        edge = jnp.concatenate(state_row, axis=1) + jnp.concatenate(dx_state_row, axis=1)
        edge_sum = head_sums(jnp.broadcast_to(edge, (8, HALF)))[0:1]
        at_last = lax.broadcasted_iota(jnp.int32, (SPAN, LANES), 0) == SPAN - 1
        d_cum = out_sum - in_sum + jnp.where(at_last, edge_sum, 0.0)
        upper = (col >= row).astype(f32)
        d_log = dot(upper, d_cum, precision=exact_prec)
        drate_ref[0:1, :] += jnp.sum(d_log * dt, axis=0, keepdims=True)
        ddt_ref[rows, :] = d_log * rate_ref[0:1, :] * sig_ref[rows, :] + in_sum * ratio_ref[rows, :]
        return 0

    lax.fori_loop(0, spans, body, 0)


GROUP = ("t1", "t0")
COPIES = ("part", "w1", "w0")
EVERYONE = ("part", "t1", "t0", "w1", "w0")


VMEM_LIMIT = 63 * 1024 * 1024


def in_vmem(kernel, out_shape, name, scratch=()):
    return pl.pallas_call(
        kernel,
        out_shape=out_shape,
        scratch_shapes=list(scratch),
        name=name,
        compiler_params=pltpu.CompilerParams(vmem_limit_bytes=VMEM_LIMIT),
    )


def shape(dims, dtype):
    return jax.ShapeDtypeStruct(dims, dtype)


def shift_part(array, by):
    size = lax.axis_size("part")
    pairs = [(i, i + by) for i in range(size) if 0 <= i + by < size]
    return lax.ppermute(array, "part", pairs)


def shards_general(
    hidden, cotangent, segments, valid, in_w, in_m, in_v, out_w, out_m, out_v, small_w, small_m, small_v,
):
    parts = lax.axis_size("part")
    wt = lax.axis_size("w1") * lax.axis_size("w0")
    part = lax.axis_index("part")
    tp = lax.axis_index("t1") * 2 + lax.axis_index("t0")
    own_rows = in_w.shape[0]
    out_rows = out_w.shape[0]
    resid = hidden[0].astype(f32)
    tok_rows = resid.shape[0]
    rows = tok_rows * TP
    spans = rows // SPAN
    seg_all = segments[0]
    pre_gain, norm_gain, conv_weight, conv_bias, dt_shift, a_logs, skips = unpack_small(small_w)

    def own_part(array, width):
        return lax.dynamic_slice_in_dim(array, tp * width, width, array.ndim - 1)

    in_copy = in_w.astype(bf16)
    slices = []
    for j in range(TP):
        slices.append(
            jnp.concatenate(
                [
                    in_copy[:, D_INNER + j * HALF : D_INNER + (j + 1) * HALF],
                    in_copy[:, 2 * D_INNER : 2 * D_INNER + SIDE],
                    in_copy[:, D_INNER + CONVCH + j * LOCAL_HEADS : D_INNER + CONVCH + (j + 1) * LOCAL_HEADS],
                    jnp.zeros((own_rows, LANES - LOCAL_HEADS), bf16),
                    in_copy[:, j * HALF : (j + 1) * HALF],
                ],
                axis=1,
            )
        )
    mine = lax.all_to_all(jnp.stack(slices), GROUP, 0, 0, tiled=False)
    w_in = lax.all_gather(mine, COPIES, axis=0, tiled=False)
    w_in = w_in.reshape(parts, wt, TP, own_rows, COLS).transpose(0, 2, 1, 3, 4).reshape(D, COLS)
    flat = [(i, (i % TP) * parts + i // TP) for i in range(parts * TP)]
    out_mine = lax.ppermute(out_w.astype(bf16), ("part", *GROUP), [(b, a) for a, b in flat])
    w_out = lax.all_gather(out_mine, COPIES, axis=0, tiled=True)

    hidden_all = lax.all_gather(hidden[0], GROUP, axis=0, tiled=True)
    back_mix = cotangent[0] * valid[0][:, None].astype(bf16)
    back_all = lax.all_gather(back_mix, GROUP, axis=0, tiled=True)

    hid = hidden_all.astype(f32)
    scale_all = lax.rsqrt(jnp.mean(hid * hid, axis=1, keepdims=True) + norm_eps)
    x_normed = (hid * scale_all * pre_gain).astype(bf16)
    projected = dot(x_normed, w_in)
    conv_in = projected[:, :COL_DT].astype(bf16)
    dt_raw = projected[:, COL_DT:COL_GATE].astype(bf16).astype(f32)
    gate_pre = projected[:, COL_GATE:]
    rim_in = shift_part(conv_in[rows - RIM :], 1)
    padded = jnp.concatenate([rim_in, conv_in], axis=0).astype(f32)
    seg_front = jnp.concatenate([jnp.full((RIM,), -1, jnp.int32), seg_all, jnp.full((RIM,), -1, jnp.int32)])
    seg_pad = lax.dynamic_slice_in_dim(seg_front, part * rows, rows + 2 * RIM)
    seg = seg_pad[RIM : RIM + rows]
    masks = [(seg_pad[k : k + rows] == seg).astype(f32)[:, None] for k in range(CONV)]
    taps = jnp.concatenate([own_part(conv_weight[:, :D_INNER], HALF), conv_weight[:, D_INNER:]], axis=1)
    bias = jnp.concatenate([own_part(conv_bias[:D_INNER], HALF), conv_bias[D_INNER:]])
    total = bias[None, :]
    for k in range(CONV):
        total = total + taps[k] * padded[k : k + rows] * masks[k]
    sig_total = jax.nn.sigmoid(total)
    activated = (total * sig_total).astype(bf16)
    x_scan = activated[:, :HALF]
    b_mat = activated[:, HALF : HALF + STATE]
    c_mat = activated[:, HALF + STATE :]

    def head_row(array):
        return jnp.pad(own_part(array, LOCAL_HEADS), (0, LANES - LOCAL_HEADS))

    shift_row = head_row(dt_shift)
    z = dt_raw + shift_row
    dt = jax.nn.softplus(z)
    sig_dt = jax.nn.sigmoid(z)
    ratio = jnp.where(dt > 1e-30, sig_dt / jnp.maximum(dt, 1e-30), 1.0)
    rate_row = -jnp.exp(head_row(a_logs))
    rate8 = jnp.broadcast_to(rate_row, (8, LANES))
    skip_chan = jnp.repeat(own_part(skips, LOCAL_HEADS), HEADDIM)
    skip8 = jnp.broadcast_to(skip_chan, (8, HALF))
    seg_spans = seg.reshape(spans, SPAN)
    seg_last = seg_spans[:, -1]
    seg_before = jnp.concatenate([seg_pad[RIM - 1 : RIM], seg_last[:-1]])
    keep = (seg_spans == seg_last[:, None]).astype(f32).reshape(rows, 1)
    inflow = (seg_spans == seg_before[:, None]).astype(f32).reshape(rows, 1)
    carry = jnp.broadcast_to((seg_last == seg_before).astype(f32)[:, None], (spans, LANES))
    seg_col = seg[:, None]

    state_shape = shape((STATE, HALF), f32)
    s_local, dec_total = in_vmem(
        functools.partial(state_kernel, spans), (state_shape, shape((8, LANES), f32)), "state"
    )(x_scan, b_mat, dt, rate8, keep, carry)
    dec_chan = jnp.repeat(dec_total[0, :LOCAL_HEADS], HEADDIM)
    s_in = jnp.zeros((STATE, HALF), f32)
    for _ in range(parts - 1):
        s_in = shift_part(dec_chan * s_in + s_local, 1)
    y_scan, states = in_vmem(
        functools.partial(scan_kernel, spans),
        (shape((rows, HALF), f32), shape((spans, STATE, HALF), f32)),
        "scan",
        [pltpu.VMEM((STATE, HALF), f32)],
    )(x_scan, b_mat, c_mat, dt, rate8, seg_col, seg_spans, keep, inflow, carry, s_in)
    y_b = (y_scan + skip_chan * x_scan.astype(f32)).astype(bf16).astype(f32)

    gain_own = own_part(norm_gain, HALF)
    sig_gate = jax.nn.sigmoid(gate_pre)
    silu_gate = gate_pre * sig_gate
    gated = y_b * silu_gate
    gate_sq = lax.psum(jnp.sum(gated * gated, axis=1), GROUP)
    scale_gate = lax.rsqrt(gate_sq / D_INNER + norm_eps)[:, None]
    normed = (gated * scale_gate * gain_own).astype(bf16)
    mixer = lax.psum_scatter(dot(normed, w_out), GROUP, scatter_dimension=0, tiled=True)
    output = (resid + mixer).astype(bf16)
    valid_rows = valid[0].astype(f32)
    res_sq = jnp.sum(valid_rows * jnp.sum(resid * resid, axis=1))
    mix_sq = jnp.sum(valid_rows * jnp.sum(mixer * mixer, axis=1))
    valid_count = jnp.sum(valid_rows)

    d_normed = dot(back_all, w_out, ((1,), (1,)))
    g_out = dot(normed, back_all, ((0,), (0,)))
    g_out = lax.psum_scatter(g_out, COPIES, scatter_dimension=0, tiled=True)
    g_out = lax.ppermute(g_out, ("part", *GROUP), flat)
    d_gain = d_normed * gain_own
    gate_dot = lax.psum(jnp.sum(gated * d_gain, axis=1), GROUP)
    d_gated = scale_gate * d_gain - gated * (scale_gate**3 * (gate_dot / D_INNER)[:, None])
    d_norm_gain = jnp.sum(gated * scale_gate * d_normed, axis=0)
    dy = (d_gated * silu_gate).astype(bf16)
    d_gate = d_gated * y_b * (sig_gate * (1.0 + gate_pre * (1.0 - sig_gate)))

    ds_local = in_vmem(functools.partial(state_back_kernel, spans), state_shape, "state_back")(
        dy, c_mat, dt, rate8, inflow, carry
    )
    ds_out = jnp.zeros((STATE, HALF), f32)
    for _ in range(parts - 1):
        ds_out = shift_part(dec_chan * ds_out + ds_local, -1)
    d_x, d_b, d_c, d_dt, d_rate, d_skip = in_vmem(
        functools.partial(scan_back_kernel, spans),
        (
            shape((rows, HALF), bf16),
            shape((rows, STATE), f32),
            shape((rows, STATE), f32),
            shape((rows, LANES), f32),
            shape((8, LANES), f32),
            shape((8, HALF), f32),
        ),
        "scan_back",
        [pltpu.VMEM((STATE, HALF), f32), pltpu.VMEM((2 * SPAN, HALF), f32)],
    )(x_scan, b_mat, c_mat, dt, ratio, sig_dt, rate8, seg_col, seg_spans, keep, inflow, carry, skip8, y_scan, states, dy, ds_out)

    d_total = jnp.concatenate([d_x.astype(f32), d_b, d_c], axis=1) * (sig_total * (1.0 + total * (1.0 - sig_total)))
    rim_back = shift_part(d_total[:RIM], -1)
    d_padded = jnp.concatenate([d_total, rim_back], axis=0)
    d_conv_in = 0.0
    for k in range(CONV):
        later = (seg_pad[2 * RIM - k : 2 * RIM - k + rows] == seg).astype(f32)[:, None]
        d_conv_in = d_conv_in + taps[k] * d_padded[RIM - k : RIM - k + rows] * later
    d_taps = jnp.stack([jnp.sum(d_total * padded[k : k + rows] * masks[k], axis=0) for k in range(CONV)])
    d_bias = jnp.sum(d_total, axis=0)
    d_proj = jnp.concatenate([d_conv_in, d_dt, d_gate], axis=1).astype(bf16)
    d_x_normed = dot(d_proj, w_in, ((1,), (1,)))
    d_x_normed = lax.psum_scatter(d_x_normed, GROUP, scatter_dimension=0, tiled=True)
    g_in = dot(x_normed, d_proj, ((0,), (0,)))
    g_in = g_in.reshape(parts, TP, wt, own_rows, COLS).transpose(0, 2, 1, 3, 4).reshape(parts * wt, TP, own_rows, COLS)
    g_in = lax.psum_scatter(g_in, COPIES, scatter_dimension=0, tiled=False)
    g_in = lax.all_to_all(g_in, GROUP, 0, 0, tiled=False)
    g_in = jnp.concatenate(
        [g_in[j, :, COL_GATE:] for j in range(TP)]
        + [g_in[j, :, :HALF] for j in range(TP)]
        + [jnp.sum(g_in[:, :, COL_SIDE:COL_DT], axis=0)]
        + [g_in[j, :, COL_DT : COL_DT + LOCAL_HEADS] for j in range(TP)],
        axis=1,
    )

    scale_own = lax.rsqrt(jnp.mean(resid * resid, axis=1, keepdims=True) + norm_eps)
    d_pre = d_x_normed * pre_gain
    dot_pre = jnp.mean(resid * d_pre, axis=1, keepdims=True)
    grad_hidden = back_mix.astype(f32) + scale_own * d_pre - resid * (scale_own**3 * dot_pre)
    d_pre_gain = jnp.sum(resid * scale_own * d_x_normed, axis=0)

    def placed(values, width):
        spread = (jnp.arange(TP) == tp).astype(f32)[:, None] * values[..., None, :]
        return spread.reshape(*values.shape[:-1], TP * width)

    d_weight = jnp.concatenate([placed(d_taps[:, :HALF], HALF), d_taps[:, HALF:]], axis=1)
    small_grad = jnp.concatenate(
        [
            d_pre_gain,
            placed(d_norm_gain, HALF),
            d_weight.reshape(-1),
            placed(d_bias[:HALF], HALF),
            d_bias[HALF:],
            placed(jnp.sum(d_dt, axis=0)[:LOCAL_HEADS], LOCAL_HEADS),
            placed((d_rate[0] * rate_row)[:LOCAL_HEADS], LOCAL_HEADS),
            placed(jnp.sum(d_skip[0].reshape(LOCAL_HEADS, HEADDIM), axis=1), LOCAL_HEADS),
            jnp.stack([res_sq, mix_sq, valid_count]),
        ]
    )
    small_total = lax.psum(small_grad, EVERYONE)
    res_total, mix_total, count_total = small_total[-3], small_total[-2], small_total[-1]
    in_m_new, in_v_new, in_w_new = adamw(in_w, in_m, in_v, g_in, 0.02, 0.1)
    out_m_new, out_v_new, out_w_new = adamw(out_w, out_m, out_v, g_out, 0.02, 0.1)
    small_m_new, small_v_new, small_w_new = adamw(small_w, small_m, small_v, small_total[:-3], 0.2, 0.0)
    rms = jnp.stack([jnp.sqrt(res_total / (count_total * D)), jnp.sqrt(mix_total / (count_total * D))])
    return (
        output[None], grad_hidden[None], in_m_new, in_v_new, in_w_new, out_m_new, out_v_new, out_w_new,
        small_m_new, small_v_new, small_w_new, rms,
    )


MESH = pl.DeviceIdType.MESH
T0, T1, DIAG, CORE, SIDEWAYS, PART = ("t0",), ("t1",), ("t1", "t0"), ("w0",), ("w1",), ("part",)
SIDE_CORE = ("w1", "w0")
HOPS = (None, T0, T1, DIAG)
HBM = pl.BlockSpec(memory_space=pl.ANY)
VMEM = pl.BlockSpec(memory_space=pltpu.VMEM)
MAIN = COL_GATE
CHANS = HALF + SIDE
FRONT = 16
TILE = 8
QUARTER = HALF // 2
NORM_ROW = D // LANES
TAP_ROW = NORM_ROW + D_INNER // LANES
TAP_ROWS = CONVCH // LANES
HEAD_ROW = TAP_ROW + (CONV + 1) * TAP_ROWS
SMALL_ROWS = HEAD_ROW + 2
BOX_ROWS = SMALL_ROWS + 8
OWN_NORM = NORM_ROW
OWN_TAP = OWN_NORM + HALF // LANES
OWN_SIDE = OWN_TAP + (CONV + 1) * (HALF // LANES)
OWN_HEAD = OWN_SIDE + (CONV + 1) * (SIDE // LANES)
OWN_SUMS = OWN_HEAD + 3
OWN_ROWS = 64


def place():
    return tuple(lax.axis_index(a) for a in EVERYONE)


def across(flips):
    return {a: 1 - lax.axis_index(a) for a in flips}


def group_blocks():
    _, t1, t0, _, _ = place()
    return [(t1, t0), (t1, 1 - t0), (1 - t1, t0), (1 - t1, 1 - t0)]


def greet(neighbours):
    barrier = pltpu.get_barrier_semaphore()
    for flips in neighbours:
        pl.semaphore_signal(barrier, inc=1, device_id=across(flips), device_id_type=MESH)


def greeted(neighbours):
    pl.semaphore_wait(pltpu.get_barrier_semaphore(), len(neighbours))


class Copies:
    def __init__(self, local_sem, send_sem, recv_sem):
        self.local_sem, self.send_sem, self.recv_sem = local_sem, send_sem, recv_sem
        self.sent, self.kept, self.in_flight, self.on_device = 0, 0, [], []

    def send(self, src, dst, flips):
        copy = pltpu.make_async_remote_copy(
            src_ref=src,
            dst_ref=dst,
            send_sem=self.send_sem.at[self.sent],
            recv_sem=self.recv_sem.at[self.sent],
            device_id=across(flips),
            device_id_type=MESH,
        )
        copy.start()
        self.sent += 1
        self.in_flight.append(copy)
        return copy

    def keep(self, src, dst):
        copy = pltpu.make_async_copy(src, dst, self.local_sem.at[self.kept])
        copy.start()
        self.kept += 1
        self.on_device.append(copy)
        return copy

    def settle(self, copy):
        copy.wait()
        self.on_device = [other for other in self.on_device if other is not copy]

    def left(self, copies):
        for copy in copies:
            copy.wait_send()
            self.in_flight = [other for other in self.in_flight if other is not copy]

    def drain(self):
        for copy in self.in_flight:
            copy.wait_send()
        for copy in self.on_device:
            copy.wait()
        self.in_flight, self.on_device = [], []


def sems(remote, local=1):
    return [
        pltpu.SemaphoreType.DMA((local,)),
        pltpu.SemaphoreType.DMA((remote,)),
        pltpu.SemaphoreType.DMA((remote,)),
    ]


class GroupGather:
    def __init__(self, copies, src, dst):
        self.copies, self.dst = copies, dst
        self.rows = src.shape[0]
        self.halves = (0, self.rows // 2)
        own = group_blocks()[0]
        self.src, self.own, self.size = src, copies.keep(src, self.at(own, 0, self.rows)), self.rows // 2
        self.along_t1, self.along_t0, self.diagonal = self.start(T1), [], []

    def start(self, flips):
        own = group_blocks()[0]
        return [
            self.copies.send(self.src.at[pl.ds(h, self.size)], self.at(own, h, self.size), flips) for h in self.halves
        ]

    def start_t0(self):
        self.along_t0 = self.start(T0)

    def at(self, block, first, size):
        return self.dst.at[pl.ds(pl.multiple_of((block[0] * 2 + block[1]) * self.rows + first, size), size)]

    def hand_on(self):
        beside = group_blocks()[2]
        for copy, h in zip(self.along_t1, self.halves):
            copy.wait_recv()
            here = self.at(beside, h, self.rows // 2)
            self.diagonal.append(self.copies.send(here, here, T0))

    def finish(self):
        for copy in self.along_t0 + self.diagonal:
            copy.wait_recv()


class WeightGather:
    def __init__(self, copies, dst, rows, group):
        self.copies, self.dst, self.rows, self.group = copies, dst, rows, group
        self.by_part, self.by_side, self.by_core = [], [], []

    def at(self, part, w1, w0, block):
        index = part
        if self.group:
            index = (index * 2 + block[0]) * 2 + block[1]
        index = (index * 2 + w1) * 2 + w0
        return self.dst.at[pl.ds(pl.multiple_of(index * self.rows, self.rows), self.rows)]

    def mine(self, block):
        p, _, _, w1, w0 = place()
        return self.at(p, w1, w0, block)

    def spread(self, src, block):
        dst = self.mine(block)
        self.by_part.append((self.copies.send(src, dst, PART), block))
        self.by_side.append((self.copies.send(src, dst, SIDEWAYS), block))
        self.by_core.append(self.copies.send(src, dst, CORE))

    def swap(self, src):
        own, *others = group_blocks()

        def slice_of(block):
            return src.at[block_rows(block, self.rows)]

        self.swaps = [(self.copies.send(slice_of(b), self.mine(own), flips), b) for b, flips in zip(others, HOPS[1:])]
        self.kept = self.copies.keep(slice_of(own), self.mine(own))
        self.spread(slice_of(own), own)

    def spread_swapped(self):
        for copy, block in self.swaps:
            copy.wait_recv()
            self.spread(self.mine(block), block)

    def pass_core(self, part, w1, block):
        here = self.at(part, w1, lax.axis_index("w0"), block)
        self.by_core.append(self.copies.send(here, here, CORE))

    def hand_on(self):
        p, _, _, w1, w0 = place()
        self.again = []
        for (copy, block), (side, _) in zip(self.by_part, self.by_side):
            side.wait_recv()
            self.pass_core(p, 1 - w1, block)
            copy.wait_recv()
            here = self.at(1 - p, w1, w0, block)
            self.again.append((self.copies.send(here, here, SIDEWAYS), block))
            self.pass_core(1 - p, w1, block)

    def hand_on_last(self):
        p, _, _, w1, _ = place()
        for copy, block in self.again:
            copy.wait_recv()
            self.pass_core(1 - p, 1 - w1, block)

    def finish(self):
        for copy in self.by_core:
            copy.wait_recv()


class GradientSum:
    def __init__(self, copies, srcs, rows, bufs, group):
        self.copies, self.srcs, self.rows, self.group = copies, srcs, rows, group
        self.core, self.sides, self.fars = bufs[:3]
        self.lasts = bufs[3] if group else None
        self.blocks = group_blocks() if group else [()]
        self.order = (1, 2, 3, 0) if group else (0,)
        p, _, _, w1, _ = place()
        self.parts, self.sides_of = (1 - p, p), (1 - w1, w1)
        self.core_copies, self.side_copies, self.far_copies, self.last_copies = {}, {}, {}, {}

    def at(self, block, side, w0):
        index = block[0] * 2 + block[1] if self.group else 0
        index = (index * 2 + side) * 2 + w0
        return pl.ds(pl.multiple_of(index * self.rows, self.rows), self.rows)

    def place(self, i, j):
        return self.at(self.blocks[i], self.sides_of[j], lax.axis_index("w0"))

    def pass_on(self, k, i, j, value, dst, flips):
        here = self.place(i, j)
        self.srcs[k][here, :] = value.astype(bf16)
        return self.copies.send(self.srcs[k].at[here], dst, flips)

    def added(self, k, i, j, *more):
        q, block, side = self.parts[k], self.blocks[i], self.sides_of[j]
        self.core_copies[k, i, j].wait_recv()
        value = self.srcs[k][self.place(i, j), :].astype(f32)
        value = value + self.core[(q, side, *block)].astype(f32)
        for other in more:
            value = value + other.astype(f32)
        return value

    def cores(self, k):
        w0 = lax.axis_index("w0")
        for j in range(2):
            for i in self.order:
                q, block, side = self.parts[k], self.blocks[i], self.sides_of[j]
                src = self.srcs[k].at[self.at(block, side, 1 - w0)]
                self.core_copies[k, i, j] = self.copies.send(src, self.core.at[(q, side, *block)], CORE)

    def left(self):
        for copies in (self.core_copies, self.side_copies, self.far_copies, self.last_copies):
            self.copies.left(copies.values())

    def to_sides(self, k):
        for i in self.order:
            self.side_copies[k, i] = self.pass_on(k, i, 0, self.added(k, i, 0), self.sides.at[k, i], SIDEWAYS)

    def to_part(self, which=None):
        for i in self.order if which is None else which:
            self.side_copies[0, i].wait_recv()
            value = self.added(0, i, 1, self.sides[0, i])
            self.far_copies[i] = self.pass_on(0, i, 1, value, self.fars.at[i], PART)

    def total(self, i):
        self.side_copies[1, i].wait_recv()
        self.far_copies[i].wait_recv()
        return self.added(1, i, 1, self.sides[1, i], self.fars[i])

    def to_group(self, store):
        for i in self.order:
            value = self.total(i)
            if i == 0:
                store(0, value)
            else:
                self.last_copies[i] = self.pass_on(1, i, 1, value, self.lasts.at[i - 1], HOPS[i])

    def finish(self, store):
        for i, copy in self.last_copies.items():
            copy.wait_recv()
            store(i, self.lasts[i - 1].astype(f32))


class GroupScatter:
    def __init__(self, copies, src, bufs):
        self.copies, self.src = copies, src
        self.here, self.pass_on, self.last = bufs
        self.rows = self.here.shape[0]

    def block(self, i):
        return block_rows(group_blocks()[i], self.rows)

    def left(self):
        self.copies.left([self.own_copy, self.pass_copy])

    def to_t0(self, i):
        copy = self.copies.send(self.src.at[self.block(i)], self.here if i == 1 else self.pass_on, T0)
        if i == 1:
            self.own_copy = copy
        else:
            self.pass_copy = copy

    def to_t1(self):
        self.pass_copy.wait_recv()
        here = self.block(2)
        self.src[here, :] = (self.src[here, :].astype(f32) + self.pass_on[...].astype(f32)).astype(bf16)
        self.last_copy = self.copies.send(self.src.at[here], self.last, T1)

    def finish(self):
        self.own_copy.wait_recv()
        self.last_copy.wait_recv()
        return self.here[...].astype(f32) + self.last[...].astype(f32)


def scatter_buffers(rows):
    return [pltpu.VMEM((rows, D), bf16)] * 3


def sum_buffers(rows, cols, group):
    buf = lambda *lead: pltpu.VMEM((*lead, rows, cols), bf16)
    if not group:
        return [buf(2, 2), buf(2, 1), buf(1)]
    return [buf(2, 2, 2, 2), buf(2, 4), buf(4), buf(3)]


def block_rows(block, size):
    return pl.ds(pl.multiple_of((block[0] * 2 + block[1]) * size, size), size)


def lane_of(h):
    return h if h < LOCAL_HEADS // 2 else h + HEADS // 2 - LOCAL_HEADS // 2


def own_pair(cols, h):
    lane = lax.broadcasted_iota(jnp.int32, (cols.shape[0], LANES), 1)
    first, second = lane_of(h), lane_of(h + 1)
    return jnp.where(lane < HEADDIM, cols[:, first : first + 1], cols[:, second : second + 1])


def own_sums(values):
    width = values.shape[1]
    head = lax.broadcasted_iota(jnp.int32, (width, LANES), 0) // HEADDIM
    lane = lax.broadcasted_iota(jnp.int32, (width, LANES), 1)
    pick = (jnp.where(head < LOCAL_HEADS // 2, head, head + lane_of(LOCAL_HEADS) - LOCAL_HEADS) == lane).astype(bf16)
    high = values.astype(bf16)
    low = (values - high.astype(f32)).astype(bf16)
    return dot(high, pick) + dot(low, pick)


def head_lanes(values, back=False):
    first = (lax.axis_index("t1") * 2 + lax.axis_index("t0")) * (LOCAL_HEADS // 2)
    return pltpu.roll(values, first if back else LANES - first, 1)


def own_row(first, k):
    tp = lax.axis_index("t1") * 2 + lax.axis_index("t0")
    third = QUARTER // LANES
    return pl.ds(first + (k // third) * (D_INNER // 2 // LANES) + tp * third + k % third, 1)


def own_chans(j):
    return [slice(first + j * QUARTER, first + (j + 1) * QUARTER) for first in (0, D_INNER // 2)]


EVERY_NEIGHBOUR = (T0, T1, DIAG, CORE, SIDEWAYS, SIDE_CORE, PART)


def main_kernel(
    spans, hid_ref, inw_hbm, outw_hbm, cot_hbm, inside_ref, valid_ref, small_ref, segs_ref,
    cotv_out, mixer_out, ggate_out, gmain_out, dx_out, gout_out, total_ref,
    h_ref, xn_ref, win_ref, convp_ref, x_ref, b_ref, c_ref, dtot_ref, dt_ref, z_ref, cum_ref, y_ref, st_ref,
    wgate_ref, wout_ref, back_ref, normed_ref, mix_ref, dy_ref, dgate_ref, dmain_ref, dgain_ref, taps_ref, heads_ref, chans_ref,
    marks_ref, carry_ref, s_ref, pass_ref, got_ref, rim_ref, gated_ref, gate_ref, dn_ref,
    stat_ref, stats_ref, dyg_ref, passb_ref, gotb_ref, rims_ref, rimr_ref, hsum_ref, dskip_ref, dtaps_ref,
    dpre_ref, box_ref, boxes_ref, gm_ref, segc_ref, segr_ref, validc_ref,
    *rest,
):
    go_bufs, gg_bufs, gm_bufs, mix_bufs, dx_bufs = rest[:3], rest[3:7], rest[7:11], rest[11:14], rest[14:17]
    local_sem, send_sem, recv_sem = rest[17:]
    greet(EVERY_NEIGHBOUR)
    p, _, _, _, _ = place()
    rows_all = spans * SPAN
    tokens = hid_ref.shape[0]
    own_rows, out_rows = inw_hbm.shape[0], outw_hbm.shape[0]
    lane = lax.broadcasted_iota(jnp.int32, (1, LANES), 1)
    wm_ref = dmain_ref.at[pl.ds(0, TP * own_rows)]
    wg_ref = dgate_ref.at[pl.ds(0, TP * own_rows)]
    wo_ref = mix_ref.at[pl.ds(0, out_rows)]
    cotv_ref = mix_ref.at[pl.ds(tokens, tokens)]
    dxi_ref, prod_ref = gated_ref, gate_ref

    def side_at(c, which):
        return (slice(spans * STATE, spans * STATE + SPAN), pl.ds(pl.multiple_of((which * spans + c) * STATE, STATE), STATE))


    copies = Copies(local_sem, send_sem, recv_sem)
    loads = [
        copies.keep(inw_hbm.at[:, pl.ds(k * HALF, HALF)], gate_ref.at[pl.ds(k * own_rows, own_rows)])
        for k in range(2 * D_INNER // HALF)
    ]
    loads += [
        copies.keep(outw_hbm.at[:, pl.ds(k * HALF, HALF)], dn_ref.at[pl.ds(k * out_rows, out_rows)]) for k in range(D // HALF)
    ]
    loads.append(copies.keep(cot_hbm, cotv_ref))

    def column(row):
        return jnp.transpose(jnp.broadcast_to(row, (LANES, SPAN)))[:, 0:1]

    for c in range(spans):
        row = segs_ref[0:1, pl.ds(pl.multiple_of(p * rows_all + c * SPAN, LANES), SPAN)].astype(f32)
        segr_ref[c : c + 1, :] = row
        segc_ref[FRONT + c * SPAN : FRONT + (c + 1) * SPAN, :] = column(row)
    around = rows_all - SPAN
    row = segs_ref[0:1, pl.ds(pl.multiple_of(p * around, LANES), SPAN)].astype(f32)
    segc_ref[0:FRONT, :] = jnp.where(p == 1, column(row)[SPAN - FRONT :], -1.0)
    row = segs_ref[0:1, pl.ds(pl.multiple_of(rows_all + p * around, LANES), SPAN)].astype(f32)
    segc_ref[FRONT + rows_all :, :] = jnp.where(p == 0, column(row)[0:FRONT], -1.0)
    stat_ref[0] = jnp.zeros_like(stat_ref[0])
    stat_ref[0, 0:1, 0:tokens] = valid_ref[...].astype(f32)
    validc_ref[...] = column(stat_ref[0, 0:1, 0:SPAN])[0:tokens]

    side = inside_ref[:, 0 : SIDE + HEADS]
    dt_cols = jnp.concatenate([side[:, SIDE:], jnp.zeros((own_rows, LANES - HEADS), f32)], axis=1)
    for copy in loads:
        copies.settle(copy)
    cotv_ref[...] = (cotv_ref[...].astype(f32) * validc_ref[...]).astype(bf16)

    def master(first):
        return gate_ref[first // HALF * own_rows : (first // HALF + 1) * own_rows, first % HALF : first % HALF + QUARTER]

    for j in range(TP):
        at = slice(j * own_rows, (j + 1) * own_rows)
        for k, chans in enumerate(own_chans(j)):
            part = slice(k * QUARTER, (k + 1) * QUARTER)
            wg_ref[at, part] = master(chans.start).astype(bf16)
            wm_ref[at, part] = master(D_INNER + chans.start).astype(bf16)
        wm_ref[at, HALF:CHANS] = side[:, :SIDE].astype(bf16)
        dt_own = (lane % (HEADS // 2) // (LOCAL_HEADS // 2) == j) & (lane < HEADS)
        wm_ref[at, CHANS:MAIN] = jnp.where(dt_own, dt_cols, 0.0).astype(bf16)
    for k in range(D // HALF):
        wo_ref[:, k * HALF : (k + 1) * HALF] = dn_ref[k * out_rows : (k + 1) * out_rows, :].astype(bf16)

    greeted(EVERY_NEIGHBOUR)
    mains = WeightGather(copies, win_ref, own_rows, True)
    mains.swap(wm_ref)
    hids = GroupGather(copies, hid_ref, h_ref)
    hids.start_t0()
    copies.keep(cotv_ref, cotv_out)

    for k in range(HALF // LANES):
        lanes = slice(k * LANES, (k + 1) * LANES)
        chans_ref[1:2, lanes] = small_ref[own_row(NORM_ROW, k), :]
        for j in range(CONV + 1):
            taps_ref[j : j + 1, lanes] = small_ref[own_row(TAP_ROW + TAP_ROWS * j, k), :]
    for k in range(SIDE // LANES):
        lanes = slice(HALF + k * LANES, HALF + (k + 1) * LANES)
        for j in range(CONV + 1):
            row = TAP_ROW + TAP_ROWS * j + D_INNER // LANES + k
            taps_ref[j : j + 1, lanes] = small_ref[row : row + 1, :]
    head_row = jnp.broadcast_to(small_ref[HEAD_ROW : HEAD_ROW + 1, :], (TILE, LANES))
    next_row = jnp.broadcast_to(small_ref[HEAD_ROW + 1 : HEAD_ROW + 2, :], (TILE, LANES))
    a_log = pltpu.roll(head_row, LANES - HEADS, 1)
    lane8 = lax.broadcasted_iota(jnp.int32, (TILE, LANES), 1)
    spill = LANES - 2 * HEADS
    skip = jnp.where(lane8 < spill, pltpu.roll(head_row, spill, 1), pltpu.roll(next_row, spill, 1))
    own = lane8 < HEADS
    heads_ref[0:1, :] = head_lanes(jnp.where(own, head_row, 0.0))[0:1]
    heads_ref[1:2, :] = -jnp.exp(head_lanes(jnp.where(own, a_log, 0.0))[0:1])
    skip = head_lanes(jnp.where(own, skip, 0.0))[0:1]
    for q in range(PAIRS):
        chans_ref[0:1, q * LANES : (q + 1) * LANES] = own_pair(skip, 2 * q)

    def mark(first, count):
        seg = segc_ref[pl.ds(first, FRONT + count), :]
        here = seg[FRONT:]
        last = seg[FRONT + count - 1 :]
        before = seg[FRONT - 1 : FRONT]
        cols = {k: seg[FRONT - RIM + k : FRONT - RIM + k + count] == here for k in range(RIM)}
        cols[6], cols[7] = here == last, here == before
        lane_m = lax.broadcasted_iota(jnp.int32, (count, TILE), 1)
        marks = jnp.zeros((count, TILE), f32)
        for k, col in cols.items():
            marks = jnp.where(lane_m == k, jnp.where(col, 1.0, 0.0), marks)
        marks_ref[pl.ds(first, count), :] = marks
        return jnp.broadcast_to(jnp.where(last == before, 1.0, 0.0), (1, LANES))

    for c in range(spans):
        carry_ref[c : c + 1, :] = mark(c * SPAN, SPAN)
    mark(rows_all, TILE)
    blocks = group_blocks()

    def norm(block):
        rows = block_rows(block, tokens)
        hid = h_ref[rows, :].astype(f32)
        scale = lax.rsqrt(jnp.sum(hid * hid, axis=1, keepdims=True) / D + norm_eps)
        for k in range(D // LANES):
            lanes = slice(k * LANES, (k + 1) * LANES)
            xn_ref[rows, lanes] = (h_ref[rows, lanes].astype(f32) * scale * small_ref[k : k + 1, :]).astype(bf16)

    mains.spread_swapped()
    copies.settle(hids.own)
    norm(blocks[0])
    gates = WeightGather(copies, wgate_ref, own_rows, True)
    gates.swap(wg_ref)
    hids.hand_on()
    norm(blocks[2])
    mains.hand_on()
    gates.spread_swapped()
    hids.finish()
    cots = GroupGather(copies, cotv_ref, back_ref)
    cots.start_t0()
    norm(blocks[1])
    norm(blocks[3])
    mains.hand_on_last()
    outs = WeightGather(copies, wout_ref, out_rows, False)
    outs.spread(wo_ref, ())
    outs_kept = copies.keep(wo_ref, outs.mine(()))
    mains.finish()
    copies.settle(mains.kept)

    def project(c, _):
        rows = span_rows(c)
        xn = xn_ref[rows, :]
        at = pl.ds(pl.multiple_of(FRONT + c * SPAN, FRONT), SPAN)
        for k in range(CHANS // 256):
            cols = slice(k * 256, (k + 1) * 256)
            convp_ref[at, cols] = dot(xn, win_ref[:, cols]).astype(bf16)
        dt_raw = dot(xn, win_ref[:, CHANS:MAIN]).astype(bf16).astype(f32)
        z = head_lanes(dt_raw) + heads_ref[0:1, :]
        z_ref[rows, :] = z
        small = jnp.exp(-jnp.abs(z))
        one_more = 1.0 + small
        is_one = one_more == 1.0
        log_more = jnp.where(is_one, small, jnp.log(one_more) * small / jnp.where(is_one, 1.0, one_more - 1.0))
        dt_ref[rows, :] = jnp.maximum(z, 0.0) + log_more
        return 0

    lax.fori_loop(0, spans, project, 0)
    rim = copies.send(convp_ref.at[pl.ds(rows_all, FRONT)], rim_ref, PART)
    gates.hand_on()
    s_ref[...] = jnp.zeros_like(s_ref)
    dgain_ref[...] = jnp.zeros_like(dgain_ref)

    def convolve(c, _):
        rows = span_rows(c)
        wide = pl.ds(pl.multiple_of(c * SPAN, SPAN), SPAN + FRONT)
        masks = [jnp.broadcast_to(marks_ref[rows, j : j + 1], (SPAN, LANES)) for j in range(RIM)]
        for k in range(CHANS // LANES):
            lanes = slice(k * LANES, (k + 1) * LANES)
            values = convp_ref[wide, lanes].astype(f32)
            total = taps_ref[CONV : CONV + 1, lanes] + taps_ref[RIM : RIM + 1, lanes] * values[FRONT:]
            for j in range(RIM):
                first = FRONT - RIM + j
                total = total + taps_ref[j : j + 1, lanes] * values[first : first + SPAN] * masks[j]
            sig = 1.0 / (1.0 + jnp.exp(-total))
            value = (total * sig).astype(bf16)
            dtot_ref[rows, lanes] = sig * (1.0 + total * (1.0 - sig))
            if k < HALF // LANES:
                x_ref[rows, lanes] = value
            elif k == HALF // LANES:
                b_ref[rows, :] = value
            else:
                c_ref[rows, :] = value
        return 0

    lax.fori_loop(1, spans, convolve, 0)
    rim.wait_recv()
    convp_ref[0:FRONT, :] = jnp.where(p == 1, rim_ref[...].astype(f32), 0.0).astype(bf16)
    lax.fori_loop(0, 1, convolve, 0)
    gates.hand_on_last()

    def local_states(c, _):
        rows = span_rows(c)
        dt, cum = span_decay(dt_ref, heads_ref, c, 1)
        cum_ref[rows, :] = cum
        last = cum[SPAN - 1 : SPAN, :]
        end_weight = jnp.exp(last - cum) * dt * marks_ref[rows, 6:7]
        decay = jnp.exp(last) * carry_ref[pl.ds(c, 1), :]
        b = b_ref[rows, :]
        st_ref[c] = s_ref[...]
        for q in range(PAIRS):
            lanes = slice(q * LANES, (q + 1) * LANES)
            dyg_ref[rows, lanes] = (x_ref[rows, lanes].astype(f32) * own_pair(end_weight, 2 * q)).astype(bf16)
            s_ref[:, lanes] = s_ref[:, lanes] * own_pair(decay, 2 * q)
        s_ref[...] += dot(b, dyg_ref[rows, :], ((0,), (0,)))
        return 0

    lax.fori_loop(0, spans, local_states, 0)
    pass_ref[...] = s_ref[...].astype(bf16)
    state = copies.send(pass_ref, got_ref, PART)
    cots.hand_on()
    outs.hand_on()

    def inside(c, _):
        rows = span_rows(c)
        cum = cum_ref[rows, :]
        back_log = jnp.transpose(cum - jnp.log(dt_ref[rows, :]))
        scores = dot(c_ref[rows, :], b_ref[rows, :], ((1,), (1,)))
        row = lax.broadcasted_iota(jnp.int32, (SPAN, SPAN), 0)
        col = lax.broadcasted_iota(jnp.int32, (SPAN, SPAN), 1)
        mask = (row >= col) & (segc_ref[pl.ds(pl.multiple_of(FRONT + c * SPAN, FRONT), SPAN), :] == segr_ref[pl.ds(c, 1), :])
        lane = lax.broadcasted_iota(jnp.int32, (SPAN, LANES), 1)
        for q in range(PAIRS):
            lanes = slice(q * LANES, (q + 1) * LANES)
            x = x_ref[rows, lanes]
            parts = []
            for h in (lane_of(2 * q), lane_of(2 * q + 1)):
                gap = cum[:, h : h + 1] - back_log[h : h + 1, :]
                weighted = scores * jnp.exp(jnp.where(mask, gap, -1e30))
                parts.append(dot(weighted.astype(bf16), x))
            y_ref[rows, lanes] = jnp.where(lane < HEADDIM, parts[0], parts[1])
        return 0

    lax.fori_loop(0, spans, inside, 0)
    state.wait_recv()
    s_ref[...] = got_ref[...].astype(f32) * p.astype(f32)

    def across_spans(c, _):
        rows = span_rows(c)
        cum = cum_ref[rows, :]
        decay = jnp.exp(cum[SPAN - 1 : SPAN, :]) * carry_ref[pl.ds(c, 1), :]
        gain = jnp.exp(cum) * marks_ref[rows, 7:8]
        cc = c_ref[rows, :]
        for q in range(PAIRS):
            lanes = slice(q * LANES, (q + 1) * LANES)
            entering = s_ref[:, lanes]
            full = st_ref[c, :, lanes] + entering
            st_ref[c, :, lanes] = full
            y_ref[rows, lanes] += dot(cc, full.astype(bf16)) * own_pair(gain, 2 * q)
            s_ref[:, lanes] = entering * own_pair(decay, 2 * q)
        return 0

    lax.fori_loop(0, spans, across_spans, 0)
    gates.finish()
    copies.settle(gates.kept)

    def put_stat(k, c, column):
        wide = jnp.transpose(jnp.broadcast_to(column, (SPAN, LANES)))
        stat_ref[k, :, span_rows(c)] = wide[0:TILE, :]

    def exchange(k):
        return [copies.send(stat_ref.at[k], stats_ref.at[k, i], flips) for i, flips in enumerate(HOPS[1:])]

    def get_stat(k, c):
        cols = span_rows(c)
        total = stat_ref[k, :, cols] + stats_ref[k, 0, :, cols] + stats_ref[k, 1, :, cols] + stats_ref[k, 2, :, cols]
        return jnp.transpose(jnp.broadcast_to(total[0:1, :], (LANES, SPAN)))[:, 0:1] / D_INNER

    def values(rows, lanes):
        y_b = (y_ref[rows, lanes] + chans_ref[0:1, lanes] * x_ref[rows, lanes].astype(f32)).astype(bf16).astype(f32)
        gate = gate_ref[rows, lanes]
        sig = 1.0 / (1.0 + jnp.exp(-gate))
        return y_b, gate, sig

    def gating(c, _):
        rows = span_rows(c)
        xn = xn_ref[rows, :]
        total = jnp.zeros((SPAN, 1), f32)
        for k in range(HALF // 256):
            lanes = slice(k * 256, (k + 1) * 256)
            gate_ref[rows, lanes] = dot(xn, wgate_ref[:, lanes])
            y_b, gate, sig = values(rows, lanes)
            gated = y_b * (gate * sig)
            gated_ref[rows, lanes] = gated
            total = total + jnp.sum(gated * gated, axis=1, keepdims=True)
        put_stat(0, c, total)
        return 0

    lax.fori_loop(0, spans, gating, 0)
    outs.hand_on_last()
    squares = exchange(0)
    cots.finish()
    copies.settle(cots.own)
    outs.finish()
    copies.settle(outs_kept)

    def pull_out(c, _):
        rows = span_rows(c)
        back = back_ref[rows, :]
        total = jnp.zeros((SPAN, 1), f32)
        for k in range(HALF // 256):
            lanes = slice(k * 256, (k + 1) * 256)
            d_normed = dot(back, wout_ref[lanes, :], ((1,), (1,)))
            dn_ref[rows, lanes] = d_normed
            total = total + jnp.sum(gated_ref[rows, lanes] * (d_normed * chans_ref[1:2, lanes]), axis=1, keepdims=True)
        put_stat(1, c, total)
        return 0

    lax.fori_loop(0, spans, pull_out, 0)
    for copy in squares:
        copy.wait_recv()
    dots = exchange(1)

    def push_out(c, _):
        rows = span_rows(c)
        scale = lax.rsqrt(get_stat(0, c) + norm_eps)
        for k in range(HALF // 256):
            lanes = slice(k * 256, (k + 1) * 256)
            scaled = gated_ref[rows, lanes] * scale
            normed_ref[rows, lanes] = (scaled * chans_ref[1:2, lanes]).astype(bf16)
            dgain_ref[0:1, lanes] += jnp.sum(scaled * dn_ref[rows, lanes], axis=0, keepdims=True)
        normed = normed_ref[rows, :]
        for k in range(D // 256):
            cols = slice(k * 256, (k + 1) * 256)
            mix_ref[rows, cols] = dot(normed, wout_ref[:, cols]).astype(bf16)
        return 0

    copies.drain()
    lax.fori_loop(0, spans, push_out, 0)
    mixes = GroupScatter(copies, mix_ref, mix_bufs)
    mixes.to_t0(3)
    mixes.to_t0(1)
    for q in range(2):
        normed = normed_ref[:, q * HALF // 2 : (q + 1) * HALF // 2]
        for k in range(D // 512):
            cols = slice(k * 512, (k + 1) * 512)
            wout_ref[q * HALF // 2 : (q + 1) * HALF // 2, cols] = dot(normed, back_ref[:, cols], ((0,), (0,))).astype(bf16)
    go_halves = [wout_ref.at[pl.ds(pl.multiple_of(q * (HALF // 2), HALF // 2), HALF // 2)] for q in (1 - p, p)]
    g_out = GradientSum(copies, go_halves, out_rows, go_bufs, False)
    g_out.cores(0)
    g_out.cores(1)
    for copy in dots:
        copy.wait_recv()

    def back_gate(c, _):
        rows = span_rows(c)
        scale = lax.rsqrt(get_stat(0, c) + norm_eps)
        pulled = get_stat(1, c) * (scale * scale * scale)
        for k in range(HALF // LANES):
            lanes = slice(k * LANES, (k + 1) * LANES)
            y_b, gate, sig = values(rows, lanes)
            d_gated = scale * (dn_ref[rows, lanes] * chans_ref[1:2, lanes]) - gated_ref[rows, lanes] * pulled
            dy_ref[rows, lanes] = (d_gated * (gate * sig)).astype(bf16)
            dgate_ref[rows, lanes] = (d_gated * y_b * (sig * (1.0 + gate * (1.0 - sig)))).astype(bf16)
        return 0

    lax.fori_loop(0, spans, back_gate, 0)
    g_out.to_sides(0)
    s_ref[...] = jnp.zeros_like(s_ref)
    hsum_ref[...] = jnp.zeros_like(hsum_ref)
    dskip_ref[...] = jnp.zeros_like(dskip_ref)
    dtaps_ref[...] = jnp.zeros_like(dtaps_ref)

    def local_states(step, _):
        c = spans - 1 - step
        rows = span_rows(c)
        cum = cum_ref[rows, :]
        decay = jnp.exp(cum[SPAN - 1 : SPAN, :]) * carry_ref[pl.ds(c, 1), :]
        gain = jnp.exp(cum) * marks_ref[rows, 7:8]
        cc = c_ref[rows, :]
        for q in range(PAIRS):
            lanes = slice(q * LANES, (q + 1) * LANES)
            dyg = (dy_ref[rows, lanes].astype(f32) * own_pair(gain, 2 * q)).astype(bf16)
            dyg_ref[rows, lanes] = dyg
            ds = s_ref[:, lanes]
            dn_ref[pl.ds(pl.multiple_of(c * STATE, STATE), STATE), lanes] = ds
            s_ref[:, lanes] = ds * own_pair(decay, 2 * q)
        s_ref[...] += dot(cc, dyg_ref[rows, :], ((0,), (0,)))
        return 0

    lax.fori_loop(0, spans, local_states, 0)
    passb_ref[...] = s_ref[...].astype(bf16)
    state = copies.send(passb_ref, gotb_ref, PART)

    width = D // 4
    gg_halves = [back_ref.at[:, pl.ds(k * HALF, HALF)] for k in range(2)]
    g_gate = GradientSum(copies, gg_halves, own_rows, gg_bufs, True)

    def gate_gradient(far):
        for half in range(2):
            first = pl.multiple_of(((1 - p if far else p) * 2 + half) * width, width)
            piece = dot(xn_ref[:, pl.ds(first, width)], dgate_ref[...], ((0,), (0,)))
            gg_halves[0 if far else 1][half * width : (half + 1) * width, :] = piece.astype(bf16)

    gate_gradient(True)
    g_gate.cores(0)
    gate_gradient(False)
    g_gate.cores(1)
    g_gate.to_sides(0)
    g_out.to_part()
    g_out.to_sides(1)
    g_gate.to_sides(1)

    def inside(c, _):
        rows = span_rows(c)
        cum = cum_ref[rows, :]
        fore_log = jnp.transpose(cum)
        back_log = cum - jnp.log(dt_ref[rows, :])
        b = b_ref[rows, :]
        cc = c_ref[rows, :]
        scores = dot(b, cc, ((1,), (1,)))
        row = lax.broadcasted_iota(jnp.int32, (SPAN, SPAN), 0)
        col = lax.broadcasted_iota(jnp.int32, (SPAN, SPAN), 1)
        mask = (col >= row) & (segc_ref[pl.ds(pl.multiple_of(FRONT + c * SPAN, FRONT), SPAN), :] == segr_ref[pl.ds(c, 1), :])
        lane = lax.broadcasted_iota(jnp.int32, (SPAN, LANES), 1)
        d_scores = jnp.zeros((SPAN, SPAN), f32)
        dc = dot(dyg_ref[rows, :], st_ref[c].astype(bf16), ((1,), (1,)))
        for q in range(PAIRS):
            lanes = slice(q * LANES, (q + 1) * LANES)
            x = x_ref[rows, lanes]
            dy = dy_ref[rows, lanes]
            xf = x.astype(f32)
            parts = []
            for k in range(2):
                h = lane_of(2 * q + k)
                gap = fore_log[h : h + 1, :] - back_log[:, h : h + 1]
                decay_mat = jnp.exp(jnp.where(mask, gap, -1e30))
                parts.append(dot((scores * decay_mat).astype(bf16), dy))
                own = (lane < HEADDIM) if k == 0 else (lane >= HEADDIM)
                d_weights = dot(jnp.where(own, xf, 0.0).astype(bf16), dy, ((1,), (1,)))
                d_scores = d_scores + d_weights * decay_mat
            dxi_ref[rows, lanes] = jnp.where(lane < HEADDIM, parts[0], parts[1])
            dskip_ref[0:1, lanes] += jnp.sum(dy.astype(f32) * xf, axis=0, keepdims=True)
        d_scores_b = d_scores.astype(bf16)
        dn_ref[side_at(c, 0)] = dot(d_scores_b, cc)
        dn_ref[side_at(c, 1)] = dc + dot(d_scores_b, b, ((0,), (0,)))
        return 0

    lax.fori_loop(0, spans, inside, 0)
    mixes.to_t1()
    state.wait_recv()
    s_ref[...] = gotb_ref[...].astype(f32) * (1 - p).astype(f32)

    def across_spans(step, _):
        c = spans - 1 - step
        rows = span_rows(c)
        dt = dt_ref[rows, :]
        cum = cum_ref[rows, :]
        last = cum[SPAN - 1 : SPAN, :]
        end_weight = jnp.exp(last - cum) * dt * marks_ref[rows, 6:7]
        decay = jnp.exp(last) * carry_ref[pl.ds(c, 1), :]
        b = b_ref[rows, :]
        db = dn_ref[side_at(c, 0)]
        edges, ds_all = [], []
        for q in range(PAIRS):
            lanes = slice(q * LANES, (q + 1) * LANES)
            xf = x_ref[rows, lanes].astype(f32)
            dyf = dy_ref[rows, lanes].astype(f32)
            ew = own_pair(end_weight, 2 * q)
            dec = own_pair(decay, 2 * q)
            entering = s_ref[:, lanes]
            ds = dn_ref[pl.ds(pl.multiple_of(c * STATE, STATE), STATE), lanes] + entering
            s_ref[:, lanes] = entering * dec
            ds_b = ds.astype(bf16)
            dyg_ref[rows, lanes] = (xf * ew).astype(bf16)
            ds_all.append(ds_b)
            dx_state = dot(b, ds_b) * ew
            dx = dxi_ref[rows, lanes] + dx_state
            edges.append(
                jnp.sum(ds * st_ref[c, :, lanes], axis=0, keepdims=True) * dec
                + jnp.sum(dx_state * xf, axis=0, keepdims=True)
            )
            prod_ref[0:SPAN, lanes] = dyf * y_ref[rows, lanes]
            prod_ref[SPAN : 2 * SPAN, lanes] = xf * dx
            d_x = (dx + dyf * chans_ref[0:1, lanes]).astype(bf16).astype(f32)
            dtot_ref[rows, lanes] = d_x * dtot_ref[rows, lanes]
        db = db + dot(dyg_ref[rows, :], jnp.concatenate(ds_all, axis=1), ((1,), (1,)))
        dtot_ref[rows, HALF : HALF + STATE] = db * dtot_ref[rows, HALF : HALF + STATE]
        dtot_ref[rows, HALF + STATE :] = dn_ref[side_at(c, 1)] * dtot_ref[rows, HALF + STATE :]
        sums = own_sums(prod_ref[0 : 2 * SPAN, :])
        out_sum, in_sum = sums[:SPAN], sums[SPAN:]
        edge_sum = own_sums(jnp.broadcast_to(jnp.concatenate(edges, axis=1), (TILE, HALF)))[0:1]
        at_last = lax.broadcasted_iota(jnp.int32, (SPAN, LANES), 0) == SPAN - 1
        d_cum = out_sum - in_sum + jnp.where(at_last, edge_sum, 0.0)
        row = lax.broadcasted_iota(jnp.int32, (SPAN, SPAN), 0)
        col = lax.broadcasted_iota(jnp.int32, (SPAN, SPAN), 1)
        d_log = dot((col >= row).astype(f32), d_cum, precision=exact_prec)
        z = z_ref[rows, :]
        small = jnp.exp(-jnp.abs(z))
        sig = jnp.where(z >= 0.0, 1.0, small) / (1.0 + small)
        ratio = jnp.where(dt > 1e-30, sig / jnp.maximum(dt, 1e-30), 1.0)
        d_dt = d_log * heads_ref[1:2, :] * sig + in_sum * ratio
        hsum_ref[0:1, :] += jnp.sum(d_log * dt, axis=0, keepdims=True)
        hsum_ref[1:2, :] += jnp.sum(d_dt, axis=0, keepdims=True)
        dmain_ref[rows, CHANS:MAIN] = head_lanes(d_dt, back=True).astype(bf16)
        return 0

    lax.fori_loop(0, spans, across_spans, 0)
    rims_ref[...] = dtot_ref[0:TILE, :]
    rim = copies.send(rims_ref, rimr_ref, PART)
    g_gate.to_part()

    def convolve(c, _):
        rows = span_rows(c)
        fore = pl.ds(pl.multiple_of(c * SPAN, SPAN), SPAN + FRONT)
        hind = pl.ds(pl.multiple_of(c * SPAN, SPAN), SPAN + TILE)
        masks = [jnp.broadcast_to(marks_ref[hind, j : j + 1], (SPAN + TILE, LANES)) for j in range(RIM)]
        for k in range(CHANS // LANES):
            lanes = slice(k * LANES, (k + 1) * LANES)
            later = dtot_ref[hind, lanes]
            earlier = convp_ref[fore, lanes].astype(f32)
            own = later[0:SPAN]
            d_conv = taps_ref[RIM : RIM + 1, lanes] * own
            dtaps_ref[RIM : RIM + 1, lanes] += jnp.sum(own * earlier[FRONT:], axis=0, keepdims=True)
            dtaps_ref[CONV : CONV + 1, lanes] += jnp.sum(own, axis=0, keepdims=True)
            for j in range(RIM):
                lag = RIM - j
                seen = later * masks[j]
                d_conv = d_conv + taps_ref[j : j + 1, lanes] * seen[lag : lag + SPAN]
                dtaps_ref[j : j + 1, lanes] += jnp.sum(
                    seen[0:SPAN] * earlier[FRONT - lag : FRONT - lag + SPAN], axis=0, keepdims=True
                )
            dmain_ref[rows, lanes] = d_conv.astype(bf16)
        return 0

    lax.fori_loop(0, spans - 1, convolve, 0)
    rim.wait_recv()
    dtot_ref[pl.ds(spans * SPAN, TILE), :] = jnp.where(p == 0, rimr_ref[...], 0.0)
    lax.fori_loop(spans - 1, spans, convolve, 0)

    mixes.left()
    dpre_ref[...] = jnp.zeros_like(dpre_ref)

    def token_grad(block, keep):
        rows = block_rows(block, tokens)
        d_main = dmain_ref[rows, :]
        d_gate = dgate_ref[rows, :]
        hid = h_ref[rows, :].astype(f32)
        scale = lax.rsqrt(jnp.sum(hid * hid, axis=1, keepdims=True) / D + norm_eps)
        for k in range(D // 256):
            cols = slice(k * 256, (k + 1) * 256)
            part = dot(d_main, win_ref[cols, :], ((1,), (1,))) + dot(d_gate, wgate_ref[cols, :], ((1,), (1,)))
            dpre_ref[0:1, cols] += jnp.sum(h_ref[rows, cols].astype(f32) * scale * part, axis=0, keepdims=True)
            if keep:
                first = k * 256 // HALF * tokens
                y_ref[first : first + tokens, k * 256 % HALF : k * 256 % HALF + 256] = part
            else:
                mix_ref[rows, cols] = part.astype(bf16)

    def store_gate(i, value):
        kept = pl.ds(2 * SPAN + i * own_rows, own_rows)
        gate_ref[kept, :] = value
        copies.keep(gate_ref.at[kept], ggate_out.at[blocks[i][0], blocks[i][1]])

    def store_main(i, value):
        for first, count in ((0, HALF), (HALF, MAIN - HALF)):
            kept = pl.ds((first // HALF * TP + i) * own_rows, own_rows)
            gated_ref[kept, 0:count] = value[:, first : first + count]
            copies.keep(
                gated_ref.at[kept, pl.ds(0, count)], gmain_out.at[blocks[i][0], blocks[i][1], :, pl.ds(first, count)]
            )

    total = g_out.total(0)
    for k in range(D // HALF):
        kept = pl.ds(2 * TP * own_rows + k * out_rows, out_rows)
        gated_ref[kept, :] = total[:, k * HALF : (k + 1) * HALF]
        copies.keep(gated_ref.at[kept], gout_out.at[:, pl.ds(k * HALF, HALF)])
    g_out.left()
    gm_halves = [wout_ref.at[:, pl.ds(0, MAIN)], gm_ref]

    def grad_half(far):
        part = 1 - p if far else p
        out = gm_halves[0 if far else 1]

        def piece(i, _):
            xn = xn_ref[:, pl.ds(pl.multiple_of((part * 2 + i) * width, width), width)]
            rows = pl.ds(pl.multiple_of(i * width, width), width)
            for k in range(MAIN // 384):
                cols = slice(k * 384, (k + 1) * 384)
                out[rows, cols] = dot(xn, dmain_ref[:, cols], ((0,), (0,))).astype(bf16)
            return 0

        lax.fori_loop(0, 2, piece, 0)

    grad_half(True)
    g_main = GradientSum(copies, gm_halves, own_rows, gm_bufs, True)
    g_main.cores(0)
    dxs = GroupScatter(copies, mix_ref, dx_bufs)
    token_grad(blocks[3], False)
    dxs.to_t0(3)
    g_main.to_sides(0)
    token_grad(blocks[1], False)
    dxs.to_t0(1)
    grad_half(False)
    g_main.cores(1)
    g_main.to_part((1,))
    g_gate.to_group(store_gate)
    g_main.to_part((2,))
    g_main.to_sides(1)
    g_main.to_part((3,))

    mixer = mix_ref[mixes.block(0), :].astype(f32) + mixes.finish()
    copies.left([mixes.last_copy])
    for k in range(D // HALF):
        kept = pl.ds(spans * STATE + k * tokens, tokens)
        dn_ref[kept, :] = mixer[:, k * HALF : (k + 1) * HALF]
        copies.keep(dn_ref.at[kept], mixer_out.at[:, pl.ds(k * HALF, HALF)])
    hid = h_ref[mixes.block(0), :].astype(f32)
    valid = validc_ref[...]
    counts = [jnp.sum(valid * jnp.sum(v * v, axis=1, keepdims=True), axis=0, keepdims=True) for v in (hid, mixer)]
    counts.append(jnp.sum(valid, axis=0, keepdims=True))
    scalars = jnp.zeros((1, LANES), f32)
    for k in range(3):
        scalars = jnp.where(lane == k, counts[k], scalars)
    box = box_ref.at[0]
    box[...] = jnp.zeros_like(box)
    box[OWN_SUMS : OWN_SUMS + 1, :] = scalars

    token_grad(blocks[2], False)
    g_main.to_part((0,))
    dxs.to_t1()
    token_grad(blocks[0], True)

    for k in range(D // LANES):
        box[k : k + 1, :] = dpre_ref[0:1, k * LANES : (k + 1) * LANES]
    for k in range(HALF // LANES):
        lanes = slice(k * LANES, (k + 1) * LANES)
        box[OWN_NORM + k : OWN_NORM + k + 1, :] = dgain_ref[0:1, lanes]
        for j in range(CONV + 1):
            row = OWN_TAP + j * (HALF // LANES) + k
            box[row : row + 1, :] = dtaps_ref[j : j + 1, lanes]
    for k in range(SIDE // LANES):
        lanes = slice(HALF + k * LANES, HALF + (k + 1) * LANES)
        for j in range(CONV + 1):
            row = OWN_SIDE + j * (SIDE // LANES) + k
            box[row : row + 1, :] = dtaps_ref[j : j + 1, lanes]
    hsum_ref[0:1, :] = hsum_ref[0:1, :] * heads_ref[1:2, :]
    hsum_ref[2:3, :] = own_sums(dskip_ref[...])[0:1, :]
    lane8 = lax.broadcasted_iota(jnp.int32, (TILE, LANES), 1)
    box[OWN_HEAD : OWN_HEAD + 3, :] = jnp.where(lane8 < HEADS, head_lanes(hsum_ref[...], back=True), 0.0)[0:3]

    def small_step(k, hops):
        return [copies.send(box_ref.at[k], boxes_ref.at[k, i], flips) for i, flips in enumerate(hops)]

    def small_add(k, sent):
        total = box_ref[k]
        for i, copy in enumerate(sent):
            copy.wait_recv()
            total = total + boxes_ref[k, i]
        box_ref[k + 1] = total

    small = small_step(0, (CORE, SIDEWAYS, SIDE_CORE))
    g_gate.finish(store_gate)
    small_add(0, small)
    small = small_step(1, (PART,))
    small_add(1, small)
    small = small_step(2, (T0, T1, DIAG))
    g_main.to_group(store_main)
    dx = dxs.finish()
    for k in range(D // HALF):
        kept = pl.ds(k * tokens, tokens)
        y_ref[kept, :] += dx[:, k * HALF : (k + 1) * HALF]
        copies.keep(y_ref.at[kept], dx_out.at[:, pl.ds(k * HALF, HALF)])
    small_add(2, small)
    total_ref[...] = jnp.zeros_like(total_ref)
    total_ref[0:NORM_ROW, :] = box_ref[3, 0:NORM_ROW]
    third = QUARTER // LANES
    runs = [(OWN_NORM, NORM_ROW)]
    runs += [(OWN_TAP + j * 2 * third, TAP_ROW + j * TAP_ROWS) for j in range(CONV + 1)]
    for i, block in enumerate(blocks):
        source = box_ref.at[2] if i == 0 else boxes_ref.at[2, i - 1]
        place_at = (block[0] * 2 + block[1]) * third
        for own, first in runs:
            for k in range(2 * third):
                row = first + k // third * (D_INNER // 2 // LANES) + place_at + k % third
                total_ref[pl.ds(row, 1), :] = source[own + k : own + k + 1, :]
    for j in range(CONV + 1):
        row, own = TAP_ROW + TAP_ROWS * j + D_INNER // LANES, OWN_SIDE + j * (SIDE // LANES)
        total_ref[row : row + SIDE // LANES, :] = box_ref[3, own : own + SIDE // LANES]
    d_rate, d_shift, d_skip = (
        jnp.broadcast_to(box_ref[3, OWN_HEAD + k : OWN_HEAD + k + 1], (TILE, LANES)) for k in range(3)
    )
    spill = LANES - 2 * HEADS
    joined = d_shift + pltpu.roll(d_rate, HEADS, 1) + jnp.where(lane8 >= 2 * HEADS, pltpu.roll(d_skip, 2 * HEADS, 1), 0.0)
    total_ref[HEAD_ROW : HEAD_ROW + 1, :] = joined[0:1]
    spilled = jnp.where(lane8 < HEADS - spill, pltpu.roll(d_skip, LANES - spill, 1), 0.0)
    total_ref[HEAD_ROW + 1 : HEAD_ROW + 2, :] = spilled[0:1]
    total_ref[SMALL_ROWS : SMALL_ROWS + 1, :] = box_ref[3, OWN_SUMS : OWN_SUMS + 1]
    g_main.finish(store_main)
    copies.drain()


def update_kernel(
    hid_ref, mixer_ref, dx_ref, back_ref, gmain_ref, ggate_ref, gout_ref, total_ref,
    inw_ref, inm_ref, inv_ref, outw_ref, outm_ref, outv_ref, small_ref, smallm_ref, smallv_ref,
    output_ref, gh_ref, inm_out, inv_out, inw_out, outm_out, outv_out, outw_out, smallm_out, smallv_out, smallw_out, rms_ref,
):
    hid = hid_ref[...].astype(f32)
    output_ref[...] = (hid + mixer_ref[...]).astype(bf16)
    scale = lax.rsqrt(jnp.sum(hid * hid, axis=1, keepdims=True) / D + norm_eps)
    pulled = 0.0
    for k in range(NORM_ROW):
        lanes = slice(k * LANES, (k + 1) * LANES)
        d_pre = dx_ref[:, lanes] * small_ref[k : k + 1, :]
        gh_ref[:, lanes] = back_ref[:, lanes].astype(f32) + scale * d_pre
        pulled = pulled + jnp.sum(hid[:, lanes] * d_pre, axis=1, keepdims=True)
    gh_ref[...] -= hid * (pulled / D * (scale * scale * scale))

    def update(refs, outs, cols, grad, rate=0.02, decay=0.1):
        weight, moment, second = (ref[:, cols] for ref in refs)
        for out, value in zip(outs, adamw(weight, moment, second, grad, rate, decay)):
            out[:, cols] = value

    every = slice(None)
    update((outw_ref, outm_ref, outv_ref), (outm_out, outv_out, outw_out), every, gout_ref[...])
    in_refs, in_outs = (inw_ref, inm_ref, inv_ref), (inm_out, inv_out, inw_out)
    for j in range(TP):
        for k, chans in enumerate(own_chans(j)):
            part = slice(k * QUARTER, (k + 1) * QUARTER)
            update(in_refs, in_outs, chans, ggate_ref[j // 2, j % 2, :, part])
            scan = slice(D_INNER + chans.start, D_INNER + chans.stop)
            update(in_refs, in_outs, scan, gmain_ref[j // 2, j % 2, :, part])
    rest_grad = gmain_ref[0, 0, :, HALF:] + gmain_ref[0, 1, :, HALF:] + gmain_ref[1, 0, :, HALF:] + gmain_ref[1, 1, :, HALF:]
    first = 2 * D_INNER
    update(in_refs, in_outs, slice(first, first + SIDE), rest_grad[:, :SIDE])
    update(in_refs, in_outs, slice(first + SIDE, first + SIDE + HEADS), rest_grad[:, SIDE : SIDE + HEADS])

    @pl.when(pl.program_id(0) == 0)
    def _():
        update(
            (small_ref, smallm_ref, smallv_ref), (smallm_out, smallv_out, smallw_out), every, total_ref[0:SMALL_ROWS, :], 0.2, 0.0
        )
        totals = total_ref[SMALL_ROWS:, :]
        rms_ref[...] = jnp.sqrt(totals / (totals[0:1, 2:3] * D))


def linked(kernel, name, collective_id, in_specs, outs, scratch):
    return pl.pallas_call(
        kernel,
        name=name,
        grid=(1,),
        in_specs=in_specs,
        out_shape=tuple(o for o, _ in outs),
        out_specs=tuple(s for _, s in outs),
        scratch_shapes=scratch,
        compiler_params=pltpu.CompilerParams(
            collective_id=collective_id, has_side_effects=True, vmem_limit_bytes=VMEM_LIMIT
        ),
    )


def shards_linked(
    hidden, cotangent, segments, valid, in_w, in_m, in_v, out_w, out_m, out_v, small_w, small_m, small_v,
):
    own_rows, out_rows = in_w.shape[0], out_w.shape[0]
    tok_rows = hidden.shape[1]
    rows = tok_rows * TP
    spans = rows // SPAN
    small_size = small_w.shape[0]

    def small_box(array):
        return jnp.pad(array, (0, SMALL_ROWS * LANES - small_size)).reshape(SMALL_ROWS, LANES)

    small_w, small_m, small_v = small_box(small_w), small_box(small_m), small_box(small_v)

    wide = (rows, D)
    half = (rows, HALF)
    lanes = (rows, LANES)
    side = (rows, STATE)
    state = (STATE, HALF)
    main_outs = (
        (shape((tok_rows, D), bf16), HBM),
        (shape((tok_rows, D), f32), HBM),
        (shape((2, 2, own_rows, HALF), f32), HBM),
        (shape((2, 2, own_rows, MAIN), f32), HBM),
        (shape((tok_rows, D), f32), HBM),
        (shape((out_rows, D), f32), HBM),
        (shape((BOX_ROWS, LANES), f32), VMEM),
    )
    main_scratch = (
        (wide, bf16),
        (wide, bf16),
        ((D, MAIN), bf16),
        ((rows + FRONT, CHANS), bf16),
        (half, bf16),
        (side, bf16),
        (side, bf16),
        ((rows + FRONT, CHANS), f32),
        (lanes, f32),
        (lanes, f32),
        (lanes, f32),
        (half, f32),
        ((spans, *state), f32),
        ((D, HALF), bf16),
        ((HALF, D), bf16),
        (wide, bf16),
        (half, bf16),
        (wide, bf16),
        (half, bf16),
        (half, bf16),
        ((rows, MAIN), bf16),
        ((TILE, HALF), f32),
        ((TILE, CHANS), f32),
        ((TILE, LANES), f32),
        ((TILE, HALF), f32),
        ((rows + TILE, TILE), f32),
        ((spans, LANES), f32),
        (state, f32),
        (state, bf16),
        (state, bf16),
        ((FRONT, CHANS), bf16),
        (half, f32),
        (half, f32),
        (half, f32),
        ((2, TILE, rows), f32),
        ((2, 3, TILE, rows), f32),
        (half, bf16),
        (state, bf16),
        (state, bf16),
        ((TILE, CHANS), f32),
        ((TILE, CHANS), f32),
        ((TILE, LANES), f32),
        ((TILE, HALF), f32),
        ((TILE, CHANS), f32),
        ((TILE, D), f32),
        ((4, OWN_ROWS, LANES), f32),
        ((3, 3, OWN_ROWS, LANES), f32),
        ((D // 2, MAIN), bf16),
        ((rows + 2 * FRONT, 1), f32),
        ((TILE, SPAN), f32),
        ((tok_rows, 1), f32),
    )
    side_cols = pl.BlockSpec((own_rows, MAIN - HALF), lambda i: (0, 2 * D_INNER // (MAIN - HALF)))
    back_own, mixer, g_gate, g_main, d_x_normed, g_out, totals = linked(
        functools.partial(main_kernel, spans), "main", 1, [*[HBM] * 4, side_cols, *[VMEM] * 3], main_outs,
        [
            *[pltpu.VMEM(dims, dtype) for dims, dtype in main_scratch],
            *sum_buffers(out_rows, D, False),
            *sum_buffers(own_rows, HALF, True),
            *sum_buffers(own_rows, MAIN, True),
            *scatter_buffers(tok_rows),
            *scatter_buffers(tok_rows),
            *sems(200, 48),
        ],
    )(hidden[0], in_w, out_w, cotangent[0], in_w, valid, small_w, segments)

    steps = own_rows // (2 * TILE)

    def cut(dims, axis=0):
        block = tuple(size // steps if k == axis else size for k, size in enumerate(dims))
        return pl.BlockSpec(block, lambda i: tuple(i if k == axis else 0 for k in range(len(dims))))

    def fixed(dims):
        return pl.BlockSpec(dims, lambda i: (0, 0))

    tokens, matrix_in, matrix_out, small_dims = (tok_rows, D), in_w.shape, out_w.shape, (SMALL_ROWS, LANES)
    out_dims = [tokens] * 2 + [matrix_in] * 3 + [matrix_out] * 3
    (
        output, grad_hidden, in_m_new, in_v_new, in_w_new, out_m_new, out_v_new, out_w_new,
        small_m_new, small_v_new, small_w_new, rms,
    ) = pl.pallas_call(
        update_kernel,
        name="update",
        grid=(steps,),
        in_specs=[
            *[cut(tokens)] * 4,
            cut(g_main.shape, 2),
            cut(g_gate.shape, 2),
            cut(matrix_out),
            fixed((BOX_ROWS, LANES)),
            *[cut(matrix_in)] * 3,
            *[cut(matrix_out)] * 3,
            *[fixed(small_dims)] * 3,
        ],
        out_shape=[
            *[shape(dims, bf16 if k == 0 else f32) for k, dims in enumerate(out_dims)],
            *[shape(small_dims, f32)] * 3,
            shape((TILE, LANES), f32),
        ],
        out_specs=[*[cut(dims) for dims in out_dims], *[fixed(small_dims)] * 3, fixed((TILE, LANES))],
        compiler_params=pltpu.CompilerParams(vmem_limit_bytes=VMEM_LIMIT),
    )(
        hidden[0], mixer, d_x_normed, back_own, g_main, g_gate, g_out, totals,
        in_w, in_m, in_v, out_w, out_m, out_v, small_w, small_m, small_v,
    )
    small_m_new, small_v_new, small_w_new = (
        array.reshape(-1)[:small_size] for array in (small_m_new, small_v_new, small_w_new)
    )
    return (
        output[None], grad_hidden[None], in_m_new, in_v_new, in_w_new, out_m_new, out_v_new, out_w_new,
        small_m_new, small_v_new, small_w_new, rms[0, :2],
    )


def solution(mesh):
    seq, wt = mesh.shape["seq"], mesh.shape["wt"]
    split = Mesh(mesh.devices.reshape(seq // TP, 2, 2, wt // 2, 2), EVERYONE)
    streams = ("w1", "w0")
    tokens = ("part", "t1", "t0")
    matrix = P(EVERYONE, None)
    stream = P(streams, tokens, None)
    size = mesh.devices.size
    fits = seq == 2 * TP and wt == 4 and D // size % 16 == 0 and D_INNER // size % 16 == 0
    return jax.shard_map(
        shards_linked if fits else shards_general,
        mesh=split,
        in_specs=(
            stream, stream, P(streams, None), P(streams, tokens), matrix, matrix, matrix, matrix, matrix, matrix, P(), P(), P(),
        ),
        out_specs=(stream, stream, matrix, matrix, matrix, matrix, matrix, matrix, P(), P(), P(), P()),
        check_vma=False,
    )
```

```python
import functools

import jax
import jax.numpy as jnp
from jax import lax
from jax.experimental import pallas as pl
from jax.experimental.pallas import tpu as pltpu
from jax.sharding import Mesh
from jax.sharding import PartitionSpec as P

D = 1536
D_INNER = 3072
HEADS = 48
HEADDIM = 64
STATE = 128
CONV = 4
SPAN = 256
STEP = 4
CONVCH = 3328
TP = 4
RIM = CONV - 1
LANES = 128
HALF = D_INNER // TP
LOCAL_HEADS = HEADS // TP
PAIRS = LOCAL_HEADS // 2
SIDE = 2 * STATE
COL_SIDE = HALF
COL_DT = HALF + SIDE
COL_GATE = COL_DT + LANES
COLS = COL_GATE + HALF

bf16 = jnp.bfloat16
f32 = jnp.float32
exact_prec = lax.Precision.HIGHEST
norm_eps = 1e-05
adam_eps = 1e-08


def dot(a, b, dims=((1,), (0,)), precision=None):
    return lax.dot_general(a, b, (dims, ((), ())), precision=precision, preferred_element_type=f32)


def unpack_small(small):
    first = D
    second = first + D_INNER
    third = second + CONV * CONVCH
    fourth = third + CONVCH
    fifth = fourth + HEADS
    sixth = fifth + HEADS
    return (
        small[:first],
        small[first:second],
        small[second:third].reshape(CONV, CONVCH),
        small[third:fourth],
        small[fourth:fifth],
        small[fifth:sixth],
        small[sixth:],
    )


def adamw(weight, moment, second, grad, rate, decay):
    moment_new = 0.5 * moment + 0.5 * grad
    second_new = 0.5 * second + 0.5 * grad * grad
    first_hat = moment_new / (1.0 - 0.5**STEP)
    second_hat = second_new / (1.0 - 0.5**STEP)
    weight_new = weight - rate * (first_hat / (jnp.sqrt(second_hat) + adam_eps) + decay * weight)
    return (moment_new, second_new, weight_new)


def pair_cols(cols, h):
    lane = lax.broadcasted_iota(jnp.int32, (cols.shape[0], LANES), 1)
    return jnp.where(lane < HEADDIM, cols[:, h : h + 1], cols[:, h + 1 : h + 2])


def span_rows(c):
    return pl.ds(pl.multiple_of(c * SPAN, SPAN), SPAN)


def span_decay(dt_ref, rate_ref, c, at=0):
    dt = dt_ref[span_rows(c), :]
    row = lax.broadcasted_iota(jnp.int32, (SPAN, SPAN), 0)
    col = lax.broadcasted_iota(jnp.int32, (SPAN, SPAN), 1)
    lower = (row >= col).astype(f32)
    return dt, dot(lower, dt * rate_ref[at : at + 1, :], precision=exact_prec)


def state_kernel(spans, x_ref, b_ref, dt_ref, rate_ref, keep_ref, carry_ref, s_ref, dec_ref):
    s_ref[...] = jnp.zeros_like(s_ref)
    dec_ref[...] = jnp.ones_like(dec_ref)

    def body(c, _):
        rows = span_rows(c)
        dt, cum = span_decay(dt_ref, rate_ref, c)
        last = cum[SPAN - 1 : SPAN, :]
        end_weight = jnp.exp(last - cum) * dt * keep_ref[rows, :]
        decay = jnp.exp(last) * carry_ref[pl.ds(c, 1), :]
        dec_ref[...] = dec_ref[...] * decay
        b = b_ref[rows, :]
        for p in range(PAIRS):
            lanes = slice(p * LANES, (p + 1) * LANES)
            xw = (x_ref[rows, lanes].astype(f32) * pair_cols(end_weight, 2 * p)).astype(bf16)
            fresh = dot(b, xw, ((0,), (0,)))
            s_ref[:, lanes] = s_ref[:, lanes] * pair_cols(decay, 2 * p) + fresh
        return 0

    lax.fori_loop(0, spans, body, 0)


def scan_kernel(
    spans, x_ref, b_ref, c_ref, dt_ref, rate_ref, segc_ref, segr_ref, keep_ref, inflow_ref, carry_ref, s_in_ref,
    y_ref, st_ref, s_ref,
):
    s_ref[...] = s_in_ref[...]

    def body(c, _):
        rows = span_rows(c)
        dt, cum = span_decay(dt_ref, rate_ref, c)
        last = cum[SPAN - 1 : SPAN, :]
        end_weight = jnp.exp(last - cum) * dt * keep_ref[rows, :]
        decay = jnp.exp(last) * carry_ref[pl.ds(c, 1), :]
        gain = jnp.exp(cum) * inflow_ref[rows, :]
        back_log = jnp.transpose(cum - jnp.log(dt))
        b = b_ref[rows, :]
        cc = c_ref[rows, :]
        scores = dot(cc, b, ((1,), (1,)))
        row = lax.broadcasted_iota(jnp.int32, (SPAN, SPAN), 0)
        col = lax.broadcasted_iota(jnp.int32, (SPAN, SPAN), 1)
        mask = (row >= col) & (segc_ref[rows, :] == segr_ref[pl.ds(c, 1), :])
        lane = lax.broadcasted_iota(jnp.int32, (SPAN, LANES), 1)
        st_ref[c] = s_ref[...]
        for p in range(PAIRS):
            lanes = slice(p * LANES, (p + 1) * LANES)
            x = x_ref[rows, lanes]
            parts = []
            for h in (2 * p, 2 * p + 1):
                gap = cum[:, h : h + 1] - back_log[h : h + 1, :]
                weights = scores * jnp.exp(jnp.where(mask, gap, -1e30))
                parts.append(dot(weights.astype(bf16), x))
            y = jnp.where(lane < HEADDIM, parts[0], parts[1])
            state = s_ref[:, lanes]
            y = y + dot(cc, state.astype(bf16)) * pair_cols(gain, 2 * p)
            y_ref[rows, lanes] = y
            xw = (x.astype(f32) * pair_cols(end_weight, 2 * p)).astype(bf16)
            s_ref[:, lanes] = state * pair_cols(decay, 2 * p) + dot(b, xw, ((0,), (0,)))
        return 0

    lax.fori_loop(0, spans, body, 0)


def state_back_kernel(spans, dy_ref, c_ref, dt_ref, rate_ref, inflow_ref, carry_ref, s_ref):
    s_ref[...] = jnp.zeros_like(s_ref)

    def body(step, _):
        c = spans - 1 - step
        rows = span_rows(c)
        dt, cum = span_decay(dt_ref, rate_ref, c)
        decay = jnp.exp(cum[SPAN - 1 : SPAN, :]) * carry_ref[pl.ds(c, 1), :]
        gain = jnp.exp(cum) * inflow_ref[rows, :]
        cc = c_ref[rows, :]
        for p in range(PAIRS):
            lanes = slice(p * LANES, (p + 1) * LANES)
            dyg = (dy_ref[rows, lanes].astype(f32) * pair_cols(gain, 2 * p)).astype(bf16)
            s_ref[:, lanes] = s_ref[:, lanes] * pair_cols(decay, 2 * p) + dot(cc, dyg, ((0,), (0,)))
        return 0

    lax.fori_loop(0, spans, body, 0)


def head_sums(values):
    width = values.shape[1]
    chan = lax.broadcasted_iota(jnp.int32, (width, LANES), 0)
    head = lax.broadcasted_iota(jnp.int32, (width, LANES), 1)
    pick = (chan // HEADDIM == head).astype(bf16)
    high = values.astype(bf16)
    low = (values - high.astype(f32)).astype(bf16)
    return dot(high, pick) + dot(low, pick)


def scan_back_kernel(
    spans, x_ref, b_ref, c_ref, dt_ref, ratio_ref, sig_ref, rate_ref, segc_ref, segr_ref, keep_ref, inflow_ref, carry_ref, skip_ref,
    y_ref, st_ref, dy_ref, ds_out_ref,
    dx_ref, db_ref, dc_ref, ddt_ref, drate_ref, dskip_ref,
    ds_ref, prod_ref,
):
    ds_ref[...] = ds_out_ref[...]
    drate_ref[...] = jnp.zeros_like(drate_ref)
    dskip_ref[...] = jnp.zeros_like(dskip_ref)

    def body(step, _):
        c = spans - 1 - step
        rows = span_rows(c)
        dt, cum = span_decay(dt_ref, rate_ref, c)
        last = cum[SPAN - 1 : SPAN, :]
        end_weight = jnp.exp(last - cum) * dt * keep_ref[rows, :]
        decay = jnp.exp(last) * carry_ref[pl.ds(c, 1), :]
        gain = jnp.exp(cum) * inflow_ref[rows, :]
        fore_log = jnp.transpose(cum)
        back_log = cum - jnp.log(dt)
        b = b_ref[rows, :]
        cc = c_ref[rows, :]
        scores = dot(b, cc, ((1,), (1,)))
        row = lax.broadcasted_iota(jnp.int32, (SPAN, SPAN), 0)
        col = lax.broadcasted_iota(jnp.int32, (SPAN, SPAN), 1)
        mask = (col >= row) & (segc_ref[rows, :] == segr_ref[pl.ds(c, 1), :])
        lane = lax.broadcasted_iota(jnp.int32, (SPAN, LANES), 1)
        d_scores = jnp.zeros((SPAN, SPAN), f32)
        db = jnp.zeros((SPAN, STATE), f32)
        dc = jnp.zeros((SPAN, STATE), f32)
        state_row = []
        dx_state_row = []
        for p in range(PAIRS):
            lanes = slice(p * LANES, (p + 1) * LANES)
            x = x_ref[rows, lanes]
            dy = dy_ref[rows, lanes]
            xf = x.astype(f32)
            dyf = dy.astype(f32)
            parts = []
            for k in range(2):
                h = 2 * p + k
                gap = fore_log[h : h + 1, :] - back_log[:, h : h + 1]
                decay_mat = jnp.exp(jnp.where(mask, gap, -1e30))
                weights = (scores * decay_mat).astype(bf16)
                parts.append(dot(weights, dy))
                own = (lane < HEADDIM) if k == 0 else (lane >= HEADDIM)
                d_weights = dot(jnp.where(own, xf, 0.0).astype(bf16), dy, ((1,), (1,)))
                d_scores = d_scores + d_weights * decay_mat
            dx = jnp.where(lane < HEADDIM, parts[0], parts[1])
            dyg = (dyf * pair_cols(gain, 2 * p)).astype(bf16)
            ew = pair_cols(end_weight, 2 * p)
            xw = (xf * ew).astype(bf16)
            state = st_ref[c, :, lanes]
            ds = ds_ref[:, lanes]
            state_b = state.astype(bf16)
            ds_b = ds.astype(bf16)
            dc = dc + dot(dyg, state_b, ((1,), (1,)))
            db = db + dot(xw, ds_b, ((1,), (1,)))
            dx_state = dot(b, ds_b) * ew
            dx = dx + dx_state
            dec = pair_cols(decay, 2 * p)
            state_row.append(jnp.sum(ds * state, axis=0, keepdims=True) * dec)
            dx_state_row.append(jnp.sum(dx_state * xf, axis=0, keepdims=True))
            ds_ref[:, lanes] = ds * dec + dot(cc, dyg, ((0,), (0,)))
            prod_ref[0:SPAN, lanes] = dyf * y_ref[rows, lanes]
            prod_ref[SPAN : 2 * SPAN, lanes] = xf * dx
            dskip_ref[0:1, lanes] += jnp.sum(dyf * xf, axis=0, keepdims=True)
            dx_ref[rows, lanes] = (dx + dyf * skip_ref[0:1, lanes]).astype(bf16)
        d_scores_b = d_scores.astype(bf16)
        db_ref[rows, :] = db + dot(d_scores_b, cc)
        dc_ref[rows, :] = dc + dot(d_scores_b, b, ((0,), (0,)))
        sums = head_sums(prod_ref[...])
        out_sum, in_sum = sums[:SPAN], sums[SPAN:]
        edge = jnp.concatenate(state_row, axis=1) + jnp.concatenate(dx_state_row, axis=1)
        edge_sum = head_sums(jnp.broadcast_to(edge, (8, HALF)))[0:1]
        at_last = lax.broadcasted_iota(jnp.int32, (SPAN, LANES), 0) == SPAN - 1
        d_cum = out_sum - in_sum + jnp.where(at_last, edge_sum, 0.0)
        upper = (col >= row).astype(f32)
        d_log = dot(upper, d_cum, precision=exact_prec)
        drate_ref[0:1, :] += jnp.sum(d_log * dt, axis=0, keepdims=True)
        ddt_ref[rows, :] = d_log * rate_ref[0:1, :] * sig_ref[rows, :] + in_sum * ratio_ref[rows, :]
        return 0

    lax.fori_loop(0, spans, body, 0)


GROUP = ("t1", "t0")
COPIES = ("part", "w1", "w0")
EVERYONE = ("part", "t1", "t0", "w1", "w0")


VMEM_LIMIT = 63 * 1024 * 1024


def in_vmem(kernel, out_shape, name, scratch=()):
    return pl.pallas_call(
        kernel,
        out_shape=out_shape,
        scratch_shapes=list(scratch),
        name=name,
        compiler_params=pltpu.CompilerParams(vmem_limit_bytes=VMEM_LIMIT),
    )


def shape(dims, dtype):
    return jax.ShapeDtypeStruct(dims, dtype)


def shift_part(array, by):
    size = lax.axis_size("part")
    pairs = [(i, i + by) for i in range(size) if 0 <= i + by < size]
    return lax.ppermute(array, "part", pairs)


def shards_general(
    hidden, cotangent, segments, valid, in_w, in_m, in_v, out_w, out_m, out_v, small_w, small_m, small_v,
):
    parts = lax.axis_size("part")
    wt = lax.axis_size("w1") * lax.axis_size("w0")
    part = lax.axis_index("part")
    tp = lax.axis_index("t1") * 2 + lax.axis_index("t0")
    own_rows = in_w.shape[0]
    out_rows = out_w.shape[0]
    resid = hidden[0].astype(f32)
    tok_rows = resid.shape[0]
    rows = tok_rows * TP
    spans = rows // SPAN
    seg_all = segments[0]
    pre_gain, norm_gain, conv_weight, conv_bias, dt_shift, a_logs, skips = unpack_small(small_w)

    def own_part(array, width):
        return lax.dynamic_slice_in_dim(array, tp * width, width, array.ndim - 1)

    in_copy = in_w.astype(bf16)
    slices = []
    for j in range(TP):
        slices.append(
            jnp.concatenate(
                [
                    in_copy[:, D_INNER + j * HALF : D_INNER + (j + 1) * HALF],
                    in_copy[:, 2 * D_INNER : 2 * D_INNER + SIDE],
                    in_copy[:, D_INNER + CONVCH + j * LOCAL_HEADS : D_INNER + CONVCH + (j + 1) * LOCAL_HEADS],
                    jnp.zeros((own_rows, LANES - LOCAL_HEADS), bf16),
                    in_copy[:, j * HALF : (j + 1) * HALF],
                ],
                axis=1,
            )
        )
    mine = lax.all_to_all(jnp.stack(slices), GROUP, 0, 0, tiled=False)
    w_in = lax.all_gather(mine, COPIES, axis=0, tiled=False)
    w_in = w_in.reshape(parts, wt, TP, own_rows, COLS).transpose(0, 2, 1, 3, 4).reshape(D, COLS)
    flat = [(i, (i % TP) * parts + i // TP) for i in range(parts * TP)]
    out_mine = lax.ppermute(out_w.astype(bf16), ("part", *GROUP), [(b, a) for a, b in flat])
    w_out = lax.all_gather(out_mine, COPIES, axis=0, tiled=True)

    hidden_all = lax.all_gather(hidden[0], GROUP, axis=0, tiled=True)
    back_mix = cotangent[0] * valid[0][:, None].astype(bf16)
    back_all = lax.all_gather(back_mix, GROUP, axis=0, tiled=True)

    hid = hidden_all.astype(f32)
    scale_all = lax.rsqrt(jnp.mean(hid * hid, axis=1, keepdims=True) + norm_eps)
    x_normed = (hid * scale_all * pre_gain).astype(bf16)
    projected = dot(x_normed, w_in)
    conv_in = projected[:, :COL_DT].astype(bf16)
    dt_raw = projected[:, COL_DT:COL_GATE].astype(bf16).astype(f32)
    gate_pre = projected[:, COL_GATE:]
    rim_in = shift_part(conv_in[rows - RIM :], 1)
    padded = jnp.concatenate([rim_in, conv_in], axis=0).astype(f32)
    seg_front = jnp.concatenate([jnp.full((RIM,), -1, jnp.int32), seg_all, jnp.full((RIM,), -1, jnp.int32)])
    seg_pad = lax.dynamic_slice_in_dim(seg_front, part * rows, rows + 2 * RIM)
    seg = seg_pad[RIM : RIM + rows]
    masks = [(seg_pad[k : k + rows] == seg).astype(f32)[:, None] for k in range(CONV)]
    taps = jnp.concatenate([own_part(conv_weight[:, :D_INNER], HALF), conv_weight[:, D_INNER:]], axis=1)
    bias = jnp.concatenate([own_part(conv_bias[:D_INNER], HALF), conv_bias[D_INNER:]])
    total = bias[None, :]
    for k in range(CONV):
        total = total + taps[k] * padded[k : k + rows] * masks[k]
    sig_total = jax.nn.sigmoid(total)
    activated = (total * sig_total).astype(bf16)
    x_scan = activated[:, :HALF]
    b_mat = activated[:, HALF : HALF + STATE]
    c_mat = activated[:, HALF + STATE :]

    def head_row(array):
        return jnp.pad(own_part(array, LOCAL_HEADS), (0, LANES - LOCAL_HEADS))

    shift_row = head_row(dt_shift)
    z = dt_raw + shift_row
    dt = jax.nn.softplus(z)
    sig_dt = jax.nn.sigmoid(z)
    ratio = jnp.where(dt > 1e-30, sig_dt / jnp.maximum(dt, 1e-30), 1.0)
    rate_row = -jnp.exp(head_row(a_logs))
    rate8 = jnp.broadcast_to(rate_row, (8, LANES))
    skip_chan = jnp.repeat(own_part(skips, LOCAL_HEADS), HEADDIM)
    skip8 = jnp.broadcast_to(skip_chan, (8, HALF))
    seg_spans = seg.reshape(spans, SPAN)
    seg_last = seg_spans[:, -1]
    seg_before = jnp.concatenate([seg_pad[RIM - 1 : RIM], seg_last[:-1]])
    keep = (seg_spans == seg_last[:, None]).astype(f32).reshape(rows, 1)
    inflow = (seg_spans == seg_before[:, None]).astype(f32).reshape(rows, 1)
    carry = jnp.broadcast_to((seg_last == seg_before).astype(f32)[:, None], (spans, LANES))
    seg_col = seg[:, None]

    state_shape = shape((STATE, HALF), f32)
    s_local, dec_total = in_vmem(
        functools.partial(state_kernel, spans), (state_shape, shape((8, LANES), f32)), "state"
    )(x_scan, b_mat, dt, rate8, keep, carry)
    dec_chan = jnp.repeat(dec_total[0, :LOCAL_HEADS], HEADDIM)
    s_in = jnp.zeros((STATE, HALF), f32)
    for _ in range(parts - 1):
        s_in = shift_part(dec_chan * s_in + s_local, 1)
    y_scan, states = in_vmem(
        functools.partial(scan_kernel, spans),
        (shape((rows, HALF), f32), shape((spans, STATE, HALF), f32)),
        "scan",
        [pltpu.VMEM((STATE, HALF), f32)],
    )(x_scan, b_mat, c_mat, dt, rate8, seg_col, seg_spans, keep, inflow, carry, s_in)
    y_b = (y_scan + skip_chan * x_scan.astype(f32)).astype(bf16).astype(f32)

    gain_own = own_part(norm_gain, HALF)
    sig_gate = jax.nn.sigmoid(gate_pre)
    silu_gate = gate_pre * sig_gate
    gated = y_b * silu_gate
    gate_sq = lax.psum(jnp.sum(gated * gated, axis=1), GROUP)
    scale_gate = lax.rsqrt(gate_sq / D_INNER + norm_eps)[:, None]
    normed = (gated * scale_gate * gain_own).astype(bf16)
    mixer = lax.psum_scatter(dot(normed, w_out), GROUP, scatter_dimension=0, tiled=True)
    output = (resid + mixer).astype(bf16)
    valid_rows = valid[0].astype(f32)
    res_sq = jnp.sum(valid_rows * jnp.sum(resid * resid, axis=1))
    mix_sq = jnp.sum(valid_rows * jnp.sum(mixer * mixer, axis=1))
    valid_count = jnp.sum(valid_rows)

    d_normed = dot(back_all, w_out, ((1,), (1,)))
    g_out = dot(normed, back_all, ((0,), (0,)))
    g_out = lax.psum_scatter(g_out, COPIES, scatter_dimension=0, tiled=True)
    g_out = lax.ppermute(g_out, ("part", *GROUP), flat)
    d_gain = d_normed * gain_own
    gate_dot = lax.psum(jnp.sum(gated * d_gain, axis=1), GROUP)
    d_gated = scale_gate * d_gain - gated * (scale_gate**3 * (gate_dot / D_INNER)[:, None])
    d_norm_gain = jnp.sum(gated * scale_gate * d_normed, axis=0)
    dy = (d_gated * silu_gate).astype(bf16)
    d_gate = d_gated * y_b * (sig_gate * (1.0 + gate_pre * (1.0 - sig_gate)))

    ds_local = in_vmem(functools.partial(state_back_kernel, spans), state_shape, "state_back")(
        dy, c_mat, dt, rate8, inflow, carry
    )
    ds_out = jnp.zeros((STATE, HALF), f32)
    for _ in range(parts - 1):
        ds_out = shift_part(dec_chan * ds_out + ds_local, -1)
    d_x, d_b, d_c, d_dt, d_rate, d_skip = in_vmem(
        functools.partial(scan_back_kernel, spans),
        (
            shape((rows, HALF), bf16),
            shape((rows, STATE), f32),
            shape((rows, STATE), f32),
            shape((rows, LANES), f32),
            shape((8, LANES), f32),
            shape((8, HALF), f32),
        ),
        "scan_back",
        [pltpu.VMEM((STATE, HALF), f32), pltpu.VMEM((2 * SPAN, HALF), f32)],
    )(x_scan, b_mat, c_mat, dt, ratio, sig_dt, rate8, seg_col, seg_spans, keep, inflow, carry, skip8, y_scan, states, dy, ds_out)

    d_total = jnp.concatenate([d_x.astype(f32), d_b, d_c], axis=1) * (sig_total * (1.0 + total * (1.0 - sig_total)))
    rim_back = shift_part(d_total[:RIM], -1)
    d_padded = jnp.concatenate([d_total, rim_back], axis=0)
    d_conv_in = 0.0
    for k in range(CONV):
        later = (seg_pad[2 * RIM - k : 2 * RIM - k + rows] == seg).astype(f32)[:, None]
        d_conv_in = d_conv_in + taps[k] * d_padded[RIM - k : RIM - k + rows] * later
    d_taps = jnp.stack([jnp.sum(d_total * padded[k : k + rows] * masks[k], axis=0) for k in range(CONV)])
    d_bias = jnp.sum(d_total, axis=0)
    d_proj = jnp.concatenate([d_conv_in, d_dt, d_gate], axis=1).astype(bf16)
    d_x_normed = dot(d_proj, w_in, ((1,), (1,)))
    d_x_normed = lax.psum_scatter(d_x_normed, GROUP, scatter_dimension=0, tiled=True)
    g_in = dot(x_normed, d_proj, ((0,), (0,)))
    g_in = g_in.reshape(parts, TP, wt, own_rows, COLS).transpose(0, 2, 1, 3, 4).reshape(parts * wt, TP, own_rows, COLS)
    g_in = lax.psum_scatter(g_in, COPIES, scatter_dimension=0, tiled=False)
    g_in = lax.all_to_all(g_in, GROUP, 0, 0, tiled=False)
    g_in = jnp.concatenate(
        [g_in[j, :, COL_GATE:] for j in range(TP)]
        + [g_in[j, :, :HALF] for j in range(TP)]
        + [jnp.sum(g_in[:, :, COL_SIDE:COL_DT], axis=0)]
        + [g_in[j, :, COL_DT : COL_DT + LOCAL_HEADS] for j in range(TP)],
        axis=1,
    )

    scale_own = lax.rsqrt(jnp.mean(resid * resid, axis=1, keepdims=True) + norm_eps)
    d_pre = d_x_normed * pre_gain
    dot_pre = jnp.mean(resid * d_pre, axis=1, keepdims=True)
    grad_hidden = back_mix.astype(f32) + scale_own * d_pre - resid * (scale_own**3 * dot_pre)
    d_pre_gain = jnp.sum(resid * scale_own * d_x_normed, axis=0)

    def placed(values, width):
        spread = (jnp.arange(TP) == tp).astype(f32)[:, None] * values[..., None, :]
        return spread.reshape(*values.shape[:-1], TP * width)

    d_weight = jnp.concatenate([placed(d_taps[:, :HALF], HALF), d_taps[:, HALF:]], axis=1)
    small_grad = jnp.concatenate(
        [
            d_pre_gain,
            placed(d_norm_gain, HALF),
            d_weight.reshape(-1),
            placed(d_bias[:HALF], HALF),
            d_bias[HALF:],
            placed(jnp.sum(d_dt, axis=0)[:LOCAL_HEADS], LOCAL_HEADS),
            placed((d_rate[0] * rate_row)[:LOCAL_HEADS], LOCAL_HEADS),
            placed(jnp.sum(d_skip[0].reshape(LOCAL_HEADS, HEADDIM), axis=1), LOCAL_HEADS),
            jnp.stack([res_sq, mix_sq, valid_count]),
        ]
    )
    small_total = lax.psum(small_grad, EVERYONE)
    res_total, mix_total, count_total = small_total[-3], small_total[-2], small_total[-1]
    in_m_new, in_v_new, in_w_new = adamw(in_w, in_m, in_v, g_in, 0.02, 0.1)
    out_m_new, out_v_new, out_w_new = adamw(out_w, out_m, out_v, g_out, 0.02, 0.1)
    small_m_new, small_v_new, small_w_new = adamw(small_w, small_m, small_v, small_total[:-3], 0.2, 0.0)
    rms = jnp.stack([jnp.sqrt(res_total / (count_total * D)), jnp.sqrt(mix_total / (count_total * D))])
    return (
        output[None], grad_hidden[None], in_m_new, in_v_new, in_w_new, out_m_new, out_v_new, out_w_new,
        small_m_new, small_v_new, small_w_new, rms,
    )


MESH = pl.DeviceIdType.MESH
T0, T1, DIAG, CORE, SIDEWAYS, PART = ("t0",), ("t1",), ("t1", "t0"), ("w0",), ("w1",), ("part",)
SIDE_CORE = ("w1", "w0")
HOPS = (None, T0, T1, DIAG)
HBM = pl.BlockSpec(memory_space=pl.ANY)
VMEM = pl.BlockSpec(memory_space=pltpu.VMEM)
MAIN = COL_GATE
CHANS = HALF + SIDE
FRONT = 16
TILE = 8
QUARTER = HALF // 2
NORM_ROW = D // LANES
TAP_ROW = NORM_ROW + D_INNER // LANES
TAP_ROWS = CONVCH // LANES
HEAD_ROW = TAP_ROW + (CONV + 1) * TAP_ROWS
SMALL_ROWS = HEAD_ROW + 2
BOX_ROWS = SMALL_ROWS + 8
OWN_NORM = NORM_ROW
OWN_TAP = OWN_NORM + HALF // LANES
OWN_SIDE = OWN_TAP + (CONV + 1) * (HALF // LANES)
OWN_HEAD = OWN_SIDE + (CONV + 1) * (SIDE // LANES)
OWN_SUMS = OWN_HEAD + 3
OWN_ROWS = 64


def place():
    return tuple(lax.axis_index(a) for a in EVERYONE)


def across(flips):
    return {a: 1 - lax.axis_index(a) for a in flips}


def group_blocks():
    _, t1, t0, _, _ = place()
    return [(t1, t0), (t1, 1 - t0), (1 - t1, t0), (1 - t1, 1 - t0)]


def greet(neighbours):
    barrier = pltpu.get_barrier_semaphore()
    for flips in neighbours:
        pl.semaphore_signal(barrier, inc=1, device_id=across(flips), device_id_type=MESH)


def greeted(neighbours):
    pl.semaphore_wait(pltpu.get_barrier_semaphore(), len(neighbours))


class Copies:
    def __init__(self, local_sem, send_sem, recv_sem):
        self.local_sem, self.send_sem, self.recv_sem = local_sem, send_sem, recv_sem
        self.sent, self.kept, self.in_flight, self.on_device = 0, 0, [], []

    def send(self, src, dst, flips):
        copy = pltpu.make_async_remote_copy(
            src_ref=src,
            dst_ref=dst,
            send_sem=self.send_sem.at[self.sent],
            recv_sem=self.recv_sem.at[self.sent],
            device_id=across(flips),
            device_id_type=MESH,
        )
        copy.start()
        self.sent += 1
        self.in_flight.append(copy)
        return copy

    def keep(self, src, dst):
        copy = pltpu.make_async_copy(src, dst, self.local_sem.at[self.kept])
        copy.start()
        self.kept += 1
        self.on_device.append(copy)
        return copy

    def settle(self, copy):
        copy.wait()
        self.on_device = [other for other in self.on_device if other is not copy]

    def left(self, copies):
        for copy in copies:
            copy.wait_send()
            self.in_flight = [other for other in self.in_flight if other is not copy]

    def drain(self):
        for copy in self.in_flight:
            copy.wait_send()
        for copy in self.on_device:
            copy.wait()
        self.in_flight, self.on_device = [], []


def sems(remote, local=1):
    return [
        pltpu.SemaphoreType.DMA((local,)),
        pltpu.SemaphoreType.DMA((remote,)),
        pltpu.SemaphoreType.DMA((remote,)),
    ]


class GroupGather:
    def __init__(self, copies, src, dst):
        self.copies, self.dst = copies, dst
        self.rows = src.shape[0]
        self.halves = (0, self.rows // 2)
        own = group_blocks()[0]
        self.src, self.own, self.size = src, copies.keep(src, self.at(own, 0, self.rows)), self.rows // 2
        self.along_t1, self.along_t0, self.diagonal = self.start(T1), [], []

    def start(self, flips):
        own = group_blocks()[0]
        return [
            self.copies.send(self.src.at[pl.ds(h, self.size)], self.at(own, h, self.size), flips) for h in self.halves
        ]

    def start_t0(self):
        self.along_t0 = self.start(T0)

    def at(self, block, first, size):
        return self.dst.at[pl.ds(pl.multiple_of((block[0] * 2 + block[1]) * self.rows + first, size), size)]

    def hand_on(self):
        beside = group_blocks()[2]
        for copy, h in zip(self.along_t1, self.halves):
            copy.wait_recv()
            here = self.at(beside, h, self.rows // 2)
            self.diagonal.append(self.copies.send(here, here, T0))

    def finish(self):
        for copy in self.along_t0 + self.diagonal:
            copy.wait_recv()


class WeightGather:
    def __init__(self, copies, dst, rows, group):
        self.copies, self.dst, self.rows, self.group = copies, dst, rows, group
        self.by_part, self.by_side, self.by_core = [], [], []

    def at(self, part, w1, w0, block):
        index = part
        if self.group:
            index = (index * 2 + block[0]) * 2 + block[1]
        index = (index * 2 + w1) * 2 + w0
        return self.dst.at[pl.ds(pl.multiple_of(index * self.rows, self.rows), self.rows)]

    def mine(self, block):
        p, _, _, w1, w0 = place()
        return self.at(p, w1, w0, block)

    def spread(self, src, block):
        dst = self.mine(block)
        self.by_part.append((self.copies.send(src, dst, PART), block))
        self.by_side.append((self.copies.send(src, dst, SIDEWAYS), block))
        self.by_core.append(self.copies.send(src, dst, CORE))

    def swap(self, src):
        own, *others = group_blocks()

        def slice_of(block):
            return src.at[block_rows(block, self.rows)]

        self.swaps = [(self.copies.send(slice_of(b), self.mine(own), flips), b) for b, flips in zip(others, HOPS[1:])]
        self.kept = self.copies.keep(slice_of(own), self.mine(own))
        self.spread(slice_of(own), own)

    def spread_swapped(self):
        for copy, block in self.swaps:
            copy.wait_recv()
            self.spread(self.mine(block), block)

    def pass_core(self, part, w1, block):
        here = self.at(part, w1, lax.axis_index("w0"), block)
        self.by_core.append(self.copies.send(here, here, CORE))

    def hand_on(self):
        p, _, _, w1, w0 = place()
        self.again = []
        for (copy, block), (side, _) in zip(self.by_part, self.by_side):
            side.wait_recv()
            self.pass_core(p, 1 - w1, block)
            copy.wait_recv()
            here = self.at(1 - p, w1, w0, block)
            self.again.append((self.copies.send(here, here, SIDEWAYS), block))
            self.pass_core(1 - p, w1, block)

    def hand_on_last(self):
        p, _, _, w1, _ = place()
        for copy, block in self.again:
            copy.wait_recv()
            self.pass_core(1 - p, 1 - w1, block)

    def finish(self):
        for copy in self.by_core:
            copy.wait_recv()


class GradientSum:
    def __init__(self, copies, srcs, rows, bufs, group):
        self.copies, self.srcs, self.rows, self.group = copies, srcs, rows, group
        self.core, self.sides, self.fars = bufs[:3]
        self.lasts = bufs[3] if group else None
        self.blocks = group_blocks() if group else [()]
        self.order = (1, 2, 3, 0) if group else (0,)
        p, _, _, w1, _ = place()
        self.parts, self.sides_of = (1 - p, p), (1 - w1, w1)
        self.core_copies, self.side_copies, self.far_copies, self.last_copies = {}, {}, {}, {}

    def at(self, block, side, w0):
        index = block[0] * 2 + block[1] if self.group else 0
        index = (index * 2 + side) * 2 + w0
        return pl.ds(pl.multiple_of(index * self.rows, self.rows), self.rows)

    def place(self, i, j):
        return self.at(self.blocks[i], self.sides_of[j], lax.axis_index("w0"))

    def pass_on(self, k, i, j, value, dst, flips):
        here = self.place(i, j)
        self.srcs[k][here, :] = value.astype(bf16)
        return self.copies.send(self.srcs[k].at[here], dst, flips)

    def added(self, k, i, j, *more):
        q, block, side = self.parts[k], self.blocks[i], self.sides_of[j]
        self.core_copies[k, i, j].wait_recv()
        value = self.srcs[k][self.place(i, j), :].astype(f32)
        value = value + self.core[(q, side, *block)].astype(f32)
        for other in more:
            value = value + other.astype(f32)
        return value

    def cores(self, k):
        w0 = lax.axis_index("w0")
        for j in range(2):
            for i in self.order:
                q, block, side = self.parts[k], self.blocks[i], self.sides_of[j]
                src = self.srcs[k].at[self.at(block, side, 1 - w0)]
                self.core_copies[k, i, j] = self.copies.send(src, self.core.at[(q, side, *block)], CORE)

    def left(self):
        for copies in (self.core_copies, self.side_copies, self.far_copies, self.last_copies):
            self.copies.left(copies.values())

    def to_sides(self, k):
        for i in self.order:
            self.side_copies[k, i] = self.pass_on(k, i, 0, self.added(k, i, 0), self.sides.at[k, i], SIDEWAYS)

    def to_part(self, which=None):
        for i in self.order if which is None else which:
            self.side_copies[0, i].wait_recv()
            value = self.added(0, i, 1, self.sides[0, i])
            self.far_copies[i] = self.pass_on(0, i, 1, value, self.fars.at[i], PART)

    def total(self, i):
        self.side_copies[1, i].wait_recv()
        self.far_copies[i].wait_recv()
        return self.added(1, i, 1, self.sides[1, i], self.fars[i])

    def to_group(self, store):
        for i in self.order:
            value = self.total(i)
            if i == 0:
                store(0, value)
            else:
                self.last_copies[i] = self.pass_on(1, i, 1, value, self.lasts.at[i - 1], HOPS[i])

    def finish(self, store):
        for i, copy in self.last_copies.items():
            copy.wait_recv()
            store(i, self.lasts[i - 1].astype(f32))


class GroupScatter:
    def __init__(self, copies, src, bufs):
        self.copies, self.src = copies, src
        self.here, self.pass_on, self.last = bufs
        self.rows = self.here.shape[0]

    def block(self, i):
        return block_rows(group_blocks()[i], self.rows)

    def left(self):
        self.copies.left([self.own_copy, self.pass_copy])

    def to_t0(self, i):
        copy = self.copies.send(self.src.at[self.block(i)], self.here if i == 1 else self.pass_on, T0)
        if i == 1:
            self.own_copy = copy
        else:
            self.pass_copy = copy

    def to_t1(self):
        self.pass_copy.wait_recv()
        here = self.block(2)
        self.src[here, :] = (self.src[here, :].astype(f32) + self.pass_on[...].astype(f32)).astype(bf16)
        self.last_copy = self.copies.send(self.src.at[here], self.last, T1)

    def finish(self):
        self.own_copy.wait_recv()
        self.last_copy.wait_recv()
        return self.here[...].astype(f32) + self.last[...].astype(f32)


def scatter_buffers(rows):
    return [pltpu.VMEM((rows, D), bf16)] * 3


def sum_buffers(rows, cols, group):
    buf = lambda *lead: pltpu.VMEM((*lead, rows, cols), bf16)
    if not group:
        return [buf(2, 2), buf(2, 1), buf(1)]
    return [buf(2, 2, 2, 2), buf(2, 4), buf(4), buf(3)]


def block_rows(block, size):
    return pl.ds(pl.multiple_of((block[0] * 2 + block[1]) * size, size), size)


def lane_of(h):
    return h if h < LOCAL_HEADS // 2 else h + HEADS // 2 - LOCAL_HEADS // 2


def own_pair(cols, h):
    lane = lax.broadcasted_iota(jnp.int32, (cols.shape[0], LANES), 1)
    first, second = lane_of(h), lane_of(h + 1)
    return jnp.where(lane < HEADDIM, cols[:, first : first + 1], cols[:, second : second + 1])


def own_sums(values):
    width = values.shape[1]
    head = lax.broadcasted_iota(jnp.int32, (width, LANES), 0) // HEADDIM
    lane = lax.broadcasted_iota(jnp.int32, (width, LANES), 1)
    pick = (jnp.where(head < LOCAL_HEADS // 2, head, head + lane_of(LOCAL_HEADS) - LOCAL_HEADS) == lane).astype(bf16)
    high = values.astype(bf16)
    low = (values - high.astype(f32)).astype(bf16)
    return dot(high, pick) + dot(low, pick)


def head_lanes(values, back=False):
    first = (lax.axis_index("t1") * 2 + lax.axis_index("t0")) * (LOCAL_HEADS // 2)
    return pltpu.roll(values, first if back else LANES - first, 1)


def own_row(first, k):
    tp = lax.axis_index("t1") * 2 + lax.axis_index("t0")
    third = QUARTER // LANES
    return pl.ds(first + (k // third) * (D_INNER // 2 // LANES) + tp * third + k % third, 1)


def own_chans(j):
    return [slice(first + j * QUARTER, first + (j + 1) * QUARTER) for first in (0, D_INNER // 2)]


EVERY_NEIGHBOUR = (T0, T1, DIAG, CORE, SIDEWAYS, SIDE_CORE, PART)


def main_kernel(
    spans, hid_ref, inw_hbm, outw_hbm, cot_hbm, inside_ref, valid_ref, small_ref, segs_ref,
    cotv_out, mixer_out, ggate_out, gmain_out, dx_out, gout_out, total_ref,
    h_ref, xn_ref, win_ref, convp_ref, x_ref, b_ref, c_ref, dtot_ref, dt_ref, z_ref, cum_ref, y_ref, st_ref,
    wgate_ref, wout_ref, back_ref, normed_ref, mix_ref, dy_ref, dgate_ref, dmain_ref, dgain_ref, taps_ref, heads_ref, chans_ref,
    marks_ref, carry_ref, s_ref, pass_ref, got_ref, rim_ref, gated_ref, gate_ref, dn_ref,
    stat_ref, stats_ref, dyg_ref, passb_ref, gotb_ref, rims_ref, rimr_ref, hsum_ref, dskip_ref, dtaps_ref,
    dpre_ref, box_ref, boxes_ref, gm_ref, segc_ref, segr_ref, validc_ref,
    *rest,
):
    go_bufs, gg_bufs, gm_bufs, mix_bufs, dx_bufs = rest[:3], rest[3:7], rest[7:11], rest[11:14], rest[14:17]
    local_sem, send_sem, recv_sem = rest[17:]
    greet(EVERY_NEIGHBOUR)
    p, _, _, _, _ = place()
    rows_all = spans * SPAN
    tokens = hid_ref.shape[0]
    own_rows, out_rows = inw_hbm.shape[0], outw_hbm.shape[0]
    lane = lax.broadcasted_iota(jnp.int32, (1, LANES), 1)
    wm_ref = dmain_ref.at[pl.ds(0, TP * own_rows)]
    wg_ref = dgate_ref.at[pl.ds(0, TP * own_rows)]
    wo_ref = mix_ref.at[pl.ds(0, out_rows)]
    cotv_ref = mix_ref.at[pl.ds(tokens, tokens)]
    dxi_ref, prod_ref = gated_ref, gate_ref

    def side_at(c, which):
        return (slice(spans * STATE, spans * STATE + SPAN), pl.ds(pl.multiple_of((which * spans + c) * STATE, STATE), STATE))


    copies = Copies(local_sem, send_sem, recv_sem)
    loads = [
        copies.keep(inw_hbm.at[:, pl.ds(k * HALF, HALF)], gate_ref.at[pl.ds(k * own_rows, own_rows)])
        for k in range(2 * D_INNER // HALF)
    ]
    loads += [
        copies.keep(outw_hbm.at[:, pl.ds(k * HALF, HALF)], dn_ref.at[pl.ds(k * out_rows, out_rows)]) for k in range(D // HALF)
    ]
    loads.append(copies.keep(cot_hbm, cotv_ref))

    side = inside_ref[:, 0 : SIDE + HEADS]
    dt_cols = jnp.concatenate([side[:, SIDE:], jnp.zeros((own_rows, LANES - HEADS), f32)], axis=1)
    for copy in loads:
        copies.settle(copy)

    def master(first):
        return gate_ref[first // HALF * own_rows : (first // HALF + 1) * own_rows, first % HALF : first % HALF + QUARTER]

    for j in range(TP):
        at = slice(j * own_rows, (j + 1) * own_rows)
        for k, chans in enumerate(own_chans(j)):
            part = slice(k * QUARTER, (k + 1) * QUARTER)
            wg_ref[at, part] = master(chans.start).astype(bf16)
            wm_ref[at, part] = master(D_INNER + chans.start).astype(bf16)
        wm_ref[at, HALF:CHANS] = side[:, :SIDE].astype(bf16)
        dt_own = (lane % (HEADS // 2) // (LOCAL_HEADS // 2) == j) & (lane < HEADS)
        wm_ref[at, CHANS:MAIN] = jnp.where(dt_own, dt_cols, 0.0).astype(bf16)
    for k in range(D // HALF):
        wo_ref[:, k * HALF : (k + 1) * HALF] = dn_ref[k * out_rows : (k + 1) * out_rows, :].astype(bf16)

    greeted(EVERY_NEIGHBOUR)
    mains = WeightGather(copies, win_ref, own_rows, True)
    mains.swap(wm_ref)
    hids = GroupGather(copies, hid_ref, h_ref)
    hids.start_t0()

    def column(row):
        return jnp.transpose(jnp.broadcast_to(row, (LANES, SPAN)))[:, 0:1]

    for c in range(spans):
        row = segs_ref[0:1, pl.ds(pl.multiple_of(p * rows_all + c * SPAN, LANES), SPAN)].astype(f32)
        segr_ref[c : c + 1, :] = row
        segc_ref[FRONT + c * SPAN : FRONT + (c + 1) * SPAN, :] = column(row)
    around = rows_all - SPAN
    row = segs_ref[0:1, pl.ds(pl.multiple_of(p * around, LANES), SPAN)].astype(f32)
    segc_ref[0:FRONT, :] = jnp.where(p == 1, column(row)[SPAN - FRONT :], -1.0)
    row = segs_ref[0:1, pl.ds(pl.multiple_of(rows_all + p * around, LANES), SPAN)].astype(f32)
    segc_ref[FRONT + rows_all :, :] = jnp.where(p == 0, column(row)[0:FRONT], -1.0)
    stat_ref[0] = jnp.zeros_like(stat_ref[0])
    stat_ref[0, 0:1, 0:tokens] = valid_ref[...].astype(f32)
    validc_ref[...] = column(stat_ref[0, 0:1, 0:SPAN])[0:tokens]
    cotv_ref[...] = (cotv_ref[...].astype(f32) * validc_ref[...]).astype(bf16)
    copies.keep(cotv_ref, cotv_out)

    for k in range(HALF // LANES):
        lanes = slice(k * LANES, (k + 1) * LANES)
        chans_ref[1:2, lanes] = small_ref[own_row(NORM_ROW, k), :]
        for j in range(CONV + 1):
            taps_ref[j : j + 1, lanes] = small_ref[own_row(TAP_ROW + TAP_ROWS * j, k), :]
    for k in range(SIDE // LANES):
        lanes = slice(HALF + k * LANES, HALF + (k + 1) * LANES)
        for j in range(CONV + 1):
            row = TAP_ROW + TAP_ROWS * j + D_INNER // LANES + k
            taps_ref[j : j + 1, lanes] = small_ref[row : row + 1, :]
    head_row = jnp.broadcast_to(small_ref[HEAD_ROW : HEAD_ROW + 1, :], (TILE, LANES))
    next_row = jnp.broadcast_to(small_ref[HEAD_ROW + 1 : HEAD_ROW + 2, :], (TILE, LANES))
    a_log = pltpu.roll(head_row, LANES - HEADS, 1)
    lane8 = lax.broadcasted_iota(jnp.int32, (TILE, LANES), 1)
    spill = LANES - 2 * HEADS
    skip = jnp.where(lane8 < spill, pltpu.roll(head_row, spill, 1), pltpu.roll(next_row, spill, 1))
    own = lane8 < HEADS
    heads_ref[0:1, :] = head_lanes(jnp.where(own, head_row, 0.0))[0:1]
    heads_ref[1:2, :] = -jnp.exp(head_lanes(jnp.where(own, a_log, 0.0))[0:1])
    skip = head_lanes(jnp.where(own, skip, 0.0))[0:1]
    for q in range(PAIRS):
        chans_ref[0:1, q * LANES : (q + 1) * LANES] = own_pair(skip, 2 * q)

    def mark(first, count):
        seg = segc_ref[pl.ds(first, FRONT + count), :]
        here = seg[FRONT:]
        last = seg[FRONT + count - 1 :]
        before = seg[FRONT - 1 : FRONT]
        cols = {k: seg[FRONT - RIM + k : FRONT - RIM + k + count] == here for k in range(RIM)}
        cols[6], cols[7] = here == last, here == before
        lane_m = lax.broadcasted_iota(jnp.int32, (count, TILE), 1)
        marks = jnp.zeros((count, TILE), f32)
        for k, col in cols.items():
            marks = jnp.where(lane_m == k, jnp.where(col, 1.0, 0.0), marks)
        marks_ref[pl.ds(first, count), :] = marks
        return jnp.broadcast_to(jnp.where(last == before, 1.0, 0.0), (1, LANES))

    for c in range(spans):
        carry_ref[c : c + 1, :] = mark(c * SPAN, SPAN)
    mark(rows_all, TILE)
    blocks = group_blocks()

    def norm(block):
        rows = block_rows(block, tokens)
        hid = h_ref[rows, :].astype(f32)
        scale = lax.rsqrt(jnp.sum(hid * hid, axis=1, keepdims=True) / D + norm_eps)
        for k in range(D // LANES):
            lanes = slice(k * LANES, (k + 1) * LANES)
            xn_ref[rows, lanes] = (h_ref[rows, lanes].astype(f32) * scale * small_ref[k : k + 1, :]).astype(bf16)

    mains.spread_swapped()
    copies.settle(hids.own)
    norm(blocks[0])
    gates = WeightGather(copies, wgate_ref, own_rows, True)
    gates.swap(wg_ref)
    hids.hand_on()
    norm(blocks[2])
    mains.hand_on()
    gates.spread_swapped()
    outs = WeightGather(copies, wout_ref, out_rows, False)
    outs.spread(wo_ref, ())
    outs_kept = copies.keep(wo_ref, outs.mine(()))
    hids.finish()
    cots = GroupGather(copies, cotv_ref, back_ref)
    cots.start_t0()
    norm(blocks[1])
    norm(blocks[3])
    mains.hand_on_last()
    mains.finish()
    copies.settle(mains.kept)

    def project(c, _):
        rows = span_rows(c)
        xn = xn_ref[rows, :]
        at = pl.ds(pl.multiple_of(FRONT + c * SPAN, FRONT), SPAN)
        for k in range(CHANS // 256):
            cols = slice(k * 256, (k + 1) * 256)
            convp_ref[at, cols] = dot(xn, win_ref[:, cols]).astype(bf16)
        dt_raw = dot(xn, win_ref[:, CHANS:MAIN]).astype(bf16).astype(f32)
        z = head_lanes(dt_raw) + heads_ref[0:1, :]
        z_ref[rows, :] = z
        small = jnp.exp(-jnp.abs(z))
        one_more = 1.0 + small
        is_one = one_more == 1.0
        log_more = jnp.where(is_one, small, jnp.log(one_more) * small / jnp.where(is_one, 1.0, one_more - 1.0))
        dt_ref[rows, :] = jnp.maximum(z, 0.0) + log_more
        return 0

    lax.fori_loop(0, spans, project, 0)
    rim = copies.send(convp_ref.at[pl.ds(rows_all, FRONT)], rim_ref, PART)
    gates.hand_on()
    s_ref[...] = jnp.zeros_like(s_ref)
    dgain_ref[...] = jnp.zeros_like(dgain_ref)

    def convolve(c, _):
        rows = span_rows(c)
        wide = pl.ds(pl.multiple_of(c * SPAN, SPAN), SPAN + FRONT)
        masks = [jnp.broadcast_to(marks_ref[rows, j : j + 1], (SPAN, LANES)) for j in range(RIM)]
        for k in range(CHANS // LANES):
            lanes = slice(k * LANES, (k + 1) * LANES)
            values = convp_ref[wide, lanes].astype(f32)
            total = taps_ref[CONV : CONV + 1, lanes] + taps_ref[RIM : RIM + 1, lanes] * values[FRONT:]
            for j in range(RIM):
                first = FRONT - RIM + j
                total = total + taps_ref[j : j + 1, lanes] * values[first : first + SPAN] * masks[j]
            sig = 1.0 / (1.0 + jnp.exp(-total))
            value = (total * sig).astype(bf16)
            dtot_ref[rows, lanes] = sig * (1.0 + total * (1.0 - sig))
            if k < HALF // LANES:
                x_ref[rows, lanes] = value
            elif k == HALF // LANES:
                b_ref[rows, :] = value
            else:
                c_ref[rows, :] = value
        return 0

    lax.fori_loop(1, spans, convolve, 0)
    rim.wait_recv()
    convp_ref[0:FRONT, :] = jnp.where(p == 1, rim_ref[...].astype(f32), 0.0).astype(bf16)
    lax.fori_loop(0, 1, convolve, 0)
    gates.hand_on_last()

    def local_states(c, _):
        rows = span_rows(c)
        dt, cum = span_decay(dt_ref, heads_ref, c, 1)
        cum_ref[rows, :] = cum
        last = cum[SPAN - 1 : SPAN, :]
        end_weight = jnp.exp(last - cum) * dt * marks_ref[rows, 6:7]
        decay = jnp.exp(last) * carry_ref[pl.ds(c, 1), :]
        b = b_ref[rows, :]
        st_ref[c] = s_ref[...]
        for q in range(PAIRS):
            lanes = slice(q * LANES, (q + 1) * LANES)
            dyg_ref[rows, lanes] = (x_ref[rows, lanes].astype(f32) * own_pair(end_weight, 2 * q)).astype(bf16)
            s_ref[:, lanes] = s_ref[:, lanes] * own_pair(decay, 2 * q)
        s_ref[...] += dot(b, dyg_ref[rows, :], ((0,), (0,)))
        return 0

    lax.fori_loop(0, spans, local_states, 0)
    pass_ref[...] = s_ref[...].astype(bf16)
    state = copies.send(pass_ref, got_ref, PART)
    cots.hand_on()
    outs.hand_on()

    def inside(c, _):
        rows = span_rows(c)
        cum = cum_ref[rows, :]
        back_log = jnp.transpose(cum - jnp.log(dt_ref[rows, :]))
        scores = dot(c_ref[rows, :], b_ref[rows, :], ((1,), (1,)))
        row = lax.broadcasted_iota(jnp.int32, (SPAN, SPAN), 0)
        col = lax.broadcasted_iota(jnp.int32, (SPAN, SPAN), 1)
        mask = (row >= col) & (segc_ref[pl.ds(pl.multiple_of(FRONT + c * SPAN, FRONT), SPAN), :] == segr_ref[pl.ds(c, 1), :])
        lane = lax.broadcasted_iota(jnp.int32, (SPAN, LANES), 1)
        for q in range(PAIRS):
            lanes = slice(q * LANES, (q + 1) * LANES)
            x = x_ref[rows, lanes]
            parts = []
            for h in (lane_of(2 * q), lane_of(2 * q + 1)):
                gap = cum[:, h : h + 1] - back_log[h : h + 1, :]
                weighted = scores * jnp.exp(jnp.where(mask, gap, -1e30))
                parts.append(dot(weighted.astype(bf16), x))
            y_ref[rows, lanes] = jnp.where(lane < HEADDIM, parts[0], parts[1])
        return 0

    lax.fori_loop(0, spans, inside, 0)
    state.wait_recv()
    s_ref[...] = got_ref[...].astype(f32) * p.astype(f32)

    def across_spans(c, _):
        rows = span_rows(c)
        cum = cum_ref[rows, :]
        decay = jnp.exp(cum[SPAN - 1 : SPAN, :]) * carry_ref[pl.ds(c, 1), :]
        gain = jnp.exp(cum) * marks_ref[rows, 7:8]
        cc = c_ref[rows, :]
        for q in range(PAIRS):
            lanes = slice(q * LANES, (q + 1) * LANES)
            entering = s_ref[:, lanes]
            full = st_ref[c, :, lanes] + entering
            st_ref[c, :, lanes] = full
            y_ref[rows, lanes] += dot(cc, full.astype(bf16)) * own_pair(gain, 2 * q)
            s_ref[:, lanes] = entering * own_pair(decay, 2 * q)
        return 0

    lax.fori_loop(0, spans, across_spans, 0)
    gates.finish()
    copies.settle(gates.kept)

    def put_stat(k, c, column):
        wide = jnp.transpose(jnp.broadcast_to(column, (SPAN, LANES)))
        stat_ref[k, :, span_rows(c)] = wide[0:TILE, :]

    def exchange(k):
        return [copies.send(stat_ref.at[k], stats_ref.at[k, i], flips) for i, flips in enumerate(HOPS[1:])]

    def get_stat(k, c):
        cols = span_rows(c)
        total = stat_ref[k, :, cols] + stats_ref[k, 0, :, cols] + stats_ref[k, 1, :, cols] + stats_ref[k, 2, :, cols]
        return jnp.transpose(jnp.broadcast_to(total[0:1, :], (LANES, SPAN)))[:, 0:1] / D_INNER

    def values(rows, lanes):
        y_b = (y_ref[rows, lanes] + chans_ref[0:1, lanes] * x_ref[rows, lanes].astype(f32)).astype(bf16).astype(f32)
        gate = gate_ref[rows, lanes]
        sig = 1.0 / (1.0 + jnp.exp(-gate))
        return y_b, gate, sig

    def gating(c, _):
        rows = span_rows(c)
        xn = xn_ref[rows, :]
        total = jnp.zeros((SPAN, 1), f32)
        for k in range(HALF // 256):
            lanes = slice(k * 256, (k + 1) * 256)
            gate_ref[rows, lanes] = dot(xn, wgate_ref[:, lanes])
            y_b, gate, sig = values(rows, lanes)
            gated = y_b * (gate * sig)
            gated_ref[rows, lanes] = gated
            total = total + jnp.sum(gated * gated, axis=1, keepdims=True)
        put_stat(0, c, total)
        return 0

    lax.fori_loop(0, spans, gating, 0)
    outs.hand_on_last()
    squares = exchange(0)
    cots.finish()
    copies.settle(cots.own)
    outs.finish()
    copies.settle(outs_kept)

    def pull_out(c, _):
        rows = span_rows(c)
        back = back_ref[rows, :]
        total = jnp.zeros((SPAN, 1), f32)
        for k in range(HALF // 256):
            lanes = slice(k * 256, (k + 1) * 256)
            d_normed = dot(back, wout_ref[lanes, :], ((1,), (1,)))
            dn_ref[rows, lanes] = d_normed
            total = total + jnp.sum(gated_ref[rows, lanes] * (d_normed * chans_ref[1:2, lanes]), axis=1, keepdims=True)
        put_stat(1, c, total)
        return 0

    lax.fori_loop(0, spans, pull_out, 0)
    for copy in squares:
        copy.wait_recv()
    dots = exchange(1)

    def push_out(c, _):
        rows = span_rows(c)
        scale = lax.rsqrt(get_stat(0, c) + norm_eps)
        for k in range(HALF // 256):
            lanes = slice(k * 256, (k + 1) * 256)
            scaled = gated_ref[rows, lanes] * scale
            normed_ref[rows, lanes] = (scaled * chans_ref[1:2, lanes]).astype(bf16)
            dgain_ref[0:1, lanes] += jnp.sum(scaled * dn_ref[rows, lanes], axis=0, keepdims=True)
        normed = normed_ref[rows, :]
        for k in range(D // 256):
            cols = slice(k * 256, (k + 1) * 256)
            mix_ref[rows, cols] = dot(normed, wout_ref[:, cols]).astype(bf16)
        return 0

    copies.drain()
    lax.fori_loop(0, spans, push_out, 0)
    mixes = GroupScatter(copies, mix_ref, mix_bufs)
    mixes.to_t0(3)
    mixes.to_t0(1)
    for q in range(2):
        normed = normed_ref[:, q * HALF // 2 : (q + 1) * HALF // 2]
        for k in range(D // 512):
            cols = slice(k * 512, (k + 1) * 512)
            wout_ref[q * HALF // 2 : (q + 1) * HALF // 2, cols] = dot(normed, back_ref[:, cols], ((0,), (0,))).astype(bf16)
    go_halves = [wout_ref.at[pl.ds(pl.multiple_of(q * (HALF // 2), HALF // 2), HALF // 2)] for q in (1 - p, p)]
    g_out = GradientSum(copies, go_halves, out_rows, go_bufs, False)
    g_out.cores(0)
    g_out.cores(1)
    for copy in dots:
        copy.wait_recv()

    def back_gate(c, _):
        rows = span_rows(c)
        scale = lax.rsqrt(get_stat(0, c) + norm_eps)
        pulled = get_stat(1, c) * (scale * scale * scale)
        for k in range(HALF // LANES):
            lanes = slice(k * LANES, (k + 1) * LANES)
            y_b, gate, sig = values(rows, lanes)
            d_gated = scale * (dn_ref[rows, lanes] * chans_ref[1:2, lanes]) - gated_ref[rows, lanes] * pulled
            dy_ref[rows, lanes] = (d_gated * (gate * sig)).astype(bf16)
            dgate_ref[rows, lanes] = (d_gated * y_b * (sig * (1.0 + gate * (1.0 - sig)))).astype(bf16)
        return 0

    lax.fori_loop(0, spans, back_gate, 0)
    g_out.to_sides(0)
    s_ref[...] = jnp.zeros_like(s_ref)
    hsum_ref[...] = jnp.zeros_like(hsum_ref)
    dskip_ref[...] = jnp.zeros_like(dskip_ref)
    dtaps_ref[...] = jnp.zeros_like(dtaps_ref)

    def local_states(step, _):
        c = spans - 1 - step
        rows = span_rows(c)
        cum = cum_ref[rows, :]
        decay = jnp.exp(cum[SPAN - 1 : SPAN, :]) * carry_ref[pl.ds(c, 1), :]
        gain = jnp.exp(cum) * marks_ref[rows, 7:8]
        cc = c_ref[rows, :]
        for q in range(PAIRS):
            lanes = slice(q * LANES, (q + 1) * LANES)
            dyg = (dy_ref[rows, lanes].astype(f32) * own_pair(gain, 2 * q)).astype(bf16)
            dyg_ref[rows, lanes] = dyg
            ds = s_ref[:, lanes]
            dn_ref[pl.ds(pl.multiple_of(c * STATE, STATE), STATE), lanes] = ds
            s_ref[:, lanes] = ds * own_pair(decay, 2 * q)
        s_ref[...] += dot(cc, dyg_ref[rows, :], ((0,), (0,)))
        return 0

    lax.fori_loop(0, spans, local_states, 0)
    passb_ref[...] = s_ref[...].astype(bf16)
    state = copies.send(passb_ref, gotb_ref, PART)

    width = D // 4
    gg_halves = [back_ref.at[:, pl.ds(k * HALF, HALF)] for k in range(2)]
    g_gate = GradientSum(copies, gg_halves, own_rows, gg_bufs, True)

    def gate_gradient(far):
        for half in range(2):
            first = pl.multiple_of(((1 - p if far else p) * 2 + half) * width, width)
            piece = dot(xn_ref[:, pl.ds(first, width)], dgate_ref[...], ((0,), (0,)))
            gg_halves[0 if far else 1][half * width : (half + 1) * width, :] = piece.astype(bf16)

    gate_gradient(True)
    g_gate.cores(0)
    gate_gradient(False)
    g_gate.cores(1)
    g_gate.to_sides(0)
    g_out.to_part()
    g_out.to_sides(1)
    g_gate.to_sides(1)

    def inside(c, _):
        rows = span_rows(c)
        cum = cum_ref[rows, :]
        fore_log = jnp.transpose(cum)
        back_log = cum - jnp.log(dt_ref[rows, :])
        b = b_ref[rows, :]
        cc = c_ref[rows, :]
        scores = dot(b, cc, ((1,), (1,)))
        early, late = slice(0, SPAN // 2), slice(SPAN // 2, SPAN)
        seg_col = segc_ref[pl.ds(pl.multiple_of(FRONT + c * SPAN, FRONT), SPAN), :]
        seg_row = segr_ref[pl.ds(c, 1), :]
        row = lax.broadcasted_iota(jnp.int32, (SPAN // 2, SPAN), 0)
        col = lax.broadcasted_iota(jnp.int32, (SPAN // 2, SPAN), 1)
        mask_early = (col >= row) & (seg_col[early] == seg_row)
        mask_late = (col >= row)[:, early] & (seg_col[late] == seg_row[:, late])
        lane = lax.broadcasted_iota(jnp.int32, (SPAN, LANES), 1)
        d_early = jnp.zeros((SPAN // 2, SPAN), f32)
        d_late = jnp.zeros((SPAN // 2, SPAN // 2), f32)
        dc = dot(dyg_ref[rows, :], st_ref[c].astype(bf16), ((1,), (1,)))
        for q in range(PAIRS):
            lanes = slice(q * LANES, (q + 1) * LANES)
            x = x_ref[rows, lanes]
            dy = dy_ref[rows, lanes]
            xf = x.astype(f32)
            parts = []
            for k in range(2):
                h = lane_of(2 * q + k)
                gap = fore_log[h : h + 1, :] - back_log[early, h : h + 1]
                decay_early = jnp.exp(jnp.where(mask_early, gap, -1e30))
                gap = fore_log[h : h + 1, late] - back_log[late, h : h + 1]
                decay_late = jnp.exp(jnp.where(mask_late, gap, -1e30))
                dx_early = dot((scores[early] * decay_early).astype(bf16), dy)
                dx_late = dot((scores[late, late] * decay_late).astype(bf16), dy[late])
                parts.append(jnp.concatenate([dx_early, dx_late], axis=0))
                own = (lane < HEADDIM) if k == 0 else (lane >= HEADDIM)
                x_own = jnp.where(own, xf, 0.0).astype(bf16)
                d_early = d_early + dot(x_own[early], dy, ((1,), (1,))) * decay_early
                d_late = d_late + dot(x_own[late], dy[late], ((1,), (1,))) * decay_late
            dxi_ref[rows, lanes] = jnp.where(lane < HEADDIM, parts[0], parts[1])
            dskip_ref[0:1, lanes] += jnp.sum(dy.astype(f32) * xf, axis=0, keepdims=True)
        d_early_b, d_late_b = d_early.astype(bf16), d_late.astype(bf16)
        dn_ref[side_at(c, 0)] = jnp.concatenate([dot(d_early_b, cc), dot(d_late_b, cc[late])], axis=0)
        later = dot(d_early_b[:, late], b[early], ((0,), (0,))) + dot(d_late_b, b[late], ((0,), (0,)))
        earlier = dot(d_early_b[:, early], b[early], ((0,), (0,)))
        dn_ref[side_at(c, 1)] = dc + jnp.concatenate([earlier, later], axis=0)
        return 0

    lax.fori_loop(0, spans, inside, 0)
    mixes.to_t1()
    state.wait_recv()
    s_ref[...] = gotb_ref[...].astype(f32) * (1 - p).astype(f32)

    def across_spans(step, _):
        c = spans - 1 - step
        rows = span_rows(c)
        dt = dt_ref[rows, :]
        cum = cum_ref[rows, :]
        last = cum[SPAN - 1 : SPAN, :]
        end_weight = jnp.exp(last - cum) * dt * marks_ref[rows, 6:7]
        decay = jnp.exp(last) * carry_ref[pl.ds(c, 1), :]
        b = b_ref[rows, :]
        db = dn_ref[side_at(c, 0)]
        edges, ds_all = [], []
        for q in range(PAIRS):
            lanes = slice(q * LANES, (q + 1) * LANES)
            xf = x_ref[rows, lanes].astype(f32)
            dyf = dy_ref[rows, lanes].astype(f32)
            ew = own_pair(end_weight, 2 * q)
            dec = own_pair(decay, 2 * q)
            entering = s_ref[:, lanes]
            ds = dn_ref[pl.ds(pl.multiple_of(c * STATE, STATE), STATE), lanes] + entering
            s_ref[:, lanes] = entering * dec
            ds_b = ds.astype(bf16)
            dyg_ref[rows, lanes] = (xf * ew).astype(bf16)
            ds_all.append(ds_b)
            dx_state = dot(b, ds_b) * ew
            dx = dxi_ref[rows, lanes] + dx_state
            edges.append(
                jnp.sum(ds * st_ref[c, :, lanes], axis=0, keepdims=True) * dec
                + jnp.sum(dx_state * xf, axis=0, keepdims=True)
            )
            prod_ref[0:SPAN, lanes] = dyf * y_ref[rows, lanes]
            prod_ref[SPAN : 2 * SPAN, lanes] = xf * dx
            d_x = (dx + dyf * chans_ref[0:1, lanes]).astype(bf16).astype(f32)
            dtot_ref[rows, lanes] = d_x * dtot_ref[rows, lanes]
        db = db + dot(dyg_ref[rows, :], jnp.concatenate(ds_all, axis=1), ((1,), (1,)))
        dtot_ref[rows, HALF : HALF + STATE] = db * dtot_ref[rows, HALF : HALF + STATE]
        dtot_ref[rows, HALF + STATE :] = dn_ref[side_at(c, 1)] * dtot_ref[rows, HALF + STATE :]
        sums = own_sums(prod_ref[0 : 2 * SPAN, :])
        out_sum, in_sum = sums[:SPAN], sums[SPAN:]
        edge_sum = own_sums(jnp.broadcast_to(jnp.concatenate(edges, axis=1), (TILE, HALF)))[0:1]
        at_last = lax.broadcasted_iota(jnp.int32, (SPAN, LANES), 0) == SPAN - 1
        d_cum = out_sum - in_sum + jnp.where(at_last, edge_sum, 0.0)
        row = lax.broadcasted_iota(jnp.int32, (SPAN, SPAN), 0)
        col = lax.broadcasted_iota(jnp.int32, (SPAN, SPAN), 1)
        d_log = dot((col >= row).astype(f32), d_cum, precision=exact_prec)
        z = z_ref[rows, :]
        small = jnp.exp(-jnp.abs(z))
        sig = jnp.where(z >= 0.0, 1.0, small) / (1.0 + small)
        ratio = jnp.where(dt > 1e-30, sig / jnp.maximum(dt, 1e-30), 1.0)
        d_dt = d_log * heads_ref[1:2, :] * sig + in_sum * ratio
        hsum_ref[0:1, :] += jnp.sum(d_log * dt, axis=0, keepdims=True)
        hsum_ref[1:2, :] += jnp.sum(d_dt, axis=0, keepdims=True)
        dmain_ref[rows, CHANS:MAIN] = head_lanes(d_dt, back=True).astype(bf16)
        return 0

    lax.fori_loop(0, spans, across_spans, 0)
    rims_ref[...] = dtot_ref[0:TILE, :]
    rim = copies.send(rims_ref, rimr_ref, PART)
    g_gate.to_part()

    def convolve(c, _):
        rows = span_rows(c)
        fore = pl.ds(pl.multiple_of(c * SPAN, SPAN), SPAN + FRONT)
        hind = pl.ds(pl.multiple_of(c * SPAN, SPAN), SPAN + TILE)
        masks = [jnp.broadcast_to(marks_ref[hind, j : j + 1], (SPAN + TILE, LANES)) for j in range(RIM)]
        for k in range(CHANS // LANES):
            lanes = slice(k * LANES, (k + 1) * LANES)
            later = dtot_ref[hind, lanes]
            earlier = convp_ref[fore, lanes].astype(f32)
            own = later[0:SPAN]
            d_conv = taps_ref[RIM : RIM + 1, lanes] * own
            dtaps_ref[RIM : RIM + 1, lanes] += jnp.sum(own * earlier[FRONT:], axis=0, keepdims=True)
            dtaps_ref[CONV : CONV + 1, lanes] += jnp.sum(own, axis=0, keepdims=True)
            for j in range(RIM):
                lag = RIM - j
                seen = later * masks[j]
                d_conv = d_conv + taps_ref[j : j + 1, lanes] * seen[lag : lag + SPAN]
                dtaps_ref[j : j + 1, lanes] += jnp.sum(
                    seen[0:SPAN] * earlier[FRONT - lag : FRONT - lag + SPAN], axis=0, keepdims=True
                )
            dmain_ref[rows, lanes] = d_conv.astype(bf16)
        return 0

    lax.fori_loop(0, spans - 1, convolve, 0)
    rim.wait_recv()
    dtot_ref[pl.ds(spans * SPAN, TILE), :] = jnp.where(p == 0, rimr_ref[...], 0.0)
    lax.fori_loop(spans - 1, spans, convolve, 0)

    mixes.left()
    dpre_ref[...] = jnp.zeros_like(dpre_ref)

    def token_grad(block, keep):
        rows = block_rows(block, tokens)
        d_main = dmain_ref[rows, :]
        d_gate = dgate_ref[rows, :]
        hid = h_ref[rows, :].astype(f32)
        scale = lax.rsqrt(jnp.sum(hid * hid, axis=1, keepdims=True) / D + norm_eps)
        for k in range(D // 256):
            cols = slice(k * 256, (k + 1) * 256)
            part = dot(d_main, win_ref[cols, :], ((1,), (1,))) + dot(d_gate, wgate_ref[cols, :], ((1,), (1,)))
            dpre_ref[0:1, cols] += jnp.sum(h_ref[rows, cols].astype(f32) * scale * part, axis=0, keepdims=True)
            if keep:
                first = k * 256 // HALF * tokens
                y_ref[first : first + tokens, k * 256 % HALF : k * 256 % HALF + 256] = part
            else:
                mix_ref[rows, cols] = part.astype(bf16)

    def store_gate(i, value):
        kept = pl.ds(2 * SPAN + i * own_rows, own_rows)
        gate_ref[kept, :] = value
        copies.keep(gate_ref.at[kept], ggate_out.at[blocks[i][0], blocks[i][1]])

    def store_main(i, value):
        for first, count in ((0, HALF), (HALF, MAIN - HALF)):
            kept = pl.ds((first // HALF * TP + i) * own_rows, own_rows)
            gated_ref[kept, 0:count] = value[:, first : first + count]
            copies.keep(
                gated_ref.at[kept, pl.ds(0, count)], gmain_out.at[blocks[i][0], blocks[i][1], :, pl.ds(first, count)]
            )

    total = g_out.total(0)
    for k in range(D // HALF):
        kept = pl.ds(2 * TP * own_rows + k * out_rows, out_rows)
        gated_ref[kept, :] = total[:, k * HALF : (k + 1) * HALF]
        copies.keep(gated_ref.at[kept], gout_out.at[:, pl.ds(k * HALF, HALF)])
    g_out.left()
    gm_halves = [wout_ref.at[:, pl.ds(0, MAIN)], gm_ref]

    def grad_half(far):
        part = 1 - p if far else p
        out = gm_halves[0 if far else 1]

        def piece(i, _):
            xn = xn_ref[:, pl.ds(pl.multiple_of((part * 2 + i) * width, width), width)]
            rows = pl.ds(pl.multiple_of(i * width, width), width)
            for k in range(MAIN // 384):
                cols = slice(k * 384, (k + 1) * 384)
                out[rows, cols] = dot(xn, dmain_ref[:, cols], ((0,), (0,))).astype(bf16)
            return 0

        lax.fori_loop(0, 2, piece, 0)

    grad_half(True)
    g_main = GradientSum(copies, gm_halves, own_rows, gm_bufs, True)
    g_main.cores(0)
    dxs = GroupScatter(copies, mix_ref, dx_bufs)
    token_grad(blocks[3], False)
    dxs.to_t0(3)
    g_main.to_sides(0)
    token_grad(blocks[1], False)
    dxs.to_t0(1)
    grad_half(False)
    g_main.cores(1)
    g_main.to_part((1,))
    g_gate.to_group(store_gate)
    g_main.to_part((2,))
    g_main.to_sides(1)
    g_main.to_part((3,))

    mixer = mix_ref[mixes.block(0), :].astype(f32) + mixes.finish()
    copies.left([mixes.last_copy])
    for k in range(D // HALF):
        kept = pl.ds(spans * STATE + k * tokens, tokens)
        dn_ref[kept, :] = mixer[:, k * HALF : (k + 1) * HALF]
        copies.keep(dn_ref.at[kept], mixer_out.at[:, pl.ds(k * HALF, HALF)])
    hid = h_ref[mixes.block(0), :].astype(f32)
    valid = validc_ref[...]
    counts = [jnp.sum(valid * jnp.sum(v * v, axis=1, keepdims=True), axis=0, keepdims=True) for v in (hid, mixer)]
    counts.append(jnp.sum(valid, axis=0, keepdims=True))
    scalars = jnp.zeros((1, LANES), f32)
    for k in range(3):
        scalars = jnp.where(lane == k, counts[k], scalars)
    box = box_ref.at[0]
    box[...] = jnp.zeros_like(box)
    box[OWN_SUMS : OWN_SUMS + 1, :] = scalars

    token_grad(blocks[2], False)
    g_main.to_part((0,))
    dxs.to_t1()
    token_grad(blocks[0], True)

    for k in range(D // LANES):
        box[k : k + 1, :] = dpre_ref[0:1, k * LANES : (k + 1) * LANES]
    for k in range(HALF // LANES):
        lanes = slice(k * LANES, (k + 1) * LANES)
        box[OWN_NORM + k : OWN_NORM + k + 1, :] = dgain_ref[0:1, lanes]
        for j in range(CONV + 1):
            row = OWN_TAP + j * (HALF // LANES) + k
            box[row : row + 1, :] = dtaps_ref[j : j + 1, lanes]
    for k in range(SIDE // LANES):
        lanes = slice(HALF + k * LANES, HALF + (k + 1) * LANES)
        for j in range(CONV + 1):
            row = OWN_SIDE + j * (SIDE // LANES) + k
            box[row : row + 1, :] = dtaps_ref[j : j + 1, lanes]
    hsum_ref[0:1, :] = hsum_ref[0:1, :] * heads_ref[1:2, :]
    hsum_ref[2:3, :] = own_sums(dskip_ref[...])[0:1, :]
    lane8 = lax.broadcasted_iota(jnp.int32, (TILE, LANES), 1)
    box[OWN_HEAD : OWN_HEAD + 3, :] = jnp.where(lane8 < HEADS, head_lanes(hsum_ref[...], back=True), 0.0)[0:3]

    def small_step(k, hops):
        return [copies.send(box_ref.at[k], boxes_ref.at[k, i], flips) for i, flips in enumerate(hops)]

    def small_add(k, sent):
        total = box_ref[k]
        for i, copy in enumerate(sent):
            copy.wait_recv()
            total = total + boxes_ref[k, i]
        box_ref[k + 1] = total

    small = small_step(0, (CORE, SIDEWAYS, SIDE_CORE))
    g_gate.finish(store_gate)
    small_add(0, small)
    small = small_step(1, (PART,))
    small_add(1, small)
    small = small_step(2, (T0, T1, DIAG))
    g_main.to_group(store_main)
    dx = dxs.finish()
    for k in range(D // HALF):
        kept = pl.ds(k * tokens, tokens)
        y_ref[kept, :] += dx[:, k * HALF : (k + 1) * HALF]
        copies.keep(y_ref.at[kept], dx_out.at[:, pl.ds(k * HALF, HALF)])
    small_add(2, small)
    total_ref[...] = jnp.zeros_like(total_ref)
    total_ref[0:NORM_ROW, :] = box_ref[3, 0:NORM_ROW]
    third = QUARTER // LANES
    runs = [(OWN_NORM, NORM_ROW)]
    runs += [(OWN_TAP + j * 2 * third, TAP_ROW + j * TAP_ROWS) for j in range(CONV + 1)]
    for i, block in enumerate(blocks):
        source = box_ref.at[2] if i == 0 else boxes_ref.at[2, i - 1]
        place_at = (block[0] * 2 + block[1]) * third
        for own, first in runs:
            for k in range(2 * third):
                row = first + k // third * (D_INNER // 2 // LANES) + place_at + k % third
                total_ref[pl.ds(row, 1), :] = source[own + k : own + k + 1, :]
    for j in range(CONV + 1):
        row, own = TAP_ROW + TAP_ROWS * j + D_INNER // LANES, OWN_SIDE + j * (SIDE // LANES)
        total_ref[row : row + SIDE // LANES, :] = box_ref[3, own : own + SIDE // LANES]
    d_rate, d_shift, d_skip = (
        jnp.broadcast_to(box_ref[3, OWN_HEAD + k : OWN_HEAD + k + 1], (TILE, LANES)) for k in range(3)
    )
    spill = LANES - 2 * HEADS
    joined = d_shift + pltpu.roll(d_rate, HEADS, 1) + jnp.where(lane8 >= 2 * HEADS, pltpu.roll(d_skip, 2 * HEADS, 1), 0.0)
    total_ref[HEAD_ROW : HEAD_ROW + 1, :] = joined[0:1]
    spilled = jnp.where(lane8 < HEADS - spill, pltpu.roll(d_skip, LANES - spill, 1), 0.0)
    total_ref[HEAD_ROW + 1 : HEAD_ROW + 2, :] = spilled[0:1]
    total_ref[SMALL_ROWS : SMALL_ROWS + 1, :] = box_ref[3, OWN_SUMS : OWN_SUMS + 1]
    g_main.finish(store_main)
    copies.drain()


def update_kernel(
    hid_ref, mixer_ref, dx_ref, back_ref, gmain_ref, ggate_ref, gout_ref, total_ref,
    inw_ref, inm_ref, inv_ref, outw_ref, outm_ref, outv_ref, small_ref,
    output_ref, gh_ref, inm_out, inv_out, inw_out, outm_out, outv_out, outw_out, rms_ref,
):
    hid = hid_ref[...].astype(f32)
    output_ref[...] = (hid + mixer_ref[...]).astype(bf16)
    scale = lax.rsqrt(jnp.sum(hid * hid, axis=1, keepdims=True) / D + norm_eps)
    pulled = 0.0
    for k in range(NORM_ROW):
        lanes = slice(k * LANES, (k + 1) * LANES)
        d_pre = dx_ref[:, lanes] * small_ref[k : k + 1, :]
        gh_ref[:, lanes] = back_ref[:, lanes].astype(f32) + scale * d_pre
        pulled = pulled + jnp.sum(hid[:, lanes] * d_pre, axis=1, keepdims=True)
    gh_ref[...] -= hid * (pulled / D * (scale * scale * scale))

    def update(refs, outs, cols, grad, rate=0.02, decay=0.1):
        weight, moment, second = (ref[:, cols] for ref in refs)
        for out, value in zip(outs, adamw(weight, moment, second, grad, rate, decay)):
            out[:, cols] = value

    every = slice(None)
    update((outw_ref, outm_ref, outv_ref), (outm_out, outv_out, outw_out), every, gout_ref[...])
    in_refs, in_outs = (inw_ref, inm_ref, inv_ref), (inm_out, inv_out, inw_out)
    for j in range(TP):
        for k, chans in enumerate(own_chans(j)):
            part = slice(k * QUARTER, (k + 1) * QUARTER)
            update(in_refs, in_outs, chans, ggate_ref[j // 2, j % 2, :, part])
            scan = slice(D_INNER + chans.start, D_INNER + chans.stop)
            update(in_refs, in_outs, scan, gmain_ref[j // 2, j % 2, :, part])
    rest_grad = gmain_ref[0, 0, :, HALF:] + gmain_ref[0, 1, :, HALF:] + gmain_ref[1, 0, :, HALF:] + gmain_ref[1, 1, :, HALF:]
    first = 2 * D_INNER
    update(in_refs, in_outs, slice(first, first + SIDE), rest_grad[:, :SIDE])
    update(in_refs, in_outs, slice(first + SIDE, first + SIDE + HEADS), rest_grad[:, SIDE : SIDE + HEADS])

    @pl.when(pl.program_id(0) == 0)
    def _():
        totals = total_ref[SMALL_ROWS:, :]
        rms_ref[...] = jnp.sqrt(totals / (totals[0:1, 2:3] * D))


def linked(kernel, name, collective_id, in_specs, outs, scratch):
    return pl.pallas_call(
        kernel,
        name=name,
        grid=(1,),
        in_specs=in_specs,
        out_shape=tuple(o for o, _ in outs),
        out_specs=tuple(s for _, s in outs),
        scratch_shapes=scratch,
        compiler_params=pltpu.CompilerParams(
            collective_id=collective_id, has_side_effects=True, vmem_limit_bytes=VMEM_LIMIT
        ),
    )


def shards_linked(
    hidden, cotangent, segments, valid, in_w, in_m, in_v, out_w, out_m, out_v, small_w, small_m, small_v,
):
    own_rows, out_rows = in_w.shape[0], out_w.shape[0]
    tok_rows = hidden.shape[1]
    rows = tok_rows * TP
    spans = rows // SPAN
    small_size = small_w.shape[0]

    def small_box(array):
        return jnp.pad(array, (0, SMALL_ROWS * LANES - small_size)).reshape(SMALL_ROWS, LANES)

    small_rows = small_box(small_w)

    wide = (rows, D)
    half = (rows, HALF)
    lanes = (rows, LANES)
    side = (rows, STATE)
    state = (STATE, HALF)
    main_outs = (
        (shape((tok_rows, D), bf16), HBM),
        (shape((tok_rows, D), f32), HBM),
        (shape((2, 2, own_rows, HALF), f32), HBM),
        (shape((2, 2, own_rows, MAIN), f32), HBM),
        (shape((tok_rows, D), f32), HBM),
        (shape((out_rows, D), f32), HBM),
        (shape((BOX_ROWS, LANES), f32), VMEM),
    )
    main_scratch = (
        (wide, bf16),
        (wide, bf16),
        ((D, MAIN), bf16),
        ((rows + FRONT, CHANS), bf16),
        (half, bf16),
        (side, bf16),
        (side, bf16),
        ((rows + FRONT, CHANS), f32),
        (lanes, f32),
        (lanes, f32),
        (lanes, f32),
        (half, f32),
        ((spans, *state), f32),
        ((D, HALF), bf16),
        ((HALF, D), bf16),
        (wide, bf16),
        (half, bf16),
        (wide, bf16),
        (half, bf16),
        (half, bf16),
        ((rows, MAIN), bf16),
        ((TILE, HALF), f32),
        ((TILE, CHANS), f32),
        ((TILE, LANES), f32),
        ((TILE, HALF), f32),
        ((rows + TILE, TILE), f32),
        ((spans, LANES), f32),
        (state, f32),
        (state, bf16),
        (state, bf16),
        ((FRONT, CHANS), bf16),
        (half, f32),
        (half, f32),
        (half, f32),
        ((2, TILE, rows), f32),
        ((2, 3, TILE, rows), f32),
        (half, bf16),
        (state, bf16),
        (state, bf16),
        ((TILE, CHANS), f32),
        ((TILE, CHANS), f32),
        ((TILE, LANES), f32),
        ((TILE, HALF), f32),
        ((TILE, CHANS), f32),
        ((TILE, D), f32),
        ((4, OWN_ROWS, LANES), f32),
        ((3, 3, OWN_ROWS, LANES), f32),
        ((D // 2, MAIN), bf16),
        ((rows + 2 * FRONT, 1), f32),
        ((TILE, SPAN), f32),
        ((tok_rows, 1), f32),
    )
    side_cols = pl.BlockSpec((own_rows, MAIN - HALF), lambda i: (0, 2 * D_INNER // (MAIN - HALF)))
    back_own, mixer, g_gate, g_main, d_x_normed, g_out, totals = linked(
        functools.partial(main_kernel, spans), "main", 1, [*[HBM] * 4, side_cols, *[VMEM] * 3], main_outs,
        [
            *[pltpu.VMEM(dims, dtype) for dims, dtype in main_scratch],
            *sum_buffers(out_rows, D, False),
            *sum_buffers(own_rows, HALF, True),
            *sum_buffers(own_rows, MAIN, True),
            *scatter_buffers(tok_rows),
            *scatter_buffers(tok_rows),
            *sems(200, 48),
        ],
    )(hidden[0], in_w, out_w, cotangent[0], in_w, valid, small_rows, segments)

    steps = own_rows // (2 * TILE)

    def cut(dims, axis=0):
        block = tuple(size // steps if k == axis else size for k, size in enumerate(dims))
        return pl.BlockSpec(block, lambda i: tuple(i if k == axis else 0 for k in range(len(dims))))

    def fixed(dims):
        return pl.BlockSpec(dims, lambda i: (0, 0))

    tokens, matrix_in, matrix_out, small_dims = (tok_rows, D), in_w.shape, out_w.shape, (SMALL_ROWS, LANES)
    out_dims = [tokens] * 2 + [matrix_in] * 3 + [matrix_out] * 3
    (
        output, grad_hidden, in_m_new, in_v_new, in_w_new, out_m_new, out_v_new, out_w_new, rms,
    ) = pl.pallas_call(
        update_kernel,
        name="update",
        grid=(steps,),
        in_specs=[
            *[cut(tokens)] * 4,
            cut(g_main.shape, 2),
            cut(g_gate.shape, 2),
            cut(matrix_out),
            fixed((BOX_ROWS, LANES)),
            *[cut(matrix_in)] * 3,
            *[cut(matrix_out)] * 3,
            fixed(small_dims),
        ],
        out_shape=[
            *[shape(dims, bf16 if k == 0 else f32) for k, dims in enumerate(out_dims)],
            shape((TILE, LANES), f32),
        ],
        out_specs=[*[cut(dims) for dims in out_dims], fixed((TILE, LANES))],
        compiler_params=pltpu.CompilerParams(vmem_limit_bytes=VMEM_LIMIT),
    )(
        hidden[0], mixer, d_x_normed, back_own, g_main, g_gate, g_out, totals,
        in_w, in_m, in_v, out_w, out_m, out_v, small_rows,
    )
    small_grad = totals[:SMALL_ROWS].reshape(-1)[:small_size]
    small_m_new, small_v_new, small_w_new = adamw(small_w, small_m, small_v, small_grad, 0.2, 0.0)
    return (
        output[None], grad_hidden[None], in_m_new, in_v_new, in_w_new, out_m_new, out_v_new, out_w_new,
        small_m_new, small_v_new, small_w_new, rms[0, :2],
    )


def solution(mesh):
    seq, wt = mesh.shape["seq"], mesh.shape["wt"]
    split = Mesh(mesh.devices.reshape(seq // TP, 2, 2, wt // 2, 2), EVERYONE)
    streams = ("w1", "w0")
    tokens = ("part", "t1", "t0")
    matrix = P(EVERYONE, None)
    stream = P(streams, tokens, None)
    size = mesh.devices.size
    fits = seq == 2 * TP and wt == 4 and D // size % 16 == 0 and D_INNER // size % 16 == 0
    return jax.shard_map(
        shards_linked if fits else shards_general,
        mesh=split,
        in_specs=(
            stream, stream, P(streams, None), P(streams, tokens), matrix, matrix, matrix, matrix, matrix, matrix, P(), P(), P(),
        ),
        out_specs=(stream, stream, matrix, matrix, matrix, matrix, matrix, matrix, P(), P(), P(), P()),
        check_vma=False,
    )
```

```python
import functools

import jax
import jax.numpy as jnp
from jax import lax
from jax.experimental import pallas as pl
from jax.experimental.pallas import tpu as pltpu
from jax.sharding import Mesh
from jax.sharding import PartitionSpec as P

D = 1536
D_INNER = 3072
HEADS = 48
HEADDIM = 64
STATE = 128
CONV = 4
SPAN = 256
STEP = 4
CONVCH = 3328
TP = 4
RIM = CONV - 1
LANES = 128
HALF = D_INNER // TP
LOCAL_HEADS = HEADS // TP
PAIRS = LOCAL_HEADS // 2
SIDE = 2 * STATE
COL_SIDE = HALF
COL_DT = HALF + SIDE
COL_GATE = COL_DT + LANES
COLS = COL_GATE + HALF

bf16 = jnp.bfloat16
f32 = jnp.float32
exact_prec = lax.Precision.HIGHEST
norm_eps = 1e-05
adam_eps = 1e-08


def dot(a, b, dims=((1,), (0,)), precision=None):
    return lax.dot_general(a, b, (dims, ((), ())), precision=precision, preferred_element_type=f32)


def unpack_small(small):
    first = D
    second = first + D_INNER
    third = second + CONV * CONVCH
    fourth = third + CONVCH
    fifth = fourth + HEADS
    sixth = fifth + HEADS
    return (
        small[:first],
        small[first:second],
        small[second:third].reshape(CONV, CONVCH),
        small[third:fourth],
        small[fourth:fifth],
        small[fifth:sixth],
        small[sixth:],
    )


def adamw(weight, moment, second, grad, rate, decay):
    moment_new = 0.5 * moment + 0.5 * grad
    second_new = 0.5 * second + 0.5 * grad * grad
    first_hat = moment_new / (1.0 - 0.5**STEP)
    second_hat = second_new / (1.0 - 0.5**STEP)
    weight_new = weight - rate * (first_hat / (jnp.sqrt(second_hat) + adam_eps) + decay * weight)
    return (moment_new, second_new, weight_new)


def pair_cols(cols, h):
    lane = lax.broadcasted_iota(jnp.int32, (cols.shape[0], LANES), 1)
    return jnp.where(lane < HEADDIM, cols[:, h : h + 1], cols[:, h + 1 : h + 2])


def span_rows(c):
    return pl.ds(pl.multiple_of(c * SPAN, SPAN), SPAN)


def span_decay(dt_ref, rate_ref, c, at=0):
    dt = dt_ref[span_rows(c), :]
    row = lax.broadcasted_iota(jnp.int32, (SPAN, SPAN), 0)
    col = lax.broadcasted_iota(jnp.int32, (SPAN, SPAN), 1)
    lower = (row >= col).astype(f32)
    return dt, dot(lower, dt * rate_ref[at : at + 1, :], precision=exact_prec)


def state_kernel(spans, x_ref, b_ref, dt_ref, rate_ref, keep_ref, carry_ref, s_ref, dec_ref):
    s_ref[...] = jnp.zeros_like(s_ref)
    dec_ref[...] = jnp.ones_like(dec_ref)

    def body(c, _):
        rows = span_rows(c)
        dt, cum = span_decay(dt_ref, rate_ref, c)
        last = cum[SPAN - 1 : SPAN, :]
        end_weight = jnp.exp(last - cum) * dt * keep_ref[rows, :]
        decay = jnp.exp(last) * carry_ref[pl.ds(c, 1), :]
        dec_ref[...] = dec_ref[...] * decay
        b = b_ref[rows, :]
        for p in range(PAIRS):
            lanes = slice(p * LANES, (p + 1) * LANES)
            xw = (x_ref[rows, lanes].astype(f32) * pair_cols(end_weight, 2 * p)).astype(bf16)
            fresh = dot(b, xw, ((0,), (0,)))
            s_ref[:, lanes] = s_ref[:, lanes] * pair_cols(decay, 2 * p) + fresh
        return 0

    lax.fori_loop(0, spans, body, 0)


def scan_kernel(
    spans, x_ref, b_ref, c_ref, dt_ref, rate_ref, segc_ref, segr_ref, keep_ref, inflow_ref, carry_ref, s_in_ref,
    y_ref, st_ref, s_ref,
):
    s_ref[...] = s_in_ref[...]

    def body(c, _):
        rows = span_rows(c)
        dt, cum = span_decay(dt_ref, rate_ref, c)
        last = cum[SPAN - 1 : SPAN, :]
        end_weight = jnp.exp(last - cum) * dt * keep_ref[rows, :]
        decay = jnp.exp(last) * carry_ref[pl.ds(c, 1), :]
        gain = jnp.exp(cum) * inflow_ref[rows, :]
        back_log = jnp.transpose(cum - jnp.log(dt))
        b = b_ref[rows, :]
        cc = c_ref[rows, :]
        scores = dot(cc, b, ((1,), (1,)))
        row = lax.broadcasted_iota(jnp.int32, (SPAN, SPAN), 0)
        col = lax.broadcasted_iota(jnp.int32, (SPAN, SPAN), 1)
        mask = (row >= col) & (segc_ref[rows, :] == segr_ref[pl.ds(c, 1), :])
        lane = lax.broadcasted_iota(jnp.int32, (SPAN, LANES), 1)
        st_ref[c] = s_ref[...]
        for p in range(PAIRS):
            lanes = slice(p * LANES, (p + 1) * LANES)
            x = x_ref[rows, lanes]
            parts = []
            for h in (2 * p, 2 * p + 1):
                gap = cum[:, h : h + 1] - back_log[h : h + 1, :]
                weights = scores * jnp.exp(jnp.where(mask, gap, -1e30))
                parts.append(dot(weights.astype(bf16), x))
            y = jnp.where(lane < HEADDIM, parts[0], parts[1])
            state = s_ref[:, lanes]
            y = y + dot(cc, state.astype(bf16)) * pair_cols(gain, 2 * p)
            y_ref[rows, lanes] = y
            xw = (x.astype(f32) * pair_cols(end_weight, 2 * p)).astype(bf16)
            s_ref[:, lanes] = state * pair_cols(decay, 2 * p) + dot(b, xw, ((0,), (0,)))
        return 0

    lax.fori_loop(0, spans, body, 0)


def state_back_kernel(spans, dy_ref, c_ref, dt_ref, rate_ref, inflow_ref, carry_ref, s_ref):
    s_ref[...] = jnp.zeros_like(s_ref)

    def body(step, _):
        c = spans - 1 - step
        rows = span_rows(c)
        dt, cum = span_decay(dt_ref, rate_ref, c)
        decay = jnp.exp(cum[SPAN - 1 : SPAN, :]) * carry_ref[pl.ds(c, 1), :]
        gain = jnp.exp(cum) * inflow_ref[rows, :]
        cc = c_ref[rows, :]
        for p in range(PAIRS):
            lanes = slice(p * LANES, (p + 1) * LANES)
            dyg = (dy_ref[rows, lanes].astype(f32) * pair_cols(gain, 2 * p)).astype(bf16)
            s_ref[:, lanes] = s_ref[:, lanes] * pair_cols(decay, 2 * p) + dot(cc, dyg, ((0,), (0,)))
        return 0

    lax.fori_loop(0, spans, body, 0)


def head_sums(values):
    width = values.shape[1]
    chan = lax.broadcasted_iota(jnp.int32, (width, LANES), 0)
    head = lax.broadcasted_iota(jnp.int32, (width, LANES), 1)
    pick = (chan // HEADDIM == head).astype(bf16)
    high = values.astype(bf16)
    low = (values - high.astype(f32)).astype(bf16)
    return dot(high, pick) + dot(low, pick)


def scan_back_kernel(
    spans, x_ref, b_ref, c_ref, dt_ref, ratio_ref, sig_ref, rate_ref, segc_ref, segr_ref, keep_ref, inflow_ref, carry_ref, skip_ref,
    y_ref, st_ref, dy_ref, ds_out_ref,
    dx_ref, db_ref, dc_ref, ddt_ref, drate_ref, dskip_ref,
    ds_ref, prod_ref,
):
    ds_ref[...] = ds_out_ref[...]
    drate_ref[...] = jnp.zeros_like(drate_ref)
    dskip_ref[...] = jnp.zeros_like(dskip_ref)

    def body(step, _):
        c = spans - 1 - step
        rows = span_rows(c)
        dt, cum = span_decay(dt_ref, rate_ref, c)
        last = cum[SPAN - 1 : SPAN, :]
        end_weight = jnp.exp(last - cum) * dt * keep_ref[rows, :]
        decay = jnp.exp(last) * carry_ref[pl.ds(c, 1), :]
        gain = jnp.exp(cum) * inflow_ref[rows, :]
        fore_log = jnp.transpose(cum)
        back_log = cum - jnp.log(dt)
        b = b_ref[rows, :]
        cc = c_ref[rows, :]
        scores = dot(b, cc, ((1,), (1,)))
        row = lax.broadcasted_iota(jnp.int32, (SPAN, SPAN), 0)
        col = lax.broadcasted_iota(jnp.int32, (SPAN, SPAN), 1)
        mask = (col >= row) & (segc_ref[rows, :] == segr_ref[pl.ds(c, 1), :])
        lane = lax.broadcasted_iota(jnp.int32, (SPAN, LANES), 1)
        d_scores = jnp.zeros((SPAN, SPAN), f32)
        db = jnp.zeros((SPAN, STATE), f32)
        dc = jnp.zeros((SPAN, STATE), f32)
        state_row = []
        dx_state_row = []
        for p in range(PAIRS):
            lanes = slice(p * LANES, (p + 1) * LANES)
            x = x_ref[rows, lanes]
            dy = dy_ref[rows, lanes]
            xf = x.astype(f32)
            dyf = dy.astype(f32)
            parts = []
            for k in range(2):
                h = 2 * p + k
                gap = fore_log[h : h + 1, :] - back_log[:, h : h + 1]
                decay_mat = jnp.exp(jnp.where(mask, gap, -1e30))
                weights = (scores * decay_mat).astype(bf16)
                parts.append(dot(weights, dy))
                own = (lane < HEADDIM) if k == 0 else (lane >= HEADDIM)
                d_weights = dot(jnp.where(own, xf, 0.0).astype(bf16), dy, ((1,), (1,)))
                d_scores = d_scores + d_weights * decay_mat
            dx = jnp.where(lane < HEADDIM, parts[0], parts[1])
            dyg = (dyf * pair_cols(gain, 2 * p)).astype(bf16)
            ew = pair_cols(end_weight, 2 * p)
            xw = (xf * ew).astype(bf16)
            state = st_ref[c, :, lanes]
            ds = ds_ref[:, lanes]
            state_b = state.astype(bf16)
            ds_b = ds.astype(bf16)
            dc = dc + dot(dyg, state_b, ((1,), (1,)))
            db = db + dot(xw, ds_b, ((1,), (1,)))
            dx_state = dot(b, ds_b) * ew
            dx = dx + dx_state
            dec = pair_cols(decay, 2 * p)
            state_row.append(jnp.sum(ds * state, axis=0, keepdims=True) * dec)
            dx_state_row.append(jnp.sum(dx_state * xf, axis=0, keepdims=True))
            ds_ref[:, lanes] = ds * dec + dot(cc, dyg, ((0,), (0,)))
            prod_ref[0:SPAN, lanes] = dyf * y_ref[rows, lanes]
            prod_ref[SPAN : 2 * SPAN, lanes] = xf * dx
            dskip_ref[0:1, lanes] += jnp.sum(dyf * xf, axis=0, keepdims=True)
            dx_ref[rows, lanes] = (dx + dyf * skip_ref[0:1, lanes]).astype(bf16)
        d_scores_b = d_scores.astype(bf16)
        db_ref[rows, :] = db + dot(d_scores_b, cc)
        dc_ref[rows, :] = dc + dot(d_scores_b, b, ((0,), (0,)))
        sums = head_sums(prod_ref[...])
        out_sum, in_sum = sums[:SPAN], sums[SPAN:]
        edge = jnp.concatenate(state_row, axis=1) + jnp.concatenate(dx_state_row, axis=1)
        edge_sum = head_sums(jnp.broadcast_to(edge, (8, HALF)))[0:1]
        at_last = lax.broadcasted_iota(jnp.int32, (SPAN, LANES), 0) == SPAN - 1
        d_cum = out_sum - in_sum + jnp.where(at_last, edge_sum, 0.0)
        upper = (col >= row).astype(f32)
        d_log = dot(upper, d_cum, precision=exact_prec)
        drate_ref[0:1, :] += jnp.sum(d_log * dt, axis=0, keepdims=True)
        ddt_ref[rows, :] = d_log * rate_ref[0:1, :] * sig_ref[rows, :] + in_sum * ratio_ref[rows, :]
        return 0

    lax.fori_loop(0, spans, body, 0)


GROUP = ("t1", "t0")
COPIES = ("part", "w1", "w0")
EVERYONE = ("part", "t1", "t0", "w1", "w0")


VMEM_LIMIT = 63 * 1024 * 1024


def in_vmem(kernel, out_shape, name, scratch=()):
    return pl.pallas_call(
        kernel,
        out_shape=out_shape,
        scratch_shapes=list(scratch),
        name=name,
        compiler_params=pltpu.CompilerParams(vmem_limit_bytes=VMEM_LIMIT),
    )


def shape(dims, dtype):
    return jax.ShapeDtypeStruct(dims, dtype)


def shift_part(array, by):
    size = lax.axis_size("part")
    pairs = [(i, i + by) for i in range(size) if 0 <= i + by < size]
    return lax.ppermute(array, "part", pairs)


def shards_general(
    hidden, cotangent, segments, valid, in_w, in_m, in_v, out_w, out_m, out_v, small_w, small_m, small_v,
):
    parts = lax.axis_size("part")
    wt = lax.axis_size("w1") * lax.axis_size("w0")
    part = lax.axis_index("part")
    tp = lax.axis_index("t1") * 2 + lax.axis_index("t0")
    own_rows = in_w.shape[0]
    out_rows = out_w.shape[0]
    resid = hidden[0].astype(f32)
    tok_rows = resid.shape[0]
    rows = tok_rows * TP
    spans = rows // SPAN
    seg_all = segments[0]
    pre_gain, norm_gain, conv_weight, conv_bias, dt_shift, a_logs, skips = unpack_small(small_w)

    def own_part(array, width):
        return lax.dynamic_slice_in_dim(array, tp * width, width, array.ndim - 1)

    in_copy = in_w.astype(bf16)
    slices = []
    for j in range(TP):
        slices.append(
            jnp.concatenate(
                [
                    in_copy[:, D_INNER + j * HALF : D_INNER + (j + 1) * HALF],
                    in_copy[:, 2 * D_INNER : 2 * D_INNER + SIDE],
                    in_copy[:, D_INNER + CONVCH + j * LOCAL_HEADS : D_INNER + CONVCH + (j + 1) * LOCAL_HEADS],
                    jnp.zeros((own_rows, LANES - LOCAL_HEADS), bf16),
                    in_copy[:, j * HALF : (j + 1) * HALF],
                ],
                axis=1,
            )
        )
    mine = lax.all_to_all(jnp.stack(slices), GROUP, 0, 0, tiled=False)
    w_in = lax.all_gather(mine, COPIES, axis=0, tiled=False)
    w_in = w_in.reshape(parts, wt, TP, own_rows, COLS).transpose(0, 2, 1, 3, 4).reshape(D, COLS)
    flat = [(i, (i % TP) * parts + i // TP) for i in range(parts * TP)]
    out_mine = lax.ppermute(out_w.astype(bf16), ("part", *GROUP), [(b, a) for a, b in flat])
    w_out = lax.all_gather(out_mine, COPIES, axis=0, tiled=True)

    hidden_all = lax.all_gather(hidden[0], GROUP, axis=0, tiled=True)
    back_mix = cotangent[0] * valid[0][:, None].astype(bf16)
    back_all = lax.all_gather(back_mix, GROUP, axis=0, tiled=True)

    hid = hidden_all.astype(f32)
    scale_all = lax.rsqrt(jnp.mean(hid * hid, axis=1, keepdims=True) + norm_eps)
    x_normed = (hid * scale_all * pre_gain).astype(bf16)
    projected = dot(x_normed, w_in)
    conv_in = projected[:, :COL_DT].astype(bf16)
    dt_raw = projected[:, COL_DT:COL_GATE].astype(bf16).astype(f32)
    gate_pre = projected[:, COL_GATE:]
    rim_in = shift_part(conv_in[rows - RIM :], 1)
    padded = jnp.concatenate([rim_in, conv_in], axis=0).astype(f32)
    seg_front = jnp.concatenate([jnp.full((RIM,), -1, jnp.int32), seg_all, jnp.full((RIM,), -1, jnp.int32)])
    seg_pad = lax.dynamic_slice_in_dim(seg_front, part * rows, rows + 2 * RIM)
    seg = seg_pad[RIM : RIM + rows]
    masks = [(seg_pad[k : k + rows] == seg).astype(f32)[:, None] for k in range(CONV)]
    taps = jnp.concatenate([own_part(conv_weight[:, :D_INNER], HALF), conv_weight[:, D_INNER:]], axis=1)
    bias = jnp.concatenate([own_part(conv_bias[:D_INNER], HALF), conv_bias[D_INNER:]])
    total = bias[None, :]
    for k in range(CONV):
        total = total + taps[k] * padded[k : k + rows] * masks[k]
    sig_total = jax.nn.sigmoid(total)
    activated = (total * sig_total).astype(bf16)
    x_scan = activated[:, :HALF]
    b_mat = activated[:, HALF : HALF + STATE]
    c_mat = activated[:, HALF + STATE :]

    def head_row(array):
        return jnp.pad(own_part(array, LOCAL_HEADS), (0, LANES - LOCAL_HEADS))

    shift_row = head_row(dt_shift)
    z = dt_raw + shift_row
    dt = jax.nn.softplus(z)
    sig_dt = jax.nn.sigmoid(z)
    ratio = jnp.where(dt > 1e-30, sig_dt / jnp.maximum(dt, 1e-30), 1.0)
    rate_row = -jnp.exp(head_row(a_logs))
    rate8 = jnp.broadcast_to(rate_row, (8, LANES))
    skip_chan = jnp.repeat(own_part(skips, LOCAL_HEADS), HEADDIM)
    skip8 = jnp.broadcast_to(skip_chan, (8, HALF))
    seg_spans = seg.reshape(spans, SPAN)
    seg_last = seg_spans[:, -1]
    seg_before = jnp.concatenate([seg_pad[RIM - 1 : RIM], seg_last[:-1]])
    keep = (seg_spans == seg_last[:, None]).astype(f32).reshape(rows, 1)
    inflow = (seg_spans == seg_before[:, None]).astype(f32).reshape(rows, 1)
    carry = jnp.broadcast_to((seg_last == seg_before).astype(f32)[:, None], (spans, LANES))
    seg_col = seg[:, None]

    state_shape = shape((STATE, HALF), f32)
    s_local, dec_total = in_vmem(
        functools.partial(state_kernel, spans), (state_shape, shape((8, LANES), f32)), "state"
    )(x_scan, b_mat, dt, rate8, keep, carry)
    dec_chan = jnp.repeat(dec_total[0, :LOCAL_HEADS], HEADDIM)
    s_in = jnp.zeros((STATE, HALF), f32)
    for _ in range(parts - 1):
        s_in = shift_part(dec_chan * s_in + s_local, 1)
    y_scan, states = in_vmem(
        functools.partial(scan_kernel, spans),
        (shape((rows, HALF), f32), shape((spans, STATE, HALF), f32)),
        "scan",
        [pltpu.VMEM((STATE, HALF), f32)],
    )(x_scan, b_mat, c_mat, dt, rate8, seg_col, seg_spans, keep, inflow, carry, s_in)
    y_b = (y_scan + skip_chan * x_scan.astype(f32)).astype(bf16).astype(f32)

    gain_own = own_part(norm_gain, HALF)
    sig_gate = jax.nn.sigmoid(gate_pre)
    silu_gate = gate_pre * sig_gate
    gated = y_b * silu_gate
    gate_sq = lax.psum(jnp.sum(gated * gated, axis=1), GROUP)
    scale_gate = lax.rsqrt(gate_sq / D_INNER + norm_eps)[:, None]
    normed = (gated * scale_gate * gain_own).astype(bf16)
    mixer = lax.psum_scatter(dot(normed, w_out), GROUP, scatter_dimension=0, tiled=True)
    output = (resid + mixer).astype(bf16)
    valid_rows = valid[0].astype(f32)
    res_sq = jnp.sum(valid_rows * jnp.sum(resid * resid, axis=1))
    mix_sq = jnp.sum(valid_rows * jnp.sum(mixer * mixer, axis=1))
    valid_count = jnp.sum(valid_rows)

    d_normed = dot(back_all, w_out, ((1,), (1,)))
    g_out = dot(normed, back_all, ((0,), (0,)))
    g_out = lax.psum_scatter(g_out, COPIES, scatter_dimension=0, tiled=True)
    g_out = lax.ppermute(g_out, ("part", *GROUP), flat)
    d_gain = d_normed * gain_own
    gate_dot = lax.psum(jnp.sum(gated * d_gain, axis=1), GROUP)
    d_gated = scale_gate * d_gain - gated * (scale_gate**3 * (gate_dot / D_INNER)[:, None])
    d_norm_gain = jnp.sum(gated * scale_gate * d_normed, axis=0)
    dy = (d_gated * silu_gate).astype(bf16)
    d_gate = d_gated * y_b * (sig_gate * (1.0 + gate_pre * (1.0 - sig_gate)))

    ds_local = in_vmem(functools.partial(state_back_kernel, spans), state_shape, "state_back")(
        dy, c_mat, dt, rate8, inflow, carry
    )
    ds_out = jnp.zeros((STATE, HALF), f32)
    for _ in range(parts - 1):
        ds_out = shift_part(dec_chan * ds_out + ds_local, -1)
    d_x, d_b, d_c, d_dt, d_rate, d_skip = in_vmem(
        functools.partial(scan_back_kernel, spans),
        (
            shape((rows, HALF), bf16),
            shape((rows, STATE), f32),
            shape((rows, STATE), f32),
            shape((rows, LANES), f32),
            shape((8, LANES), f32),
            shape((8, HALF), f32),
        ),
        "scan_back",
        [pltpu.VMEM((STATE, HALF), f32), pltpu.VMEM((2 * SPAN, HALF), f32)],
    )(x_scan, b_mat, c_mat, dt, ratio, sig_dt, rate8, seg_col, seg_spans, keep, inflow, carry, skip8, y_scan, states, dy, ds_out)

    d_total = jnp.concatenate([d_x.astype(f32), d_b, d_c], axis=1) * (sig_total * (1.0 + total * (1.0 - sig_total)))
    rim_back = shift_part(d_total[:RIM], -1)
    d_padded = jnp.concatenate([d_total, rim_back], axis=0)
    d_conv_in = 0.0
    for k in range(CONV):
        later = (seg_pad[2 * RIM - k : 2 * RIM - k + rows] == seg).astype(f32)[:, None]
        d_conv_in = d_conv_in + taps[k] * d_padded[RIM - k : RIM - k + rows] * later
    d_taps = jnp.stack([jnp.sum(d_total * padded[k : k + rows] * masks[k], axis=0) for k in range(CONV)])
    d_bias = jnp.sum(d_total, axis=0)
    d_proj = jnp.concatenate([d_conv_in, d_dt, d_gate], axis=1).astype(bf16)
    d_x_normed = dot(d_proj, w_in, ((1,), (1,)))
    d_x_normed = lax.psum_scatter(d_x_normed, GROUP, scatter_dimension=0, tiled=True)
    g_in = dot(x_normed, d_proj, ((0,), (0,)))
    g_in = g_in.reshape(parts, TP, wt, own_rows, COLS).transpose(0, 2, 1, 3, 4).reshape(parts * wt, TP, own_rows, COLS)
    g_in = lax.psum_scatter(g_in, COPIES, scatter_dimension=0, tiled=False)
    g_in = lax.all_to_all(g_in, GROUP, 0, 0, tiled=False)
    g_in = jnp.concatenate(
        [g_in[j, :, COL_GATE:] for j in range(TP)]
        + [g_in[j, :, :HALF] for j in range(TP)]
        + [jnp.sum(g_in[:, :, COL_SIDE:COL_DT], axis=0)]
        + [g_in[j, :, COL_DT : COL_DT + LOCAL_HEADS] for j in range(TP)],
        axis=1,
    )

    scale_own = lax.rsqrt(jnp.mean(resid * resid, axis=1, keepdims=True) + norm_eps)
    d_pre = d_x_normed * pre_gain
    dot_pre = jnp.mean(resid * d_pre, axis=1, keepdims=True)
    grad_hidden = back_mix.astype(f32) + scale_own * d_pre - resid * (scale_own**3 * dot_pre)
    d_pre_gain = jnp.sum(resid * scale_own * d_x_normed, axis=0)

    def placed(values, width):
        spread = (jnp.arange(TP) == tp).astype(f32)[:, None] * values[..., None, :]
        return spread.reshape(*values.shape[:-1], TP * width)

    d_weight = jnp.concatenate([placed(d_taps[:, :HALF], HALF), d_taps[:, HALF:]], axis=1)
    small_grad = jnp.concatenate(
        [
            d_pre_gain,
            placed(d_norm_gain, HALF),
            d_weight.reshape(-1),
            placed(d_bias[:HALF], HALF),
            d_bias[HALF:],
            placed(jnp.sum(d_dt, axis=0)[:LOCAL_HEADS], LOCAL_HEADS),
            placed((d_rate[0] * rate_row)[:LOCAL_HEADS], LOCAL_HEADS),
            placed(jnp.sum(d_skip[0].reshape(LOCAL_HEADS, HEADDIM), axis=1), LOCAL_HEADS),
            jnp.stack([res_sq, mix_sq, valid_count]),
        ]
    )
    small_total = lax.psum(small_grad, EVERYONE)
    res_total, mix_total, count_total = small_total[-3], small_total[-2], small_total[-1]
    in_m_new, in_v_new, in_w_new = adamw(in_w, in_m, in_v, g_in, 0.02, 0.1)
    out_m_new, out_v_new, out_w_new = adamw(out_w, out_m, out_v, g_out, 0.02, 0.1)
    small_m_new, small_v_new, small_w_new = adamw(small_w, small_m, small_v, small_total[:-3], 0.2, 0.0)
    rms = jnp.stack([jnp.sqrt(res_total / (count_total * D)), jnp.sqrt(mix_total / (count_total * D))])
    return (
        output[None], grad_hidden[None], in_m_new, in_v_new, in_w_new, out_m_new, out_v_new, out_w_new,
        small_m_new, small_v_new, small_w_new, rms,
    )


MESH = pl.DeviceIdType.MESH
T0, T1, DIAG, CORE, SIDEWAYS, PART = ("t0",), ("t1",), ("t1", "t0"), ("w0",), ("w1",), ("part",)
SIDE_CORE = ("w1", "w0")
HOPS = (None, T0, T1, DIAG)
HBM = pl.BlockSpec(memory_space=pl.ANY)
VMEM = pl.BlockSpec(memory_space=pltpu.VMEM)
MAIN = COL_GATE
CHANS = HALF + SIDE
FRONT = 16
TILE = 8
QUARTER = HALF // 2
NORM_ROW = D // LANES
TAP_ROW = NORM_ROW + D_INNER // LANES
TAP_ROWS = CONVCH // LANES
HEAD_ROW = TAP_ROW + (CONV + 1) * TAP_ROWS
SMALL_ROWS = HEAD_ROW + 2
BOX_ROWS = SMALL_ROWS + 8
OWN_NORM = NORM_ROW
OWN_TAP = OWN_NORM + HALF // LANES
OWN_SIDE = OWN_TAP + (CONV + 1) * (HALF // LANES)
OWN_HEAD = OWN_SIDE + (CONV + 1) * (SIDE // LANES)
OWN_SUMS = OWN_HEAD + 3
OWN_ROWS = 64


def place():
    return tuple(lax.axis_index(a) for a in EVERYONE)


def across(flips):
    return {a: 1 - lax.axis_index(a) for a in flips}


def group_blocks():
    _, t1, t0, _, _ = place()
    return [(t1, t0), (t1, 1 - t0), (1 - t1, t0), (1 - t1, 1 - t0)]


def greet(neighbours):
    barrier = pltpu.get_barrier_semaphore()
    for flips in neighbours:
        pl.semaphore_signal(barrier, inc=1, device_id=across(flips), device_id_type=MESH)


def greeted(neighbours):
    pl.semaphore_wait(pltpu.get_barrier_semaphore(), len(neighbours))


class Copies:
    def __init__(self, local_sem, send_sem, recv_sem):
        self.local_sem, self.send_sem, self.recv_sem = local_sem, send_sem, recv_sem
        self.sent, self.kept, self.in_flight, self.on_device = 0, 0, [], []

    def send(self, src, dst, flips):
        copy = pltpu.make_async_remote_copy(
            src_ref=src,
            dst_ref=dst,
            send_sem=self.send_sem.at[self.sent],
            recv_sem=self.recv_sem.at[self.sent],
            device_id=across(flips),
            device_id_type=MESH,
        )
        copy.start()
        self.sent += 1
        self.in_flight.append(copy)
        return copy

    def keep(self, src, dst):
        copy = pltpu.make_async_copy(src, dst, self.local_sem.at[self.kept])
        copy.start()
        self.kept += 1
        self.on_device.append(copy)
        return copy

    def settle(self, copy):
        copy.wait()
        self.on_device = [other for other in self.on_device if other is not copy]

    def left(self, copies):
        for copy in copies:
            copy.wait_send()
            self.in_flight = [other for other in self.in_flight if other is not copy]

    def drain(self):
        for copy in self.in_flight:
            copy.wait_send()
        for copy in self.on_device:
            copy.wait()
        self.in_flight, self.on_device = [], []


def sems(remote, local=1):
    return [
        pltpu.SemaphoreType.DMA((local,)),
        pltpu.SemaphoreType.DMA((remote,)),
        pltpu.SemaphoreType.DMA((remote,)),
    ]


class GroupGather:
    def __init__(self, copies, src, dst):
        self.copies, self.dst = copies, dst
        self.rows = src.shape[0]
        self.halves = (0, self.rows // 2)
        own = group_blocks()[0]
        self.src, self.own, self.size = src, copies.keep(src, self.at(own, 0, self.rows)), self.rows // 2
        self.along_t1, self.along_t0, self.diagonal = self.start(T1), [], []

    def start(self, flips):
        own = group_blocks()[0]
        return [
            self.copies.send(self.src.at[pl.ds(h, self.size)], self.at(own, h, self.size), flips) for h in self.halves
        ]

    def start_t0(self):
        self.along_t0 = self.start(T0)

    def at(self, block, first, size):
        return self.dst.at[pl.ds(pl.multiple_of((block[0] * 2 + block[1]) * self.rows + first, size), size)]

    def hand_on(self):
        beside = group_blocks()[2]
        for copy, h in zip(self.along_t1, self.halves):
            copy.wait_recv()
            here = self.at(beside, h, self.rows // 2)
            self.diagonal.append(self.copies.send(here, here, T0))

    def finish(self):
        for copy in self.along_t0 + self.diagonal:
            copy.wait_recv()


class WeightGather:
    def __init__(self, copies, dst, rows, group):
        self.copies, self.dst, self.rows, self.group = copies, dst, rows, group
        self.by_part, self.by_side, self.by_core = [], [], []

    def at(self, part, w1, w0, block):
        index = part
        if self.group:
            index = (index * 2 + block[0]) * 2 + block[1]
        index = (index * 2 + w1) * 2 + w0
        return self.dst.at[pl.ds(pl.multiple_of(index * self.rows, self.rows), self.rows)]

    def mine(self, block):
        p, _, _, w1, w0 = place()
        return self.at(p, w1, w0, block)

    def spread(self, src, block):
        dst = self.mine(block)
        self.by_part.append((self.copies.send(src, dst, PART), block))
        self.by_side.append((self.copies.send(src, dst, SIDEWAYS), block))
        self.by_core.append(self.copies.send(src, dst, CORE))

    def swap(self, src):
        own, *others = group_blocks()

        def slice_of(block):
            return src.at[block_rows(block, self.rows)]

        self.swaps = [(self.copies.send(slice_of(b), self.mine(own), flips), b) for b, flips in zip(others, HOPS[1:])]
        self.kept = self.copies.keep(slice_of(own), self.mine(own))
        self.spread(slice_of(own), own)

    def spread_swapped(self):
        for copy, block in self.swaps:
            copy.wait_recv()
            self.spread(self.mine(block), block)

    def pass_core(self, part, w1, block):
        here = self.at(part, w1, lax.axis_index("w0"), block)
        self.by_core.append(self.copies.send(here, here, CORE))

    def hand_on(self):
        p, _, _, w1, w0 = place()
        self.again = []
        for (copy, block), (side, _) in zip(self.by_part, self.by_side):
            side.wait_recv()
            self.pass_core(p, 1 - w1, block)
            copy.wait_recv()
            here = self.at(1 - p, w1, w0, block)
            self.again.append((self.copies.send(here, here, SIDEWAYS), block))
            self.pass_core(1 - p, w1, block)

    def hand_on_last(self):
        p, _, _, w1, _ = place()
        for copy, block in self.again:
            copy.wait_recv()
            self.pass_core(1 - p, 1 - w1, block)

    def finish(self):
        for copy in self.by_core:
            copy.wait_recv()


class GradientSum:
    def __init__(self, copies, srcs, rows, bufs, group):
        self.copies, self.srcs, self.rows, self.group = copies, srcs, rows, group
        self.core, self.sides, self.fars = bufs[:3]
        self.lasts = bufs[3] if group else None
        self.blocks = group_blocks() if group else [()]
        self.order = (1, 2, 3, 0) if group else (0,)
        p, _, _, w1, _ = place()
        self.parts, self.sides_of = (1 - p, p), (1 - w1, w1)
        self.core_copies, self.side_copies, self.far_copies, self.last_copies = {}, {}, {}, {}

    def at(self, block, side, w0):
        index = block[0] * 2 + block[1] if self.group else 0
        index = (index * 2 + side) * 2 + w0
        return pl.ds(pl.multiple_of(index * self.rows, self.rows), self.rows)

    def place(self, i, j):
        return self.at(self.blocks[i], self.sides_of[j], lax.axis_index("w0"))

    def pass_on(self, k, i, j, value, dst, flips):
        here = self.place(i, j)
        self.srcs[k][here, :] = value.astype(bf16)
        return self.copies.send(self.srcs[k].at[here], dst, flips)

    def added(self, k, i, j, *more):
        q, block, side = self.parts[k], self.blocks[i], self.sides_of[j]
        self.core_copies[k, i, j].wait_recv()
        value = self.srcs[k][self.place(i, j), :].astype(f32)
        value = value + self.core[(q, side, *block)].astype(f32)
        for other in more:
            value = value + other.astype(f32)
        return value

    def cores(self, k):
        w0 = lax.axis_index("w0")
        for j in range(2):
            for i in self.order:
                q, block, side = self.parts[k], self.blocks[i], self.sides_of[j]
                src = self.srcs[k].at[self.at(block, side, 1 - w0)]
                self.core_copies[k, i, j] = self.copies.send(src, self.core.at[(q, side, *block)], CORE)

    def left(self):
        for copies in (self.core_copies, self.side_copies, self.far_copies, self.last_copies):
            self.copies.left(copies.values())

    def to_sides(self, k):
        for i in self.order:
            self.side_copies[k, i] = self.pass_on(k, i, 0, self.added(k, i, 0), self.sides.at[k, i], SIDEWAYS)

    def to_part(self, which=None):
        for i in self.order if which is None else which:
            self.side_copies[0, i].wait_recv()
            value = self.added(0, i, 1, self.sides[0, i])
            self.far_copies[i] = self.pass_on(0, i, 1, value, self.fars.at[i], PART)

    def total(self, i):
        self.side_copies[1, i].wait_recv()
        self.far_copies[i].wait_recv()
        return self.added(1, i, 1, self.sides[1, i], self.fars[i])

    def to_group(self, store):
        for i in self.order:
            value = self.total(i)
            if i == 0:
                store(0, value)
            else:
                self.last_copies[i] = self.pass_on(1, i, 1, value, self.lasts.at[i - 1], HOPS[i])

    def finish(self, store):
        for i, copy in self.last_copies.items():
            copy.wait_recv()
            store(i, self.lasts[i - 1].astype(f32))


class GroupScatter:
    def __init__(self, copies, src, bufs):
        self.copies, self.src = copies, src
        self.here, self.pass_on, self.last = bufs
        self.rows = self.here.shape[0]

    def block(self, i):
        return block_rows(group_blocks()[i], self.rows)

    def left(self):
        self.copies.left([self.own_copy, self.pass_copy])

    def to_t0(self, i):
        copy = self.copies.send(self.src.at[self.block(i)], self.here if i == 1 else self.pass_on, T0)
        if i == 1:
            self.own_copy = copy
        else:
            self.pass_copy = copy

    def to_t1(self):
        self.pass_copy.wait_recv()
        here = self.block(2)
        self.src[here, :] = (self.src[here, :].astype(f32) + self.pass_on[...].astype(f32)).astype(bf16)
        self.last_copy = self.copies.send(self.src.at[here], self.last, T1)

    def finish(self):
        self.own_copy.wait_recv()
        self.last_copy.wait_recv()
        return self.here[...].astype(f32) + self.last[...].astype(f32)


def scatter_buffers(rows):
    return [pltpu.VMEM((rows, D), bf16)] * 3


def sum_buffers(rows, cols, group):
    buf = lambda *lead: pltpu.VMEM((*lead, rows, cols), bf16)
    if not group:
        return [buf(2, 2), buf(2, 1), buf(1)]
    return [buf(2, 2, 2, 2), buf(2, 4), buf(4), buf(3)]


def block_rows(block, size):
    return pl.ds(pl.multiple_of((block[0] * 2 + block[1]) * size, size), size)


def lane_of(h):
    return h if h < LOCAL_HEADS // 2 else h + HEADS // 2 - LOCAL_HEADS // 2


def own_pair(cols, h):
    lane = lax.broadcasted_iota(jnp.int32, (cols.shape[0], LANES), 1)
    first, second = lane_of(h), lane_of(h + 1)
    return jnp.where(lane < HEADDIM, cols[:, first : first + 1], cols[:, second : second + 1])


def own_sums(values):
    width = values.shape[1]
    head = lax.broadcasted_iota(jnp.int32, (width, LANES), 0) // HEADDIM
    lane = lax.broadcasted_iota(jnp.int32, (width, LANES), 1)
    pick = (jnp.where(head < LOCAL_HEADS // 2, head, head + lane_of(LOCAL_HEADS) - LOCAL_HEADS) == lane).astype(bf16)
    high = values.astype(bf16)
    low = (values - high.astype(f32)).astype(bf16)
    return dot(high, pick) + dot(low, pick)


def head_lanes(values, back=False):
    first = (lax.axis_index("t1") * 2 + lax.axis_index("t0")) * (LOCAL_HEADS // 2)
    return pltpu.roll(values, first if back else LANES - first, 1)


def own_row(first, k):
    tp = lax.axis_index("t1") * 2 + lax.axis_index("t0")
    third = QUARTER // LANES
    return pl.ds(first + (k // third) * (D_INNER // 2 // LANES) + tp * third + k % third, 1)


def own_chans(j):
    return [slice(first + j * QUARTER, first + (j + 1) * QUARTER) for first in (0, D_INNER // 2)]


EVERY_NEIGHBOUR = (T0, T1, DIAG, CORE, SIDEWAYS, SIDE_CORE, PART)


def main_kernel(
    spans, hid_ref, inw_hbm, outw_hbm, cot_hbm, inside_ref, valid_ref, small_ref, segs_ref,
    cotv_out, mixer_out, ggate_out, gmain_out, dx_out, gout_out, total_ref,
    h_ref, xn_ref, win_ref, convp_ref, x_ref, b_ref, c_ref, dtot_ref, dt_ref, z_ref, cum_ref, y_ref, st_ref,
    wgate_ref, wout_ref, back_ref, normed_ref, mix_ref, dy_ref, dgate_ref, dmain_ref, dgain_ref, taps_ref, heads_ref, chans_ref,
    marks_ref, carry_ref, s_ref, pass_ref, got_ref, rim_ref, gated_ref, gate_ref, dn_ref,
    stat_ref, stats_ref, dyg_ref, passb_ref, gotb_ref, rims_ref, rimr_ref, hsum_ref, dskip_ref, dtaps_ref,
    dpre_ref, box_ref, boxes_ref, gm_ref, segc_ref, segr_ref, validc_ref,
    *rest,
):
    go_bufs, gg_bufs, gm_bufs, mix_bufs, dx_bufs = rest[:3], rest[3:7], rest[7:11], rest[11:14], rest[14:17]
    local_sem, send_sem, recv_sem = rest[17:]
    greet(EVERY_NEIGHBOUR)
    p, _, _, _, _ = place()
    rows_all = spans * SPAN
    tokens = hid_ref.shape[0]
    own_rows, out_rows = inw_hbm.shape[0], outw_hbm.shape[0]
    lane = lax.broadcasted_iota(jnp.int32, (1, LANES), 1)
    wm_ref = dmain_ref.at[pl.ds(0, TP * own_rows)]
    wg_ref = dgate_ref.at[pl.ds(0, TP * own_rows)]
    wo_ref = mix_ref.at[pl.ds(0, out_rows)]
    cotv_ref = mix_ref.at[pl.ds(tokens, tokens)]
    dxi_ref, prod_ref = gated_ref, gate_ref

    def side_at(c, which):
        return (slice(spans * STATE, spans * STATE + SPAN), pl.ds(pl.multiple_of((which * spans + c) * STATE, STATE), STATE))


    copies = Copies(local_sem, send_sem, recv_sem)
    loads = [
        copies.keep(inw_hbm.at[:, pl.ds(k * HALF, HALF)], gate_ref.at[pl.ds(k * own_rows, own_rows)])
        for k in range(2 * D_INNER // HALF)
    ]
    loads += [
        copies.keep(outw_hbm.at[:, pl.ds(k * HALF, HALF)], dn_ref.at[pl.ds(k * out_rows, out_rows)]) for k in range(D // HALF)
    ]
    loads.append(copies.keep(cot_hbm, cotv_ref))

    side = inside_ref[:, 0 : SIDE + HEADS]
    dt_cols = jnp.concatenate([side[:, SIDE:], jnp.zeros((own_rows, LANES - HEADS), f32)], axis=1)
    for copy in loads:
        copies.settle(copy)

    def master(first):
        return gate_ref[first // HALF * own_rows : (first // HALF + 1) * own_rows, first % HALF : first % HALF + QUARTER]

    for j in range(TP):
        at = slice(j * own_rows, (j + 1) * own_rows)
        for k, chans in enumerate(own_chans(j)):
            part = slice(k * QUARTER, (k + 1) * QUARTER)
            wg_ref[at, part] = master(chans.start).astype(bf16)
            wm_ref[at, part] = master(D_INNER + chans.start).astype(bf16)
        wm_ref[at, HALF:CHANS] = side[:, :SIDE].astype(bf16)
        dt_own = (lane % (HEADS // 2) // (LOCAL_HEADS // 2) == j) & (lane < HEADS)
        wm_ref[at, CHANS:MAIN] = jnp.where(dt_own, dt_cols, 0.0).astype(bf16)
    for k in range(D // HALF):
        wo_ref[:, k * HALF : (k + 1) * HALF] = dn_ref[k * out_rows : (k + 1) * out_rows, :].astype(bf16)

    greeted(EVERY_NEIGHBOUR)
    mains = WeightGather(copies, win_ref, own_rows, True)
    mains.swap(wm_ref)
    hids = GroupGather(copies, hid_ref, h_ref)
    hids.start_t0()

    def column(row):
        return jnp.transpose(jnp.broadcast_to(row, (LANES, SPAN)))[:, 0:1]

    for c in range(spans):
        row = segs_ref[0:1, pl.ds(pl.multiple_of(p * rows_all + c * SPAN, LANES), SPAN)].astype(f32)
        segr_ref[c : c + 1, :] = row
        segc_ref[FRONT + c * SPAN : FRONT + (c + 1) * SPAN, :] = column(row)
    around = rows_all - SPAN
    row = segs_ref[0:1, pl.ds(pl.multiple_of(p * around, LANES), SPAN)].astype(f32)
    segc_ref[0:FRONT, :] = jnp.where(p == 1, column(row)[SPAN - FRONT :], -1.0)
    row = segs_ref[0:1, pl.ds(pl.multiple_of(rows_all + p * around, LANES), SPAN)].astype(f32)
    segc_ref[FRONT + rows_all :, :] = jnp.where(p == 0, column(row)[0:FRONT], -1.0)
    stat_ref[0] = jnp.zeros_like(stat_ref[0])
    stat_ref[0, 0:1, 0:tokens] = valid_ref[...].astype(f32)
    validc_ref[...] = column(stat_ref[0, 0:1, 0:SPAN])[0:tokens]
    cotv_ref[...] = (cotv_ref[...].astype(f32) * validc_ref[...]).astype(bf16)
    copies.keep(cotv_ref, cotv_out)

    for k in range(HALF // LANES):
        lanes = slice(k * LANES, (k + 1) * LANES)
        chans_ref[1:2, lanes] = small_ref[own_row(NORM_ROW, k), :]
        for j in range(CONV + 1):
            taps_ref[j : j + 1, lanes] = small_ref[own_row(TAP_ROW + TAP_ROWS * j, k), :]
    for k in range(SIDE // LANES):
        lanes = slice(HALF + k * LANES, HALF + (k + 1) * LANES)
        for j in range(CONV + 1):
            row = TAP_ROW + TAP_ROWS * j + D_INNER // LANES + k
            taps_ref[j : j + 1, lanes] = small_ref[row : row + 1, :]
    head_row = jnp.broadcast_to(small_ref[HEAD_ROW : HEAD_ROW + 1, :], (TILE, LANES))
    next_row = jnp.broadcast_to(small_ref[HEAD_ROW + 1 : HEAD_ROW + 2, :], (TILE, LANES))
    a_log = pltpu.roll(head_row, LANES - HEADS, 1)
    lane8 = lax.broadcasted_iota(jnp.int32, (TILE, LANES), 1)
    spill = LANES - 2 * HEADS
    skip = jnp.where(lane8 < spill, pltpu.roll(head_row, spill, 1), pltpu.roll(next_row, spill, 1))
    own = lane8 < HEADS
    heads_ref[0:1, :] = head_lanes(jnp.where(own, head_row, 0.0))[0:1]
    heads_ref[1:2, :] = -jnp.exp(head_lanes(jnp.where(own, a_log, 0.0))[0:1])
    skip = head_lanes(jnp.where(own, skip, 0.0))[0:1]
    for q in range(PAIRS):
        chans_ref[0:1, q * LANES : (q + 1) * LANES] = own_pair(skip, 2 * q)

    def mark(first, count):
        seg = segc_ref[pl.ds(first, FRONT + count), :]
        here = seg[FRONT:]
        last = seg[FRONT + count - 1 :]
        before = seg[FRONT - 1 : FRONT]
        cols = {k: seg[FRONT - RIM + k : FRONT - RIM + k + count] == here for k in range(RIM)}
        cols[6], cols[7] = here == last, here == before
        lane_m = lax.broadcasted_iota(jnp.int32, (count, TILE), 1)
        marks = jnp.zeros((count, TILE), f32)
        for k, col in cols.items():
            marks = jnp.where(lane_m == k, jnp.where(col, 1.0, 0.0), marks)
        marks_ref[pl.ds(first, count), :] = marks
        return jnp.broadcast_to(jnp.where(last == before, 1.0, 0.0), (1, LANES))

    for c in range(spans):
        carry_ref[c : c + 1, :] = mark(c * SPAN, SPAN)
    mark(rows_all, TILE)
    blocks = group_blocks()

    def norm(block):
        rows = block_rows(block, tokens)
        hid = h_ref[rows, :].astype(f32)
        scale = lax.rsqrt(jnp.sum(hid * hid, axis=1, keepdims=True) / D + norm_eps)
        for k in range(D // LANES):
            lanes = slice(k * LANES, (k + 1) * LANES)
            xn_ref[rows, lanes] = (h_ref[rows, lanes].astype(f32) * scale * small_ref[k : k + 1, :]).astype(bf16)

    mains.spread_swapped()
    copies.settle(hids.own)
    norm(blocks[0])
    gates = WeightGather(copies, wgate_ref, own_rows, True)
    gates.swap(wg_ref)
    hids.hand_on()
    norm(blocks[2])
    mains.hand_on()
    gates.spread_swapped()
    outs = WeightGather(copies, wout_ref, out_rows, False)
    outs.spread(wo_ref, ())
    outs_kept = copies.keep(wo_ref, outs.mine(()))
    hids.finish()
    cots = GroupGather(copies, cotv_ref, back_ref)
    cots.start_t0()
    norm(blocks[1])
    norm(blocks[3])
    mains.hand_on_last()
    mains.finish()
    copies.settle(mains.kept)

    def project(c, _):
        rows = span_rows(c)
        xn = xn_ref[rows, :]
        at = pl.ds(pl.multiple_of(FRONT + c * SPAN, FRONT), SPAN)
        for k in range(CHANS // 256):
            cols = slice(k * 256, (k + 1) * 256)
            convp_ref[at, cols] = dot(xn, win_ref[:, cols]).astype(bf16)
        dt_raw = dot(xn, win_ref[:, CHANS:MAIN]).astype(bf16).astype(f32)
        z = head_lanes(dt_raw) + heads_ref[0:1, :]
        z_ref[rows, :] = z
        small = jnp.exp(-jnp.abs(z))
        one_more = 1.0 + small
        is_one = one_more == 1.0
        log_more = jnp.where(is_one, small, jnp.log(one_more) * small / jnp.where(is_one, 1.0, one_more - 1.0))
        dt_ref[rows, :] = jnp.maximum(z, 0.0) + log_more
        return 0

    lax.fori_loop(0, spans, project, 0)
    rim = copies.send(convp_ref.at[pl.ds(rows_all, FRONT)], rim_ref, PART)
    gates.hand_on()
    s_ref[...] = jnp.zeros_like(s_ref)
    dgain_ref[...] = jnp.zeros_like(dgain_ref)

    def convolve(c, _):
        rows = span_rows(c)
        wide = pl.ds(pl.multiple_of(c * SPAN, SPAN), SPAN + FRONT)
        masks = [jnp.broadcast_to(marks_ref[rows, j : j + 1], (SPAN, LANES)) for j in range(RIM)]
        for k in range(CHANS // LANES):
            lanes = slice(k * LANES, (k + 1) * LANES)
            values = convp_ref[wide, lanes].astype(f32)
            total = taps_ref[CONV : CONV + 1, lanes] + taps_ref[RIM : RIM + 1, lanes] * values[FRONT:]
            for j in range(RIM):
                first = FRONT - RIM + j
                total = total + taps_ref[j : j + 1, lanes] * values[first : first + SPAN] * masks[j]
            sig = 1.0 / (1.0 + jnp.exp(-total))
            value = (total * sig).astype(bf16)
            dtot_ref[rows, lanes] = sig * (1.0 + total * (1.0 - sig))
            if k < HALF // LANES:
                x_ref[rows, lanes] = value
            elif k == HALF // LANES:
                b_ref[rows, :] = value
            else:
                c_ref[rows, :] = value
        return 0

    lax.fori_loop(1, spans, convolve, 0)
    rim.wait_recv()
    convp_ref[0:FRONT, :] = jnp.where(p == 1, rim_ref[...].astype(f32), 0.0).astype(bf16)
    lax.fori_loop(0, 1, convolve, 0)
    gates.hand_on_last()

    def local_states(c, _):
        rows = span_rows(c)
        dt, cum = span_decay(dt_ref, heads_ref, c, 1)
        cum_ref[rows, :] = cum
        last = cum[SPAN - 1 : SPAN, :]
        end_weight = jnp.exp(last - cum) * dt * marks_ref[rows, 6:7]
        decay = jnp.exp(last) * carry_ref[pl.ds(c, 1), :]
        b = b_ref[rows, :]
        st_ref[c] = s_ref[...]
        for q in range(PAIRS):
            lanes = slice(q * LANES, (q + 1) * LANES)
            dyg_ref[rows, lanes] = (x_ref[rows, lanes].astype(f32) * own_pair(end_weight, 2 * q)).astype(bf16)
            s_ref[:, lanes] = s_ref[:, lanes] * own_pair(decay, 2 * q)
        s_ref[...] += dot(b, dyg_ref[rows, :], ((0,), (0,)))
        return 0

    lax.fori_loop(0, spans, local_states, 0)
    pass_ref[...] = s_ref[...].astype(bf16)
    state = copies.send(pass_ref, got_ref, PART)
    cots.hand_on()
    outs.hand_on()

    def inside(c, _):
        rows = span_rows(c)
        cum = cum_ref[rows, :]
        back_log = jnp.transpose(cum - jnp.log(dt_ref[rows, :]))
        scores = dot(c_ref[rows, :], b_ref[rows, :], ((1,), (1,)))
        early, late = slice(0, SPAN // 2), slice(SPAN // 2, SPAN)
        seg_col = segc_ref[pl.ds(pl.multiple_of(FRONT + c * SPAN, FRONT), SPAN), :]
        seg_row = segr_ref[pl.ds(c, 1), :]
        row = lax.broadcasted_iota(jnp.int32, (SPAN // 2, SPAN), 0)
        col = lax.broadcasted_iota(jnp.int32, (SPAN // 2, SPAN), 1)
        mask_early = (row >= col)[:, early] & (seg_col[early] == seg_row[:, early])
        mask_late = (row + SPAN // 2 >= col) & (seg_col[late] == seg_row)
        lane = lax.broadcasted_iota(jnp.int32, (SPAN, LANES), 1)
        for q in range(PAIRS):
            lanes = slice(q * LANES, (q + 1) * LANES)
            x = x_ref[rows, lanes]
            parts = []
            for h in (lane_of(2 * q), lane_of(2 * q + 1)):
                gap = cum[early, h : h + 1] - back_log[h : h + 1, early]
                weighted = scores[early, early] * jnp.exp(jnp.where(mask_early, gap, -1e30))
                y_early = dot(weighted.astype(bf16), x[early])
                gap = cum[late, h : h + 1] - back_log[h : h + 1, :]
                weighted = scores[late] * jnp.exp(jnp.where(mask_late, gap, -1e30))
                parts.append(jnp.concatenate([y_early, dot(weighted.astype(bf16), x)], axis=0))
            y_ref[rows, lanes] = jnp.where(lane < HEADDIM, parts[0], parts[1])
        return 0

    lax.fori_loop(0, spans, inside, 0)
    state.wait_recv()
    s_ref[...] = got_ref[...].astype(f32) * p.astype(f32)

    def across_spans(c, _):
        rows = span_rows(c)
        cum = cum_ref[rows, :]
        decay = jnp.exp(cum[SPAN - 1 : SPAN, :]) * carry_ref[pl.ds(c, 1), :]
        gain = jnp.exp(cum) * marks_ref[rows, 7:8]
        cc = c_ref[rows, :]
        for q in range(PAIRS):
            lanes = slice(q * LANES, (q + 1) * LANES)
            entering = s_ref[:, lanes]
            full = st_ref[c, :, lanes] + entering
            st_ref[c, :, lanes] = full
            y_ref[rows, lanes] += dot(cc, full.astype(bf16)) * own_pair(gain, 2 * q)
            s_ref[:, lanes] = entering * own_pair(decay, 2 * q)
        return 0

    lax.fori_loop(0, spans, across_spans, 0)
    gates.finish()
    copies.settle(gates.kept)

    def put_stat(k, c, column):
        wide = jnp.transpose(jnp.broadcast_to(column, (SPAN, LANES)))
        stat_ref[k, :, span_rows(c)] = wide[0:TILE, :]

    def exchange(k):
        return [copies.send(stat_ref.at[k], stats_ref.at[k, i], flips) for i, flips in enumerate(HOPS[1:])]

    def get_stat(k, c):
        cols = span_rows(c)
        total = stat_ref[k, :, cols] + stats_ref[k, 0, :, cols] + stats_ref[k, 1, :, cols] + stats_ref[k, 2, :, cols]
        return jnp.transpose(jnp.broadcast_to(total[0:1, :], (LANES, SPAN)))[:, 0:1] / D_INNER

    def values(rows, lanes):
        y_b = (y_ref[rows, lanes] + chans_ref[0:1, lanes] * x_ref[rows, lanes].astype(f32)).astype(bf16).astype(f32)
        gate = gate_ref[rows, lanes]
        sig = 1.0 / (1.0 + jnp.exp(-gate))
        return y_b, gate, sig

    def gating(c, _):
        rows = span_rows(c)
        xn = xn_ref[rows, :]
        total = jnp.zeros((SPAN, 1), f32)
        for k in range(HALF // 256):
            lanes = slice(k * 256, (k + 1) * 256)
            gate_ref[rows, lanes] = dot(xn, wgate_ref[:, lanes])
            y_b, gate, sig = values(rows, lanes)
            gated = y_b * (gate * sig)
            gated_ref[rows, lanes] = gated
            total = total + jnp.sum(gated * gated, axis=1, keepdims=True)
        put_stat(0, c, total)
        return 0

    lax.fori_loop(0, spans, gating, 0)
    outs.hand_on_last()
    squares = exchange(0)
    cots.finish()
    copies.settle(cots.own)
    outs.finish()
    copies.settle(outs_kept)

    def pull_out(c, _):
        rows = span_rows(c)
        back = back_ref[rows, :]
        total = jnp.zeros((SPAN, 1), f32)
        for k in range(HALF // 256):
            lanes = slice(k * 256, (k + 1) * 256)
            d_normed = dot(back, wout_ref[lanes, :], ((1,), (1,)))
            dn_ref[rows, lanes] = d_normed
            total = total + jnp.sum(gated_ref[rows, lanes] * (d_normed * chans_ref[1:2, lanes]), axis=1, keepdims=True)
        put_stat(1, c, total)
        return 0

    lax.fori_loop(0, spans, pull_out, 0)
    for copy in squares:
        copy.wait_recv()
    dots = exchange(1)

    def push_out(c, _):
        rows = span_rows(c)
        scale = lax.rsqrt(get_stat(0, c) + norm_eps)
        for k in range(HALF // 256):
            lanes = slice(k * 256, (k + 1) * 256)
            scaled = gated_ref[rows, lanes] * scale
            normed_ref[rows, lanes] = (scaled * chans_ref[1:2, lanes]).astype(bf16)
            dgain_ref[0:1, lanes] += jnp.sum(scaled * dn_ref[rows, lanes], axis=0, keepdims=True)
        normed = normed_ref[rows, :]
        for k in range(D // 256):
            cols = slice(k * 256, (k + 1) * 256)
            mix_ref[rows, cols] = dot(normed, wout_ref[:, cols]).astype(bf16)
        return 0

    copies.drain()
    lax.fori_loop(0, spans, push_out, 0)
    mixes = GroupScatter(copies, mix_ref, mix_bufs)
    mixes.to_t0(3)
    mixes.to_t0(1)
    for q in range(2):
        normed = normed_ref[:, q * HALF // 2 : (q + 1) * HALF // 2]
        for k in range(D // 512):
            cols = slice(k * 512, (k + 1) * 512)
            wout_ref[q * HALF // 2 : (q + 1) * HALF // 2, cols] = dot(normed, back_ref[:, cols], ((0,), (0,))).astype(bf16)
    go_halves = [wout_ref.at[pl.ds(pl.multiple_of(q * (HALF // 2), HALF // 2), HALF // 2)] for q in (1 - p, p)]
    g_out = GradientSum(copies, go_halves, out_rows, go_bufs, False)
    g_out.cores(0)
    g_out.cores(1)
    for copy in dots:
        copy.wait_recv()

    def back_gate(c, _):
        rows = span_rows(c)
        scale = lax.rsqrt(get_stat(0, c) + norm_eps)
        pulled = get_stat(1, c) * (scale * scale * scale)
        for k in range(HALF // LANES):
            lanes = slice(k * LANES, (k + 1) * LANES)
            y_b, gate, sig = values(rows, lanes)
            d_gated = scale * (dn_ref[rows, lanes] * chans_ref[1:2, lanes]) - gated_ref[rows, lanes] * pulled
            dy_ref[rows, lanes] = (d_gated * (gate * sig)).astype(bf16)
            dgate_ref[rows, lanes] = (d_gated * y_b * (sig * (1.0 + gate * (1.0 - sig)))).astype(bf16)
        return 0

    lax.fori_loop(0, spans, back_gate, 0)
    g_out.to_sides(0)
    s_ref[...] = jnp.zeros_like(s_ref)
    hsum_ref[...] = jnp.zeros_like(hsum_ref)
    dskip_ref[...] = jnp.zeros_like(dskip_ref)
    dtaps_ref[...] = jnp.zeros_like(dtaps_ref)

    def local_states(step, _):
        c = spans - 1 - step
        rows = span_rows(c)
        cum = cum_ref[rows, :]
        decay = jnp.exp(cum[SPAN - 1 : SPAN, :]) * carry_ref[pl.ds(c, 1), :]
        gain = jnp.exp(cum) * marks_ref[rows, 7:8]
        cc = c_ref[rows, :]
        for q in range(PAIRS):
            lanes = slice(q * LANES, (q + 1) * LANES)
            dyg = (dy_ref[rows, lanes].astype(f32) * own_pair(gain, 2 * q)).astype(bf16)
            dyg_ref[rows, lanes] = dyg
            ds = s_ref[:, lanes]
            dn_ref[pl.ds(pl.multiple_of(c * STATE, STATE), STATE), lanes] = ds
            s_ref[:, lanes] = ds * own_pair(decay, 2 * q)
        s_ref[...] += dot(cc, dyg_ref[rows, :], ((0,), (0,)))
        return 0

    lax.fori_loop(0, spans, local_states, 0)
    passb_ref[...] = s_ref[...].astype(bf16)
    state = copies.send(passb_ref, gotb_ref, PART)

    width = D // 4
    gg_halves = [back_ref.at[:, pl.ds(k * HALF, HALF)] for k in range(2)]
    g_gate = GradientSum(copies, gg_halves, own_rows, gg_bufs, True)

    def gate_gradient(far):
        for half in range(2):
            first = pl.multiple_of(((1 - p if far else p) * 2 + half) * width, width)
            piece = dot(xn_ref[:, pl.ds(first, width)], dgate_ref[...], ((0,), (0,)))
            gg_halves[0 if far else 1][half * width : (half + 1) * width, :] = piece.astype(bf16)

    gate_gradient(True)
    g_gate.cores(0)
    gate_gradient(False)
    g_gate.cores(1)
    g_gate.to_sides(0)
    g_out.to_part()
    g_out.to_sides(1)
    g_gate.to_sides(1)

    def inside(c, _):
        rows = span_rows(c)
        cum = cum_ref[rows, :]
        fore_log = jnp.transpose(cum)
        back_log = cum - jnp.log(dt_ref[rows, :])
        b = b_ref[rows, :]
        cc = c_ref[rows, :]
        scores = dot(b, cc, ((1,), (1,)))
        early, late = slice(0, SPAN // 2), slice(SPAN // 2, SPAN)
        seg_col = segc_ref[pl.ds(pl.multiple_of(FRONT + c * SPAN, FRONT), SPAN), :]
        seg_row = segr_ref[pl.ds(c, 1), :]
        row = lax.broadcasted_iota(jnp.int32, (SPAN // 2, SPAN), 0)
        col = lax.broadcasted_iota(jnp.int32, (SPAN // 2, SPAN), 1)
        mask_early = (col >= row) & (seg_col[early] == seg_row)
        mask_late = (col >= row)[:, early] & (seg_col[late] == seg_row[:, late])
        lane = lax.broadcasted_iota(jnp.int32, (SPAN, LANES), 1)
        d_early = jnp.zeros((SPAN // 2, SPAN), f32)
        d_late = jnp.zeros((SPAN // 2, SPAN // 2), f32)
        dc = dot(dyg_ref[rows, :], st_ref[c].astype(bf16), ((1,), (1,)))
        for q in range(PAIRS):
            lanes = slice(q * LANES, (q + 1) * LANES)
            x = x_ref[rows, lanes]
            dy = dy_ref[rows, lanes]
            xf = x.astype(f32)
            parts = []
            for k in range(2):
                h = lane_of(2 * q + k)
                gap = fore_log[h : h + 1, :] - back_log[early, h : h + 1]
                decay_early = jnp.exp(jnp.where(mask_early, gap, -1e30))
                gap = fore_log[h : h + 1, late] - back_log[late, h : h + 1]
                decay_late = jnp.exp(jnp.where(mask_late, gap, -1e30))
                dx_early = dot((scores[early] * decay_early).astype(bf16), dy)
                dx_late = dot((scores[late, late] * decay_late).astype(bf16), dy[late])
                parts.append(jnp.concatenate([dx_early, dx_late], axis=0))
                own = (lane < HEADDIM) if k == 0 else (lane >= HEADDIM)
                x_own = jnp.where(own, xf, 0.0).astype(bf16)
                d_early = d_early + dot(x_own[early], dy, ((1,), (1,))) * decay_early
                d_late = d_late + dot(x_own[late], dy[late], ((1,), (1,))) * decay_late
            dxi_ref[rows, lanes] = jnp.where(lane < HEADDIM, parts[0], parts[1])
            dskip_ref[0:1, lanes] += jnp.sum(dy.astype(f32) * xf, axis=0, keepdims=True)
        d_early_b, d_late_b = d_early.astype(bf16), d_late.astype(bf16)
        dn_ref[side_at(c, 0)] = jnp.concatenate([dot(d_early_b, cc), dot(d_late_b, cc[late])], axis=0)
        later = dot(d_early_b[:, late], b[early], ((0,), (0,))) + dot(d_late_b, b[late], ((0,), (0,)))
        earlier = dot(d_early_b[:, early], b[early], ((0,), (0,)))
        dn_ref[side_at(c, 1)] = dc + jnp.concatenate([earlier, later], axis=0)
        return 0

    lax.fori_loop(0, spans, inside, 0)
    mixes.to_t1()
    state.wait_recv()
    s_ref[...] = gotb_ref[...].astype(f32) * (1 - p).astype(f32)

    def across_spans(step, _):
        c = spans - 1 - step
        rows = span_rows(c)
        dt = dt_ref[rows, :]
        cum = cum_ref[rows, :]
        last = cum[SPAN - 1 : SPAN, :]
        end_weight = jnp.exp(last - cum) * dt * marks_ref[rows, 6:7]
        decay = jnp.exp(last) * carry_ref[pl.ds(c, 1), :]
        b = b_ref[rows, :]
        db = dn_ref[side_at(c, 0)]
        edges, ds_all = [], []
        for q in range(PAIRS):
            lanes = slice(q * LANES, (q + 1) * LANES)
            xf = x_ref[rows, lanes].astype(f32)
            dyf = dy_ref[rows, lanes].astype(f32)
            ew = own_pair(end_weight, 2 * q)
            dec = own_pair(decay, 2 * q)
            entering = s_ref[:, lanes]
            ds = dn_ref[pl.ds(pl.multiple_of(c * STATE, STATE), STATE), lanes] + entering
            s_ref[:, lanes] = entering * dec
            ds_b = ds.astype(bf16)
            dyg_ref[rows, lanes] = (xf * ew).astype(bf16)
            ds_all.append(ds_b)
            dx_state = dot(b, ds_b) * ew
            dx = dxi_ref[rows, lanes] + dx_state
            edges.append(
                jnp.sum(ds * st_ref[c, :, lanes], axis=0, keepdims=True) * dec
                + jnp.sum(dx_state * xf, axis=0, keepdims=True)
            )
            prod_ref[0:SPAN, lanes] = dyf * y_ref[rows, lanes]
            prod_ref[SPAN : 2 * SPAN, lanes] = xf * dx
            d_x = (dx + dyf * chans_ref[0:1, lanes]).astype(bf16).astype(f32)
            dtot_ref[rows, lanes] = d_x * dtot_ref[rows, lanes]
        db = db + dot(dyg_ref[rows, :], jnp.concatenate(ds_all, axis=1), ((1,), (1,)))
        dtot_ref[rows, HALF : HALF + STATE] = db * dtot_ref[rows, HALF : HALF + STATE]
        dtot_ref[rows, HALF + STATE :] = dn_ref[side_at(c, 1)] * dtot_ref[rows, HALF + STATE :]
        sums = own_sums(prod_ref[0 : 2 * SPAN, :])
        out_sum, in_sum = sums[:SPAN], sums[SPAN:]
        edge_sum = own_sums(jnp.broadcast_to(jnp.concatenate(edges, axis=1), (TILE, HALF)))[0:1]
        at_last = lax.broadcasted_iota(jnp.int32, (SPAN, LANES), 0) == SPAN - 1
        d_cum = out_sum - in_sum + jnp.where(at_last, edge_sum, 0.0)
        row = lax.broadcasted_iota(jnp.int32, (SPAN, SPAN), 0)
        col = lax.broadcasted_iota(jnp.int32, (SPAN, SPAN), 1)
        d_log = dot((col >= row).astype(f32), d_cum, precision=exact_prec)
        z = z_ref[rows, :]
        small = jnp.exp(-jnp.abs(z))
        sig = jnp.where(z >= 0.0, 1.0, small) / (1.0 + small)
        ratio = jnp.where(dt > 1e-30, sig / jnp.maximum(dt, 1e-30), 1.0)
        d_dt = d_log * heads_ref[1:2, :] * sig + in_sum * ratio
        hsum_ref[0:1, :] += jnp.sum(d_log * dt, axis=0, keepdims=True)
        hsum_ref[1:2, :] += jnp.sum(d_dt, axis=0, keepdims=True)
        dmain_ref[rows, CHANS:MAIN] = head_lanes(d_dt, back=True).astype(bf16)
        return 0

    lax.fori_loop(0, spans, across_spans, 0)
    rims_ref[...] = dtot_ref[0:TILE, :]
    rim = copies.send(rims_ref, rimr_ref, PART)
    g_gate.to_part()

    def convolve(c, _):
        rows = span_rows(c)
        fore = pl.ds(pl.multiple_of(c * SPAN, SPAN), SPAN + FRONT)
        hind = pl.ds(pl.multiple_of(c * SPAN, SPAN), SPAN + TILE)
        masks = [jnp.broadcast_to(marks_ref[hind, j : j + 1], (SPAN + TILE, LANES)) for j in range(RIM)]
        for k in range(CHANS // LANES):
            lanes = slice(k * LANES, (k + 1) * LANES)
            later = dtot_ref[hind, lanes]
            earlier = convp_ref[fore, lanes].astype(f32)
            own = later[0:SPAN]
            d_conv = taps_ref[RIM : RIM + 1, lanes] * own
            dtaps_ref[RIM : RIM + 1, lanes] += jnp.sum(own * earlier[FRONT:], axis=0, keepdims=True)
            dtaps_ref[CONV : CONV + 1, lanes] += jnp.sum(own, axis=0, keepdims=True)
            for j in range(RIM):
                lag = RIM - j
                seen = later * masks[j]
                d_conv = d_conv + taps_ref[j : j + 1, lanes] * seen[lag : lag + SPAN]
                dtaps_ref[j : j + 1, lanes] += jnp.sum(
                    seen[0:SPAN] * earlier[FRONT - lag : FRONT - lag + SPAN], axis=0, keepdims=True
                )
            dmain_ref[rows, lanes] = d_conv.astype(bf16)
        return 0

    lax.fori_loop(0, spans - 1, convolve, 0)
    rim.wait_recv()
    dtot_ref[pl.ds(spans * SPAN, TILE), :] = jnp.where(p == 0, rimr_ref[...], 0.0)
    lax.fori_loop(spans - 1, spans, convolve, 0)

    mixes.left()
    dpre_ref[...] = jnp.zeros_like(dpre_ref)

    def token_grad(block, keep):
        rows = block_rows(block, tokens)
        d_main = dmain_ref[rows, :]
        d_gate = dgate_ref[rows, :]
        hid = h_ref[rows, :].astype(f32)
        scale = lax.rsqrt(jnp.sum(hid * hid, axis=1, keepdims=True) / D + norm_eps)
        for k in range(D // 256):
            cols = slice(k * 256, (k + 1) * 256)
            part = dot(d_main, win_ref[cols, :], ((1,), (1,))) + dot(d_gate, wgate_ref[cols, :], ((1,), (1,)))
            dpre_ref[0:1, cols] += jnp.sum(h_ref[rows, cols].astype(f32) * scale * part, axis=0, keepdims=True)
            if keep:
                first = k * 256 // HALF * tokens
                y_ref[first : first + tokens, k * 256 % HALF : k * 256 % HALF + 256] = part
            else:
                mix_ref[rows, cols] = part.astype(bf16)

    def store_gate(i, value):
        kept = pl.ds(2 * SPAN + i * own_rows, own_rows)
        gate_ref[kept, :] = value
        copies.keep(gate_ref.at[kept], ggate_out.at[blocks[i][0], blocks[i][1]])

    def store_main(i, value):
        for first, count in ((0, HALF), (HALF, MAIN - HALF)):
            kept = pl.ds((first // HALF * TP + i) * own_rows, own_rows)
            gated_ref[kept, 0:count] = value[:, first : first + count]
            copies.keep(
                gated_ref.at[kept, pl.ds(0, count)], gmain_out.at[blocks[i][0], blocks[i][1], :, pl.ds(first, count)]
            )

    total = g_out.total(0)
    for k in range(D // HALF):
        kept = pl.ds(2 * TP * own_rows + k * out_rows, out_rows)
        gated_ref[kept, :] = total[:, k * HALF : (k + 1) * HALF]
        copies.keep(gated_ref.at[kept], gout_out.at[:, pl.ds(k * HALF, HALF)])
    g_out.left()
    gm_halves = [wout_ref.at[:, pl.ds(0, MAIN)], gm_ref]

    def grad_half(far):
        part = 1 - p if far else p
        out = gm_halves[0 if far else 1]

        def piece(i, _):
            xn = xn_ref[:, pl.ds(pl.multiple_of((part * 2 + i) * width, width), width)]
            rows = pl.ds(pl.multiple_of(i * width, width), width)
            for k in range(MAIN // 384):
                cols = slice(k * 384, (k + 1) * 384)
                out[rows, cols] = dot(xn, dmain_ref[:, cols], ((0,), (0,))).astype(bf16)
            return 0

        lax.fori_loop(0, 2, piece, 0)

    grad_half(True)
    g_main = GradientSum(copies, gm_halves, own_rows, gm_bufs, True)
    g_main.cores(0)
    dxs = GroupScatter(copies, mix_ref, dx_bufs)
    token_grad(blocks[3], False)
    dxs.to_t0(3)
    g_main.to_sides(0)
    token_grad(blocks[1], False)
    dxs.to_t0(1)
    grad_half(False)
    g_main.cores(1)
    g_main.to_part((1,))
    g_gate.to_group(store_gate)
    g_main.to_part((2,))
    g_main.to_sides(1)
    g_main.to_part((3,))

    mixer = mix_ref[mixes.block(0), :].astype(f32) + mixes.finish()
    copies.left([mixes.last_copy])
    for k in range(D // HALF):
        kept = pl.ds(spans * STATE + k * tokens, tokens)
        dn_ref[kept, :] = mixer[:, k * HALF : (k + 1) * HALF]
        copies.keep(dn_ref.at[kept], mixer_out.at[:, pl.ds(k * HALF, HALF)])
    hid = h_ref[mixes.block(0), :].astype(f32)
    valid = validc_ref[...]
    counts = [jnp.sum(valid * jnp.sum(v * v, axis=1, keepdims=True), axis=0, keepdims=True) for v in (hid, mixer)]
    counts.append(jnp.sum(valid, axis=0, keepdims=True))
    scalars = jnp.zeros((1, LANES), f32)
    for k in range(3):
        scalars = jnp.where(lane == k, counts[k], scalars)
    box = box_ref.at[0]
    box[...] = jnp.zeros_like(box)
    box[OWN_SUMS : OWN_SUMS + 1, :] = scalars

    token_grad(blocks[2], False)
    g_main.to_part((0,))
    dxs.to_t1()
    token_grad(blocks[0], True)

    for k in range(D // LANES):
        box[k : k + 1, :] = dpre_ref[0:1, k * LANES : (k + 1) * LANES]
    for k in range(HALF // LANES):
        lanes = slice(k * LANES, (k + 1) * LANES)
        box[OWN_NORM + k : OWN_NORM + k + 1, :] = dgain_ref[0:1, lanes]
        for j in range(CONV + 1):
            row = OWN_TAP + j * (HALF // LANES) + k
            box[row : row + 1, :] = dtaps_ref[j : j + 1, lanes]
    for k in range(SIDE // LANES):
        lanes = slice(HALF + k * LANES, HALF + (k + 1) * LANES)
        for j in range(CONV + 1):
            row = OWN_SIDE + j * (SIDE // LANES) + k
            box[row : row + 1, :] = dtaps_ref[j : j + 1, lanes]
    hsum_ref[0:1, :] = hsum_ref[0:1, :] * heads_ref[1:2, :]
    hsum_ref[2:3, :] = own_sums(dskip_ref[...])[0:1, :]
    lane8 = lax.broadcasted_iota(jnp.int32, (TILE, LANES), 1)
    box[OWN_HEAD : OWN_HEAD + 3, :] = jnp.where(lane8 < HEADS, head_lanes(hsum_ref[...], back=True), 0.0)[0:3]

    def small_step(k, hops):
        return [copies.send(box_ref.at[k], boxes_ref.at[k, i], flips) for i, flips in enumerate(hops)]

    def small_add(k, sent):
        total = box_ref[k]
        for i, copy in enumerate(sent):
            copy.wait_recv()
            total = total + boxes_ref[k, i]
        box_ref[k + 1] = total

    small = small_step(0, (CORE, SIDEWAYS, SIDE_CORE))
    g_gate.finish(store_gate)
    small_add(0, small)
    small = small_step(1, (PART,))
    small_add(1, small)
    small = small_step(2, (T0, T1, DIAG))
    g_main.to_group(store_main)
    dx = dxs.finish()
    for k in range(D // HALF):
        kept = pl.ds(k * tokens, tokens)
        y_ref[kept, :] += dx[:, k * HALF : (k + 1) * HALF]
        copies.keep(y_ref.at[kept], dx_out.at[:, pl.ds(k * HALF, HALF)])
    small_add(2, small)
    total_ref[...] = jnp.zeros_like(total_ref)
    total_ref[0:NORM_ROW, :] = box_ref[3, 0:NORM_ROW]
    third = QUARTER // LANES
    runs = [(OWN_NORM, NORM_ROW)]
    runs += [(OWN_TAP + j * 2 * third, TAP_ROW + j * TAP_ROWS) for j in range(CONV + 1)]
    for i, block in enumerate(blocks):
        source = box_ref.at[2] if i == 0 else boxes_ref.at[2, i - 1]
        place_at = (block[0] * 2 + block[1]) * third
        for own, first in runs:
            for k in range(2 * third):
                row = first + k // third * (D_INNER // 2 // LANES) + place_at + k % third
                total_ref[pl.ds(row, 1), :] = source[own + k : own + k + 1, :]
    for j in range(CONV + 1):
        row, own = TAP_ROW + TAP_ROWS * j + D_INNER // LANES, OWN_SIDE + j * (SIDE // LANES)
        total_ref[row : row + SIDE // LANES, :] = box_ref[3, own : own + SIDE // LANES]
    d_rate, d_shift, d_skip = (
        jnp.broadcast_to(box_ref[3, OWN_HEAD + k : OWN_HEAD + k + 1], (TILE, LANES)) for k in range(3)
    )
    spill = LANES - 2 * HEADS
    joined = d_shift + pltpu.roll(d_rate, HEADS, 1) + jnp.where(lane8 >= 2 * HEADS, pltpu.roll(d_skip, 2 * HEADS, 1), 0.0)
    total_ref[HEAD_ROW : HEAD_ROW + 1, :] = joined[0:1]
    spilled = jnp.where(lane8 < HEADS - spill, pltpu.roll(d_skip, LANES - spill, 1), 0.0)
    total_ref[HEAD_ROW + 1 : HEAD_ROW + 2, :] = spilled[0:1]
    total_ref[SMALL_ROWS : SMALL_ROWS + 1, :] = box_ref[3, OWN_SUMS : OWN_SUMS + 1]
    g_main.finish(store_main)
    copies.drain()


def update_kernel(
    hid_ref, mixer_ref, dx_ref, back_ref, gmain_ref, ggate_ref, gout_ref, total_ref,
    inw_ref, inm_ref, inv_ref, outw_ref, outm_ref, outv_ref, small_ref,
    output_ref, gh_ref, inm_out, inv_out, inw_out, outm_out, outv_out, outw_out, rms_ref,
):
    hid = hid_ref[...].astype(f32)
    output_ref[...] = (hid + mixer_ref[...]).astype(bf16)
    scale = lax.rsqrt(jnp.sum(hid * hid, axis=1, keepdims=True) / D + norm_eps)
    pulled = 0.0
    for k in range(NORM_ROW):
        lanes = slice(k * LANES, (k + 1) * LANES)
        d_pre = dx_ref[:, lanes] * small_ref[k : k + 1, :]
        gh_ref[:, lanes] = back_ref[:, lanes].astype(f32) + scale * d_pre
        pulled = pulled + jnp.sum(hid[:, lanes] * d_pre, axis=1, keepdims=True)
    gh_ref[...] -= hid * (pulled / D * (scale * scale * scale))

    def update(refs, outs, cols, grad, rate=0.02, decay=0.1):
        weight, moment, second = (ref[:, cols] for ref in refs)
        for out, value in zip(outs, adamw(weight, moment, second, grad, rate, decay)):
            out[:, cols] = value

    every = slice(None)
    update((outw_ref, outm_ref, outv_ref), (outm_out, outv_out, outw_out), every, gout_ref[...])
    in_refs, in_outs = (inw_ref, inm_ref, inv_ref), (inm_out, inv_out, inw_out)
    for j in range(TP):
        for k, chans in enumerate(own_chans(j)):
            part = slice(k * QUARTER, (k + 1) * QUARTER)
            update(in_refs, in_outs, chans, ggate_ref[j // 2, j % 2, :, part])
            scan = slice(D_INNER + chans.start, D_INNER + chans.stop)
            update(in_refs, in_outs, scan, gmain_ref[j // 2, j % 2, :, part])
    rest_grad = gmain_ref[0, 0, :, HALF:] + gmain_ref[0, 1, :, HALF:] + gmain_ref[1, 0, :, HALF:] + gmain_ref[1, 1, :, HALF:]
    first = 2 * D_INNER
    update(in_refs, in_outs, slice(first, first + SIDE), rest_grad[:, :SIDE])
    update(in_refs, in_outs, slice(first + SIDE, first + SIDE + HEADS), rest_grad[:, SIDE : SIDE + HEADS])

    @pl.when(pl.program_id(0) == 0)
    def _():
        totals = total_ref[SMALL_ROWS:, :]
        rms_ref[...] = jnp.sqrt(totals / (totals[0:1, 2:3] * D))


def linked(kernel, name, collective_id, in_specs, outs, scratch):
    return pl.pallas_call(
        kernel,
        name=name,
        grid=(1,),
        in_specs=in_specs,
        out_shape=tuple(o for o, _ in outs),
        out_specs=tuple(s for _, s in outs),
        scratch_shapes=scratch,
        compiler_params=pltpu.CompilerParams(
            collective_id=collective_id, has_side_effects=True, vmem_limit_bytes=VMEM_LIMIT
        ),
    )


def shards_linked(
    hidden, cotangent, segments, valid, in_w, in_m, in_v, out_w, out_m, out_v, small_w, small_m, small_v,
):
    own_rows, out_rows = in_w.shape[0], out_w.shape[0]
    tok_rows = hidden.shape[1]
    rows = tok_rows * TP
    spans = rows // SPAN
    small_size = small_w.shape[0]

    def small_box(array):
        return jnp.pad(array, (0, SMALL_ROWS * LANES - small_size)).reshape(SMALL_ROWS, LANES)

    small_rows = small_box(small_w)

    wide = (rows, D)
    half = (rows, HALF)
    lanes = (rows, LANES)
    side = (rows, STATE)
    state = (STATE, HALF)
    main_outs = (
        (shape((tok_rows, D), bf16), HBM),
        (shape((tok_rows, D), f32), HBM),
        (shape((2, 2, own_rows, HALF), f32), HBM),
        (shape((2, 2, own_rows, MAIN), f32), HBM),
        (shape((tok_rows, D), f32), HBM),
        (shape((out_rows, D), f32), HBM),
        (shape((BOX_ROWS, LANES), f32), VMEM),
    )
    main_scratch = (
        (wide, bf16),
        (wide, bf16),
        ((D, MAIN), bf16),
        ((rows + FRONT, CHANS), bf16),
        (half, bf16),
        (side, bf16),
        (side, bf16),
        ((rows + FRONT, CHANS), f32),
        (lanes, f32),
        (lanes, f32),
        (lanes, f32),
        (half, f32),
        ((spans, *state), f32),
        ((D, HALF), bf16),
        ((HALF, D), bf16),
        (wide, bf16),
        (half, bf16),
        (wide, bf16),
        (half, bf16),
        (half, bf16),
        ((rows, MAIN), bf16),
        ((TILE, HALF), f32),
        ((TILE, CHANS), f32),
        ((TILE, LANES), f32),
        ((TILE, HALF), f32),
        ((rows + TILE, TILE), f32),
        ((spans, LANES), f32),
        (state, f32),
        (state, bf16),
        (state, bf16),
        ((FRONT, CHANS), bf16),
        (half, f32),
        (half, f32),
        (half, f32),
        ((2, TILE, rows), f32),
        ((2, 3, TILE, rows), f32),
        (half, bf16),
        (state, bf16),
        (state, bf16),
        ((TILE, CHANS), f32),
        ((TILE, CHANS), f32),
        ((TILE, LANES), f32),
        ((TILE, HALF), f32),
        ((TILE, CHANS), f32),
        ((TILE, D), f32),
        ((4, OWN_ROWS, LANES), f32),
        ((3, 3, OWN_ROWS, LANES), f32),
        ((D // 2, MAIN), bf16),
        ((rows + 2 * FRONT, 1), f32),
        ((TILE, SPAN), f32),
        ((tok_rows, 1), f32),
    )
    side_cols = pl.BlockSpec((own_rows, MAIN - HALF), lambda i: (0, 2 * D_INNER // (MAIN - HALF)))
    back_own, mixer, g_gate, g_main, d_x_normed, g_out, totals = linked(
        functools.partial(main_kernel, spans), "main", 1, [*[HBM] * 4, side_cols, *[VMEM] * 3], main_outs,
        [
            *[pltpu.VMEM(dims, dtype) for dims, dtype in main_scratch],
            *sum_buffers(out_rows, D, False),
            *sum_buffers(own_rows, HALF, True),
            *sum_buffers(own_rows, MAIN, True),
            *scatter_buffers(tok_rows),
            *scatter_buffers(tok_rows),
            *sems(200, 48),
        ],
    )(hidden[0], in_w, out_w, cotangent[0], in_w, valid, small_rows, segments)

    steps = own_rows // (3 * TILE)

    def cut(dims, axis=0):
        block = tuple(size // steps if k == axis else size for k, size in enumerate(dims))
        return pl.BlockSpec(block, lambda i: tuple(i if k == axis else 0 for k in range(len(dims))))

    def fixed(dims):
        return pl.BlockSpec(dims, lambda i: (0, 0))

    tokens, matrix_in, matrix_out, small_dims = (tok_rows, D), in_w.shape, out_w.shape, (SMALL_ROWS, LANES)
    out_dims = [tokens] * 2 + [matrix_in] * 3 + [matrix_out] * 3
    (
        output, grad_hidden, in_m_new, in_v_new, in_w_new, out_m_new, out_v_new, out_w_new, rms,
    ) = pl.pallas_call(
        update_kernel,
        name="update",
        grid=(steps,),
        in_specs=[
            *[cut(tokens)] * 4,
            cut(g_main.shape, 2),
            cut(g_gate.shape, 2),
            cut(matrix_out),
            fixed((BOX_ROWS, LANES)),
            *[cut(matrix_in)] * 3,
            *[cut(matrix_out)] * 3,
            fixed(small_dims),
        ],
        out_shape=[
            *[shape(dims, bf16 if k == 0 else f32) for k, dims in enumerate(out_dims)],
            shape((TILE, LANES), f32),
        ],
        out_specs=[*[cut(dims) for dims in out_dims], fixed((TILE, LANES))],
        compiler_params=pltpu.CompilerParams(vmem_limit_bytes=VMEM_LIMIT),
    )(
        hidden[0], mixer, d_x_normed, back_own, g_main, g_gate, g_out, totals,
        in_w, in_m, in_v, out_w, out_m, out_v, small_rows,
    )
    small_grad = totals[:SMALL_ROWS].reshape(-1)[:small_size]
    small_m_new, small_v_new, small_w_new = adamw(small_w, small_m, small_v, small_grad, 0.2, 0.0)
    return (
        output[None], grad_hidden[None], in_m_new, in_v_new, in_w_new, out_m_new, out_v_new, out_w_new,
        small_m_new, small_v_new, small_w_new, rms[0, :2],
    )


def solution(mesh):
    seq, wt = mesh.shape["seq"], mesh.shape["wt"]
    split = Mesh(mesh.devices.reshape(seq // TP, 2, 2, wt // 2, 2), EVERYONE)
    streams = ("w1", "w0")
    tokens = ("part", "t1", "t0")
    matrix = P(EVERYONE, None)
    stream = P(streams, tokens, None)
    size = mesh.devices.size
    fits = seq == 2 * TP and wt == 4 and D // size % 16 == 0 and D_INNER // size % 16 == 0
    return jax.shard_map(
        shards_linked if fits else shards_general,
        mesh=split,
        in_specs=(
            stream, stream, P(streams, None), P(streams, tokens), matrix, matrix, matrix, matrix, matrix, matrix, P(), P(), P(),
        ),
        out_specs=(stream, stream, matrix, matrix, matrix, matrix, matrix, matrix, P(), P(), P(), P()),
        check_vma=False,
    )
```

```python
import functools

import jax
import jax.numpy as jnp
from jax import lax
from jax.experimental import pallas as pl
from jax.experimental.pallas import tpu as pltpu
from jax.sharding import Mesh
from jax.sharding import PartitionSpec as P

D = 1536
D_INNER = 3072
HEADS = 48
HEADDIM = 64
STATE = 128
CONV = 4
SPAN = 256
STEP = 4
CONVCH = 3328
TP = 4
RIM = CONV - 1
LANES = 128
HALF = D_INNER // TP
LOCAL_HEADS = HEADS // TP
PAIRS = LOCAL_HEADS // 2
SIDE = 2 * STATE
COL_SIDE = HALF
COL_DT = HALF + SIDE
COL_GATE = COL_DT + LANES
COLS = COL_GATE + HALF

bf16 = jnp.bfloat16
f32 = jnp.float32
exact_prec = lax.Precision.HIGHEST
norm_eps = 1e-05
adam_eps = 1e-08


def dot(a, b, dims=((1,), (0,)), precision=None):
    return lax.dot_general(a, b, (dims, ((), ())), precision=precision, preferred_element_type=f32)


def unpack_small(small):
    first = D
    second = first + D_INNER
    third = second + CONV * CONVCH
    fourth = third + CONVCH
    fifth = fourth + HEADS
    sixth = fifth + HEADS
    return (
        small[:first],
        small[first:second],
        small[second:third].reshape(CONV, CONVCH),
        small[third:fourth],
        small[fourth:fifth],
        small[fifth:sixth],
        small[sixth:],
    )


def adamw(weight, moment, second, grad, rate, decay):
    moment_new = 0.5 * moment + 0.5 * grad
    second_new = 0.5 * second + 0.5 * grad * grad
    first_hat = moment_new / (1.0 - 0.5**STEP)
    second_hat = second_new / (1.0 - 0.5**STEP)
    weight_new = weight - rate * (first_hat / (jnp.sqrt(second_hat) + adam_eps) + decay * weight)
    return (moment_new, second_new, weight_new)


def pair_cols(cols, h):
    lane = lax.broadcasted_iota(jnp.int32, (cols.shape[0], LANES), 1)
    return jnp.where(lane < HEADDIM, cols[:, h : h + 1], cols[:, h + 1 : h + 2])


def span_rows(c):
    return pl.ds(pl.multiple_of(c * SPAN, SPAN), SPAN)


def triangle_dot(mask, values):
    high = values.astype(bf16)
    rest = values - high.astype(f32)
    middle = rest.astype(bf16)
    low = (rest - middle.astype(f32)).astype(bf16)
    sums = dot(mask.astype(bf16), jnp.concatenate([high, middle, low], axis=1))
    width = values.shape[1]
    return sums[:, :width] + (sums[:, width : 2 * width] + sums[:, 2 * width :])


def span_decay(dt_ref, rate_ref, c, at=0):
    dt = dt_ref[span_rows(c), :]
    row = lax.broadcasted_iota(jnp.int32, (SPAN, SPAN), 0)
    col = lax.broadcasted_iota(jnp.int32, (SPAN, SPAN), 1)
    return dt, triangle_dot(row >= col, dt * rate_ref[at : at + 1, :])


def state_kernel(spans, x_ref, b_ref, dt_ref, rate_ref, keep_ref, carry_ref, s_ref, dec_ref):
    s_ref[...] = jnp.zeros_like(s_ref)
    dec_ref[...] = jnp.ones_like(dec_ref)

    def body(c, _):
        rows = span_rows(c)
        dt, cum = span_decay(dt_ref, rate_ref, c)
        last = cum[SPAN - 1 : SPAN, :]
        end_weight = jnp.exp(last - cum) * dt * keep_ref[rows, :]
        decay = jnp.exp(last) * carry_ref[pl.ds(c, 1), :]
        dec_ref[...] = dec_ref[...] * decay
        b = b_ref[rows, :]
        for p in range(PAIRS):
            lanes = slice(p * LANES, (p + 1) * LANES)
            xw = (x_ref[rows, lanes].astype(f32) * pair_cols(end_weight, 2 * p)).astype(bf16)
            fresh = dot(b, xw, ((0,), (0,)))
            s_ref[:, lanes] = s_ref[:, lanes] * pair_cols(decay, 2 * p) + fresh
        return 0

    lax.fori_loop(0, spans, body, 0)


def scan_kernel(
    spans, x_ref, b_ref, c_ref, dt_ref, rate_ref, segc_ref, segr_ref, keep_ref, inflow_ref, carry_ref, s_in_ref,
    y_ref, st_ref, s_ref,
):
    s_ref[...] = s_in_ref[...]

    def body(c, _):
        rows = span_rows(c)
        dt, cum = span_decay(dt_ref, rate_ref, c)
        last = cum[SPAN - 1 : SPAN, :]
        end_weight = jnp.exp(last - cum) * dt * keep_ref[rows, :]
        decay = jnp.exp(last) * carry_ref[pl.ds(c, 1), :]
        gain = jnp.exp(cum) * inflow_ref[rows, :]
        back_log = jnp.transpose(cum - jnp.log(dt))
        b = b_ref[rows, :]
        cc = c_ref[rows, :]
        scores = dot(cc, b, ((1,), (1,)))
        row = lax.broadcasted_iota(jnp.int32, (SPAN, SPAN), 0)
        col = lax.broadcasted_iota(jnp.int32, (SPAN, SPAN), 1)
        mask = (row >= col) & (segc_ref[rows, :] == segr_ref[pl.ds(c, 1), :])
        lane = lax.broadcasted_iota(jnp.int32, (SPAN, LANES), 1)
        st_ref[c] = s_ref[...]
        for p in range(PAIRS):
            lanes = slice(p * LANES, (p + 1) * LANES)
            x = x_ref[rows, lanes]
            parts = []
            for h in (2 * p, 2 * p + 1):
                gap = cum[:, h : h + 1] - back_log[h : h + 1, :]
                weights = scores * jnp.exp(jnp.where(mask, gap, -1e30))
                parts.append(dot(weights.astype(bf16), x))
            y = jnp.where(lane < HEADDIM, parts[0], parts[1])
            state = s_ref[:, lanes]
            y = y + dot(cc, state.astype(bf16)) * pair_cols(gain, 2 * p)
            y_ref[rows, lanes] = y
            xw = (x.astype(f32) * pair_cols(end_weight, 2 * p)).astype(bf16)
            s_ref[:, lanes] = state * pair_cols(decay, 2 * p) + dot(b, xw, ((0,), (0,)))
        return 0

    lax.fori_loop(0, spans, body, 0)


def state_back_kernel(spans, dy_ref, c_ref, dt_ref, rate_ref, inflow_ref, carry_ref, s_ref):
    s_ref[...] = jnp.zeros_like(s_ref)

    def body(step, _):
        c = spans - 1 - step
        rows = span_rows(c)
        dt, cum = span_decay(dt_ref, rate_ref, c)
        decay = jnp.exp(cum[SPAN - 1 : SPAN, :]) * carry_ref[pl.ds(c, 1), :]
        gain = jnp.exp(cum) * inflow_ref[rows, :]
        cc = c_ref[rows, :]
        for p in range(PAIRS):
            lanes = slice(p * LANES, (p + 1) * LANES)
            dyg = (dy_ref[rows, lanes].astype(f32) * pair_cols(gain, 2 * p)).astype(bf16)
            s_ref[:, lanes] = s_ref[:, lanes] * pair_cols(decay, 2 * p) + dot(cc, dyg, ((0,), (0,)))
        return 0

    lax.fori_loop(0, spans, body, 0)


def head_sums(values):
    width = values.shape[1]
    chan = lax.broadcasted_iota(jnp.int32, (width, LANES), 0)
    head = lax.broadcasted_iota(jnp.int32, (width, LANES), 1)
    pick = (chan // HEADDIM == head).astype(bf16)
    high = values.astype(bf16)
    low = (values - high.astype(f32)).astype(bf16)
    return dot(high, pick) + dot(low, pick)


def scan_back_kernel(
    spans, x_ref, b_ref, c_ref, dt_ref, ratio_ref, sig_ref, rate_ref, segc_ref, segr_ref, keep_ref, inflow_ref, carry_ref, skip_ref,
    y_ref, st_ref, dy_ref, ds_out_ref,
    dx_ref, db_ref, dc_ref, ddt_ref, drate_ref, dskip_ref,
    ds_ref, prod_ref,
):
    ds_ref[...] = ds_out_ref[...]
    drate_ref[...] = jnp.zeros_like(drate_ref)
    dskip_ref[...] = jnp.zeros_like(dskip_ref)

    def body(step, _):
        c = spans - 1 - step
        rows = span_rows(c)
        dt, cum = span_decay(dt_ref, rate_ref, c)
        last = cum[SPAN - 1 : SPAN, :]
        end_weight = jnp.exp(last - cum) * dt * keep_ref[rows, :]
        decay = jnp.exp(last) * carry_ref[pl.ds(c, 1), :]
        gain = jnp.exp(cum) * inflow_ref[rows, :]
        fore_log = jnp.transpose(cum)
        back_log = cum - jnp.log(dt)
        b = b_ref[rows, :]
        cc = c_ref[rows, :]
        scores = dot(b, cc, ((1,), (1,)))
        row = lax.broadcasted_iota(jnp.int32, (SPAN, SPAN), 0)
        col = lax.broadcasted_iota(jnp.int32, (SPAN, SPAN), 1)
        mask = (col >= row) & (segc_ref[rows, :] == segr_ref[pl.ds(c, 1), :])
        lane = lax.broadcasted_iota(jnp.int32, (SPAN, LANES), 1)
        d_scores = jnp.zeros((SPAN, SPAN), f32)
        db = jnp.zeros((SPAN, STATE), f32)
        dc = jnp.zeros((SPAN, STATE), f32)
        state_row = []
        dx_state_row = []
        for p in range(PAIRS):
            lanes = slice(p * LANES, (p + 1) * LANES)
            x = x_ref[rows, lanes]
            dy = dy_ref[rows, lanes]
            xf = x.astype(f32)
            dyf = dy.astype(f32)
            parts = []
            for k in range(2):
                h = 2 * p + k
                gap = fore_log[h : h + 1, :] - back_log[:, h : h + 1]
                decay_mat = jnp.exp(jnp.where(mask, gap, -1e30))
                weights = (scores * decay_mat).astype(bf16)
                parts.append(dot(weights, dy))
                own = (lane < HEADDIM) if k == 0 else (lane >= HEADDIM)
                d_weights = dot(jnp.where(own, xf, 0.0).astype(bf16), dy, ((1,), (1,)))
                d_scores = d_scores + d_weights * decay_mat
            dx = jnp.where(lane < HEADDIM, parts[0], parts[1])
            dyg = (dyf * pair_cols(gain, 2 * p)).astype(bf16)
            ew = pair_cols(end_weight, 2 * p)
            xw = (xf * ew).astype(bf16)
            state = st_ref[c, :, lanes]
            ds = ds_ref[:, lanes]
            state_b = state.astype(bf16)
            ds_b = ds.astype(bf16)
            dc = dc + dot(dyg, state_b, ((1,), (1,)))
            db = db + dot(xw, ds_b, ((1,), (1,)))
            dx_state = dot(b, ds_b) * ew
            dx = dx + dx_state
            dec = pair_cols(decay, 2 * p)
            state_row.append(jnp.sum(ds * state, axis=0, keepdims=True) * dec)
            dx_state_row.append(jnp.sum(dx_state * xf, axis=0, keepdims=True))
            ds_ref[:, lanes] = ds * dec + dot(cc, dyg, ((0,), (0,)))
            prod_ref[0:SPAN, lanes] = dyf * y_ref[rows, lanes]
            prod_ref[SPAN : 2 * SPAN, lanes] = xf * dx
            dskip_ref[0:1, lanes] += jnp.sum(dyf * xf, axis=0, keepdims=True)
            dx_ref[rows, lanes] = (dx + dyf * skip_ref[0:1, lanes]).astype(bf16)
        d_scores_b = d_scores.astype(bf16)
        db_ref[rows, :] = db + dot(d_scores_b, cc)
        dc_ref[rows, :] = dc + dot(d_scores_b, b, ((0,), (0,)))
        sums = head_sums(prod_ref[...])
        out_sum, in_sum = sums[:SPAN], sums[SPAN:]
        edge = jnp.concatenate(state_row, axis=1) + jnp.concatenate(dx_state_row, axis=1)
        edge_sum = head_sums(jnp.broadcast_to(edge, (8, HALF)))[0:1]
        at_last = lax.broadcasted_iota(jnp.int32, (SPAN, LANES), 0) == SPAN - 1
        d_cum = out_sum - in_sum + jnp.where(at_last, edge_sum, 0.0)
        d_log = triangle_dot(col >= row, d_cum)
        drate_ref[0:1, :] += jnp.sum(d_log * dt, axis=0, keepdims=True)
        ddt_ref[rows, :] = d_log * rate_ref[0:1, :] * sig_ref[rows, :] + in_sum * ratio_ref[rows, :]
        return 0

    lax.fori_loop(0, spans, body, 0)


GROUP = ("t1", "t0")
COPIES = ("part", "w1", "w0")
EVERYONE = ("part", "t1", "t0", "w1", "w0")


VMEM_LIMIT = 63 * 1024 * 1024


def in_vmem(kernel, out_shape, name, scratch=()):
    return pl.pallas_call(
        kernel,
        out_shape=out_shape,
        scratch_shapes=list(scratch),
        name=name,
        compiler_params=pltpu.CompilerParams(vmem_limit_bytes=VMEM_LIMIT),
    )


def shape(dims, dtype):
    return jax.ShapeDtypeStruct(dims, dtype)


def shift_part(array, by):
    size = lax.axis_size("part")
    pairs = [(i, i + by) for i in range(size) if 0 <= i + by < size]
    return lax.ppermute(array, "part", pairs)


def shards_general(
    hidden, cotangent, segments, valid, in_w, in_m, in_v, out_w, out_m, out_v, small_w, small_m, small_v,
):
    parts = lax.axis_size("part")
    wt = lax.axis_size("w1") * lax.axis_size("w0")
    part = lax.axis_index("part")
    tp = lax.axis_index("t1") * 2 + lax.axis_index("t0")
    own_rows = in_w.shape[0]
    out_rows = out_w.shape[0]
    resid = hidden[0].astype(f32)
    tok_rows = resid.shape[0]
    rows = tok_rows * TP
    spans = rows // SPAN
    seg_all = segments[0]
    pre_gain, norm_gain, conv_weight, conv_bias, dt_shift, a_logs, skips = unpack_small(small_w)

    def own_part(array, width):
        return lax.dynamic_slice_in_dim(array, tp * width, width, array.ndim - 1)

    in_copy = in_w.astype(bf16)
    slices = []
    for j in range(TP):
        slices.append(
            jnp.concatenate(
                [
                    in_copy[:, D_INNER + j * HALF : D_INNER + (j + 1) * HALF],
                    in_copy[:, 2 * D_INNER : 2 * D_INNER + SIDE],
                    in_copy[:, D_INNER + CONVCH + j * LOCAL_HEADS : D_INNER + CONVCH + (j + 1) * LOCAL_HEADS],
                    jnp.zeros((own_rows, LANES - LOCAL_HEADS), bf16),
                    in_copy[:, j * HALF : (j + 1) * HALF],
                ],
                axis=1,
            )
        )
    mine = lax.all_to_all(jnp.stack(slices), GROUP, 0, 0, tiled=False)
    w_in = lax.all_gather(mine, COPIES, axis=0, tiled=False)
    w_in = w_in.reshape(parts, wt, TP, own_rows, COLS).transpose(0, 2, 1, 3, 4).reshape(D, COLS)
    flat = [(i, (i % TP) * parts + i // TP) for i in range(parts * TP)]
    out_mine = lax.ppermute(out_w.astype(bf16), ("part", *GROUP), [(b, a) for a, b in flat])
    w_out = lax.all_gather(out_mine, COPIES, axis=0, tiled=True)

    hidden_all = lax.all_gather(hidden[0], GROUP, axis=0, tiled=True)
    back_mix = cotangent[0] * valid[0][:, None].astype(bf16)
    back_all = lax.all_gather(back_mix, GROUP, axis=0, tiled=True)

    hid = hidden_all.astype(f32)
    scale_all = lax.rsqrt(jnp.mean(hid * hid, axis=1, keepdims=True) + norm_eps)
    x_normed = (hid * scale_all * pre_gain).astype(bf16)
    projected = dot(x_normed, w_in)
    conv_in = projected[:, :COL_DT].astype(bf16)
    dt_raw = projected[:, COL_DT:COL_GATE].astype(bf16).astype(f32)
    gate_pre = projected[:, COL_GATE:]
    rim_in = shift_part(conv_in[rows - RIM :], 1)
    padded = jnp.concatenate([rim_in, conv_in], axis=0).astype(f32)
    seg_front = jnp.concatenate([jnp.full((RIM,), -1, jnp.int32), seg_all, jnp.full((RIM,), -1, jnp.int32)])
    seg_pad = lax.dynamic_slice_in_dim(seg_front, part * rows, rows + 2 * RIM)
    seg = seg_pad[RIM : RIM + rows]
    masks = [(seg_pad[k : k + rows] == seg).astype(f32)[:, None] for k in range(CONV)]
    taps = jnp.concatenate([own_part(conv_weight[:, :D_INNER], HALF), conv_weight[:, D_INNER:]], axis=1)
    bias = jnp.concatenate([own_part(conv_bias[:D_INNER], HALF), conv_bias[D_INNER:]])
    total = bias[None, :]
    for k in range(CONV):
        total = total + taps[k] * padded[k : k + rows] * masks[k]
    sig_total = jax.nn.sigmoid(total)
    activated = (total * sig_total).astype(bf16)
    x_scan = activated[:, :HALF]
    b_mat = activated[:, HALF : HALF + STATE]
    c_mat = activated[:, HALF + STATE :]

    def head_row(array):
        return jnp.pad(own_part(array, LOCAL_HEADS), (0, LANES - LOCAL_HEADS))

    shift_row = head_row(dt_shift)
    z = dt_raw + shift_row
    dt = jax.nn.softplus(z)
    sig_dt = jax.nn.sigmoid(z)
    ratio = jnp.where(dt > 1e-30, sig_dt / jnp.maximum(dt, 1e-30), 1.0)
    rate_row = -jnp.exp(head_row(a_logs))
    rate8 = jnp.broadcast_to(rate_row, (8, LANES))
    skip_chan = jnp.repeat(own_part(skips, LOCAL_HEADS), HEADDIM)
    skip8 = jnp.broadcast_to(skip_chan, (8, HALF))
    seg_spans = seg.reshape(spans, SPAN)
    seg_last = seg_spans[:, -1]
    seg_before = jnp.concatenate([seg_pad[RIM - 1 : RIM], seg_last[:-1]])
    keep = (seg_spans == seg_last[:, None]).astype(f32).reshape(rows, 1)
    inflow = (seg_spans == seg_before[:, None]).astype(f32).reshape(rows, 1)
    carry = jnp.broadcast_to((seg_last == seg_before).astype(f32)[:, None], (spans, LANES))
    seg_col = seg[:, None]

    state_shape = shape((STATE, HALF), f32)
    s_local, dec_total = in_vmem(
        functools.partial(state_kernel, spans), (state_shape, shape((8, LANES), f32)), "state"
    )(x_scan, b_mat, dt, rate8, keep, carry)
    dec_chan = jnp.repeat(dec_total[0, :LOCAL_HEADS], HEADDIM)
    s_in = jnp.zeros((STATE, HALF), f32)
    for _ in range(parts - 1):
        s_in = shift_part(dec_chan * s_in + s_local, 1)
    y_scan, states = in_vmem(
        functools.partial(scan_kernel, spans),
        (shape((rows, HALF), f32), shape((spans, STATE, HALF), f32)),
        "scan",
        [pltpu.VMEM((STATE, HALF), f32)],
    )(x_scan, b_mat, c_mat, dt, rate8, seg_col, seg_spans, keep, inflow, carry, s_in)
    y_b = (y_scan + skip_chan * x_scan.astype(f32)).astype(bf16).astype(f32)

    gain_own = own_part(norm_gain, HALF)
    sig_gate = jax.nn.sigmoid(gate_pre)
    silu_gate = gate_pre * sig_gate
    gated = y_b * silu_gate
    gate_sq = lax.psum(jnp.sum(gated * gated, axis=1), GROUP)
    scale_gate = lax.rsqrt(gate_sq / D_INNER + norm_eps)[:, None]
    normed = (gated * scale_gate * gain_own).astype(bf16)
    mixer = lax.psum_scatter(dot(normed, w_out), GROUP, scatter_dimension=0, tiled=True)
    output = (resid + mixer).astype(bf16)
    valid_rows = valid[0].astype(f32)
    res_sq = jnp.sum(valid_rows * jnp.sum(resid * resid, axis=1))
    mix_sq = jnp.sum(valid_rows * jnp.sum(mixer * mixer, axis=1))
    valid_count = jnp.sum(valid_rows)

    d_normed = dot(back_all, w_out, ((1,), (1,)))
    g_out = dot(normed, back_all, ((0,), (0,)))
    g_out = lax.psum_scatter(g_out, COPIES, scatter_dimension=0, tiled=True)
    g_out = lax.ppermute(g_out, ("part", *GROUP), flat)
    d_gain = d_normed * gain_own
    gate_dot = lax.psum(jnp.sum(gated * d_gain, axis=1), GROUP)
    d_gated = scale_gate * d_gain - gated * (scale_gate**3 * (gate_dot / D_INNER)[:, None])
    d_norm_gain = jnp.sum(gated * scale_gate * d_normed, axis=0)
    dy = (d_gated * silu_gate).astype(bf16)
    d_gate = d_gated * y_b * (sig_gate * (1.0 + gate_pre * (1.0 - sig_gate)))

    ds_local = in_vmem(functools.partial(state_back_kernel, spans), state_shape, "state_back")(
        dy, c_mat, dt, rate8, inflow, carry
    )
    ds_out = jnp.zeros((STATE, HALF), f32)
    for _ in range(parts - 1):
        ds_out = shift_part(dec_chan * ds_out + ds_local, -1)
    d_x, d_b, d_c, d_dt, d_rate, d_skip = in_vmem(
        functools.partial(scan_back_kernel, spans),
        (
            shape((rows, HALF), bf16),
            shape((rows, STATE), f32),
            shape((rows, STATE), f32),
            shape((rows, LANES), f32),
            shape((8, LANES), f32),
            shape((8, HALF), f32),
        ),
        "scan_back",
        [pltpu.VMEM((STATE, HALF), f32), pltpu.VMEM((2 * SPAN, HALF), f32)],
    )(x_scan, b_mat, c_mat, dt, ratio, sig_dt, rate8, seg_col, seg_spans, keep, inflow, carry, skip8, y_scan, states, dy, ds_out)

    d_total = jnp.concatenate([d_x.astype(f32), d_b, d_c], axis=1) * (sig_total * (1.0 + total * (1.0 - sig_total)))
    rim_back = shift_part(d_total[:RIM], -1)
    d_padded = jnp.concatenate([d_total, rim_back], axis=0)
    d_conv_in = 0.0
    for k in range(CONV):
        later = (seg_pad[2 * RIM - k : 2 * RIM - k + rows] == seg).astype(f32)[:, None]
        d_conv_in = d_conv_in + taps[k] * d_padded[RIM - k : RIM - k + rows] * later
    d_taps = jnp.stack([jnp.sum(d_total * padded[k : k + rows] * masks[k], axis=0) for k in range(CONV)])
    d_bias = jnp.sum(d_total, axis=0)
    d_proj = jnp.concatenate([d_conv_in, d_dt, d_gate], axis=1).astype(bf16)
    d_x_normed = dot(d_proj, w_in, ((1,), (1,)))
    d_x_normed = lax.psum_scatter(d_x_normed, GROUP, scatter_dimension=0, tiled=True)
    g_in = dot(x_normed, d_proj, ((0,), (0,)))
    g_in = g_in.reshape(parts, TP, wt, own_rows, COLS).transpose(0, 2, 1, 3, 4).reshape(parts * wt, TP, own_rows, COLS)
    g_in = lax.psum_scatter(g_in, COPIES, scatter_dimension=0, tiled=False)
    g_in = lax.all_to_all(g_in, GROUP, 0, 0, tiled=False)
    g_in = jnp.concatenate(
        [g_in[j, :, COL_GATE:] for j in range(TP)]
        + [g_in[j, :, :HALF] for j in range(TP)]
        + [jnp.sum(g_in[:, :, COL_SIDE:COL_DT], axis=0)]
        + [g_in[j, :, COL_DT : COL_DT + LOCAL_HEADS] for j in range(TP)],
        axis=1,
    )

    scale_own = lax.rsqrt(jnp.mean(resid * resid, axis=1, keepdims=True) + norm_eps)
    d_pre = d_x_normed * pre_gain
    dot_pre = jnp.mean(resid * d_pre, axis=1, keepdims=True)
    grad_hidden = back_mix.astype(f32) + scale_own * d_pre - resid * (scale_own**3 * dot_pre)
    d_pre_gain = jnp.sum(resid * scale_own * d_x_normed, axis=0)

    def placed(values, width):
        spread = (jnp.arange(TP) == tp).astype(f32)[:, None] * values[..., None, :]
        return spread.reshape(*values.shape[:-1], TP * width)

    d_weight = jnp.concatenate([placed(d_taps[:, :HALF], HALF), d_taps[:, HALF:]], axis=1)
    small_grad = jnp.concatenate(
        [
            d_pre_gain,
            placed(d_norm_gain, HALF),
            d_weight.reshape(-1),
            placed(d_bias[:HALF], HALF),
            d_bias[HALF:],
            placed(jnp.sum(d_dt, axis=0)[:LOCAL_HEADS], LOCAL_HEADS),
            placed((d_rate[0] * rate_row)[:LOCAL_HEADS], LOCAL_HEADS),
            placed(jnp.sum(d_skip[0].reshape(LOCAL_HEADS, HEADDIM), axis=1), LOCAL_HEADS),
            jnp.stack([res_sq, mix_sq, valid_count]),
        ]
    )
    small_total = lax.psum(small_grad, EVERYONE)
    res_total, mix_total, count_total = small_total[-3], small_total[-2], small_total[-1]
    in_m_new, in_v_new, in_w_new = adamw(in_w, in_m, in_v, g_in, 0.02, 0.1)
    out_m_new, out_v_new, out_w_new = adamw(out_w, out_m, out_v, g_out, 0.02, 0.1)
    small_m_new, small_v_new, small_w_new = adamw(small_w, small_m, small_v, small_total[:-3], 0.2, 0.0)
    rms = jnp.stack([jnp.sqrt(res_total / (count_total * D)), jnp.sqrt(mix_total / (count_total * D))])
    return (
        output[None], grad_hidden[None], in_m_new, in_v_new, in_w_new, out_m_new, out_v_new, out_w_new,
        small_m_new, small_v_new, small_w_new, rms,
    )


MESH = pl.DeviceIdType.MESH
T0, T1, DIAG, CORE, SIDEWAYS, PART = ("t0",), ("t1",), ("t1", "t0"), ("w0",), ("w1",), ("part",)
SIDE_CORE = ("w1", "w0")
HOPS = (None, T0, T1, DIAG)
HBM = pl.BlockSpec(memory_space=pl.ANY)
VMEM = pl.BlockSpec(memory_space=pltpu.VMEM)
MAIN = COL_GATE
CHANS = HALF + SIDE
FRONT = 16
TILE = 8
QUARTER = HALF // 2
NORM_ROW = D // LANES
TAP_ROW = NORM_ROW + D_INNER // LANES
TAP_ROWS = CONVCH // LANES
HEAD_ROW = TAP_ROW + (CONV + 1) * TAP_ROWS
SMALL_ROWS = HEAD_ROW + 2
BOX_ROWS = SMALL_ROWS + 8
OWN_NORM = NORM_ROW
OWN_TAP = OWN_NORM + HALF // LANES
OWN_SIDE = OWN_TAP + (CONV + 1) * (HALF // LANES)
OWN_HEAD = OWN_SIDE + (CONV + 1) * (SIDE // LANES)
OWN_SUMS = OWN_HEAD + 3
OWN_ROWS = 64


def place():
    return tuple(lax.axis_index(a) for a in EVERYONE)


def across(flips):
    return {a: 1 - lax.axis_index(a) for a in flips}


def group_blocks():
    _, t1, t0, _, _ = place()
    return [(t1, t0), (t1, 1 - t0), (1 - t1, t0), (1 - t1, 1 - t0)]


def greet(neighbours):
    barrier = pltpu.get_barrier_semaphore()
    for flips in neighbours:
        pl.semaphore_signal(barrier, inc=1, device_id=across(flips), device_id_type=MESH)


def greeted(neighbours):
    pl.semaphore_wait(pltpu.get_barrier_semaphore(), len(neighbours))


class Copies:
    def __init__(self, local_sem, send_sem, recv_sem):
        self.local_sem, self.send_sem, self.recv_sem = local_sem, send_sem, recv_sem
        self.sent, self.kept, self.in_flight, self.on_device = 0, 0, [], []

    def send(self, src, dst, flips):
        copy = pltpu.make_async_remote_copy(
            src_ref=src,
            dst_ref=dst,
            send_sem=self.send_sem.at[self.sent],
            recv_sem=self.recv_sem.at[self.sent],
            device_id=across(flips),
            device_id_type=MESH,
        )
        copy.start()
        self.sent += 1
        self.in_flight.append(copy)
        return copy

    def keep(self, src, dst):
        copy = pltpu.make_async_copy(src, dst, self.local_sem.at[self.kept])
        copy.start()
        self.kept += 1
        self.on_device.append(copy)
        return copy

    def settle(self, copy):
        copy.wait()
        self.on_device = [other for other in self.on_device if other is not copy]

    def left(self, copies):
        for copy in copies:
            copy.wait_send()
            self.in_flight = [other for other in self.in_flight if other is not copy]

    def drain(self):
        for copy in self.in_flight:
            copy.wait_send()
        for copy in self.on_device:
            copy.wait()
        self.in_flight, self.on_device = [], []


def sems(remote, local=1):
    return [
        pltpu.SemaphoreType.DMA((local,)),
        pltpu.SemaphoreType.DMA((remote,)),
        pltpu.SemaphoreType.DMA((remote,)),
    ]


class GroupGather:
    def __init__(self, copies, src, dst):
        self.copies, self.dst = copies, dst
        self.rows = src.shape[0]
        self.halves = (0, self.rows // 2)
        own = group_blocks()[0]
        self.src, self.own, self.size = src, copies.keep(src, self.at(own, 0, self.rows)), self.rows // 2
        self.along_t1, self.along_t0, self.diagonal = self.start(T1), [], []

    def start(self, flips):
        own = group_blocks()[0]
        return [
            self.copies.send(self.src.at[pl.ds(h, self.size)], self.at(own, h, self.size), flips) for h in self.halves
        ]

    def start_t0(self):
        self.along_t0 = self.start(T0)

    def at(self, block, first, size):
        return self.dst.at[pl.ds(pl.multiple_of((block[0] * 2 + block[1]) * self.rows + first, size), size)]

    def hand_on(self):
        beside = group_blocks()[2]
        for copy, h in zip(self.along_t1, self.halves):
            copy.wait_recv()
            here = self.at(beside, h, self.rows // 2)
            self.diagonal.append(self.copies.send(here, here, T0))

    def finish(self):
        for copy in self.along_t0 + self.diagonal:
            copy.wait_recv()


class WeightGather:
    def __init__(self, copies, dst, rows, group):
        self.copies, self.dst, self.rows, self.group = copies, dst, rows, group
        self.by_part, self.by_side, self.by_core = [], [], []

    def at(self, part, w1, w0, block):
        index = part
        if self.group:
            index = (index * 2 + block[0]) * 2 + block[1]
        index = (index * 2 + w1) * 2 + w0
        return self.dst.at[pl.ds(pl.multiple_of(index * self.rows, self.rows), self.rows)]

    def mine(self, block):
        p, _, _, w1, w0 = place()
        return self.at(p, w1, w0, block)

    def spread(self, src, block):
        dst = self.mine(block)
        self.by_part.append((self.copies.send(src, dst, PART), block))
        self.by_side.append((self.copies.send(src, dst, SIDEWAYS), block))
        self.by_core.append(self.copies.send(src, dst, CORE))

    def swap(self, src):
        own, *others = group_blocks()

        def slice_of(block):
            return src.at[block_rows(block, self.rows)]

        self.swaps = [(self.copies.send(slice_of(b), self.mine(own), flips), b) for b, flips in zip(others, HOPS[1:])]
        self.kept = self.copies.keep(slice_of(own), self.mine(own))
        self.spread(slice_of(own), own)

    def spread_swapped(self):
        for copy, block in self.swaps:
            copy.wait_recv()
            self.spread(self.mine(block), block)

    def pass_core(self, part, w1, block):
        here = self.at(part, w1, lax.axis_index("w0"), block)
        self.by_core.append(self.copies.send(here, here, CORE))

    def hand_on(self):
        p, _, _, w1, w0 = place()
        self.again = []
        for (copy, block), (side, _) in zip(self.by_part, self.by_side):
            side.wait_recv()
            self.pass_core(p, 1 - w1, block)
            copy.wait_recv()
            here = self.at(1 - p, w1, w0, block)
            self.again.append((self.copies.send(here, here, SIDEWAYS), block))
            self.pass_core(1 - p, w1, block)

    def hand_on_last(self):
        p, _, _, w1, _ = place()
        for copy, block in self.again:
            copy.wait_recv()
            self.pass_core(1 - p, 1 - w1, block)

    def finish(self):
        for copy in self.by_core:
            copy.wait_recv()


class GradientSum:
    def __init__(self, copies, srcs, rows, bufs, group):
        self.copies, self.srcs, self.rows, self.group = copies, srcs, rows, group
        self.core, self.sides, self.fars = bufs[:3]
        self.lasts = bufs[3] if group else None
        self.blocks = group_blocks() if group else [()]
        self.order = (1, 2, 3, 0) if group else (0,)
        p, _, _, w1, _ = place()
        self.parts, self.sides_of = (1 - p, p), (1 - w1, w1)
        self.core_copies, self.side_copies, self.far_copies, self.last_copies = {}, {}, {}, {}

    def at(self, block, side, w0):
        index = block[0] * 2 + block[1] if self.group else 0
        index = (index * 2 + side) * 2 + w0
        return pl.ds(pl.multiple_of(index * self.rows, self.rows), self.rows)

    def place(self, i, j):
        return self.at(self.blocks[i], self.sides_of[j], lax.axis_index("w0"))

    def pass_on(self, k, i, j, value, dst, flips):
        here = self.place(i, j)
        self.srcs[k][here, :] = value.astype(bf16)
        return self.copies.send(self.srcs[k].at[here], dst, flips)

    def added(self, k, i, j, *more):
        q, block, side = self.parts[k], self.blocks[i], self.sides_of[j]
        self.core_copies[k, i, j].wait_recv()
        value = self.srcs[k][self.place(i, j), :].astype(f32)
        value = value + self.core[(q, side, *block)].astype(f32)
        for other in more:
            value = value + other.astype(f32)
        return value

    def cores(self, k):
        w0 = lax.axis_index("w0")
        for j in range(2):
            for i in self.order:
                q, block, side = self.parts[k], self.blocks[i], self.sides_of[j]
                src = self.srcs[k].at[self.at(block, side, 1 - w0)]
                self.core_copies[k, i, j] = self.copies.send(src, self.core.at[(q, side, *block)], CORE)

    def left(self):
        for copies in (self.core_copies, self.side_copies, self.far_copies, self.last_copies):
            self.copies.left(copies.values())

    def to_sides(self, k):
        for i in self.order:
            self.side_copies[k, i] = self.pass_on(k, i, 0, self.added(k, i, 0), self.sides.at[k, i], SIDEWAYS)

    def to_part(self, which=None):
        for i in self.order if which is None else which:
            self.side_copies[0, i].wait_recv()
            value = self.added(0, i, 1, self.sides[0, i])
            self.far_copies[i] = self.pass_on(0, i, 1, value, self.fars.at[i], PART)

    def total(self, i):
        self.side_copies[1, i].wait_recv()
        self.far_copies[i].wait_recv()
        return self.added(1, i, 1, self.sides[1, i], self.fars[i])

    def to_group(self, store):
        for i in self.order:
            value = self.total(i)
            if i == 0:
                store(0, value)
            else:
                self.last_copies[i] = self.pass_on(1, i, 1, value, self.lasts.at[i - 1], HOPS[i])

    def finish(self, store):
        for i, copy in self.last_copies.items():
            copy.wait_recv()
            store(i, self.lasts[i - 1].astype(f32))


class GroupScatter:
    def __init__(self, copies, src, bufs):
        self.copies, self.src = copies, src
        self.here, self.pass_on, self.last = bufs
        self.rows = self.here.shape[0]

    def block(self, i):
        return block_rows(group_blocks()[i], self.rows)

    def left(self):
        self.copies.left([self.own_copy, self.pass_copy])

    def to_t0(self, i):
        copy = self.copies.send(self.src.at[self.block(i)], self.here if i == 1 else self.pass_on, T0)
        if i == 1:
            self.own_copy = copy
        else:
            self.pass_copy = copy

    def to_t1(self):
        self.pass_copy.wait_recv()
        here = self.block(2)
        self.src[here, :] = (self.src[here, :].astype(f32) + self.pass_on[...].astype(f32)).astype(bf16)
        self.last_copy = self.copies.send(self.src.at[here], self.last, T1)

    def finish(self):
        self.own_copy.wait_recv()
        self.last_copy.wait_recv()
        return self.here[...].astype(f32) + self.last[...].astype(f32)


def scatter_buffers(rows):
    return [pltpu.VMEM((rows, D), bf16)] * 3


def sum_buffers(rows, cols, group):
    buf = lambda *lead: pltpu.VMEM((*lead, rows, cols), bf16)
    if not group:
        return [buf(2, 2), buf(2, 1), buf(1)]
    return [buf(2, 2, 2, 2), buf(2, 4), buf(4), buf(3)]


def block_rows(block, size):
    return pl.ds(pl.multiple_of((block[0] * 2 + block[1]) * size, size), size)


def lane_of(h):
    return h if h < LOCAL_HEADS // 2 else h + HEADS // 2 - LOCAL_HEADS // 2


def own_pair(cols, h):
    lane = lax.broadcasted_iota(jnp.int32, (cols.shape[0], LANES), 1)
    first, second = lane_of(h), lane_of(h + 1)
    return jnp.where(lane < HEADDIM, cols[:, first : first + 1], cols[:, second : second + 1])


def own_sums(values):
    width = values.shape[1]
    head = lax.broadcasted_iota(jnp.int32, (width, LANES), 0) // HEADDIM
    lane = lax.broadcasted_iota(jnp.int32, (width, LANES), 1)
    pick = (jnp.where(head < LOCAL_HEADS // 2, head, head + lane_of(LOCAL_HEADS) - LOCAL_HEADS) == lane).astype(bf16)
    high = values.astype(bf16)
    low = (values - high.astype(f32)).astype(bf16)
    return dot(high, pick) + dot(low, pick)


def head_lanes(values, back=False):
    first = (lax.axis_index("t1") * 2 + lax.axis_index("t0")) * (LOCAL_HEADS // 2)
    return pltpu.roll(values, first if back else LANES - first, 1)


def own_row(first, k):
    tp = lax.axis_index("t1") * 2 + lax.axis_index("t0")
    third = QUARTER // LANES
    return pl.ds(first + (k // third) * (D_INNER // 2 // LANES) + tp * third + k % third, 1)


def own_chans(j):
    return [slice(first + j * QUARTER, first + (j + 1) * QUARTER) for first in (0, D_INNER // 2)]


EVERY_NEIGHBOUR = (T0, T1, DIAG, CORE, SIDEWAYS, SIDE_CORE, PART)


def main_kernel(
    spans, hid_ref, inw_hbm, outw_hbm, cot_hbm, inside_ref, valid_ref, small_ref, segs_ref,
    cotv_out, mixer_out, ggate_out, gmain_out, dx_out, gout_out, total_ref,
    h_ref, xn_ref, win_ref, convp_ref, x_ref, b_ref, c_ref, dtot_ref, dt_ref, z_ref, cum_ref, y_ref, st_ref,
    wgate_ref, wout_ref, back_ref, normed_ref, mix_ref, dy_ref, dgate_ref, dmain_ref, dgain_ref, taps_ref, heads_ref, chans_ref,
    marks_ref, carry_ref, s_ref, pass_ref, got_ref, rim_ref, gated_ref, gate_ref, dn_ref,
    stat_ref, stats_ref, dyg_ref, passb_ref, gotb_ref, rims_ref, rimr_ref, hsum_ref, dskip_ref, dtaps_ref,
    dpre_ref, box_ref, boxes_ref, gm_ref, segc_ref, segr_ref, validc_ref,
    *rest,
):
    go_bufs, gg_bufs, gm_bufs, mix_bufs, dx_bufs = rest[:3], rest[3:7], rest[7:11], rest[11:14], rest[14:17]
    local_sem, send_sem, recv_sem = rest[17:]
    greet(EVERY_NEIGHBOUR)
    p, _, _, _, _ = place()
    rows_all = spans * SPAN
    tokens = hid_ref.shape[0]
    own_rows, out_rows = inw_hbm.shape[0], outw_hbm.shape[0]
    lane = lax.broadcasted_iota(jnp.int32, (1, LANES), 1)
    wm_ref = dmain_ref.at[pl.ds(0, TP * own_rows)]
    wg_ref = dgate_ref.at[pl.ds(0, TP * own_rows)]
    wo_ref = mix_ref.at[pl.ds(0, out_rows)]
    cotv_ref = mix_ref.at[pl.ds(tokens, tokens)]
    dxi_ref, prod_ref = gated_ref, gate_ref

    def side_at(c, which):
        return (slice(spans * STATE, spans * STATE + SPAN), pl.ds(pl.multiple_of((which * spans + c) * STATE, STATE), STATE))


    copies = Copies(local_sem, send_sem, recv_sem)
    loads = [
        copies.keep(inw_hbm.at[:, pl.ds(k * HALF, HALF)], gate_ref.at[pl.ds(k * own_rows, own_rows)])
        for k in range(2 * D_INNER // HALF)
    ]
    loads += [
        copies.keep(outw_hbm.at[:, pl.ds(k * HALF, HALF)], dn_ref.at[pl.ds(k * out_rows, out_rows)]) for k in range(D // HALF)
    ]
    loads.append(copies.keep(cot_hbm, cotv_ref))

    side = inside_ref[:, 0 : SIDE + HEADS]
    dt_cols = jnp.concatenate([side[:, SIDE:], jnp.zeros((own_rows, LANES - HEADS), f32)], axis=1)
    for copy in loads:
        copies.settle(copy)

    def master(first):
        return gate_ref[first // HALF * own_rows : (first // HALF + 1) * own_rows, first % HALF : first % HALF + QUARTER]

    for j in range(TP):
        at = slice(j * own_rows, (j + 1) * own_rows)
        for k, chans in enumerate(own_chans(j)):
            part = slice(k * QUARTER, (k + 1) * QUARTER)
            wg_ref[at, part] = master(chans.start).astype(bf16)
            wm_ref[at, part] = master(D_INNER + chans.start).astype(bf16)
        wm_ref[at, HALF:CHANS] = side[:, :SIDE].astype(bf16)
        dt_own = (lane % (HEADS // 2) // (LOCAL_HEADS // 2) == j) & (lane < HEADS)
        wm_ref[at, CHANS:MAIN] = jnp.where(dt_own, dt_cols, 0.0).astype(bf16)
    for k in range(D // HALF):
        wo_ref[:, k * HALF : (k + 1) * HALF] = dn_ref[k * out_rows : (k + 1) * out_rows, :].astype(bf16)

    greeted(EVERY_NEIGHBOUR)
    mains = WeightGather(copies, win_ref, own_rows, True)
    mains.swap(wm_ref)
    hids = GroupGather(copies, hid_ref, h_ref)
    hids.start_t0()

    def column(row):
        return jnp.transpose(jnp.broadcast_to(row, (LANES, SPAN)))[:, 0:1]

    for c in range(spans):
        row = segs_ref[0:1, pl.ds(pl.multiple_of(p * rows_all + c * SPAN, LANES), SPAN)].astype(f32)
        segr_ref[c : c + 1, :] = row
        segc_ref[FRONT + c * SPAN : FRONT + (c + 1) * SPAN, :] = column(row)
    around = rows_all - SPAN
    row = segs_ref[0:1, pl.ds(pl.multiple_of(p * around, LANES), SPAN)].astype(f32)
    segc_ref[0:FRONT, :] = jnp.where(p == 1, column(row)[SPAN - FRONT :], -1.0)
    row = segs_ref[0:1, pl.ds(pl.multiple_of(rows_all + p * around, LANES), SPAN)].astype(f32)
    segc_ref[FRONT + rows_all :, :] = jnp.where(p == 0, column(row)[0:FRONT], -1.0)
    stat_ref[0] = jnp.zeros_like(stat_ref[0])
    stat_ref[0, 0:1, 0:tokens] = valid_ref[...].astype(f32)
    validc_ref[...] = column(stat_ref[0, 0:1, 0:SPAN])[0:tokens]
    cotv_ref[...] = (cotv_ref[...].astype(f32) * validc_ref[...]).astype(bf16)
    copies.keep(cotv_ref, cotv_out)

    for k in range(HALF // LANES):
        lanes = slice(k * LANES, (k + 1) * LANES)
        chans_ref[1:2, lanes] = small_ref[own_row(NORM_ROW, k), :]
        for j in range(CONV + 1):
            taps_ref[j : j + 1, lanes] = small_ref[own_row(TAP_ROW + TAP_ROWS * j, k), :]
    for k in range(SIDE // LANES):
        lanes = slice(HALF + k * LANES, HALF + (k + 1) * LANES)
        for j in range(CONV + 1):
            row = TAP_ROW + TAP_ROWS * j + D_INNER // LANES + k
            taps_ref[j : j + 1, lanes] = small_ref[row : row + 1, :]
    head_row = jnp.broadcast_to(small_ref[HEAD_ROW : HEAD_ROW + 1, :], (TILE, LANES))
    next_row = jnp.broadcast_to(small_ref[HEAD_ROW + 1 : HEAD_ROW + 2, :], (TILE, LANES))
    a_log = pltpu.roll(head_row, LANES - HEADS, 1)
    lane8 = lax.broadcasted_iota(jnp.int32, (TILE, LANES), 1)
    spill = LANES - 2 * HEADS
    skip = jnp.where(lane8 < spill, pltpu.roll(head_row, spill, 1), pltpu.roll(next_row, spill, 1))
    own = lane8 < HEADS
    heads_ref[0:1, :] = head_lanes(jnp.where(own, head_row, 0.0))[0:1]
    heads_ref[1:2, :] = -jnp.exp(head_lanes(jnp.where(own, a_log, 0.0))[0:1])
    skip = head_lanes(jnp.where(own, skip, 0.0))[0:1]
    for q in range(PAIRS):
        chans_ref[0:1, q * LANES : (q + 1) * LANES] = own_pair(skip, 2 * q)

    def mark(first, count):
        seg = segc_ref[pl.ds(first, FRONT + count), :]
        here = seg[FRONT:]
        last = seg[FRONT + count - 1 :]
        before = seg[FRONT - 1 : FRONT]
        cols = {k: seg[FRONT - RIM + k : FRONT - RIM + k + count] == here for k in range(RIM)}
        cols[6], cols[7] = here == last, here == before
        lane_m = lax.broadcasted_iota(jnp.int32, (count, TILE), 1)
        marks = jnp.zeros((count, TILE), f32)
        for k, col in cols.items():
            marks = jnp.where(lane_m == k, jnp.where(col, 1.0, 0.0), marks)
        marks_ref[pl.ds(first, count), :] = marks
        return jnp.broadcast_to(jnp.where(last == before, 1.0, 0.0), (1, LANES))

    for c in range(spans):
        carry_ref[c : c + 1, :] = mark(c * SPAN, SPAN)
    mark(rows_all, TILE)
    blocks = group_blocks()

    def norm(block):
        rows = block_rows(block, tokens)
        hid = h_ref[rows, :].astype(f32)
        scale = lax.rsqrt(jnp.sum(hid * hid, axis=1, keepdims=True) / D + norm_eps)
        for k in range(D // LANES):
            lanes = slice(k * LANES, (k + 1) * LANES)
            xn_ref[rows, lanes] = (h_ref[rows, lanes].astype(f32) * scale * small_ref[k : k + 1, :]).astype(bf16)

    mains.spread_swapped()
    copies.settle(hids.own)
    norm(blocks[0])
    gates = WeightGather(copies, wgate_ref, own_rows, True)
    gates.swap(wg_ref)
    hids.hand_on()
    norm(blocks[2])
    mains.hand_on()
    gates.spread_swapped()
    outs = WeightGather(copies, wout_ref, out_rows, False)
    outs.spread(wo_ref, ())
    outs_kept = copies.keep(wo_ref, outs.mine(()))
    hids.finish()
    cots = GroupGather(copies, cotv_ref, back_ref)
    cots.start_t0()
    norm(blocks[1])
    norm(blocks[3])
    mains.hand_on_last()
    mains.finish()
    copies.settle(mains.kept)

    def project(c, _):
        rows = span_rows(c)
        xn = xn_ref[rows, :]
        at = pl.ds(pl.multiple_of(FRONT + c * SPAN, FRONT), SPAN)
        for k in range(CHANS // 256):
            cols = slice(k * 256, (k + 1) * 256)
            convp_ref[at, cols] = dot(xn, win_ref[:, cols]).astype(bf16)
        dt_raw = dot(xn, win_ref[:, CHANS:MAIN]).astype(bf16).astype(f32)
        z = head_lanes(dt_raw) + heads_ref[0:1, :]
        z_ref[rows, :] = z
        small = jnp.exp(-jnp.abs(z))
        one_more = 1.0 + small
        is_one = one_more == 1.0
        log_more = jnp.where(is_one, small, jnp.log(one_more) * small / jnp.where(is_one, 1.0, one_more - 1.0))
        dt_ref[rows, :] = jnp.maximum(z, 0.0) + log_more
        return 0

    lax.fori_loop(0, spans, project, 0)
    rim = copies.send(convp_ref.at[pl.ds(rows_all, FRONT)], rim_ref, PART)
    gates.hand_on()
    s_ref[...] = jnp.zeros_like(s_ref)
    dgain_ref[...] = jnp.zeros_like(dgain_ref)

    def convolve(c, _):
        rows = span_rows(c)
        wide = pl.ds(pl.multiple_of(c * SPAN, SPAN), SPAN + FRONT)
        masks = [jnp.broadcast_to(marks_ref[rows, j : j + 1], (SPAN, LANES)) for j in range(RIM)]
        for k in range(CHANS // LANES):
            lanes = slice(k * LANES, (k + 1) * LANES)
            values = convp_ref[wide, lanes].astype(f32)
            total = taps_ref[CONV : CONV + 1, lanes] + taps_ref[RIM : RIM + 1, lanes] * values[FRONT:]
            for j in range(RIM):
                first = FRONT - RIM + j
                total = total + taps_ref[j : j + 1, lanes] * values[first : first + SPAN] * masks[j]
            sig = 1.0 / (1.0 + jnp.exp(-total))
            value = (total * sig).astype(bf16)
            dtot_ref[rows, lanes] = sig * (1.0 + total * (1.0 - sig))
            if k < HALF // LANES:
                x_ref[rows, lanes] = value
            elif k == HALF // LANES:
                b_ref[rows, :] = value
            else:
                c_ref[rows, :] = value
        return 0

    lax.fori_loop(1, spans, convolve, 0)
    rim.wait_recv()
    convp_ref[0:FRONT, :] = jnp.where(p == 1, rim_ref[...].astype(f32), 0.0).astype(bf16)
    lax.fori_loop(0, 1, convolve, 0)
    gates.hand_on_last()

    def local_states(c, _):
        rows = span_rows(c)
        dt, cum = span_decay(dt_ref, heads_ref, c, 1)
        cum_ref[rows, :] = cum
        last = cum[SPAN - 1 : SPAN, :]
        end_weight = jnp.exp(last - cum) * dt * marks_ref[rows, 6:7]
        decay = jnp.exp(last) * carry_ref[pl.ds(c, 1), :]
        b = b_ref[rows, :]
        st_ref[c] = s_ref[...]
        for q in range(PAIRS):
            lanes = slice(q * LANES, (q + 1) * LANES)
            dyg_ref[rows, lanes] = (x_ref[rows, lanes].astype(f32) * own_pair(end_weight, 2 * q)).astype(bf16)
            s_ref[:, lanes] = s_ref[:, lanes] * own_pair(decay, 2 * q)
        s_ref[...] += dot(b, dyg_ref[rows, :], ((0,), (0,)))
        return 0

    lax.fori_loop(0, spans, local_states, 0)
    pass_ref[...] = s_ref[...].astype(bf16)
    state = copies.send(pass_ref, got_ref, PART)
    cots.hand_on()
    outs.hand_on()

    def inside(c, _):
        rows = span_rows(c)
        cum = cum_ref[rows, :]
        back_log = jnp.transpose(cum - jnp.log(dt_ref[rows, :]))
        scores = dot(c_ref[rows, :], b_ref[rows, :], ((1,), (1,)))
        early, late = slice(0, SPAN // 2), slice(SPAN // 2, SPAN)
        seg_col = segc_ref[pl.ds(pl.multiple_of(FRONT + c * SPAN, FRONT), SPAN), :]
        seg_row = segr_ref[pl.ds(c, 1), :]
        row = lax.broadcasted_iota(jnp.int32, (SPAN // 2, SPAN), 0)
        col = lax.broadcasted_iota(jnp.int32, (SPAN // 2, SPAN), 1)
        mask_early = (row >= col)[:, early] & (seg_col[early] == seg_row[:, early])
        mask_late = (row + SPAN // 2 >= col) & (seg_col[late] == seg_row)
        lane = lax.broadcasted_iota(jnp.int32, (SPAN, LANES), 1)
        for q in range(PAIRS):
            lanes = slice(q * LANES, (q + 1) * LANES)
            x = x_ref[rows, lanes]
            parts = []
            for h in (lane_of(2 * q), lane_of(2 * q + 1)):
                gap = cum[early, h : h + 1] - back_log[h : h + 1, early]
                weighted = scores[early, early] * jnp.exp(jnp.where(mask_early, gap, -1e30))
                y_early = dot(weighted.astype(bf16), x[early])
                gap = cum[late, h : h + 1] - back_log[h : h + 1, :]
                weighted = scores[late] * jnp.exp(jnp.where(mask_late, gap, -1e30))
                parts.append(jnp.concatenate([y_early, dot(weighted.astype(bf16), x)], axis=0))
            y_ref[rows, lanes] = jnp.where(lane < HEADDIM, parts[0], parts[1])
        return 0

    lax.fori_loop(0, spans, inside, 0)
    state.wait_recv()
    s_ref[...] = got_ref[...].astype(f32) * p.astype(f32)

    def across_spans(c, _):
        rows = span_rows(c)
        cum = cum_ref[rows, :]
        decay = jnp.exp(cum[SPAN - 1 : SPAN, :]) * carry_ref[pl.ds(c, 1), :]
        gain = jnp.exp(cum) * marks_ref[rows, 7:8]
        cc = c_ref[rows, :]
        for q in range(PAIRS):
            lanes = slice(q * LANES, (q + 1) * LANES)
            entering = s_ref[:, lanes]
            full = st_ref[c, :, lanes] + entering
            st_ref[c, :, lanes] = full
            y_ref[rows, lanes] += dot(cc, full.astype(bf16)) * own_pair(gain, 2 * q)
            s_ref[:, lanes] = entering * own_pair(decay, 2 * q)
        return 0

    lax.fori_loop(0, spans, across_spans, 0)
    gates.finish()
    copies.settle(gates.kept)

    def put_stat(k, c, column):
        wide = jnp.transpose(jnp.broadcast_to(column, (SPAN, LANES)))
        stat_ref[k, :, span_rows(c)] = wide[0:TILE, :]

    def exchange(k):
        return [copies.send(stat_ref.at[k], stats_ref.at[k, i], flips) for i, flips in enumerate(HOPS[1:])]

    def get_stat(k, c):
        cols = span_rows(c)
        total = stat_ref[k, :, cols] + stats_ref[k, 0, :, cols] + stats_ref[k, 1, :, cols] + stats_ref[k, 2, :, cols]
        return jnp.transpose(jnp.broadcast_to(total[0:1, :], (LANES, SPAN)))[:, 0:1] / D_INNER

    def values(rows, lanes):
        y_b = (y_ref[rows, lanes] + chans_ref[0:1, lanes] * x_ref[rows, lanes].astype(f32)).astype(bf16).astype(f32)
        gate = gate_ref[rows, lanes]
        sig = 1.0 / (1.0 + jnp.exp(-gate))
        return y_b, gate, sig

    def gating(c, _):
        rows = span_rows(c)
        xn = xn_ref[rows, :]
        total = jnp.zeros((SPAN, 1), f32)
        for k in range(HALF // 256):
            lanes = slice(k * 256, (k + 1) * 256)
            gate_ref[rows, lanes] = dot(xn, wgate_ref[:, lanes])
            y_b, gate, sig = values(rows, lanes)
            gated = y_b * (gate * sig)
            gated_ref[rows, lanes] = gated
            total = total + jnp.sum(gated * gated, axis=1, keepdims=True)
        put_stat(0, c, total)
        return 0

    lax.fori_loop(0, spans, gating, 0)
    outs.hand_on_last()
    squares = exchange(0)
    cots.finish()
    copies.settle(cots.own)
    outs.finish()
    copies.settle(outs_kept)

    def pull_out(c, _):
        rows = span_rows(c)
        back = back_ref[rows, :]
        total = jnp.zeros((SPAN, 1), f32)
        for k in range(HALF // 256):
            lanes = slice(k * 256, (k + 1) * 256)
            d_normed = dot(back, wout_ref[lanes, :], ((1,), (1,)))
            dn_ref[rows, lanes] = d_normed
            total = total + jnp.sum(gated_ref[rows, lanes] * (d_normed * chans_ref[1:2, lanes]), axis=1, keepdims=True)
        put_stat(1, c, total)
        return 0

    lax.fori_loop(0, spans, pull_out, 0)
    for copy in squares:
        copy.wait_recv()
    dots = exchange(1)

    def push_out(c, _):
        rows = span_rows(c)
        scale = lax.rsqrt(get_stat(0, c) + norm_eps)
        for k in range(HALF // 256):
            lanes = slice(k * 256, (k + 1) * 256)
            scaled = gated_ref[rows, lanes] * scale
            normed_ref[rows, lanes] = (scaled * chans_ref[1:2, lanes]).astype(bf16)
            dgain_ref[0:1, lanes] += jnp.sum(scaled * dn_ref[rows, lanes], axis=0, keepdims=True)
        normed = normed_ref[rows, :]
        for k in range(D // 256):
            cols = slice(k * 256, (k + 1) * 256)
            mix_ref[rows, cols] = dot(normed, wout_ref[:, cols]).astype(bf16)
        return 0

    copies.drain()
    lax.fori_loop(0, spans, push_out, 0)
    mixes = GroupScatter(copies, mix_ref, mix_bufs)
    mixes.to_t0(3)
    mixes.to_t0(1)
    for q in range(2):
        normed = normed_ref[:, q * HALF // 2 : (q + 1) * HALF // 2]
        for k in range(D // 512):
            cols = slice(k * 512, (k + 1) * 512)
            wout_ref[q * HALF // 2 : (q + 1) * HALF // 2, cols] = dot(normed, back_ref[:, cols], ((0,), (0,))).astype(bf16)
    go_halves = [wout_ref.at[pl.ds(pl.multiple_of(q * (HALF // 2), HALF // 2), HALF // 2)] for q in (1 - p, p)]
    g_out = GradientSum(copies, go_halves, out_rows, go_bufs, False)
    g_out.cores(0)
    g_out.cores(1)
    for copy in dots:
        copy.wait_recv()

    def back_gate(c, _):
        rows = span_rows(c)
        scale = lax.rsqrt(get_stat(0, c) + norm_eps)
        pulled = get_stat(1, c) * (scale * scale * scale)
        for k in range(HALF // LANES):
            lanes = slice(k * LANES, (k + 1) * LANES)
            y_b, gate, sig = values(rows, lanes)
            d_gated = scale * (dn_ref[rows, lanes] * chans_ref[1:2, lanes]) - gated_ref[rows, lanes] * pulled
            dy_ref[rows, lanes] = (d_gated * (gate * sig)).astype(bf16)
            dgate_ref[rows, lanes] = (d_gated * y_b * (sig * (1.0 + gate * (1.0 - sig)))).astype(bf16)
        return 0

    lax.fori_loop(0, spans, back_gate, 0)
    g_out.to_sides(0)
    s_ref[...] = jnp.zeros_like(s_ref)
    hsum_ref[...] = jnp.zeros_like(hsum_ref)
    dskip_ref[...] = jnp.zeros_like(dskip_ref)
    dtaps_ref[...] = jnp.zeros_like(dtaps_ref)

    def local_states(step, _):
        c = spans - 1 - step
        rows = span_rows(c)
        cum = cum_ref[rows, :]
        decay = jnp.exp(cum[SPAN - 1 : SPAN, :]) * carry_ref[pl.ds(c, 1), :]
        gain = jnp.exp(cum) * marks_ref[rows, 7:8]
        cc = c_ref[rows, :]
        for q in range(PAIRS):
            lanes = slice(q * LANES, (q + 1) * LANES)
            dyg = (dy_ref[rows, lanes].astype(f32) * own_pair(gain, 2 * q)).astype(bf16)
            dyg_ref[rows, lanes] = dyg
            ds = s_ref[:, lanes]
            dn_ref[pl.ds(pl.multiple_of(c * STATE, STATE), STATE), lanes] = ds
            s_ref[:, lanes] = ds * own_pair(decay, 2 * q)
        s_ref[...] += dot(cc, dyg_ref[rows, :], ((0,), (0,)))
        return 0

    lax.fori_loop(0, spans, local_states, 0)
    passb_ref[...] = s_ref[...].astype(bf16)
    state = copies.send(passb_ref, gotb_ref, PART)

    width = D // 4
    gg_halves = [back_ref.at[:, pl.ds(k * HALF, HALF)] for k in range(2)]
    g_gate = GradientSum(copies, gg_halves, own_rows, gg_bufs, True)

    def gate_gradient(far):
        for half in range(2):
            first = pl.multiple_of(((1 - p if far else p) * 2 + half) * width, width)
            piece = dot(xn_ref[:, pl.ds(first, width)], dgate_ref[...], ((0,), (0,)))
            gg_halves[0 if far else 1][half * width : (half + 1) * width, :] = piece.astype(bf16)

    gate_gradient(True)
    g_gate.cores(0)
    gate_gradient(False)
    g_gate.cores(1)
    g_gate.to_sides(0)
    g_out.to_part()
    g_out.to_sides(1)
    g_gate.to_sides(1)

    def inside(c, _):
        rows = span_rows(c)
        cum = cum_ref[rows, :]
        fore_log = jnp.transpose(cum)
        back_log = cum - jnp.log(dt_ref[rows, :])
        b = b_ref[rows, :]
        cc = c_ref[rows, :]
        scores = dot(b, cc, ((1,), (1,)))
        early, late = slice(0, SPAN // 2), slice(SPAN // 2, SPAN)
        seg_col = segc_ref[pl.ds(pl.multiple_of(FRONT + c * SPAN, FRONT), SPAN), :]
        seg_row = segr_ref[pl.ds(c, 1), :]
        row = lax.broadcasted_iota(jnp.int32, (SPAN // 2, SPAN), 0)
        col = lax.broadcasted_iota(jnp.int32, (SPAN // 2, SPAN), 1)
        mask_early = (col >= row) & (seg_col[early] == seg_row)
        mask_late = (col >= row)[:, early] & (seg_col[late] == seg_row[:, late])
        lane = lax.broadcasted_iota(jnp.int32, (SPAN, LANES), 1)
        d_early = jnp.zeros((SPAN // 2, SPAN), f32)
        d_late = jnp.zeros((SPAN // 2, SPAN // 2), f32)
        dc = dot(dyg_ref[rows, :], st_ref[c].astype(bf16), ((1,), (1,)))
        for q in range(PAIRS):
            lanes = slice(q * LANES, (q + 1) * LANES)
            x = x_ref[rows, lanes]
            dy = dy_ref[rows, lanes]
            xf = x.astype(f32)
            parts = []
            for k in range(2):
                h = lane_of(2 * q + k)
                gap = fore_log[h : h + 1, :] - back_log[early, h : h + 1]
                decay_early = jnp.exp(jnp.where(mask_early, gap, -1e30))
                gap = fore_log[h : h + 1, late] - back_log[late, h : h + 1]
                decay_late = jnp.exp(jnp.where(mask_late, gap, -1e30))
                dx_early = dot((scores[early] * decay_early).astype(bf16), dy)
                dx_late = dot((scores[late, late] * decay_late).astype(bf16), dy[late])
                parts.append(jnp.concatenate([dx_early, dx_late], axis=0))
                own = (lane < HEADDIM) if k == 0 else (lane >= HEADDIM)
                x_own = jnp.where(own, xf, 0.0).astype(bf16)
                d_early = d_early + dot(x_own[early], dy, ((1,), (1,))) * decay_early
                d_late = d_late + dot(x_own[late], dy[late], ((1,), (1,))) * decay_late
            dxi_ref[rows, lanes] = jnp.where(lane < HEADDIM, parts[0], parts[1])
            dskip_ref[0:1, lanes] += jnp.sum(dy.astype(f32) * xf, axis=0, keepdims=True)
        d_early_b, d_late_b = d_early.astype(bf16), d_late.astype(bf16)
        dn_ref[side_at(c, 0)] = jnp.concatenate([dot(d_early_b, cc), dot(d_late_b, cc[late])], axis=0)
        later = dot(d_early_b[:, late], b[early], ((0,), (0,))) + dot(d_late_b, b[late], ((0,), (0,)))
        earlier = dot(d_early_b[:, early], b[early], ((0,), (0,)))
        dn_ref[side_at(c, 1)] = dc + jnp.concatenate([earlier, later], axis=0)
        return 0

    lax.fori_loop(0, spans, inside, 0)
    mixes.to_t1()
    state.wait_recv()
    s_ref[...] = gotb_ref[...].astype(f32) * (1 - p).astype(f32)

    def across_spans(step, _):
        c = spans - 1 - step
        rows = span_rows(c)
        dt = dt_ref[rows, :]
        cum = cum_ref[rows, :]
        last = cum[SPAN - 1 : SPAN, :]
        end_weight = jnp.exp(last - cum) * dt * marks_ref[rows, 6:7]
        decay = jnp.exp(last) * carry_ref[pl.ds(c, 1), :]
        b = b_ref[rows, :]
        db = dn_ref[side_at(c, 0)]
        edges, ds_all = [], []
        for q in range(PAIRS):
            lanes = slice(q * LANES, (q + 1) * LANES)
            xf = x_ref[rows, lanes].astype(f32)
            dyf = dy_ref[rows, lanes].astype(f32)
            ew = own_pair(end_weight, 2 * q)
            dec = own_pair(decay, 2 * q)
            entering = s_ref[:, lanes]
            ds = dn_ref[pl.ds(pl.multiple_of(c * STATE, STATE), STATE), lanes] + entering
            s_ref[:, lanes] = entering * dec
            ds_b = ds.astype(bf16)
            dyg_ref[rows, lanes] = (xf * ew).astype(bf16)
            ds_all.append(ds_b)
            dx_state = dot(b, ds_b) * ew
            dx = dxi_ref[rows, lanes] + dx_state
            edges.append(
                jnp.sum(ds * st_ref[c, :, lanes], axis=0, keepdims=True) * dec
                + jnp.sum(dx_state * xf, axis=0, keepdims=True)
            )
            prod_ref[0:SPAN, lanes] = dyf * y_ref[rows, lanes]
            prod_ref[SPAN : 2 * SPAN, lanes] = xf * dx
            d_x = (dx + dyf * chans_ref[0:1, lanes]).astype(bf16).astype(f32)
            dtot_ref[rows, lanes] = d_x * dtot_ref[rows, lanes]
        db = db + dot(dyg_ref[rows, :], jnp.concatenate(ds_all, axis=1), ((1,), (1,)))
        dtot_ref[rows, HALF : HALF + STATE] = db * dtot_ref[rows, HALF : HALF + STATE]
        dtot_ref[rows, HALF + STATE :] = dn_ref[side_at(c, 1)] * dtot_ref[rows, HALF + STATE :]
        sums = own_sums(prod_ref[0 : 2 * SPAN, :])
        out_sum, in_sum = sums[:SPAN], sums[SPAN:]
        edge_sum = own_sums(jnp.broadcast_to(jnp.concatenate(edges, axis=1), (TILE, HALF)))[0:1]
        at_last = lax.broadcasted_iota(jnp.int32, (SPAN, LANES), 0) == SPAN - 1
        d_cum = out_sum - in_sum + jnp.where(at_last, edge_sum, 0.0)
        row = lax.broadcasted_iota(jnp.int32, (SPAN, SPAN), 0)
        col = lax.broadcasted_iota(jnp.int32, (SPAN, SPAN), 1)
        d_log = triangle_dot(col >= row, d_cum)
        z = z_ref[rows, :]
        small = jnp.exp(-jnp.abs(z))
        sig = jnp.where(z >= 0.0, 1.0, small) / (1.0 + small)
        ratio = jnp.where(dt > 1e-30, sig / jnp.maximum(dt, 1e-30), 1.0)
        d_dt = d_log * heads_ref[1:2, :] * sig + in_sum * ratio
        hsum_ref[0:1, :] += jnp.sum(d_log * dt, axis=0, keepdims=True)
        hsum_ref[1:2, :] += jnp.sum(d_dt, axis=0, keepdims=True)
        dmain_ref[rows, CHANS:MAIN] = head_lanes(d_dt, back=True).astype(bf16)
        return 0

    lax.fori_loop(0, spans, across_spans, 0)
    rims_ref[...] = dtot_ref[0:TILE, :]
    rim = copies.send(rims_ref, rimr_ref, PART)
    g_gate.to_part()

    def convolve(c, _):
        rows = span_rows(c)
        fore = pl.ds(pl.multiple_of(c * SPAN, SPAN), SPAN + FRONT)
        hind = pl.ds(pl.multiple_of(c * SPAN, SPAN), SPAN + TILE)
        masks = [jnp.broadcast_to(marks_ref[hind, j : j + 1], (SPAN + TILE, LANES)) for j in range(RIM)]
        for k in range(CHANS // LANES):
            lanes = slice(k * LANES, (k + 1) * LANES)
            later = dtot_ref[hind, lanes]
            earlier = convp_ref[fore, lanes].astype(f32)
            own = later[0:SPAN]
            d_conv = taps_ref[RIM : RIM + 1, lanes] * own
            dtaps_ref[RIM : RIM + 1, lanes] += jnp.sum(own * earlier[FRONT:], axis=0, keepdims=True)
            dtaps_ref[CONV : CONV + 1, lanes] += jnp.sum(own, axis=0, keepdims=True)
            for j in range(RIM):
                lag = RIM - j
                seen = later * masks[j]
                d_conv = d_conv + taps_ref[j : j + 1, lanes] * seen[lag : lag + SPAN]
                dtaps_ref[j : j + 1, lanes] += jnp.sum(
                    seen[0:SPAN] * earlier[FRONT - lag : FRONT - lag + SPAN], axis=0, keepdims=True
                )
            dmain_ref[rows, lanes] = d_conv.astype(bf16)
        return 0

    lax.fori_loop(0, spans - 1, convolve, 0)
    rim.wait_recv()
    dtot_ref[pl.ds(spans * SPAN, TILE), :] = jnp.where(p == 0, rimr_ref[...], 0.0)
    lax.fori_loop(spans - 1, spans, convolve, 0)

    mixes.left()
    dpre_ref[...] = jnp.zeros_like(dpre_ref)

    def token_grad(block, keep):
        rows = block_rows(block, tokens)
        d_main = dmain_ref[rows, :]
        d_gate = dgate_ref[rows, :]
        hid = h_ref[rows, :].astype(f32)
        scale = lax.rsqrt(jnp.sum(hid * hid, axis=1, keepdims=True) / D + norm_eps)
        for k in range(D // 256):
            cols = slice(k * 256, (k + 1) * 256)
            part = dot(d_main, win_ref[cols, :], ((1,), (1,))) + dot(d_gate, wgate_ref[cols, :], ((1,), (1,)))
            dpre_ref[0:1, cols] += jnp.sum(h_ref[rows, cols].astype(f32) * scale * part, axis=0, keepdims=True)
            if keep:
                first = k * 256 // HALF * tokens
                y_ref[first : first + tokens, k * 256 % HALF : k * 256 % HALF + 256] = part
            else:
                mix_ref[rows, cols] = part.astype(bf16)

    def store_gate(i, value):
        kept = pl.ds(2 * SPAN + i * own_rows, own_rows)
        gate_ref[kept, :] = value
        copies.keep(gate_ref.at[kept], ggate_out.at[blocks[i][0], blocks[i][1]])

    def store_main(i, value):
        for first, count in ((0, HALF), (HALF, MAIN - HALF)):
            kept = pl.ds((first // HALF * TP + i) * own_rows, own_rows)
            gated_ref[kept, 0:count] = value[:, first : first + count]
            copies.keep(
                gated_ref.at[kept, pl.ds(0, count)], gmain_out.at[blocks[i][0], blocks[i][1], :, pl.ds(first, count)]
            )

    total = g_out.total(0)
    for k in range(D // HALF):
        kept = pl.ds(2 * TP * own_rows + k * out_rows, out_rows)
        gated_ref[kept, :] = total[:, k * HALF : (k + 1) * HALF]
        copies.keep(gated_ref.at[kept], gout_out.at[:, pl.ds(k * HALF, HALF)])
    g_out.left()
    gm_halves = [wout_ref.at[:, pl.ds(0, MAIN)], gm_ref]

    def grad_half(far):
        part = 1 - p if far else p
        out = gm_halves[0 if far else 1]

        def piece(i, _):
            xn = xn_ref[:, pl.ds(pl.multiple_of((part * 2 + i) * width, width), width)]
            rows = pl.ds(pl.multiple_of(i * width, width), width)
            for k in range(MAIN // 384):
                cols = slice(k * 384, (k + 1) * 384)
                out[rows, cols] = dot(xn, dmain_ref[:, cols], ((0,), (0,))).astype(bf16)
            return 0

        lax.fori_loop(0, 2, piece, 0)

    grad_half(True)
    g_main = GradientSum(copies, gm_halves, own_rows, gm_bufs, True)
    g_main.cores(0)
    dxs = GroupScatter(copies, mix_ref, dx_bufs)
    token_grad(blocks[3], False)
    dxs.to_t0(3)
    g_main.to_sides(0)
    token_grad(blocks[1], False)
    dxs.to_t0(1)
    grad_half(False)
    g_main.cores(1)
    g_main.to_part((1,))
    g_gate.to_group(store_gate)
    g_main.to_part((2,))
    g_main.to_sides(1)
    g_main.to_part((3,))

    mixer = mix_ref[mixes.block(0), :].astype(f32) + mixes.finish()
    copies.left([mixes.last_copy])
    for k in range(D // HALF):
        kept = pl.ds(spans * STATE + k * tokens, tokens)
        dn_ref[kept, :] = mixer[:, k * HALF : (k + 1) * HALF]
        copies.keep(dn_ref.at[kept], mixer_out.at[:, pl.ds(k * HALF, HALF)])
    hid = h_ref[mixes.block(0), :].astype(f32)
    valid = validc_ref[...]
    counts = [jnp.sum(valid * jnp.sum(v * v, axis=1, keepdims=True), axis=0, keepdims=True) for v in (hid, mixer)]
    counts.append(jnp.sum(valid, axis=0, keepdims=True))
    scalars = jnp.zeros((1, LANES), f32)
    for k in range(3):
        scalars = jnp.where(lane == k, counts[k], scalars)
    box = box_ref.at[0]
    box[...] = jnp.zeros_like(box)
    box[OWN_SUMS : OWN_SUMS + 1, :] = scalars

    token_grad(blocks[2], False)
    g_main.to_part((0,))
    dxs.to_t1()
    token_grad(blocks[0], True)

    for k in range(D // LANES):
        box[k : k + 1, :] = dpre_ref[0:1, k * LANES : (k + 1) * LANES]
    for k in range(HALF // LANES):
        lanes = slice(k * LANES, (k + 1) * LANES)
        box[OWN_NORM + k : OWN_NORM + k + 1, :] = dgain_ref[0:1, lanes]
        for j in range(CONV + 1):
            row = OWN_TAP + j * (HALF // LANES) + k
            box[row : row + 1, :] = dtaps_ref[j : j + 1, lanes]
    for k in range(SIDE // LANES):
        lanes = slice(HALF + k * LANES, HALF + (k + 1) * LANES)
        for j in range(CONV + 1):
            row = OWN_SIDE + j * (SIDE // LANES) + k
            box[row : row + 1, :] = dtaps_ref[j : j + 1, lanes]
    hsum_ref[0:1, :] = hsum_ref[0:1, :] * heads_ref[1:2, :]
    hsum_ref[2:3, :] = own_sums(dskip_ref[...])[0:1, :]
    lane8 = lax.broadcasted_iota(jnp.int32, (TILE, LANES), 1)
    box[OWN_HEAD : OWN_HEAD + 3, :] = jnp.where(lane8 < HEADS, head_lanes(hsum_ref[...], back=True), 0.0)[0:3]

    def small_step(k, hops):
        return [copies.send(box_ref.at[k], boxes_ref.at[k, i], flips) for i, flips in enumerate(hops)]

    def small_add(k, sent):
        total = box_ref[k]
        for i, copy in enumerate(sent):
            copy.wait_recv()
            total = total + boxes_ref[k, i]
        box_ref[k + 1] = total

    small = small_step(0, (CORE, SIDEWAYS, SIDE_CORE))
    g_gate.finish(store_gate)
    small_add(0, small)
    small = small_step(1, (PART,))
    small_add(1, small)
    small = small_step(2, (T0, T1, DIAG))
    g_main.to_group(store_main)
    dx = dxs.finish()
    for k in range(D // HALF):
        kept = pl.ds(k * tokens, tokens)
        y_ref[kept, :] += dx[:, k * HALF : (k + 1) * HALF]
        copies.keep(y_ref.at[kept], dx_out.at[:, pl.ds(k * HALF, HALF)])
    small_add(2, small)
    total_ref[...] = jnp.zeros_like(total_ref)
    total_ref[0:NORM_ROW, :] = box_ref[3, 0:NORM_ROW]
    third = QUARTER // LANES
    runs = [(OWN_NORM, NORM_ROW)]
    runs += [(OWN_TAP + j * 2 * third, TAP_ROW + j * TAP_ROWS) for j in range(CONV + 1)]
    for i, block in enumerate(blocks):
        source = box_ref.at[2] if i == 0 else boxes_ref.at[2, i - 1]
        place_at = (block[0] * 2 + block[1]) * third
        for own, first in runs:
            for k in range(2 * third):
                row = first + k // third * (D_INNER // 2 // LANES) + place_at + k % third
                total_ref[pl.ds(row, 1), :] = source[own + k : own + k + 1, :]
    for j in range(CONV + 1):
        row, own = TAP_ROW + TAP_ROWS * j + D_INNER // LANES, OWN_SIDE + j * (SIDE // LANES)
        total_ref[row : row + SIDE // LANES, :] = box_ref[3, own : own + SIDE // LANES]
    d_rate, d_shift, d_skip = (
        jnp.broadcast_to(box_ref[3, OWN_HEAD + k : OWN_HEAD + k + 1], (TILE, LANES)) for k in range(3)
    )
    spill = LANES - 2 * HEADS
    joined = d_shift + pltpu.roll(d_rate, HEADS, 1) + jnp.where(lane8 >= 2 * HEADS, pltpu.roll(d_skip, 2 * HEADS, 1), 0.0)
    total_ref[HEAD_ROW : HEAD_ROW + 1, :] = joined[0:1]
    spilled = jnp.where(lane8 < HEADS - spill, pltpu.roll(d_skip, LANES - spill, 1), 0.0)
    total_ref[HEAD_ROW + 1 : HEAD_ROW + 2, :] = spilled[0:1]
    total_ref[SMALL_ROWS : SMALL_ROWS + 1, :] = box_ref[3, OWN_SUMS : OWN_SUMS + 1]
    g_main.finish(store_main)
    copies.drain()


def update_kernel(
    hid_ref, mixer_ref, dx_ref, back_ref, gmain_ref, ggate_ref, gout_ref, total_ref,
    inw_ref, inm_ref, inv_ref, outw_ref, outm_ref, outv_ref, small_ref,
    output_ref, gh_ref, inm_out, inv_out, inw_out, outm_out, outv_out, outw_out, rms_ref,
):
    hid = hid_ref[...].astype(f32)
    output_ref[...] = (hid + mixer_ref[...]).astype(bf16)
    scale = lax.rsqrt(jnp.sum(hid * hid, axis=1, keepdims=True) / D + norm_eps)
    pulled = 0.0
    for k in range(NORM_ROW):
        lanes = slice(k * LANES, (k + 1) * LANES)
        d_pre = dx_ref[:, lanes] * small_ref[k : k + 1, :]
        gh_ref[:, lanes] = back_ref[:, lanes].astype(f32) + scale * d_pre
        pulled = pulled + jnp.sum(hid[:, lanes] * d_pre, axis=1, keepdims=True)
    gh_ref[...] -= hid * (pulled / D * (scale * scale * scale))

    def update(refs, outs, cols, grad, rate=0.02, decay=0.1):
        weight, moment, second = (ref[:, cols] for ref in refs)
        for out, value in zip(outs, adamw(weight, moment, second, grad, rate, decay)):
            out[:, cols] = value

    every = slice(None)
    update((outw_ref, outm_ref, outv_ref), (outm_out, outv_out, outw_out), every, gout_ref[...])
    in_refs, in_outs = (inw_ref, inm_ref, inv_ref), (inm_out, inv_out, inw_out)
    for j in range(TP):
        for k, chans in enumerate(own_chans(j)):
            part = slice(k * QUARTER, (k + 1) * QUARTER)
            update(in_refs, in_outs, chans, ggate_ref[j // 2, j % 2, :, part])
            scan = slice(D_INNER + chans.start, D_INNER + chans.stop)
            update(in_refs, in_outs, scan, gmain_ref[j // 2, j % 2, :, part])
    rest_grad = gmain_ref[0, 0, :, HALF:] + gmain_ref[0, 1, :, HALF:] + gmain_ref[1, 0, :, HALF:] + gmain_ref[1, 1, :, HALF:]
    first = 2 * D_INNER
    update(in_refs, in_outs, slice(first, first + SIDE), rest_grad[:, :SIDE])
    update(in_refs, in_outs, slice(first + SIDE, first + SIDE + HEADS), rest_grad[:, SIDE : SIDE + HEADS])

    @pl.when(pl.program_id(0) == 0)
    def _():
        totals = total_ref[SMALL_ROWS:, :]
        rms_ref[...] = jnp.sqrt(totals / (totals[0:1, 2:3] * D))


def linked(kernel, name, collective_id, in_specs, outs, scratch):
    return pl.pallas_call(
        kernel,
        name=name,
        grid=(1,),
        in_specs=in_specs,
        out_shape=tuple(o for o, _ in outs),
        out_specs=tuple(s for _, s in outs),
        scratch_shapes=scratch,
        compiler_params=pltpu.CompilerParams(
            collective_id=collective_id, has_side_effects=True, vmem_limit_bytes=VMEM_LIMIT
        ),
    )


def shards_linked(
    hidden, cotangent, segments, valid, in_w, in_m, in_v, out_w, out_m, out_v, small_w, small_m, small_v,
):
    own_rows, out_rows = in_w.shape[0], out_w.shape[0]
    tok_rows = hidden.shape[1]
    rows = tok_rows * TP
    spans = rows // SPAN
    small_size = small_w.shape[0]

    def small_box(array):
        return jnp.pad(array, (0, SMALL_ROWS * LANES - small_size)).reshape(SMALL_ROWS, LANES)

    small_rows = small_box(small_w)

    wide = (rows, D)
    half = (rows, HALF)
    lanes = (rows, LANES)
    side = (rows, STATE)
    state = (STATE, HALF)
    main_outs = (
        (shape((tok_rows, D), bf16), HBM),
        (shape((tok_rows, D), f32), HBM),
        (shape((2, 2, own_rows, HALF), f32), HBM),
        (shape((2, 2, own_rows, MAIN), f32), HBM),
        (shape((tok_rows, D), f32), HBM),
        (shape((out_rows, D), f32), HBM),
        (shape((BOX_ROWS, LANES), f32), VMEM),
    )
    main_scratch = (
        (wide, bf16),
        (wide, bf16),
        ((D, MAIN), bf16),
        ((rows + FRONT, CHANS), bf16),
        (half, bf16),
        (side, bf16),
        (side, bf16),
        ((rows + FRONT, CHANS), f32),
        (lanes, f32),
        (lanes, f32),
        (lanes, f32),
        (half, f32),
        ((spans, *state), f32),
        ((D, HALF), bf16),
        ((HALF, D), bf16),
        (wide, bf16),
        (half, bf16),
        (wide, bf16),
        (half, bf16),
        (half, bf16),
        ((rows, MAIN), bf16),
        ((TILE, HALF), f32),
        ((TILE, CHANS), f32),
        ((TILE, LANES), f32),
        ((TILE, HALF), f32),
        ((rows + TILE, TILE), f32),
        ((spans, LANES), f32),
        (state, f32),
        (state, bf16),
        (state, bf16),
        ((FRONT, CHANS), bf16),
        (half, f32),
        (half, f32),
        (half, f32),
        ((2, TILE, rows), f32),
        ((2, 3, TILE, rows), f32),
        (half, bf16),
        (state, bf16),
        (state, bf16),
        ((TILE, CHANS), f32),
        ((TILE, CHANS), f32),
        ((TILE, LANES), f32),
        ((TILE, HALF), f32),
        ((TILE, CHANS), f32),
        ((TILE, D), f32),
        ((4, OWN_ROWS, LANES), f32),
        ((3, 3, OWN_ROWS, LANES), f32),
        ((D // 2, MAIN), bf16),
        ((rows + 2 * FRONT, 1), f32),
        ((TILE, SPAN), f32),
        ((tok_rows, 1), f32),
    )
    side_cols = pl.BlockSpec((own_rows, MAIN - HALF), lambda i: (0, 2 * D_INNER // (MAIN - HALF)))
    back_own, mixer, g_gate, g_main, d_x_normed, g_out, totals = linked(
        functools.partial(main_kernel, spans), "main", 1, [*[HBM] * 4, side_cols, *[VMEM] * 3], main_outs,
        [
            *[pltpu.VMEM(dims, dtype) for dims, dtype in main_scratch],
            *sum_buffers(out_rows, D, False),
            *sum_buffers(own_rows, HALF, True),
            *sum_buffers(own_rows, MAIN, True),
            *scatter_buffers(tok_rows),
            *scatter_buffers(tok_rows),
            *sems(200, 48),
        ],
    )(hidden[0], in_w, out_w, cotangent[0], in_w, valid, small_rows, segments)

    steps = own_rows // (3 * TILE)

    def cut(dims, axis=0):
        block = tuple(size // steps if k == axis else size for k, size in enumerate(dims))
        return pl.BlockSpec(block, lambda i: tuple(i if k == axis else 0 for k in range(len(dims))))

    def fixed(dims):
        return pl.BlockSpec(dims, lambda i: (0, 0))

    tokens, matrix_in, matrix_out, small_dims = (tok_rows, D), in_w.shape, out_w.shape, (SMALL_ROWS, LANES)
    out_dims = [tokens] * 2 + [matrix_in] * 3 + [matrix_out] * 3
    (
        output, grad_hidden, in_m_new, in_v_new, in_w_new, out_m_new, out_v_new, out_w_new, rms,
    ) = pl.pallas_call(
        update_kernel,
        name="update",
        grid=(steps,),
        in_specs=[
            *[cut(tokens)] * 4,
            cut(g_main.shape, 2),
            cut(g_gate.shape, 2),
            cut(matrix_out),
            fixed((BOX_ROWS, LANES)),
            *[cut(matrix_in)] * 3,
            *[cut(matrix_out)] * 3,
            fixed(small_dims),
        ],
        out_shape=[
            *[shape(dims, bf16 if k == 0 else f32) for k, dims in enumerate(out_dims)],
            shape((TILE, LANES), f32),
        ],
        out_specs=[*[cut(dims) for dims in out_dims], fixed((TILE, LANES))],
        compiler_params=pltpu.CompilerParams(vmem_limit_bytes=VMEM_LIMIT),
    )(
        hidden[0], mixer, d_x_normed, back_own, g_main, g_gate, g_out, totals,
        in_w, in_m, in_v, out_w, out_m, out_v, small_rows,
    )
    small_grad = totals[:SMALL_ROWS].reshape(-1)[:small_size]
    small_m_new, small_v_new, small_w_new = adamw(small_w, small_m, small_v, small_grad, 0.2, 0.0)
    return (
        output[None], grad_hidden[None], in_m_new, in_v_new, in_w_new, out_m_new, out_v_new, out_w_new,
        small_m_new, small_v_new, small_w_new, rms[0, :2],
    )


def solution(mesh):
    seq, wt = mesh.shape["seq"], mesh.shape["wt"]
    split = Mesh(mesh.devices.reshape(seq // TP, 2, 2, wt // 2, 2), EVERYONE)
    streams = ("w1", "w0")
    tokens = ("part", "t1", "t0")
    matrix = P(EVERYONE, None)
    stream = P(streams, tokens, None)
    size = mesh.devices.size
    fits = seq == 2 * TP and wt == 4 and D // size % 16 == 0 and D_INNER // size % 16 == 0
    return jax.shard_map(
        shards_linked if fits else shards_general,
        mesh=split,
        in_specs=(
            stream, stream, P(streams, None), P(streams, tokens), matrix, matrix, matrix, matrix, matrix, matrix, P(), P(), P(),
        ),
        out_specs=(stream, stream, matrix, matrix, matrix, matrix, matrix, matrix, P(), P(), P(), P()),
        check_vma=False,
    )
```
